32 devices in a mesh: groups: 2 (over y), down: 4 (over z), cross: 2 (over x), depth: 2 (over core).
Axes of the slice: x: 2, y: 2, z: 4, core: 2. Of those that a mesh axis runs over, the one named last changes fastest.
Arguments:
- positions: float32 [3, 16, 4, 4, 128], P(None, ('groups', 'down'), 'cross', 'depth'), parts along dimension 1, may hold values from -0.5 to 0.5
- velocities: float32 [3, 16, 4, 4, 128], P(None, ('groups', 'down'), 'cross', 'depth'), parts along dimension 1, may hold values from -6 to 6
- sphere_radii: float32 [16, 4, 4, 128], P(('groups', 'down'), 'cross', 'depth'), parts along dimension 0, may hold values from 0.08 to 0.12
- counts: int32 [16, 4, 4], P(('groups', 'down'), 'cross', 'depth'), parts along dimension 0, may hold values from 32 to 128, as said below
- coefficients: float32 [48], replicated, may hold values from -0.6 to 0.6
Outputs:
- velocity_new: float32 [3, 16, 4, 4, 128], P(None, ('groups', 'down'), 'cross', 'depth'), parts along dimension 1
- contact_force: float32 [3, 16, 4, 4, 128], P(None, ('groups', 'down'), 'cross', 'depth'), parts along dimension 1
- residual_field: float32 [16, 4, 4], P(('groups', 'down'), 'cross', 'depth'), parts along dimension 0
- gram_matrix: float32 [96, 48], P('groups'), parts along dimension 0
- moment_vector: float32 [96], P('groups'), parts along dimension 0
The draws below stay inside these ranges and needn't reach their ends.
There are 2 independent parts, one for each index of `groups`. The reference program is written for one: setup_inputs(seed, part) draws one part's arguments, and reference() takes and returns one part's arrays. A program takes and returns all parts, laid end to end along the dimension named above; an argument that names none is the same for every part. Nothing has to cross between parts.
Inputs may be any that keep to these rules, and one draw needn't show every extreme that they name: `counts`: slots 0 to count - 1 of a cell hold spheres, the rest are padding; every cell of the bottom depth layer holds 128.
All inputs are finite; a program needn't handle non-finite values.
Results may differ from the reference program's by a relative error of at most 0.0003.
Values sent between devices are 32-bit elements; how exact they have to be, the bound alone decides.
No kernel may reach another device: no remote copies, remote signals or barrier semaphores. Data moves between devices by JAX's collectives and lax.ppermute only.
A program may use at most 128 MiB of HBM per device.

```python
import jax
import jax.numpy as jnp
from jax import lax

S = 128
CX = 2
TERMS = 48
NX = 8
NY = 4
NZ = 4


def draw_counts(key, part):
    key = jax.random.fold_in(key, 11)
    height = lax.broadcasted_iota(jnp.int32, (NX, NY, NZ), 2)
    ceiling = S - height * S // (2 * NZ)
    lowest = S // 4
    random_bits = jax.random.randint(key, (NX, NY, NZ), 0, 1 << 20)
    filled = lowest + random_bits % (ceiling - lowest + 1)
    return jnp.where(height == 0, S, filled).astype(jnp.int32)


def level_of(own_key, dims, cuts, smallest, largest):
    gain = 1.0
    for dim, parts in cuts:
        heights = jax.random.uniform(jax.random.fold_in(jax.random.fold_in(own_key, 6), dim), (parts,), jnp.float32, smallest / len(cuts), largest / len(cuts))
        gain = gain * jnp.repeat(jnp.exp(heights), dims[dim] // parts).reshape((-1,) + (1,) * (len(dims) - 1 - dim))
    return gain


def scatter_about(own_key, dims, spread, limit, pieces=(), held_as=jnp.bfloat16):
    entries = jax.random.normal(own_key, dims, jnp.float32) * spread
    if len(pieces) > 0:
        entries = level_of(own_key, dims, pieces, -0.22, 0.18) * entries
    return jnp.clip(entries, min=-limit, max=limit).astype(held_as)


def setup_inputs(seed: int = 0, part: int = 0) -> dict:
    seeds = jax.random.split(jax.random.key(seed), 6)
    part_keys = jax.random.split(jax.random.fold_in(seeds[5], part), 6)
    positions = jnp.clip(jax.random.uniform(part_keys[0], (3, NX, NY, NZ, S), jnp.float32, -0.5, 0.5) * level_of(part_keys[0], (3, NX, NY, NZ, S), ((1, 4), (2, 2), (3, 2)), -0.4, 0.0), -0.5, 0.5)
    velocities = scatter_about(part_keys[1], (3, NX, NY, NZ, S), 1.0, 6.0, ((1, 4), (2, 2), (3, 2)), jnp.float32)
    sphere_radii = jnp.clip(0.08 + 0.04 * jax.random.uniform(part_keys[2], (NX, NY, NZ, S), jnp.float32) ** level_of(part_keys[2], (NX, NY, NZ, S), ((0, 4), (1, 2), (2, 2)), -0.2, 0.2), 0.08, 0.12)
    counts = draw_counts(jax.random.fold_in(jax.random.fold_in(seeds[5], part), 71), part)
    coefficients = scatter_about(seeds[4], (TERMS,), 0.1, 0.6, (), jnp.float32)
    return dict(positions=positions, velocities=velocities, sphere_radii=sphere_radii, counts=counts, coefficients=coefficients)


STIFFNESS = 100.0
DAMPING = 20.0
TIME_STEP = 0.05
KERNEL_WIDTH = 0.4
KERNEL_NORM = 64.0
SOFTENING = 0.0001
RADIUS_REF = 0.1
MASS_SHIFT = 0.1
NEIGHBOURS = tuple(((shift_x, shift_y, shift_z) for shift_x in (-1, 0, 1) for shift_y in (-1, 0, 1) for shift_z in (-1, 0, 1)))
PAIR_LIST = ((0, 0), (0, 1), (0, 2), (1, 1), (1, 2), (2, 2))

def contact(extended):
    size_x = extended.shape[1] - 2
    size_y = extended.shape[2] - 2
    size_z = extended.shape[3] - 2
    slot_count = extended.shape[4]
    centre = extended[:, 1:size_x + 1, 1:size_y + 1, 1:size_z + 1]
    self_mask = 1.0 - jnp.eye(slot_count, dtype=jnp.float32)
    totals = jnp.zeros((10,) + centre.shape[1:], jnp.float32)
    for shift_x, shift_y, shift_z in NEIGHBOURS:
        beside = extended[:, 1 + shift_x:1 + shift_x + size_x, 1 + shift_y:1 + shift_y + size_y, 1 + shift_z:1 + shift_z + size_z]
        places = jnp.stack([beside[0] + shift_x, beside[1] + shift_y, beside[2] + shift_z])
        branch = centre[0:3, ..., :, None] - places[..., None, :]
        relative = centre[3:6, ..., :, None] - beside[3:6, ..., None, :]
        squared = lax.optimization_barrier(jnp.sum(branch * branch, axis=0))
        distance = jnp.sqrt(squared + SOFTENING)
        closing = -lax.optimization_barrier(jnp.sum(relative * branch, axis=0)) / distance
        correlation = jnp.maximum(centre[6][..., :, None] + beside[6][..., None, :] - distance, 0.0)
        weight = correlation * (STIFFNESS + DAMPING * closing) / distance
        weight = weight * centre[7][..., :, None] * beside[7][..., None, :]
        if shift_x == 0 and shift_y == 0 and (shift_z == 0):
            weight = weight * self_mask
        columns = jnp.stack([jnp.ones_like(places[0]), places[0], places[1], places[2], places[0] * places[0], places[0] * places[1], places[0] * places[2], places[1] * places[1], places[1] * places[2], places[2] * places[2]])
        totals = totals + jnp.einsum('xyzij,kxyzj->kxyzi', weight, columns, precision=lax.Precision.HIGHEST)
    centres = centre[0:3]
    force = jnp.stack([centres[axis_id] * totals[0] - totals[1 + axis_id] for axis_id in range(3)])
    stress = jnp.stack([0.5 * (centres[left_index] * centres[right_index] * totals[0] - centres[left_index] * totals[1 + right_index] - centres[right_index] * totals[1 + left_index] + totals[4 + pair_id]) for pair_id, (left_index, right_index) in enumerate(PAIR_LIST)])
    return (force, stress)

def coarse(extended, moments):
    size_x = extended.shape[1] - 2
    size_y = extended.shape[2] - 2
    size_z = extended.shape[3] - 2
    fields = jnp.zeros((moments.shape[0], size_x, size_y, size_z), jnp.float32)
    for shift_x, shift_y, shift_z in NEIGHBOURS:
        beside = extended[:, 1 + shift_x:1 + shift_x + size_x, 1 + shift_y:1 + shift_y + size_y, 1 + shift_z:1 + shift_z + size_z]
        beside_moment = moments[:, 1 + shift_x:1 + shift_x + size_x, 1 + shift_y:1 + shift_y + size_y, 1 + shift_z:1 + shift_z + size_z]
        squared = (beside[0] + shift_x) ** 2 + (beside[1] + shift_y) ** 2 + (beside[2] + shift_z) ** 2
        kernel = jnp.exp(-squared / (2.0 * KERNEL_WIDTH * KERNEL_WIDTH)) * beside[7] / KERNEL_NORM
        fields = fields + lax.optimization_barrier(jnp.sum(kernel * beside_moment, axis=-1))
    return fields

def library(padded, stress):
    slopes = [(padded[:, 2:, 1:-1, 1:-1] - padded[:, :-2, 1:-1, 1:-1]) * 0.5, (padded[:, 1:-1, 2:, 1:-1] - padded[:, 1:-1, :-2, 1:-1]) * 0.5, (padded[:, 1:-1, 1:-1, 2:] - padded[:, 1:-1, 1:-1, :-2]) * 0.5]
    centre = padded[:, 1:-1, 1:-1, 1:-1]
    density = centre[0]
    strain = [[0.5 * (slopes[left_index][1 + right_index] + slopes[right_index][1 + left_index]) for right_index in range(3)] for left_index in range(3)]
    divergence = strain[0][0] + strain[1][1] + strain[2][2]
    rate_sum = jnp.zeros_like(density)
    for left_index in range(3):
        for right_index in range(3):
            entry = strain[left_index][right_index]
            if left_index == right_index:
                entry = entry - divergence / 3.0
            rate_sum = rate_sum + entry * entry
    shear_rate = jnp.sqrt(2.0 * rate_sum + 0.01)
    pressure = (stress[0] + stress[3] + stress[5]) / 3.0
    deviator = (stress[0] - pressure) ** 2 + (stress[3] - pressure) ** 2 + (stress[5] - pressure) ** 2 + 2.0 * (stress[1] ** 2 + stress[2] ** 2 + stress[4] ** 2)
    shear_stress = jnp.sqrt(0.5 * deviator + 0.01)
    pressure_scale = jnp.sqrt(pressure * pressure + 1.0)
    friction = shear_stress / pressure_scale
    inertial = shear_rate / jnp.sqrt(pressure_scale)
    features = [density, pressure / pressure_scale, shear_rate, inertial, divergence, slopes[0][0], slopes[1][0], slopes[2][0]]
    library_terms = list(features)
    for left_index in range(8):
        for right_index in range(left_index, 8):
            library_terms.append(features[left_index] * features[right_index])
    for left_index in range(1, 5):
        library_terms.append(features[left_index] ** 3)
    return (friction, jnp.stack(library_terms))

def pad_field(source, axis_first):
    widths = [(0, 0)] * source.ndim
    widths[axis_first] = (1, 1)
    widths[axis_first + 1] = (1, 1)
    wrapped = jnp.pad(source, widths, mode='wrap')
    wall_pad = [(0, 0)] * source.ndim
    wall_pad[axis_first + 2] = (1, 1)
    return jnp.pad(wrapped, wall_pad)

def grid_contact(state):
    extended = pad_field(state, 1)
    blocks = NX // CX

    def one_block(block_id):
        piece = lax.dynamic_slice_in_dim(extended, block_id * CX, CX + 2, 1)
        return contact(piece)
    force, stress = lax.map(one_block, jnp.arange(blocks, dtype=jnp.int32))
    force = jnp.transpose(force, (1, 0, 2, 3, 4, 5)).reshape(3, NX, NY, NZ, S)
    stress = jnp.transpose(stress, (1, 0, 2, 3, 4, 5)).reshape(6, NX, NY, NZ, S)
    return (force, stress)

def reference(positions, velocities, sphere_radii, counts, coefficients):
    slot_ids = lax.broadcasted_iota(jnp.int32, sphere_radii.shape, 3)
    live_slots = (slot_ids < counts[..., None]).astype(jnp.float32)
    sphere_mass = live_slots * (sphere_radii / RADIUS_REF) ** 3
    safe_mass = sphere_mass + 1.0 - live_slots
    state_start = jnp.concatenate([positions, velocities, sphere_radii[None], live_slots[None]], axis=0)
    force_start, unused = grid_contact(state_start)
    velocity_new = velocities + TIME_STEP * force_start / safe_mass
    position_new = positions + TIME_STEP * velocity_new
    state_next = jnp.concatenate([position_new, velocity_new, sphere_radii[None], live_slots[None]], axis=0)
    force_next, stress = grid_contact(state_next)
    moments = jnp.concatenate([sphere_mass[None], sphere_mass * velocity_new, stress], axis=0)
    fields = coarse(pad_field(state_next, 1), pad_field(moments, 1))
    density = fields[0]
    node_values = jnp.concatenate([density[None], fields[1:4] / (density + MASS_SHIFT)], axis=0)
    friction, library_terms = library(pad_field(node_values, 1), fields[4:10])
    residual_field = friction - lax.optimization_barrier(jnp.sum(coefficients[:, None, None, None] * library_terms, axis=0))
    node_total = NX * NY * NZ
    gram_matrix = jnp.einsum('kxyz,lxyz->kl', library_terms, library_terms, precision=lax.Precision.HIGHEST) / node_total
    moment_vector = jnp.einsum('kxyz,xyz->k', library_terms, friction, precision=lax.Precision.HIGHEST) / node_total
    return (velocity_new, force_next, residual_field, gram_matrix, moment_vector)
```

```python
import functools

import jax
import jax.numpy as jnp
from jax import lax
from jax.experimental import pallas as pl
from jax.experimental.pallas import tpu as pltpu
from jax.sharding import PartitionSpec as P

STIFFNESS = 100.0
DAMPING = 20.0
TIME_STEP = 0.05
KERNEL_WIDTH = 0.4
KERNEL_NORM = 64.0
SOFTENING = 0.0001
RADIUS_REF = 0.1
MASS_SHIFT = 0.1
DEAD = -1000.0
TERMS = 48
S = 128
F32 = jnp.float32
BF16 = jnp.bfloat16
PAIR_LIST = ((0, 0), (0, 1), (0, 2), (1, 1), (1, 2), (2, 2))
VMEM_SPEC = pl.BlockSpec(memory_space=pltpu.VMEM)
SMEM_SPEC = pl.BlockSpec(memory_space=pltpu.SMEM)
VMEM_LIMIT = 48 * 1024 * 1024


def split3(value):
    high = value.astype(BF16).astype(F32)
    rest = value - high
    middle = rest.astype(BF16).astype(F32)
    return high, middle, rest - middle


def row_ids(shape):
    return lax.broadcasted_iota(jnp.int32, shape, 0)


def pack_kernel(counts, positions, velocities, radii, own, inner):
    depth = lax.axis_index("depth")
    lanes = lax.broadcasted_iota(jnp.int32, (1, S), 1)
    for a in range(2):
        for b in range(2):
            for z in range(2):
                for k in range(3):
                    own[a, b, z, k : k + 1, :] = positions[k, a, b, z : z + 1, :]
                    own[a, b, z, 3 + k : 4 + k, :] = velocities[k, a, b, z : z + 1, :]
                live = lanes < counts[a, b, z]
                own[a, b, z, 6:7, :] = jnp.where(live, radii[a, b, z : z + 1, :], DEAD)
                own[a, b, z, 7:8, :] = jnp.zeros((1, S), F32)
            inner[a, b] = own[a, b, 1 - depth]


def local_state(raw, centre):
    rows = row_ids(raw.shape)
    shift = jnp.where(rows == 0, centre[0], jnp.where(rows == 1, centre[1], centre[2]))
    return jnp.where(rows < 3, raw + shift, raw)


def dots_of(state):
    p = [state[k : k + 1] for k in range(3)]
    v = [state[3 + k : 4 + k] for k in range(3)]
    square = p[0] * p[0] + p[1] * p[1] + p[2] * p[2]
    cross = p[0] * v[0] + p[1] * v[1] + p[2] * v[2]
    return square, cross


def neighbour_side(raw, centre, with_stress):
    state = local_state(raw, centre)
    rows = row_ids(state.shape)
    square, cross = dots_of(state)
    features = jnp.where(rows == 6, square, jnp.where(rows == 7, cross, state))
    high, middle, low = split3(features)
    ones = jnp.where(rows < 3, 1.0, 0.0).astype(F32)
    radius = jnp.where(rows == 0, raw[6:7], 0.0)
    stacked = jnp.concatenate([high, high, high, middle, middle, low, ones, radius], axis=0)
    turned = jnp.transpose(stacked)
    spread = jnp.broadcast_to(turned[:, 56:57], (S, S))
    p = [state[k : k + 1] for k in range(3)]
    first = jnp.where(
        rows == 0, 1.0, jnp.where(rows == 1, p[0], jnp.where(rows == 2, p[1], jnp.where(rows == 3, p[2], 0.0)))
    )
    if with_stress:
        for place, (left, right) in enumerate(PAIR_LIST[:4]):
            first = jnp.where(rows == 4 + place, p[left] * p[right], first)
        second = jnp.where(rows == 0, p[1] * p[2], jnp.where(rows == 1, p[2] * p[2], 0.0))
        first = jnp.concatenate([first, second], axis=0)
    parts = list(split3(first))
    if not with_stress:
        parts.append(jnp.zeros_like(first))
    columns = jnp.concatenate(parts, axis=0).astype(BF16)
    return turned.astype(BF16), spread, jnp.concatenate([columns, columns], axis=1)


def centre_side(state):
    rows = row_ids(state.shape)
    square, cross = dots_of(state)
    turned = pltpu.roll(state, 3, 0)
    back = pltpu.roll(state, 5, 0)
    near = jnp.where(rows < 3, -2.0 * state, jnp.where(rows == 6, 1.0, 0.0))
    pull = jnp.where(
        rows < 3,
        DAMPING * back,
        jnp.where(rows < 6, DAMPING * turned, jnp.where(rows == 7, -DAMPING, 0.0)),
    )
    out = []
    for table, constant in ((near, square + SOFTENING), (pull, -DAMPING * cross)):
        high, middle, low = split3(table)
        c_high, c_middle, c_low = split3(constant)
        tail = jnp.where(
            rows == 0, c_high, jnp.where(rows == 1, c_middle, jnp.where(rows == 2, c_low, 0.0))
        )
        out.append(
            jnp.concatenate(
                [high, middle, low, high, middle, high, tail, jnp.zeros_like(tail)], axis=0
            ).astype(BF16)
        )
    return out


def pair_tile(left, spread, columns, right, radius, self_lane):
    width = radius.shape[1]
    product = lax.dot_general(
        left, right, (((1,), (0,)), ((), ())), preferred_element_type=F32
    )
    squared = jnp.maximum(product[:, :width], SOFTENING)
    inverse = lax.rsqrt(squared)
    reach = jnp.concatenate([spread] * (width // S), axis=1) + radius
    weight = jnp.maximum(reach * inverse - 1.0, 0.0) * (
        STIFFNESS + product[:, width:] * inverse
    )
    if self_lane is not None:
        lanes = lax.broadcasted_iota(jnp.int32, weight.shape, 1)
        weight = jnp.where(lanes == row_ids(weight.shape) + self_lane, 0.0, weight)
    high = weight.astype(BF16)
    low = (weight - high.astype(F32)).astype(BF16)
    return lax.dot_general(
        columns,
        jnp.concatenate([high, low], axis=0),
        (((1,), (0,)), ((), ())),
        preferred_element_type=F32,
    )


def neighbour_cells(pieces):
    own, depth_halo, cross_before, cross_after, diag_before, diag_after, x_before, x_after = pieces

    def cell(x, y, slot):
        if x in (0, 3):
            face = x_before if x == 0 else x_after
            if y in (1, 2):
                return face[(y - 1) * 2 + slot] if slot < 2 else face[4 + y - 1]
            side = 6 if y == 0 else 8
            return face[side + slot] if slot < 2 else face[10 + (0 if y == 0 else 1)]
        if y in (1, 2):
            return own[x - 1, y - 1, slot] if slot < 2 else depth_halo[x - 1, y - 1]
        if slot < 2:
            return (cross_before if y == 0 else cross_after)(x - 1, slot)
        return (diag_before if y == 0 else diag_after)(x - 1)

    return cell


def contact_all(cell, depth, with_stress, left_ref, spread_ref, columns_ref, finish, radius_of):
    halo_z = 1.5 - 3.0 * depth.astype(F32)
    for x in range(4):
        for y in range(4):
            for slot in range(3):
                centre = (x - 1.5, y - 1.5, slot - 0.5 if slot < 2 else halo_z)
                place = (x * 4 + y) * 3 + slot
                left, spread, columns = neighbour_side(cell(x, y, slot), centre, with_stress)
                left_ref[place] = left
                spread_ref[place] = spread
                columns_ref[place] = columns
    inner = 1 - depth

    def one_column(step, carry):
        a = step // 2
        b = step % 2
        raws = [radius_of[a, b, z] for z in range(2)]
        states = []
        for z in range(2):
            states.append(
                local_state(raws[z], (a.astype(F32) - 0.5, b.astype(F32) - 0.5, z - 0.5))
            )
        sides = [centre_side(state) for state in states]
        right = jnp.concatenate([sides[0][0], sides[1][0], sides[0][1], sides[1][1]], axis=1)
        radius = jnp.concatenate([raws[0][6:7], raws[1][6:7]], axis=1)
        total = None
        for dx in range(3):
            for dy in range(3):
                for slot in range(2):
                    place = ((a + dx) * 4 + (b + dy)) * 3 + slot
                    self_lane = slot * S if (dx == 1 and dy == 1) else None
                    part = pair_tile(
                        left_ref[place], spread_ref[place], columns_ref[place], right, radius, self_lane
                    )
                    total = part if total is None else total + part
        upper = inner == 1
        right_inner = jnp.concatenate(
            [jnp.where(upper, sides[1][k].astype(F32), sides[0][k].astype(F32)).astype(BF16) for k in range(2)],
            axis=1,
        )
        radius_inner = jnp.where(upper, raws[1][6:7], raws[0][6:7])
        extra = None
        for dx in range(3):
            for dy in range(3):
                place = ((a + dx) * 4 + (b + dy)) * 3 + 2
                part = pair_tile(
                    left_ref[place],
                    spread_ref[place],
                    columns_ref[place],
                    right_inner,
                    radius_inner,
                    None,
                )
                extra = part if extra is None else extra + part
        rows = 16 if with_stress else 8
        total = total[:rows] + total[rows : 2 * rows] + total[2 * rows : 3 * rows]
        extra = extra[:rows] + extra[rows : 2 * rows] + extra[2 * rows : 3 * rows]
        for z in range(2):
            sums = total[:, z * S : (z + 1) * S] + jnp.where(inner == z, extra, 0.0)
            finish(a, b, z, raws[z], states[z], sums)
        return carry

    lax.fori_loop(0, 4, one_column, 0)


def force_of(state, sums):
    return [state[k : k + 1] * sums[0:1] - sums[1 + k : 2 + k] for k in range(3)]


def unpack_pieces(refs, wide):
    own, depth_halo = refs[0], refs[1]
    if wide:
        cb, ca, db, da, xb, xa = refs[2:8]
        return (
            own,
            depth_halo,
            lambda x, slot: cb[x, slot],
            lambda x, slot: ca[x, slot],
            lambda x: db[x],
            lambda x: da[x],
            xb,
            xa,
        )
    cross, diag, xb, xa = refs[2:6]
    return (
        own,
        depth_halo,
        lambda x, slot: cross[x, 1, slot],
        lambda x, slot: cross[x, 0, slot],
        lambda x: diag[x, 1],
        lambda x: diag[x, 0],
        xb,
        xa,
    )


def step_kernel(wide, *refs):
    count = 8 if wide else 6
    pieces = unpack_pieces(refs[:count], wide)
    velocity_out, own_out, inner_out, left_ref, spread_ref, columns_ref = refs[count:]
    depth = lax.axis_index("depth")
    own = pieces[0]

    def finish(a, b, z, raw, state, sums):
        force = force_of(state, sums)
        radius = raw[6:7]
        live = radius > 0.0
        scaled = radius / RADIUS_REF
        safe_mass = jnp.where(live, scaled * scaled * scaled, 1.0)
        for k in range(3):
            velocity = raw[3 + k : 4 + k] + TIME_STEP * force[k] / safe_mass
            position = raw[k : k + 1] + TIME_STEP * velocity
            velocity_out[k, a, b, z : z + 1, :] = velocity
            own_out[a, b, z, k : k + 1, :] = position
            own_out[a, b, z, 3 + k : 4 + k, :] = velocity
        own_out[a, b, z, 6:8, :] = raw[6:8]

    contact_all(
        neighbour_cells(pieces), depth, False, left_ref, spread_ref, columns_ref, finish, own
    )
    for a in range(2):
        for b in range(2):
            inner_out[a, b] = own_out[a, b, 1 - depth]


def field_kernel(wide, grid, *refs):
    count = 8 if wide else 6
    pieces = unpack_pieces(refs[:count], wide)
    force_out, node_out, left_ref, spread_ref, columns_ref = refs[count:]
    depth = lax.axis_index("depth")
    down = lax.axis_index("down")
    cross = lax.axis_index("cross")
    own = pieces[0]
    size_x, size_y, size_z = grid
    nodes = size_x * size_y * size_z
    node_out[...] = jnp.zeros((16, nodes), F32)
    rows32 = lax.broadcasted_iota(jnp.int32, (32, 1), 0)
    shift = [rows32 // 9 - 1, (rows32 // 3) % 3 - 1, rows32 % 3 - 1]
    lanes = lax.broadcasted_iota(jnp.int32, (1, nodes), 1)
    node_x = lanes // (size_y * size_z)
    node_y = (lanes // size_z) % size_y
    node_z = lanes % size_z

    def finish(a, b, z, raw, state, sums):
        force = force_of(state, sums)
        for k in range(3):
            force_out[k, a, b, z : z + 1, :] = force[k]
        x = [state[k : k + 1] for k in range(3)]
        radius = raw[6:7]
        scaled = radius / RADIUS_REF
        mass = jnp.where(radius > 0.0, scaled * scaled * scaled, 0.0)
        rows = [mass] + [mass * raw[3 + k : 4 + k] for k in range(3)]
        for pair_id, (left, right) in enumerate(PAIR_LIST):
            rows.append(
                0.5
                * (
                    x[left] * x[right] * sums[0:1]
                    - x[left] * sums[1 + right : 2 + right]
                    - x[right] * sums[1 + left : 2 + left]
                    + sums[4 + pair_id : 5 + pair_id]
                )
            )
        moments = jnp.concatenate(rows + [jnp.zeros((6, S), F32)], axis=0)
        place = [raw[k : k + 1] + shift[k].astype(F32) for k in range(3)]
        squared = place[0] * place[0] + place[1] * place[1] + place[2] * place[2]
        kernel = jnp.exp(squared * (-0.5 / (KERNEL_WIDTH * KERNEL_WIDTH))) / KERNEL_NORM
        kernel = jnp.where(rows32 < 27, kernel, 0.0)
        parts = lax.dot_general(
            moments,
            kernel,
            (((1,), (1,)), ((), ())),
            precision=lax.Precision.HIGHEST,
            preferred_element_type=F32,
        )
        target_x = (down * 2 + a - shift[0] + size_x) % size_x
        target_y = (cross * 2 + b - shift[1] + size_y) % size_y
        target_z = depth * 2 + z - shift[2]
        chosen = jnp.logical_and(
            jnp.logical_and(node_x == target_x, node_y == target_y), node_z == target_z
        )
        chosen = jnp.where(chosen, 1.0, 0.0).astype(F32)
        node_out[...] += lax.dot_general(
            parts,
            chosen,
            (((1,), (0,)), ((), ())),
            precision=lax.Precision.HIGHEST,
            preferred_element_type=F32,
        )

    contact_all(
        neighbour_cells(pieces), depth, True, left_ref, spread_ref, columns_ref, finish, own
    )


def library_kernel(grid, count, coefficients, *refs):
    parts = [ref[...] for ref in refs[:count]]
    residual_out, gram_out, moment_out, terms = refs[count:]
    while len(parts) > 1:
        parts = [parts[k] + parts[k + 1] for k in range(0, len(parts), 2)]
    fields = parts[0]
    size_x, size_y, size_z = grid
    nodes = size_x * size_y * size_z
    lanes = lax.broadcasted_iota(jnp.int32, (1, nodes), 1)
    node_x = lanes // (size_y * size_z)
    node_y = (lanes // size_z) % size_y
    node_z = lanes % size_z
    rows = row_ids((8, nodes))
    density = fields[0:1]
    values = jnp.where(rows == 0, fields[0:8], fields[0:8] / (density + MASS_SHIFT))

    def moved(value, step):
        return pltpu.roll(value, step % nodes, 1)

    plane = size_y * size_z
    slope_x = (moved(values, -plane) - moved(values, plane)) * 0.5
    after_y = jnp.where(
        node_y == size_y - 1, moved(values, (size_y - 1) * size_z), moved(values, -size_z)
    )
    before_y = jnp.where(
        node_y == 0, moved(values, -(size_y - 1) * size_z), moved(values, size_z)
    )
    slope_y = (after_y - before_y) * 0.5
    after_z = jnp.where(node_z == size_z - 1, 0.0, moved(values, -1))
    before_z = jnp.where(node_z == 0, 0.0, moved(values, 1))
    slope_z = (after_z - before_z) * 0.5
    slopes = [[table[k : k + 1] for k in range(4)] for table in (slope_x, slope_y, slope_z)]
    strain = [
        [0.5 * (slopes[left][1 + right] + slopes[right][1 + left]) for right in range(3)]
        for left in range(3)
    ]
    divergence = strain[0][0] + strain[1][1] + strain[2][2]
    rate_sum = jnp.zeros_like(density)
    for left in range(3):
        for right in range(3):
            entry = strain[left][right]
            if left == right:
                entry = entry - divergence / 3.0
            rate_sum = rate_sum + entry * entry
    shear_rate = jnp.sqrt(2.0 * rate_sum + 0.01)
    stress = [fields[4 + k : 5 + k] for k in range(6)]
    pressure = (stress[0] + stress[3] + stress[5]) / 3.0
    deviator = (
        (stress[0] - pressure) ** 2
        + (stress[3] - pressure) ** 2
        + (stress[5] - pressure) ** 2
        + 2.0 * (stress[1] ** 2 + stress[2] ** 2 + stress[4] ** 2)
    )
    shear_stress = jnp.sqrt(0.5 * deviator + 0.01)
    pressure_scale = jnp.sqrt(pressure * pressure + 1.0)
    friction = shear_stress / pressure_scale
    features = [
        density,
        pressure / pressure_scale,
        shear_rate,
        shear_rate / jnp.sqrt(pressure_scale),
        divergence,
        slopes[0][0],
        slopes[1][0],
        slopes[2][0],
    ]
    entries = list(features)
    for left in range(8):
        for right in range(left, 8):
            entries.append(features[left] * features[right])
    for left in range(1, 5):
        entries.append(features[left] * features[left] * features[left])
    model = jnp.zeros_like(density)
    for k, entry in enumerate(entries):
        terms[k : k + 1, :] = entry
        model = model + coefficients[k] * entry
    residual = friction - model
    table = terms[...]
    gram_out[...] = (
        lax.dot_general(
            table,
            table,
            (((1,), (1,)), ((), ())),
            precision=lax.Precision.HIGHEST,
            preferred_element_type=F32,
        )
        / nodes
    )
    moment = lax.dot_general(
        jnp.broadcast_to(friction, (8, nodes)),
        table,
        (((1,), (1,)), ((), ())),
        precision=lax.Precision.HIGHEST,
        preferred_element_type=F32,
    )
    moment_out[...] = moment[0:1] / nodes
    down = lax.axis_index("down")
    cross = lax.axis_index("cross")
    depth = lax.axis_index("depth")
    b_rows = lax.broadcasted_iota(jnp.int32, (2, 1), 0)
    z_lanes = lax.broadcasted_iota(jnp.int32, (2, 2), 1)
    for a in range(2):
        mine = jnp.logical_and(node_x == down * 2 + a, node_y == cross * 2 + b_rows)
        column = [
            jnp.sum(
                jnp.where(jnp.logical_and(mine, node_z == depth * 2 + z), residual, 0.0),
                axis=1,
                keepdims=True,
            )
            for z in range(2)
        ]
        residual_out[a] = jnp.where(z_lanes == 0, column[0], column[1])


def ring(axis, step):
    peers = lax.axis_size(axis)
    return [(i, (i + step) % peers) for i in range(peers)]


def exchange(own, inner):
    cross = lax.axis_size("cross")
    depth_halo = lax.ppermute(inner, "depth", [(0, 1), (1, 0)])
    if cross == 2:
        side = lax.ppermute(own, "cross", [(0, 1), (1, 0)])
        diag = lax.ppermute(inner, ("cross", "depth"), [(i, 3 - i) for i in range(4)])
        sides = [side, diag]

        def face(x):
            return jnp.concatenate(
                [
                    own[x].reshape(4, 8, S),
                    depth_halo[x],
                    side[x, 1],
                    side[x, 0],
                    diag[x, 1][None],
                    diag[x, 0][None],
                ],
                axis=0,
            )

    else:
        pairs = [(i * 2 + j, ((i + 1) % cross) * 2 + 1 - j) for i in range(cross) for j in range(2)]
        back = [(i * 2 + j, ((i - 1) % cross) * 2 + 1 - j) for i in range(cross) for j in range(2)]
        before = lax.ppermute(own[:, 1], "cross", ring("cross", 1))
        after = lax.ppermute(own[:, 0], "cross", ring("cross", -1))
        diag_before = lax.ppermute(inner[:, 1], ("cross", "depth"), pairs)
        diag_after = lax.ppermute(inner[:, 0], ("cross", "depth"), back)
        sides = [before, after, diag_before, diag_after]

        def face(x):
            return jnp.concatenate(
                [
                    own[x].reshape(4, 8, S),
                    depth_halo[x],
                    before[x],
                    after[x],
                    diag_before[x][None],
                    diag_after[x][None],
                ],
                axis=0,
            )

    x_before = lax.ppermute(face(1), "down", ring("down", 1))
    x_after = lax.ppermute(face(0), "down", ring("down", -1))
    return [own, depth_halo] + sides + [x_before, x_after]


def shared(value, axes, peers):
    return [value] + [
        lax.ppermute(value, axes, [(i, i ^ k) for i in range(peers)]) for k in range(1, peers)
    ]


def tree_sum(parts):
    while len(parts) > 1:
        parts = [parts[k] + parts[k + 1] for k in range(0, len(parts), 2)]
    return parts[0]


def body(positions, velocities, sphere_radii, counts, coefficients):
    down, cross, depth = (lax.axis_size(name) for name in ("down", "cross", "depth"))
    wide = cross != 2
    grid = (2 * down, 2 * cross, 2 * depth)
    nodes = grid[0] * grid[1] * grid[2]
    params = pltpu.CompilerParams(vmem_limit_bytes=VMEM_LIMIT)
    state_shape = jax.ShapeDtypeStruct((2, 2, 2, 8, S), F32)
    inner_shape = jax.ShapeDtypeStruct((2, 2, 8, S), F32)
    vector_shape = jax.ShapeDtypeStruct((3, 2, 2, 2, S), F32)
    own, inner = pl.pallas_call(
        pack_kernel,
        out_shape=(state_shape, inner_shape),
        in_specs=[SMEM_SPEC, VMEM_SPEC, VMEM_SPEC, VMEM_SPEC],
        out_specs=(VMEM_SPEC, VMEM_SPEC),
        compiler_params=params,
        name="pack",
    )(counts, positions, velocities, sphere_radii)

    def scratch(rows):
        return [
            pltpu.VMEM((48, S, 64), BF16),
            pltpu.VMEM((48, S, S), F32),
            pltpu.VMEM((48, rows, 2 * S), BF16),
        ]

    pieces = exchange(own, inner)
    velocity_new, own, inner = pl.pallas_call(
        functools.partial(step_kernel, wide),
        out_shape=(vector_shape, state_shape, inner_shape),
        in_specs=[VMEM_SPEC] * len(pieces),
        out_specs=(VMEM_SPEC,) * 3,
        scratch_shapes=scratch(32),
        compiler_params=params,
        name="step",
    )(*pieces)
    pieces = exchange(own, inner)
    force_next, partial = pl.pallas_call(
        functools.partial(field_kernel, wide, grid),
        out_shape=(vector_shape, jax.ShapeDtypeStruct((16, nodes), F32)),
        in_specs=[VMEM_SPEC] * len(pieces),
        out_specs=(VMEM_SPEC,) * 2,
        scratch_shapes=scratch(48),
        compiler_params=params,
        name="field",
    )(*pieces)
    partial = tree_sum(shared(partial, ("cross", "depth"), cross * depth))
    parts = shared(partial, "down", down)
    residual_field, gram_matrix, moment = pl.pallas_call(
        functools.partial(library_kernel, grid, len(parts)),
        out_shape=(
            jax.ShapeDtypeStruct((2, 2, 2), F32),
            jax.ShapeDtypeStruct((TERMS, TERMS), F32),
            jax.ShapeDtypeStruct((1, TERMS), F32),
        ),
        in_specs=[SMEM_SPEC] + [VMEM_SPEC] * len(parts),
        out_specs=(VMEM_SPEC,) * 3,
        scratch_shapes=[pltpu.VMEM((TERMS, nodes), F32)],
        compiler_params=params,
        name="library",
    )(coefficients, *parts)
    return (velocity_new, force_next, residual_field, gram_matrix, moment.reshape(TERMS))


def solution(mesh):
    return jax.shard_map(
        body,
        mesh=mesh,
        in_specs=(
            P(None, ("groups", "down"), "cross", "depth", None),
            P(None, ("groups", "down"), "cross", "depth", None),
            P(("groups", "down"), "cross", "depth", None),
            P(("groups", "down"), "cross", "depth"),
            P(),
        ),
        out_specs=(
            P(None, ("groups", "down"), "cross", "depth", None),
            P(None, ("groups", "down"), "cross", "depth", None),
            P(("groups", "down"), "cross", "depth"),
            P("groups", None),
            P("groups"),
        ),
        check_vma=False,
    )
```

```python
import functools

import jax
import jax.numpy as jnp
from jax import lax
from jax.experimental import pallas as pl
from jax.experimental.pallas import tpu as pltpu
from jax.sharding import PartitionSpec as P

STIFFNESS = 100.0
DAMPING = 20.0
TIME_STEP = 0.05
KERNEL_WIDTH = 0.4
KERNEL_NORM = 64.0
SOFTENING = 0.0001
RADIUS_REF = 0.1
MASS_SHIFT = 0.1
DEAD = -1000.0
TERMS = 48
S = 128
F32 = jnp.float32
BF16 = jnp.bfloat16
PAIR_LIST = ((0, 0), (0, 1), (0, 2), (1, 1), (1, 2), (2, 2))
VMEM_SPEC = pl.BlockSpec(memory_space=pltpu.VMEM)
SMEM_SPEC = pl.BlockSpec(memory_space=pltpu.SMEM)
VMEM_LIMIT = 48 * 1024 * 1024


def row_ids(shape):
    return lax.broadcasted_iota(jnp.int32, shape, 0)


def pack_kernel(counts, positions, velocities, radii, own, inner):
    depth = lax.axis_index("depth")
    lanes = lax.broadcasted_iota(jnp.int32, (1, S), 1)
    for a in range(2):
        for b in range(2):
            for z in range(2):
                for k in range(3):
                    own[a, b, z, k : k + 1, :] = positions[k, a, b, z : z + 1, :]
                    own[a, b, z, 3 + k : 4 + k, :] = velocities[k, a, b, z : z + 1, :]
                live = lanes < counts[a, b, z]
                own[a, b, z, 6:7, :] = jnp.where(live, radii[a, b, z : z + 1, :], DEAD)
                own[a, b, z, 7:8, :] = jnp.zeros((1, S), F32)
            inner[a, b] = own[a, b, 1 - depth]


def local_state(raw, centre):
    rows = row_ids(raw.shape)
    shift = jnp.where(rows == 0, centre[0], jnp.where(rows == 1, centre[1], centre[2]))
    return jnp.where(rows < 3, raw + shift, raw)


def neighbour_cells(pieces):
    own, depth_halo, cross_before, cross_after, diag_before, diag_after, x_before, x_after = pieces

    def cell(x, y, slot):
        if x in (0, 3):
            face = x_before if x == 0 else x_after
            if y in (1, 2):
                return face[(y - 1) * 2 + slot] if slot < 2 else face[4 + y - 1]
            side = 6 if y == 0 else 8
            return face[side + slot] if slot < 2 else face[10 + (0 if y == 0 else 1)]
        if y in (1, 2):
            return own[x - 1, y - 1, slot] if slot < 2 else depth_halo[x - 1, y - 1]
        if slot < 2:
            return (cross_before if y == 0 else cross_after)(x - 1, slot)
        return (diag_before if y == 0 else diag_after)(x - 1)

    return cell


def lane_gather(table, index):
    return jnp.take_along_axis(table, index, axis=1)


def contact_scratch():
    return [
        pltpu.VMEM((48 * 8, S), F32),
        pltpu.VMEM((8 * 48, S), jnp.int32),
        pltpu.VMEM((8 * 48, S), jnp.int32),
        pltpu.VMEM((8 * 48, S), jnp.int32),
        pltpu.VMEM((8, 48, S), jnp.int32),
        pltpu.VMEM((8, 27, 8, S), F32),
        pltpu.VMEM((8, 7, S, S), F32),
    ]


def contact_all(cell, depth, with_stress, scratch, finish, own):
    local_ref, index_ref, base_ref, amount_ref, chosen_ref, list_ref, spread_ref = scratch
    inner = 1 - depth
    halo_z = 1.5 - 3.0 * depth.astype(F32)
    for x in range(4):
        for y in range(4):
            for slot in range(3):
                centre = (x - 1.5, y - 1.5, slot - 0.5 if slot < 2 else halo_z)
                place = (x * 4 + y) * 3 + slot
                local_ref[place * 8 : place * 8 + 8, :] = local_state(cell(x, y, slot), centre)

    def own_place(a, b, z):
        return ((a + 1) * 4 + b + 1) * 3 + z

    cells = [(a, b, z) for a in range(2) for b in range(2) for z in range(2)]
    place = [local_ref[pl.ds(k, 48, stride=8), :] for k in range(3)]
    radius = local_ref[pl.ds(6, 48, stride=8), :]
    rows = lax.broadcasted_iota(jnp.int32, (48, S), 0)
    row_x, row_y, row_slot = rows // 12, (rows // 3) % 4, rows % 3

    masks = []
    for a, b, z in cells:
        mine = local_ref[own_place(a, b, z) * 8 : own_place(a, b, z) * 8 + 8, :]
        live = mine[6:7] > 0.0
        low = jnp.min(jnp.where(live, mine, 1e9), axis=1, keepdims=True)
        high = jnp.max(jnp.where(live, mine, -1e9), axis=1, keepdims=True)
        reach = radius + high[6:7]
        near = jnp.logical_and(
            jnp.logical_and(row_x >= a, row_x <= a + 2), jnp.logical_and(row_y >= b, row_y <= b + 2)
        )
        near = jnp.logical_and(near, jnp.logical_or(row_slot < 2, inner == z))
        for k in range(3):
            near = jnp.logical_and(near, place[k] + reach > low[k : k + 1])
            near = jnp.logical_and(near, place[k] - reach < high[k : k + 1])
        masks.append(jnp.where(near, 1.0, 0.0).astype(F32))
    mask = jnp.concatenate(masks, axis=0).astype(BF16)
    upper = lax.broadcasted_iota(jnp.int32, (S, 2 * S), 0) <= lax.broadcasted_iota(
        jnp.int32, (S, 2 * S), 1
    )
    upper = jnp.where(upper, 1.0, 0.0).astype(BF16)
    sums = lax.dot_general(mask, upper, (((1,), (0,)), ((), ())), preferred_element_type=F32)
    prefix, amount = sums[:, :S], sums[:, S:]
    before = lax.broadcasted_iota(jnp.int32, (48, 48), 1) < lax.broadcasted_iota(
        jnp.int32, (48, 48), 0
    )
    before = jnp.where(before, 1.0, 0.0).astype(BF16)
    totals = []
    for c in range(8):
        part = amount[c * 48 : c * 48 + 48]
        base = lax.dot_general(
            before, part.astype(BF16), (((1,), (0,)), ((), ())), preferred_element_type=F32
        )
        base_ref[c * 48 : c * 48 + 48, :] = base.astype(jnp.int32)
        totals.append((base[47:48, 0:1] + part[47:48, 0:1]).astype(jnp.int32)[0, 0])
    amount_ref[...] = amount.astype(jnp.int32)
    lanes = lax.broadcasted_iota(jnp.int32, (8 * 48, S), 1)
    wanted = lanes.astype(F32)
    index = jnp.zeros((8 * 48, S), jnp.int32)
    for step in (64, 32, 16, 8, 4, 2, 1):
        probe = lane_gather(prefix, index + (step - 1))
        index = jnp.where(probe <= wanted, index + step, index)
    index_ref[...] = index

    for c, (a, b, z) in enumerate(cells):
        raw = own[a, b, z]
        turned = jnp.transpose(local_ref[own_place(a, b, z) * 8 : own_place(a, b, z) * 8 + 8, :])
        for k in range(7):
            spread_ref[c, k] = jnp.broadcast_to(turned[:, k : k + 1], (S, S))

    block = 4 if with_stress else 8
    cell_rows = lax.broadcasted_iota(jnp.int32, (8, S), 0)
    short_lanes = lax.broadcasted_iota(jnp.int32, (48, S), 1)
    empty = jnp.where(cell_rows == 6, DEAD, 0.0).astype(F32)
    width = 9 if with_stress else 3
    for c, (a, b, z) in enumerate(cells):
        tiles = (totals[c] + (S - 1)) // S

        def gather_tile(t, carry):
            want = t * S + short_lanes - base_ref[c * 48 : c * 48 + 48, :]
            valid = jnp.logical_and(want >= 0, want < amount_ref[c * 48 : c * 48 + 48, :])
            source = lane_gather(
                index_ref[c * 48 : c * 48 + 48, :], jnp.clip(want, 0, S - 1)
            )
            chosen_ref[c] = jnp.where(valid, source, -1)
            tile = empty
            for dx in range(3):
                for dy in range(3):
                    for slot in range(3):
                        n = ((a + dx) * 4 + b + dy) * 3 + slot
                        pick = jnp.broadcast_to(chosen_ref[c, n : n + 1, :], (8, S))
                        values = lane_gather(
                            local_ref[n * 8 : n * 8 + 8, :], jnp.maximum(pick, 0)
                        )
                        tile = jnp.where(pick >= 0, values, tile)
            list_ref[c, t] = tile
            return carry

        lax.fori_loop(0, tiles, gather_tile, 0)
        columns = [[] for _ in range(width)]
        for part in range(16 // block):

            def pair_tile(t, sums):
                tile = list_ref[c, t]
                other = [jnp.broadcast_to(tile[k : k + 1], (8, S)) for k in range(7)]
                out = []
                for i in range(block):
                    row = (part * block + i) * 8
                    me = [spread_ref[c, k, row : row + 8, :] for k in range(7)]
                    r = [me[k] - other[k] for k in range(3)]
                    u = [me[3 + k] - other[3 + k] for k in range(3)]
                    squared = r[0] * r[0] + r[1] * r[1] + r[2] * r[2] + SOFTENING
                    inverse = lax.rsqrt(squared)
                    along = u[0] * r[0] + u[1] * r[1] + u[2] * r[2]
                    overlap = jnp.maximum((me[6] + other[6]) * inverse - 1.0, 0.0)
                    weight = overlap * (STIFFNESS - (DAMPING * along) * inverse)
                    pull = [weight * r[k] for k in range(3)]
                    terms = list(pull)
                    if with_stress:
                        terms += [pull[left] * r[right] for left, right in PAIR_LIST]
                    out += [sums[i * width + k] + term for k, term in enumerate(terms)]
                return tuple(out)

            sums = lax.fori_loop(
                0, tiles, pair_tile, tuple(jnp.zeros((8, S), F32) for _ in range(block * width))
            )
            for k in range(width):
                for i in range(block):
                    columns[k].append(jnp.sum(sums[i * width + k], axis=1, keepdims=True))
        lane_ids = lax.broadcasted_iota(jnp.int32, (S, S), 1)
        table = jnp.zeros((S, S), F32)
        for k in range(width):
            table = jnp.where(lane_ids == k, jnp.concatenate(columns[k], axis=0), table)
        finish(a, b, z, own[a, b, z], jnp.transpose(table)[0:16])


def unpack_pieces(refs, wide):
    own, depth_halo = refs[0], refs[1]
    if wide:
        cb, ca, db, da, xb, xa = refs[2:8]
        return (
            own,
            depth_halo,
            lambda x, slot: cb[x, slot],
            lambda x, slot: ca[x, slot],
            lambda x: db[x],
            lambda x: da[x],
            xb,
            xa,
        )
    cross, diag, xb, xa = refs[2:6]
    return (
        own,
        depth_halo,
        lambda x, slot: cross[x, 1, slot],
        lambda x, slot: cross[x, 0, slot],
        lambda x: diag[x, 1],
        lambda x: diag[x, 0],
        xb,
        xa,
    )


def step_kernel(wide, *refs):
    count = 8 if wide else 6
    pieces = unpack_pieces(refs[:count], wide)
    velocity_out, own_out, inner_out = refs[count : count + 3]
    scratch = refs[count + 3 :]
    depth = lax.axis_index("depth")
    own = pieces[0]

    def finish(a, b, z, raw, sums):
        force = [sums[k : k + 1] for k in range(3)]
        radius = raw[6:7]
        live = radius > 0.0
        scaled = radius / RADIUS_REF
        safe_mass = jnp.where(live, scaled * scaled * scaled, 1.0)
        for k in range(3):
            velocity = raw[3 + k : 4 + k] + TIME_STEP * force[k] / safe_mass
            position = raw[k : k + 1] + TIME_STEP * velocity
            velocity_out[k, a, b, z : z + 1, :] = velocity
            own_out[a, b, z, k : k + 1, :] = position
            own_out[a, b, z, 3 + k : 4 + k, :] = velocity
        own_out[a, b, z, 6:8, :] = raw[6:8]

    contact_all(neighbour_cells(pieces), depth, False, scratch, finish, own)
    for a in range(2):
        for b in range(2):
            inner_out[a, b] = own_out[a, b, 1 - depth]


def field_kernel(wide, grid, *refs):
    count = 8 if wide else 6
    pieces = unpack_pieces(refs[:count], wide)
    force_out, node_out = refs[count : count + 2]
    scratch = refs[count + 2 :]
    depth = lax.axis_index("depth")
    down = lax.axis_index("down")
    cross = lax.axis_index("cross")
    own = pieces[0]
    size_x, size_y, size_z = grid
    nodes = size_x * size_y * size_z
    node_out[...] = jnp.zeros((16, nodes), F32)
    rows32 = lax.broadcasted_iota(jnp.int32, (32, 1), 0)
    shift = [rows32 // 9 - 1, (rows32 // 3) % 3 - 1, rows32 % 3 - 1]
    lanes = lax.broadcasted_iota(jnp.int32, (1, nodes), 1)
    node_x = lanes // (size_y * size_z)
    node_y = (lanes // size_z) % size_y
    node_z = lanes % size_z

    def finish(a, b, z, raw, sums):
        force = [sums[k : k + 1] for k in range(3)]
        for k in range(3):
            force_out[k, a, b, z : z + 1, :] = force[k]
        radius = raw[6:7]
        scaled = radius / RADIUS_REF
        mass = jnp.where(radius > 0.0, scaled * scaled * scaled, 0.0)
        rows = [mass] + [mass * raw[3 + k : 4 + k] for k in range(3)]
        rows += [0.5 * sums[3 + k : 4 + k] for k in range(6)]
        moments = jnp.concatenate(rows + [jnp.zeros((6, S), F32)], axis=0)
        place = [raw[k : k + 1] + shift[k].astype(F32) for k in range(3)]
        squared = place[0] * place[0] + place[1] * place[1] + place[2] * place[2]
        kernel = jnp.exp(squared * (-0.5 / (KERNEL_WIDTH * KERNEL_WIDTH))) / KERNEL_NORM
        kernel = jnp.where(rows32 < 27, kernel, 0.0)
        parts = lax.dot_general(
            moments,
            kernel,
            (((1,), (1,)), ((), ())),
            precision=lax.Precision.HIGHEST,
            preferred_element_type=F32,
        )
        target_x = (down * 2 + a - shift[0] + size_x) % size_x
        target_y = (cross * 2 + b - shift[1] + size_y) % size_y
        target_z = depth * 2 + z - shift[2]
        chosen = jnp.logical_and(
            jnp.logical_and(node_x == target_x, node_y == target_y), node_z == target_z
        )
        chosen = jnp.where(chosen, 1.0, 0.0).astype(F32)
        node_out[...] += lax.dot_general(
            parts,
            chosen,
            (((1,), (0,)), ((), ())),
            precision=lax.Precision.HIGHEST,
            preferred_element_type=F32,
        )

    contact_all(neighbour_cells(pieces), depth, True, scratch, finish, own)


def library_kernel(grid, count, coefficients, *refs):
    parts = [ref[...] for ref in refs[:count]]
    residual_out, gram_out, moment_out, terms = refs[count:]
    while len(parts) > 1:
        parts = [parts[k] + parts[k + 1] for k in range(0, len(parts), 2)]
    fields = parts[0]
    size_x, size_y, size_z = grid
    nodes = size_x * size_y * size_z
    lanes = lax.broadcasted_iota(jnp.int32, (1, nodes), 1)
    node_x = lanes // (size_y * size_z)
    node_y = (lanes // size_z) % size_y
    node_z = lanes % size_z
    rows = row_ids((8, nodes))
    density = fields[0:1]
    values = jnp.where(rows == 0, fields[0:8], fields[0:8] / (density + MASS_SHIFT))

    def moved(value, step):
        return pltpu.roll(value, step % nodes, 1)

    plane = size_y * size_z
    slope_x = (moved(values, -plane) - moved(values, plane)) * 0.5
    after_y = jnp.where(
        node_y == size_y - 1, moved(values, (size_y - 1) * size_z), moved(values, -size_z)
    )
    before_y = jnp.where(
        node_y == 0, moved(values, -(size_y - 1) * size_z), moved(values, size_z)
    )
    slope_y = (after_y - before_y) * 0.5
    after_z = jnp.where(node_z == size_z - 1, 0.0, moved(values, -1))
    before_z = jnp.where(node_z == 0, 0.0, moved(values, 1))
    slope_z = (after_z - before_z) * 0.5
    slopes = [[table[k : k + 1] for k in range(4)] for table in (slope_x, slope_y, slope_z)]
    strain = [
        [0.5 * (slopes[left][1 + right] + slopes[right][1 + left]) for right in range(3)]
        for left in range(3)
    ]
    divergence = strain[0][0] + strain[1][1] + strain[2][2]
    rate_sum = jnp.zeros_like(density)
    for left in range(3):
        for right in range(3):
            entry = strain[left][right]
            if left == right:
                entry = entry - divergence / 3.0
            rate_sum = rate_sum + entry * entry
    shear_rate = jnp.sqrt(2.0 * rate_sum + 0.01)
    stress = [fields[4 + k : 5 + k] for k in range(6)]
    pressure = (stress[0] + stress[3] + stress[5]) / 3.0
    deviator = (
        (stress[0] - pressure) ** 2
        + (stress[3] - pressure) ** 2
        + (stress[5] - pressure) ** 2
        + 2.0 * (stress[1] ** 2 + stress[2] ** 2 + stress[4] ** 2)
    )
    shear_stress = jnp.sqrt(0.5 * deviator + 0.01)
    pressure_scale = jnp.sqrt(pressure * pressure + 1.0)
    friction = shear_stress / pressure_scale
    features = [
        density,
        pressure / pressure_scale,
        shear_rate,
        shear_rate / jnp.sqrt(pressure_scale),
        divergence,
        slopes[0][0],
        slopes[1][0],
        slopes[2][0],
    ]
    entries = list(features)
    for left in range(8):
        for right in range(left, 8):
            entries.append(features[left] * features[right])
    for left in range(1, 5):
        entries.append(features[left] * features[left] * features[left])
    model = jnp.zeros_like(density)
    for k, entry in enumerate(entries):
        terms[k : k + 1, :] = entry
        model = model + coefficients[k] * entry
    residual = friction - model
    table = terms[...]
    gram_out[...] = (
        lax.dot_general(
            table,
            table,
            (((1,), (1,)), ((), ())),
            precision=lax.Precision.HIGHEST,
            preferred_element_type=F32,
        )
        / nodes
    )
    moment = lax.dot_general(
        jnp.broadcast_to(friction, (8, nodes)),
        table,
        (((1,), (1,)), ((), ())),
        precision=lax.Precision.HIGHEST,
        preferred_element_type=F32,
    )
    moment_out[...] = moment[0:1] / nodes
    down = lax.axis_index("down")
    cross = lax.axis_index("cross")
    depth = lax.axis_index("depth")
    b_rows = lax.broadcasted_iota(jnp.int32, (2, 1), 0)
    z_lanes = lax.broadcasted_iota(jnp.int32, (2, 2), 1)
    for a in range(2):
        mine = jnp.logical_and(node_x == down * 2 + a, node_y == cross * 2 + b_rows)
        column = [
            jnp.sum(
                jnp.where(jnp.logical_and(mine, node_z == depth * 2 + z), residual, 0.0),
                axis=1,
                keepdims=True,
            )
            for z in range(2)
        ]
        residual_out[a] = jnp.where(z_lanes == 0, column[0], column[1])


def ring(axis, step):
    peers = lax.axis_size(axis)
    return [(i, (i + step) % peers) for i in range(peers)]


def exchange(own, inner):
    cross = lax.axis_size("cross")
    depth_halo = lax.ppermute(inner, "depth", [(0, 1), (1, 0)])
    if cross == 2:
        side = lax.ppermute(own, "cross", [(0, 1), (1, 0)])
        diag = lax.ppermute(inner, ("cross", "depth"), [(i, 3 - i) for i in range(4)])
        sides = [side, diag]

        def face(x):
            return jnp.concatenate(
                [
                    own[x].reshape(4, 8, S),
                    depth_halo[x],
                    side[x, 1],
                    side[x, 0],
                    diag[x, 1][None],
                    diag[x, 0][None],
                ],
                axis=0,
            )

    else:
        pairs = [(i * 2 + j, ((i + 1) % cross) * 2 + 1 - j) for i in range(cross) for j in range(2)]
        back = [(i * 2 + j, ((i - 1) % cross) * 2 + 1 - j) for i in range(cross) for j in range(2)]
        before = lax.ppermute(own[:, 1], "cross", ring("cross", 1))
        after = lax.ppermute(own[:, 0], "cross", ring("cross", -1))
        diag_before = lax.ppermute(inner[:, 1], ("cross", "depth"), pairs)
        diag_after = lax.ppermute(inner[:, 0], ("cross", "depth"), back)
        sides = [before, after, diag_before, diag_after]

        def face(x):
            return jnp.concatenate(
                [
                    own[x].reshape(4, 8, S),
                    depth_halo[x],
                    before[x],
                    after[x],
                    diag_before[x][None],
                    diag_after[x][None],
                ],
                axis=0,
            )

    x_before = lax.ppermute(face(1), "down", ring("down", 1))
    x_after = lax.ppermute(face(0), "down", ring("down", -1))
    return [own, depth_halo] + sides + [x_before, x_after]


def shared(value, axes, peers):
    return [value] + [
        lax.ppermute(value, axes, [(i, i ^ k) for i in range(peers)]) for k in range(1, peers)
    ]


def tree_sum(parts):
    while len(parts) > 1:
        parts = [parts[k] + parts[k + 1] for k in range(0, len(parts), 2)]
    return parts[0]


def body(positions, velocities, sphere_radii, counts, coefficients):
    down, cross, depth = (lax.axis_size(name) for name in ("down", "cross", "depth"))
    wide = cross != 2
    grid = (2 * down, 2 * cross, 2 * depth)
    nodes = grid[0] * grid[1] * grid[2]
    params = pltpu.CompilerParams(vmem_limit_bytes=VMEM_LIMIT)
    state_shape = jax.ShapeDtypeStruct((2, 2, 2, 8, S), F32)
    inner_shape = jax.ShapeDtypeStruct((2, 2, 8, S), F32)
    vector_shape = jax.ShapeDtypeStruct((3, 2, 2, 2, S), F32)
    own, inner = pl.pallas_call(
        pack_kernel,
        out_shape=(state_shape, inner_shape),
        in_specs=[SMEM_SPEC, VMEM_SPEC, VMEM_SPEC, VMEM_SPEC],
        out_specs=(VMEM_SPEC, VMEM_SPEC),
        compiler_params=params,
        name="pack",
    )(counts, positions, velocities, sphere_radii)

    pieces = exchange(own, inner)
    velocity_new, own, inner = pl.pallas_call(
        functools.partial(step_kernel, wide),
        out_shape=(vector_shape, state_shape, inner_shape),
        in_specs=[VMEM_SPEC] * len(pieces),
        out_specs=(VMEM_SPEC,) * 3,
        scratch_shapes=contact_scratch(),
        compiler_params=params,
        name="step",
    )(*pieces)
    pieces = exchange(own, inner)
    force_next, partial = pl.pallas_call(
        functools.partial(field_kernel, wide, grid),
        out_shape=(vector_shape, jax.ShapeDtypeStruct((16, nodes), F32)),
        in_specs=[VMEM_SPEC] * len(pieces),
        out_specs=(VMEM_SPEC,) * 2,
        scratch_shapes=contact_scratch(),
        compiler_params=params,
        name="field",
    )(*pieces)
    partial = tree_sum(shared(partial, ("cross", "depth"), cross * depth))
    parts = shared(partial, "down", down)
    residual_field, gram_matrix, moment = pl.pallas_call(
        functools.partial(library_kernel, grid, len(parts)),
        out_shape=(
            jax.ShapeDtypeStruct((2, 2, 2), F32),
            jax.ShapeDtypeStruct((TERMS, TERMS), F32),
            jax.ShapeDtypeStruct((1, TERMS), F32),
        ),
        in_specs=[SMEM_SPEC] + [VMEM_SPEC] * len(parts),
        out_specs=(VMEM_SPEC,) * 3,
        scratch_shapes=[pltpu.VMEM((TERMS, nodes), F32)],
        compiler_params=params,
        name="library",
    )(coefficients, *parts)
    return (velocity_new, force_next, residual_field, gram_matrix, moment.reshape(TERMS))


def solution(mesh):
    return jax.shard_map(
        body,
        mesh=mesh,
        in_specs=(
            P(None, ("groups", "down"), "cross", "depth", None),
            P(None, ("groups", "down"), "cross", "depth", None),
            P(("groups", "down"), "cross", "depth", None),
            P(("groups", "down"), "cross", "depth"),
            P(),
        ),
        out_specs=(
            P(None, ("groups", "down"), "cross", "depth", None),
            P(None, ("groups", "down"), "cross", "depth", None),
            P(("groups", "down"), "cross", "depth"),
            P("groups", None),
            P("groups"),
        ),
        check_vma=False,
    )
```

```python
import functools

import jax
import jax.numpy as jnp
from jax import lax
from jax.experimental import pallas as pl
from jax.experimental.pallas import tpu as pltpu
from jax.sharding import PartitionSpec as P

STIFFNESS = 100.0
DAMPING = 20.0
TIME_STEP = 0.05
KERNEL_WIDTH = 0.4
KERNEL_NORM = 64.0
SOFTENING = 0.0001
RADIUS_REF = 0.1
MASS_SHIFT = 0.1
DEAD = -1000.0
TERMS = 48
S = 128
F32 = jnp.float32
BF16 = jnp.bfloat16
CELLS = tuple((a, b, z) for a in range(2) for b in range(2) for z in range(2))
PAIRS = ((0, 2), (4, 6), (1, 3), (5, 7))
PAIR_LIST = ((0, 0), (0, 1), (0, 2), (1, 1), (1, 2), (2, 2))
VMEM_SPEC = pl.BlockSpec(memory_space=pltpu.VMEM)
SMEM_SPEC = pl.BlockSpec(memory_space=pltpu.SMEM)
VMEM_LIMIT = 48 * 1024 * 1024


def row_ids(shape):
    return lax.broadcasted_iota(jnp.int32, shape, 0)


def lane_ids(shape):
    return lax.broadcasted_iota(jnp.int32, shape, 1)


def one_hot(condition):
    return jnp.where(condition, 1.0, 0.0).astype(BF16)


def split(value):
    high = value.astype(BF16)
    return high, value - high.astype(F32)


def matmul(left, right):
    return lax.dot_general(left, right, (((1,), (0,)), ((), ())), preferred_element_type=F32)


def matmul_turned(left, right):
    return lax.dot_general(left, right, (((1,), (1,)), ((), ())), preferred_element_type=F32)


def lane_gather(table, index):
    return jnp.take_along_axis(table, index, axis=1)


def pack_kernel(
    counts, positions_hbm, velocities_hbm, radii_hbm, own, inner, positions, velocities, radii, arrived
):
    copies = [
        pltpu.make_async_copy(source, target, arrived.at[k])
        for k, (source, target) in enumerate(
            ((positions_hbm, positions), (velocities_hbm, velocities), (radii_hbm, radii))
        )
    ]
    for copy in copies:
        copy.start()
    for copy in copies:
        copy.wait()
    depth = lax.axis_index("depth")
    lanes = lane_ids((1, S))
    for c, (a, b, z) in enumerate(CELLS):
        for k in range(3):
            own[c * 8 + k : c * 8 + k + 1, :] = positions[k, a, b, z : z + 1, :]
            own[c * 8 + 3 + k : c * 8 + 4 + k, :] = velocities[k, a, b, z : z + 1, :]
        live = lanes < counts[a, b, z]
        own[c * 8 + 6 : c * 8 + 7, :] = jnp.where(live, radii[a, b, z : z + 1, :], DEAD)
        own[c * 8 + 7 : c * 8 + 8, :] = jnp.zeros((1, S), F32)
    for column in range(4):
        source = pl.multiple_of(column * 16 + (1 - depth) * 8, 8)
        inner[column * 8 : column * 8 + 8, :] = own[pl.ds(source, 8), :]


def local_state(raw, centre):
    rows = row_ids(raw.shape)
    shift = jnp.where(rows == 0, centre[0], jnp.where(rows == 1, centre[1], centre[2]))
    return jnp.where(rows < 3, raw + shift, raw)


def piece_reader(refs, wide, height):
    own, depth_halo = refs[0], refs[1]
    x_before, x_after = refs[-2], refs[-1]

    def read(ref, cell):
        return ref[cell * height : cell * height + height, :]

    def cell(x, y, slot):
        if x in (0, 3):
            face = x_before if x == 0 else x_after
            if y in (1, 2):
                return read(face, (y - 1) * 2 + slot if slot < 2 else 4 + y - 1)
            side = 0 if y == 0 else 1
            return read(face, 6 + side * 2 + slot if slot < 2 else 10 + side)
        a = x - 1
        if y in (1, 2):
            return read(own, a * 4 + (y - 1) * 2 + slot) if slot < 2 else read(depth_halo, a * 2 + y - 1)
        if wide:
            before, after, diag_before, diag_after = refs[2:6]
            if slot < 2:
                return read(before if y == 0 else after, a * 2 + slot)
            return read(diag_before if y == 0 else diag_after, a)
        side, diag = refs[2:4]
        b = 1 if y == 0 else 0
        return read(side, a * 4 + b * 2 + slot) if slot < 2 else read(diag, a * 2 + b)

    return cell


def own_place(a, b, z):
    return ((a + 1) * 4 + b + 1) * 3 + z


def extended_cells(depth):
    halo_z = 1.5 - 3.0 * depth.astype(F32)
    for x in range(4):
        for y in range(4):
            for slot in range(3):
                centre = (x - 1.5, y - 1.5, slot - 0.5 if slot < 2 else halo_z)
                yield x, y, slot, ((x * 4 + y) * 3 + slot) * 8, centre


def contact_scratch(width):
    return [
        pltpu.VMEM((48 * 8, S), F32),
        pltpu.VMEM((8 * 48, S), jnp.int32),
        pltpu.VMEM((8 * 48, S), jnp.int32),
        pltpu.VMEM((8 * 48, S), jnp.int32),
        pltpu.VMEM((8 * 48, S), jnp.int32),
        pltpu.VMEM((8, 27, 8, S), F32),
        pltpu.VMEM((8, 7, S, S), F32),
        pltpu.VMEM((8, width, S, S), F32),
    ]


def contact_all(depth, width, scratch):
    local_ref, index_ref, base_ref, amount_ref, chosen_ref, list_ref, spread_ref, sum_ref = scratch
    inner = 1 - depth
    for c, (a, b, z) in enumerate(CELLS):
        start = own_place(a, b, z) * 8
        turned = jnp.transpose(local_ref[start : start + 8, :])
        for k in range(7):
            spread_ref[c, k] = jnp.broadcast_to(turned[:, k : k + 1], (S, S))

    place = [local_ref[pl.ds(k, 48, stride=8), :] for k in range(3)]
    radius = local_ref[pl.ds(6, 48, stride=8), :]
    rows = row_ids((48, S))
    row_x, row_y, row_slot = rows // 12, (rows // 3) % 4, rows % 3
    masks = []
    for a, b, z in CELLS:
        start = own_place(a, b, z) * 8
        mine = local_ref[start : start + 8, :]
        live = mine[6:7] > 0.0
        low = jnp.min(jnp.where(live, mine, 1e9), axis=1, keepdims=True)
        high = jnp.max(jnp.where(live, mine, -1e9), axis=1, keepdims=True)
        reach = radius + high[6:7]
        near = jnp.logical_and(
            jnp.logical_and(row_x >= a, row_x <= a + 2), jnp.logical_and(row_y >= b, row_y <= b + 2)
        )
        near = jnp.logical_and(near, jnp.logical_or(row_slot < 2, inner == z))
        for k in range(3):
            near = jnp.logical_and(near, place[k] + reach > low[k : k + 1])
            near = jnp.logical_and(near, place[k] - reach < high[k : k + 1])
        masks.append(jnp.where(near, 1.0, 0.0).astype(F32))
    mask = jnp.concatenate(masks, axis=0).astype(BF16)
    upper = one_hot(row_ids((S, 2 * S)) <= lane_ids((S, 2 * S)))
    sums = matmul(mask, upper)
    prefix, amount = sums[:, :S], sums[:, S:]
    before = one_hot(lane_ids((48, 48)) < row_ids((48, 48)))
    totals = []
    for c in range(8):
        part = amount[c * 48 : c * 48 + 48]
        base = matmul(before, part.astype(BF16))
        base_ref[c * 48 : c * 48 + 48, :] = base.astype(jnp.int32)
        totals.append((base[47:48, 0:1] + part[47:48, 0:1]).astype(jnp.int32)[0, 0])
    amount_ref[...] = amount.astype(jnp.int32)
    wanted = lane_ids((8 * 48, S)).astype(F32)
    index = jnp.zeros((8 * 48, S), jnp.int32)
    for step in (64, 32, 16, 8, 4, 2, 1):
        probe = lane_gather(prefix, index + (step - 1))
        index = jnp.where(probe <= wanted, index + step, index)
    index_ref[...] = index
    tiles = [(total + (S - 1)) // S for total in totals]
    most = tiles[0]
    for count in tiles[1:]:
        most = jnp.maximum(most, count)

    empty = jnp.where(row_ids((8, S)) == 6, DEAD, 0.0).astype(F32)

    def gather_tiles(t, carry):
        want = t * S + lane_ids((8 * 48, S)) - base_ref[...]
        valid = jnp.logical_and(want >= 0, want < amount_ref[...])
        source = lane_gather(index_ref[...], jnp.clip(want, 0, S - 1))
        chosen_ref[...] = jnp.where(valid, source, -1)
        for c, (a, b, z) in enumerate(CELLS):
            tile = empty
            for dx in range(3):
                for dy in range(3):
                    for slot in range(3):
                        n = ((a + dx) * 4 + b + dy) * 3 + slot
                        pick = jnp.broadcast_to(chosen_ref[c * 48 + n : c * 48 + n + 1, :], (8, S))
                        values = lane_gather(local_ref[n * 8 : n * 8 + 8, :], jnp.maximum(pick, 0))
                        tile = jnp.where(pick >= 0, values, tile)
            list_ref[c, t] = tile
        return carry

    gather_tiles(0, 0)
    lax.fori_loop(1, most, gather_tiles, 0)

    def pair_tile(c, t, first):
        tile = list_ref[c, t]
        other = [jnp.broadcast_to(tile[k : k + 1], (8, S)) for k in range(7)]
        for block in range(16):
            row = block * 8
            me = [spread_ref[c, k, row : row + 8, :] for k in range(7)]
            r = [me[k] - other[k] for k in range(3)]
            u = [me[3 + k] - other[3 + k] for k in range(3)]
            squared = r[0] * r[0] + r[1] * r[1] + r[2] * r[2] + SOFTENING
            inverse = lax.rsqrt(squared)
            along = u[0] * r[0] + u[1] * r[1] + u[2] * r[2]
            overlap = jnp.maximum((me[6] + other[6]) * inverse - 1.0, 0.0)
            weight = overlap * (STIFFNESS - (DAMPING * along) * inverse)
            terms = [weight * r[k] for k in range(3)]
            if width == 9:
                terms += [terms[left] * r[right] for left, right in PAIR_LIST]
            for k, term in enumerate(terms):
                if first:
                    sum_ref[c, k, row : row + 8, :] = term
                else:
                    sum_ref[c, k, row : row + 8, :] += term

    for c in range(8):
        pair_tile(c, 0, True)
    for group in PAIRS:

        def later_tile(t, carry):
            for c in group:
                pair_tile(c, t, False)
            return carry

        lax.fori_loop(1, jnp.maximum(tiles[group[0]], tiles[group[1]]), later_tile, 0)
    lanes = lane_ids((S, S))
    table = jnp.zeros((S, S), F32)
    for k in range(width):
        for c in range(8):
            column = jnp.sum(sum_ref[c, k], axis=1, keepdims=True)
            table = jnp.where(lanes == k * 8 + c, column, table)
    return jnp.transpose(table)[0 : width * 8]


def mass_of(radius):
    scaled = radius / RADIUS_REF
    return scaled * scaled * scaled


def step_kernel(wide, *refs):
    count = 8 if wide else 6
    pieces, (velocity_out, own_out, inner_out) = refs[:count], refs[count : count + 3]
    scratch = refs[count + 3 :]
    own = pieces[0]
    depth = lax.axis_index("depth")
    cell = piece_reader(pieces, wide, 8)
    for x, y, slot, start, centre in extended_cells(depth):
        scratch[0][start : start + 8, :] = local_state(cell(x, y, slot), centre)
    sums = contact_all(depth, 3, scratch)
    radius = own[pl.ds(6, 8, stride=8), :]
    safe_mass = jnp.where(radius > 0.0, mass_of(radius), 1.0)
    for k in range(3):
        velocity = own[pl.ds(3 + k, 8, stride=8), :] + TIME_STEP * sums[k * 8 : k * 8 + 8] / safe_mass
        for c, (a, b, z) in enumerate(CELLS):
            own_out[c * 4 + k : c * 4 + k + 1, :] = velocity[c : c + 1]
            if z == 0:
                velocity_out[k, a, b, :, :] = velocity[c : c + 2]
    for c in range(8):
        own_out[c * 4 + 3 : c * 4 + 4, :] = jnp.zeros((1, S), F32)
    for column in range(4):
        chosen = own_out[column * 8 : column * 8 + 8, :]
        inner_out[column * 4 : column * 4 + 4, :] = jnp.where(depth == 0, chosen[4:8], chosen[0:4])


def field_kernel(wide, grid, *refs):
    count = 8 if wide else 6
    pieces, speeds = refs[:count], refs[count : 2 * count]
    force_out, node_out = refs[2 * count : 2 * count + 2]
    moment_ref = refs[2 * count + 2]
    scratch = refs[2 * count + 3 :]
    local_ref = scratch[0]
    depth = lax.axis_index("depth")
    down = lax.axis_index("down")
    cross = lax.axis_index("cross")
    cell = piece_reader(pieces, wide, 8)
    speed = piece_reader(speeds, wide, 4)
    for x, y, slot, start, centre in extended_cells(depth):
        old = cell(x, y, slot)
        new = speed(x, y, slot)[0:3]
        shift = jnp.where(
            row_ids((3, S)) == 0, centre[0], jnp.where(row_ids((3, S)) == 1, centre[1], centre[2])
        )
        local_ref[start : start + 3, :] = (old[0:3] + TIME_STEP * new) + shift
        local_ref[start + 3 : start + 6, :] = new
        local_ref[start + 6 : start + 8, :] = old[6:8]
    sums = contact_all(depth, 9, scratch)
    radius = pieces[0][pl.ds(6, 8, stride=8), :]
    mass = jnp.where(radius > 0.0, mass_of(radius), 0.0)
    moments = [mass] + [mass * speeds[0][pl.ds(k, 8, stride=4), :] for k in range(3)]
    moments += [0.5 * sums[k * 8 : k * 8 + 8] for k in range(3, 9)]
    moment_ref[...] = jnp.zeros((16, 8 * S), F32)
    for k in range(3):
        for c, (a, b, z) in enumerate(CELLS):
            if z == 0:
                force_out[k, a, b, :, :] = sums[k * 8 + c : k * 8 + c + 2]
    for m, moment in enumerate(moments):
        for c in range(8):
            moment_ref[m : m + 1, c * S : (c + 1) * S] = moment[c : c + 1]
    rows = row_ids((64, S))
    near_x, near_y, near_z = rows // 16 - 1, (rows // 4) % 4 - 1, rows % 4 - 1
    centres = [index.astype(F32) - 0.5 for index in (near_x, near_y, near_z)]
    kernels = []
    for a, b, z in CELLS:
        start = own_place(a, b, z) * 8
        squared = jnp.zeros((64, S), F32)
        for k in range(3):
            gap = local_ref[start + k : start + k + 1, :] - centres[k]
            squared = squared + gap * gap
        kernel = jnp.exp(squared * (-0.5 / (KERNEL_WIDTH * KERNEL_WIDTH))) / KERNEL_NORM
        beside = jnp.logical_and(
            jnp.logical_and(jnp.abs(near_x - a) <= 1, jnp.abs(near_y - b) <= 1),
            jnp.abs(near_z - z) <= 1,
        )
        kernels.append(jnp.where(beside, kernel, 0.0))
    kernel_high, kernel_low = split(jnp.concatenate(kernels, axis=1))
    moment_high, moment_low = split(moment_ref[...])
    wide_part = matmul_turned(
        jnp.concatenate([moment_high, moment_low.astype(BF16)], axis=0), kernel_high
    )
    near = wide_part[0:16] + wide_part[16:32] + matmul_turned(moment_high, kernel_low.astype(BF16))
    size_x, size_y, size_z = grid
    nodes = size_x * size_y * size_z
    lanes = lane_ids((64, nodes))
    row = row_ids((64, nodes))
    target_x = (down * 2 + row // 16 - 1 + size_x) % size_x
    target_y = (cross * 2 + (row // 4) % 4 - 1 + size_y) % size_y
    target_z = depth * 2 + row % 4 - 1
    inside = jnp.logical_and(target_z >= 0, target_z < size_z)
    target = (target_x * size_y + target_y) * size_z + target_z
    chosen = one_hot(jnp.logical_and(inside, lanes == target))
    near_high, rest = split(near)
    near_middle, near_low = split(rest)
    placed = matmul(
        jnp.concatenate([near_high, near_middle, near_low.astype(BF16)], axis=0), chosen
    )
    node_out[...] = placed[0:16] + placed[16:32] + placed[32:48]


def library_kernel(grid, count, coefficients, *refs):
    parts = [ref[...] for ref in refs[:count]]
    residual_out, gram_out, moment_out, terms = refs[count:]
    while len(parts) > 1:
        parts = [parts[k] + parts[k + 1] for k in range(0, len(parts), 2)]
    fields = parts[0]
    size_x, size_y, size_z = grid
    nodes = size_x * size_y * size_z
    lanes = lax.broadcasted_iota(jnp.int32, (1, nodes), 1)
    node_x = lanes // (size_y * size_z)
    node_y = (lanes // size_z) % size_y
    node_z = lanes % size_z
    rows = row_ids((8, nodes))
    density = fields[0:1]
    values = jnp.where(rows == 0, fields[0:8], fields[0:8] / (density + MASS_SHIFT))

    def moved(value, step):
        return pltpu.roll(value, step % nodes, 1)

    plane = size_y * size_z
    slope_x = (moved(values, -plane) - moved(values, plane)) * 0.5
    after_y = jnp.where(
        node_y == size_y - 1, moved(values, (size_y - 1) * size_z), moved(values, -size_z)
    )
    before_y = jnp.where(
        node_y == 0, moved(values, -(size_y - 1) * size_z), moved(values, size_z)
    )
    slope_y = (after_y - before_y) * 0.5
    after_z = jnp.where(node_z == size_z - 1, 0.0, moved(values, -1))
    before_z = jnp.where(node_z == 0, 0.0, moved(values, 1))
    slope_z = (after_z - before_z) * 0.5
    slopes = [[table[k : k + 1] for k in range(4)] for table in (slope_x, slope_y, slope_z)]
    strain = [
        [0.5 * (slopes[left][1 + right] + slopes[right][1 + left]) for right in range(3)]
        for left in range(3)
    ]
    divergence = strain[0][0] + strain[1][1] + strain[2][2]
    rate_sum = jnp.zeros_like(density)
    for left in range(3):
        for right in range(3):
            entry = strain[left][right]
            if left == right:
                entry = entry - divergence / 3.0
            rate_sum = rate_sum + entry * entry
    shear_rate = jnp.sqrt(2.0 * rate_sum + 0.01)
    stress = [fields[4 + k : 5 + k] for k in range(6)]
    pressure = (stress[0] + stress[3] + stress[5]) / 3.0
    deviator = (
        (stress[0] - pressure) ** 2
        + (stress[3] - pressure) ** 2
        + (stress[5] - pressure) ** 2
        + 2.0 * (stress[1] ** 2 + stress[2] ** 2 + stress[4] ** 2)
    )
    shear_stress = jnp.sqrt(0.5 * deviator + 0.01)
    pressure_scale = jnp.sqrt(pressure * pressure + 1.0)
    friction = shear_stress / pressure_scale
    features = [
        density,
        pressure / pressure_scale,
        shear_rate,
        shear_rate / jnp.sqrt(pressure_scale),
        divergence,
        slopes[0][0],
        slopes[1][0],
        slopes[2][0],
    ]
    entries = list(features)
    for left in range(8):
        for right in range(left, 8):
            entries.append(features[left] * features[right])
    for left in range(1, 5):
        entries.append(features[left] * features[left] * features[left])
    model = jnp.zeros_like(density)
    for k, entry in enumerate(entries):
        terms[k : k + 1, :] = entry
        model = model + coefficients[k] * entry
    residual = friction - model
    table = terms[...]
    gram_out[...] = (
        lax.dot_general(
            table,
            table,
            (((1,), (1,)), ((), ())),
            precision=lax.Precision.HIGHEST,
            preferred_element_type=F32,
        )
        / nodes
    )
    moment = lax.dot_general(
        jnp.broadcast_to(friction, (8, nodes)),
        table,
        (((1,), (1,)), ((), ())),
        precision=lax.Precision.HIGHEST,
        preferred_element_type=F32,
    )
    moment_out[...] = moment[0:1] / nodes
    down = lax.axis_index("down")
    cross = lax.axis_index("cross")
    depth = lax.axis_index("depth")
    b_rows = lax.broadcasted_iota(jnp.int32, (2, 1), 0)
    z_lanes = lax.broadcasted_iota(jnp.int32, (2, 2), 1)
    for a in range(2):
        mine = jnp.logical_and(node_x == down * 2 + a, node_y == cross * 2 + b_rows)
        column = [
            jnp.sum(
                jnp.where(jnp.logical_and(mine, node_z == depth * 2 + z), residual, 0.0),
                axis=1,
                keepdims=True,
            )
            for z in range(2)
        ]
        residual_out[a] = jnp.where(z_lanes == 0, column[0], column[1])


def ring(axis, step):
    peers = lax.axis_size(axis)
    return [(i, (i + step) % peers) for i in range(peers)]


def exchange(own, inner, height):
    cross = lax.axis_size("cross")

    def cells(block, first, count):
        return block[first * height : (first + count) * height]

    depth_halo = lax.ppermute(inner, "depth", [(0, 1), (1, 0)])
    if cross == 2:
        side = lax.ppermute(own, "cross", [(0, 1), (1, 0)])
        diag = lax.ppermute(inner, ("cross", "depth"), [(i, 3 - i) for i in range(4)])
        sides = [side, diag]

        def lateral(x):
            return [
                cells(side, x * 4 + 2, 2),
                cells(side, x * 4, 2),
                cells(diag, x * 2 + 1, 1),
                cells(diag, x * 2, 1),
            ]

    else:
        pairs = [(i * 2 + j, ((i + 1) % cross) * 2 + 1 - j) for i in range(cross) for j in range(2)]
        back = [(i * 2 + j, ((i - 1) % cross) * 2 + 1 - j) for i in range(cross) for j in range(2)]
        last = jnp.concatenate([cells(own, 2, 2), cells(own, 6, 2)], axis=0)
        first = jnp.concatenate([cells(own, 0, 2), cells(own, 4, 2)], axis=0)
        last_inner = jnp.concatenate([cells(inner, 1, 1), cells(inner, 3, 1)], axis=0)
        first_inner = jnp.concatenate([cells(inner, 0, 1), cells(inner, 2, 1)], axis=0)
        before = lax.ppermute(last, "cross", ring("cross", 1))
        after = lax.ppermute(first, "cross", ring("cross", -1))
        diag_before = lax.ppermute(last_inner, ("cross", "depth"), pairs)
        diag_after = lax.ppermute(first_inner, ("cross", "depth"), back)
        sides = [before, after, diag_before, diag_after]

        def lateral(x):
            return [
                cells(before, x * 2, 2),
                cells(after, x * 2, 2),
                cells(diag_before, x, 1),
                cells(diag_after, x, 1),
            ]

    def face(x):
        return jnp.concatenate([cells(own, x * 4, 4), cells(depth_halo, x * 2, 2)] + lateral(x), axis=0)

    x_before = lax.ppermute(face(1), "down", ring("down", 1))
    x_after = lax.ppermute(face(0), "down", ring("down", -1))
    return [own, depth_halo] + sides + [x_before, x_after]


def shared(value, axes, peers):
    return [value] + [
        lax.ppermute(value, axes, [(i, i ^ k) for i in range(peers)]) for k in range(1, peers)
    ]


def tree_sum(parts):
    while len(parts) > 1:
        parts = [parts[k] + parts[k + 1] for k in range(0, len(parts), 2)]
    return parts[0]


def body(positions, velocities, sphere_radii, counts, coefficients):
    down, cross, depth = (lax.axis_size(name) for name in ("down", "cross", "depth"))
    wide = cross != 2
    grid = (2 * down, 2 * cross, 2 * depth)
    nodes = grid[0] * grid[1] * grid[2]
    params = pltpu.CompilerParams(vmem_limit_bytes=VMEM_LIMIT)
    vector_shape = jax.ShapeDtypeStruct((3, 2, 2, 2, S), F32)

    def rows(count):
        return jax.ShapeDtypeStruct((count, S), F32)

    own, inner = pl.pallas_call(
        pack_kernel,
        out_shape=(rows(64), rows(32)),
        in_specs=[SMEM_SPEC] + [pl.BlockSpec(memory_space=pl.ANY)] * 3,
        out_specs=(VMEM_SPEC, VMEM_SPEC),
        scratch_shapes=[
            pltpu.VMEM((3, 2, 2, 2, S), F32),
            pltpu.VMEM((3, 2, 2, 2, S), F32),
            pltpu.VMEM((2, 2, 2, S), F32),
            pltpu.SemaphoreType.DMA((3,)),
        ],
        compiler_params=params,
        name="pack",
    )(counts, positions, velocities, sphere_radii)
    pieces = exchange(own, inner, 8)
    velocity_new, own_speed, inner_speed = pl.pallas_call(
        functools.partial(step_kernel, wide),
        out_shape=(vector_shape, rows(32), rows(16)),
        in_specs=[VMEM_SPEC] * len(pieces),
        out_specs=(VMEM_SPEC,) * 3,
        scratch_shapes=contact_scratch(3),
        compiler_params=params,
        name="step",
    )(*pieces)
    speeds = exchange(own_speed, inner_speed, 4)
    force_next, partial = pl.pallas_call(
        functools.partial(field_kernel, wide, grid),
        out_shape=(vector_shape, jax.ShapeDtypeStruct((16, nodes), F32)),
        in_specs=[VMEM_SPEC] * (len(pieces) + len(speeds)),
        out_specs=(VMEM_SPEC,) * 2,
        scratch_shapes=[pltpu.VMEM((16, 8 * S), F32)] + contact_scratch(9),
        compiler_params=params,
        name="field",
    )(*pieces, *speeds)
    partial = tree_sum(shared(partial, ("cross", "depth"), cross * depth))
    parts = shared(partial, "down", down)
    residual_field, gram_matrix, moment = pl.pallas_call(
        functools.partial(library_kernel, grid, len(parts)),
        out_shape=(
            jax.ShapeDtypeStruct((2, 2, 2), F32),
            jax.ShapeDtypeStruct((TERMS, TERMS), F32),
            jax.ShapeDtypeStruct((1, TERMS), F32),
        ),
        in_specs=[SMEM_SPEC] + [VMEM_SPEC] * len(parts),
        out_specs=(VMEM_SPEC,) * 3,
        scratch_shapes=[pltpu.VMEM((TERMS, nodes), F32)],
        compiler_params=params,
        name="library",
    )(coefficients, *parts)
    return (velocity_new, force_next, residual_field, gram_matrix, moment.reshape(TERMS))


def solution(mesh):
    return jax.shard_map(
        body,
        mesh=mesh,
        in_specs=(
            P(None, ("groups", "down"), "cross", "depth", None),
            P(None, ("groups", "down"), "cross", "depth", None),
            P(("groups", "down"), "cross", "depth", None),
            P(("groups", "down"), "cross", "depth"),
            P(),
        ),
        out_specs=(
            P(None, ("groups", "down"), "cross", "depth", None),
            P(None, ("groups", "down"), "cross", "depth", None),
            P(("groups", "down"), "cross", "depth"),
            P("groups", None),
            P("groups"),
        ),
        check_vma=False,
    )
```

```python
import functools

import jax
import jax.numpy as jnp
from jax import lax
from jax.experimental import pallas as pl
from jax.experimental.pallas import tpu as pltpu
from jax.sharding import PartitionSpec as P

STIFFNESS = 100.0
DAMPING = 20.0
TIME_STEP = 0.05
KERNEL_WIDTH = 0.4
KERNEL_NORM = 64.0
SOFTENING = 0.0001
RADIUS_REF = 0.1
MASS_SHIFT = 0.1
DEAD = -1000.0
TERMS = 48
S = 128
F32 = jnp.float32
BF16 = jnp.bfloat16
CELLS = tuple((a, b, z) for a in range(2) for b in range(2) for z in range(2))
PAIRS = ((0, 2), (4, 6), (1, 3), (5, 7))
PAIR_LIST = ((0, 0), (0, 1), (0, 2), (1, 1), (1, 2), (2, 2))
VMEM_SPEC = pl.BlockSpec(memory_space=pltpu.VMEM)
SMEM_SPEC = pl.BlockSpec(memory_space=pltpu.SMEM)
VMEM_LIMIT = 48 * 1024 * 1024


def row_ids(shape):
    return lax.broadcasted_iota(jnp.int32, shape, 0)


def lane_ids(shape):
    return lax.broadcasted_iota(jnp.int32, shape, 1)


def one_hot(condition):
    return jnp.where(condition, 1.0, 0.0).astype(BF16)


def split(value):
    high = value.astype(BF16)
    return high, value - high.astype(F32)


def matmul(left, right):
    return lax.dot_general(left, right, (((1,), (0,)), ((), ())), preferred_element_type=F32)


def matmul_turned(left, right):
    return lax.dot_general(left, right, (((1,), (1,)), ((), ())), preferred_element_type=F32)


def lane_gather(table, index):
    return jnp.take_along_axis(table, index, axis=1)


def pack_kernel(
    counts, positions_hbm, velocities_hbm, radii_hbm, own, inner, positions, velocities, radii, arrived
):
    copies = [
        pltpu.make_async_copy(source, target, arrived.at[k])
        for k, (source, target) in enumerate(
            ((positions_hbm, positions), (velocities_hbm, velocities), (radii_hbm, radii))
        )
    ]
    for copy in copies:
        copy.start()
    for copy in copies:
        copy.wait()
    depth = lax.axis_index("depth")
    lanes = lane_ids((1, S))
    for c, (a, b, z) in enumerate(CELLS):
        for k in range(3):
            own[c * 8 + k : c * 8 + k + 1, :] = positions[k, a, b, z : z + 1, :]
            own[c * 8 + 3 + k : c * 8 + 4 + k, :] = velocities[k, a, b, z : z + 1, :]
        live = lanes < counts[a, b, z]
        own[c * 8 + 6 : c * 8 + 7, :] = jnp.where(live, radii[a, b, z : z + 1, :], DEAD)
        own[c * 8 + 7 : c * 8 + 8, :] = jnp.zeros((1, S), F32)
    for column in range(4):
        source = pl.multiple_of(column * 16 + (1 - depth) * 8, 8)
        inner[column * 8 : column * 8 + 8, :] = own[pl.ds(source, 8), :]


def local_state(raw, centre):
    rows = row_ids(raw.shape)
    shift = jnp.where(rows == 0, centre[0], jnp.where(rows == 1, centre[1], centre[2]))
    return jnp.where(rows < 3, raw + shift, raw)


def piece_reader(refs, wide, height):
    own, depth_halo = refs[0], refs[1]
    x_before, x_after = refs[-2], refs[-1]

    def read(ref, cell):
        return ref[cell * height : cell * height + height, :]

    def cell(x, y, slot):
        if x in (0, 3):
            face = x_before if x == 0 else x_after
            if y in (1, 2):
                return read(face, (y - 1) * 2 + slot if slot < 2 else 4 + y - 1)
            side = 0 if y == 0 else 1
            return read(face, 6 + side * 2 + slot if slot < 2 else 10 + side)
        a = x - 1
        if y in (1, 2):
            return read(own, a * 4 + (y - 1) * 2 + slot) if slot < 2 else read(depth_halo, a * 2 + y - 1)
        if wide:
            before, after, diag_before, diag_after = refs[2:6]
            if slot < 2:
                return read(before if y == 0 else after, a * 2 + slot)
            return read(diag_before if y == 0 else diag_after, a)
        side, diag = refs[2:4]
        b = 1 if y == 0 else 0
        return read(side, a * 4 + b * 2 + slot) if slot < 2 else read(diag, a * 2 + b)

    return cell


def own_place(a, b, z):
    return ((a + 1) * 4 + b + 1) * 3 + z


def extended_cells(depth):
    halo_z = 1.5 - 3.0 * depth.astype(F32)
    for x in range(4):
        for y in range(4):
            for slot in range(3):
                centre = (x - 1.5, y - 1.5, slot - 0.5 if slot < 2 else halo_z)
                yield x, y, slot, ((x * 4 + y) * 3 + slot) * 8, centre


def contact_scratch(width):
    return [
        pltpu.VMEM((48 * 8, S), F32),
        pltpu.VMEM((8 * 48, S), jnp.int32),
        pltpu.VMEM((8 * 48, S), jnp.int32),
        pltpu.VMEM((8 * 48, S), jnp.int32),
        pltpu.VMEM((8 * 48, S), jnp.int32),
        pltpu.VMEM((8, 27, 8, S), F32),
        pltpu.VMEM((8, 7, S, S), F32),
        pltpu.VMEM((8, width, S, S), F32),
    ]


def contact_all(depth, width, scratch):
    local_ref, index_ref, base_ref, amount_ref, chosen_ref, list_ref, spread_ref, sum_ref = scratch
    inner = 1 - depth
    for c, (a, b, z) in enumerate(CELLS):
        start = own_place(a, b, z) * 8
        turned = jnp.transpose(local_ref[start : start + 8, :])
        for k in range(7):
            spread_ref[c, k] = jnp.broadcast_to(turned[:, k : k + 1], (S, S))

    place = [local_ref[pl.ds(k, 48, stride=8), :] for k in range(3)]
    radius = local_ref[pl.ds(6, 48, stride=8), :]
    rows = row_ids((48, S))
    row_x, row_y, row_slot = rows // 12, (rows // 3) % 4, rows % 3
    masks = []
    for a, b, z in CELLS:
        start = own_place(a, b, z) * 8
        mine = local_ref[start : start + 8, :]
        live = mine[6:7] > 0.0
        low = jnp.min(jnp.where(live, mine, 1e9), axis=1, keepdims=True)
        high = jnp.max(jnp.where(live, mine, -1e9), axis=1, keepdims=True)
        reach = radius + high[6:7]
        near = jnp.logical_and(
            jnp.logical_and(row_x >= a, row_x <= a + 2), jnp.logical_and(row_y >= b, row_y <= b + 2)
        )
        near = jnp.logical_and(near, jnp.logical_or(row_slot < 2, inner == z))
        for k in range(3):
            near = jnp.logical_and(near, place[k] + reach > low[k : k + 1])
            near = jnp.logical_and(near, place[k] - reach < high[k : k + 1])
        masks.append(jnp.where(near, 1.0, 0.0).astype(F32))
    mask = jnp.concatenate(masks, axis=0).astype(BF16)
    upper = one_hot(row_ids((S, 2 * S)) <= lane_ids((S, 2 * S)))
    sums = matmul(mask, upper)
    prefix, amount = sums[:, :S], sums[:, S:]
    before = one_hot(lane_ids((48, 48)) < row_ids((48, 48)))
    totals = []
    for c in range(8):
        part = amount[c * 48 : c * 48 + 48]
        base = matmul(before, part.astype(BF16))
        base_ref[c * 48 : c * 48 + 48, :] = base.astype(jnp.int32)
        totals.append((base[47:48, 0:1] + part[47:48, 0:1]).astype(jnp.int32)[0, 0])
    amount_ref[...] = amount.astype(jnp.int32)
    wanted = lane_ids((8 * 48, S)).astype(F32)
    index = jnp.zeros((8 * 48, S), jnp.int32)
    for step in (64, 32, 16, 8, 4, 2, 1):
        probe = lane_gather(prefix, index + (step - 1))
        index = jnp.where(probe <= wanted, index + step, index)
    index_ref[...] = index
    tiles = [(total + (S - 1)) // S for total in totals]
    most = tiles[0]
    for count in tiles[1:]:
        most = jnp.maximum(most, count)

    empty = jnp.where(row_ids((8, S)) == 6, DEAD, 0.0).astype(F32)

    def gather_tiles(t, carry):
        want = t * S + lane_ids((8 * 48, S)) - base_ref[...]
        valid = jnp.logical_and(want >= 0, want < amount_ref[...])
        source = lane_gather(index_ref[...], jnp.clip(want, 0, S - 1))
        chosen_ref[...] = jnp.where(valid, source, -1)
        for c, (a, b, z) in enumerate(CELLS):
            tile = empty
            for dx in range(3):
                for dy in range(3):
                    for slot in range(3):
                        n = ((a + dx) * 4 + b + dy) * 3 + slot
                        pick = jnp.broadcast_to(chosen_ref[c * 48 + n : c * 48 + n + 1, :], (8, S))
                        values = lane_gather(local_ref[n * 8 : n * 8 + 8, :], jnp.maximum(pick, 0))
                        tile = jnp.where(pick >= 0, values, tile)
            list_ref[c, t] = tile
        return carry

    gather_tiles(0, 0)
    lax.fori_loop(1, most, gather_tiles, 0)

    def pair_tile(c, t, first):
        tile = list_ref[c, t]
        other = [jnp.broadcast_to(tile[k : k + 1], (8, S)) for k in range(7)]
        for block in range(16):
            row = block * 8
            me = [spread_ref[c, k, row : row + 8, :] for k in range(7)]
            r = [me[k] - other[k] for k in range(3)]
            u = [me[3 + k] - other[3 + k] for k in range(3)]
            squared = r[0] * r[0] + r[1] * r[1] + r[2] * r[2] + SOFTENING
            inverse = lax.rsqrt(squared)
            along = u[0] * r[0] + u[1] * r[1] + u[2] * r[2]
            overlap = jnp.maximum((me[6] + other[6]) * inverse - 1.0, 0.0)
            weight = overlap * (STIFFNESS - (DAMPING * along) * inverse)
            terms = [weight * r[k] for k in range(3)]
            if width == 9:
                terms += [terms[left] * r[right] for left, right in PAIR_LIST]
            for k, term in enumerate(terms):
                if first:
                    sum_ref[c, k, row : row + 8, :] = term
                else:
                    sum_ref[c, k, row : row + 8, :] += term

    for c in range(8):
        pair_tile(c, 0, True)
    for group in PAIRS:

        def later_tile(t, carry):
            for c in group:
                pair_tile(c, t, False)
            return carry

        lax.fori_loop(1, jnp.maximum(tiles[group[0]], tiles[group[1]]), later_tile, 0)
    lanes = lane_ids((S, S))
    table = jnp.zeros((S, S), F32)
    for k in range(width):
        for c in range(8):
            column = jnp.sum(sum_ref[c, k], axis=1, keepdims=True)
            table = jnp.where(lanes == k * 8 + c, column, table)
    return jnp.transpose(table)[0 : width * 8]


def mass_of(radius):
    scaled = radius / RADIUS_REF
    return scaled * scaled * scaled


def step_kernel(wide, *refs):
    count = 8 if wide else 6
    pieces, (velocity_out, own_out, inner_out) = refs[:count], refs[count : count + 3]
    scratch = refs[count + 3 :]
    own = pieces[0]
    depth = lax.axis_index("depth")
    cell = piece_reader(pieces, wide, 8)
    for x, y, slot, start, centre in extended_cells(depth):
        scratch[0][start : start + 8, :] = local_state(cell(x, y, slot), centre)
    sums = contact_all(depth, 3, scratch)
    radius = own[pl.ds(6, 8, stride=8), :]
    safe_mass = jnp.where(radius > 0.0, mass_of(radius), 1.0)
    for k in range(3):
        velocity = own[pl.ds(3 + k, 8, stride=8), :] + TIME_STEP * sums[k * 8 : k * 8 + 8] / safe_mass
        for c, (a, b, z) in enumerate(CELLS):
            own_out[c * 4 + k : c * 4 + k + 1, :] = velocity[c : c + 1]
            if z == 0:
                velocity_out[k, a, b, :, :] = velocity[c : c + 2]
    for c in range(8):
        own_out[c * 4 + 3 : c * 4 + 4, :] = jnp.zeros((1, S), F32)
    for column in range(4):
        chosen = own_out[column * 8 : column * 8 + 8, :]
        inner_out[column * 4 : column * 4 + 4, :] = jnp.where(depth == 0, chosen[4:8], chosen[0:4])


def field_kernel(wide, grid, *refs):
    count = 8 if wide else 6
    pieces, speeds = refs[:count], refs[count : 2 * count]
    force_out, node_out = refs[2 * count : 2 * count + 2]
    moment_ref = refs[2 * count + 2]
    scratch = refs[2 * count + 3 :]
    local_ref = scratch[0]
    depth = lax.axis_index("depth")
    down = lax.axis_index("down")
    cross = lax.axis_index("cross")
    cell = piece_reader(pieces, wide, 8)
    speed = piece_reader(speeds, wide, 4)
    for x, y, slot, start, centre in extended_cells(depth):
        old = cell(x, y, slot)
        new = speed(x, y, slot)[0:3]
        shift = jnp.where(
            row_ids((3, S)) == 0, centre[0], jnp.where(row_ids((3, S)) == 1, centre[1], centre[2])
        )
        local_ref[start : start + 3, :] = (old[0:3] + TIME_STEP * new) + shift
        local_ref[start + 3 : start + 6, :] = new
        local_ref[start + 6 : start + 8, :] = old[6:8]
    sums = contact_all(depth, 9, scratch)
    radius = pieces[0][pl.ds(6, 8, stride=8), :]
    mass = jnp.where(radius > 0.0, mass_of(radius), 0.0)
    moments = [mass] + [mass * speeds[0][pl.ds(k, 8, stride=4), :] for k in range(3)]
    moments += [0.5 * sums[k * 8 : k * 8 + 8] for k in range(3, 9)]
    moment_ref[...] = jnp.zeros((16, 8 * S), F32)
    for k in range(3):
        for c, (a, b, z) in enumerate(CELLS):
            if z == 0:
                force_out[k, a, b, :, :] = sums[k * 8 + c : k * 8 + c + 2]
    for m, moment in enumerate(moments):
        for c in range(8):
            moment_ref[m : m + 1, c * S : (c + 1) * S] = moment[c : c + 1]
    rows = row_ids((64, S))
    near_x, near_y, near_z = rows // 16 - 1, (rows // 4) % 4 - 1, rows % 4 - 1
    centres = [index.astype(F32) - 0.5 for index in (near_x, near_y, near_z)]
    kernels = []
    for a, b, z in CELLS:
        start = own_place(a, b, z) * 8
        squared = jnp.zeros((64, S), F32)
        for k in range(3):
            gap = local_ref[start + k : start + k + 1, :] - centres[k]
            squared = squared + gap * gap
        kernel = jnp.exp(squared * (-0.5 / (KERNEL_WIDTH * KERNEL_WIDTH))) / KERNEL_NORM
        beside = jnp.logical_and(
            jnp.logical_and(jnp.abs(near_x - a) <= 1, jnp.abs(near_y - b) <= 1),
            jnp.abs(near_z - z) <= 1,
        )
        kernels.append(jnp.where(beside, kernel, 0.0))
    kernel_high, kernel_low = split(jnp.concatenate(kernels, axis=1))
    moment_high, moment_low = split(moment_ref[...])
    wide_part = matmul_turned(
        jnp.concatenate([moment_high, moment_low.astype(BF16)], axis=0), kernel_high
    )
    near = wide_part[0:16] + wide_part[16:32] + matmul_turned(moment_high, kernel_low.astype(BF16))
    size_x, size_y, size_z = grid
    nodes = size_x * size_y * size_z
    lanes = lane_ids((64, nodes))
    row = row_ids((64, nodes))
    target_x = (down * 2 + row // 16 - 1 + size_x) % size_x
    target_y = (cross * 2 + (row // 4) % 4 - 1 + size_y) % size_y
    target_z = depth * 2 + row % 4 - 1
    inside = jnp.logical_and(target_z >= 0, target_z < size_z)
    target = (target_x * size_y + target_y) * size_z + target_z
    chosen = one_hot(jnp.logical_and(inside, lanes == target))
    near_high, rest = split(near)
    near_middle, near_low = split(rest)
    placed = matmul(
        jnp.concatenate([near_high, near_middle, near_low.astype(BF16)], axis=0), chosen
    )
    node_out[...] = placed[0:16] + placed[16:32] + placed[32:48]


def library_kernel(grid, coefficients, parts, residual_out, gram_out, moment_out, terms):
    fields = jnp.sum(parts[...], axis=0)
    size_x, size_y, size_z = grid
    nodes = size_x * size_y * size_z
    lanes = lax.broadcasted_iota(jnp.int32, (1, nodes), 1)
    node_x = lanes // (size_y * size_z)
    node_y = (lanes // size_z) % size_y
    node_z = lanes % size_z
    rows = row_ids((8, nodes))
    density = fields[0:1]
    values = jnp.where(rows == 0, fields[0:8], fields[0:8] / (density + MASS_SHIFT))

    def moved(value, step):
        return pltpu.roll(value, step % nodes, 1)

    plane = size_y * size_z
    slope_x = (moved(values, -plane) - moved(values, plane)) * 0.5
    after_y = jnp.where(
        node_y == size_y - 1, moved(values, (size_y - 1) * size_z), moved(values, -size_z)
    )
    before_y = jnp.where(
        node_y == 0, moved(values, -(size_y - 1) * size_z), moved(values, size_z)
    )
    slope_y = (after_y - before_y) * 0.5
    after_z = jnp.where(node_z == size_z - 1, 0.0, moved(values, -1))
    before_z = jnp.where(node_z == 0, 0.0, moved(values, 1))
    slope_z = (after_z - before_z) * 0.5
    slopes = [[table[k : k + 1] for k in range(4)] for table in (slope_x, slope_y, slope_z)]
    strain = [
        [0.5 * (slopes[left][1 + right] + slopes[right][1 + left]) for right in range(3)]
        for left in range(3)
    ]
    divergence = strain[0][0] + strain[1][1] + strain[2][2]
    rate_sum = jnp.zeros_like(density)
    for left in range(3):
        for right in range(3):
            entry = strain[left][right]
            if left == right:
                entry = entry - divergence / 3.0
            rate_sum = rate_sum + entry * entry
    shear_rate = jnp.sqrt(2.0 * rate_sum + 0.01)
    stress = [fields[4 + k : 5 + k] for k in range(6)]
    pressure = (stress[0] + stress[3] + stress[5]) / 3.0
    deviator = (
        (stress[0] - pressure) ** 2
        + (stress[3] - pressure) ** 2
        + (stress[5] - pressure) ** 2
        + 2.0 * (stress[1] ** 2 + stress[2] ** 2 + stress[4] ** 2)
    )
    shear_stress = jnp.sqrt(0.5 * deviator + 0.01)
    pressure_scale = jnp.sqrt(pressure * pressure + 1.0)
    friction = shear_stress / pressure_scale
    features = [
        density,
        pressure / pressure_scale,
        shear_rate,
        shear_rate / jnp.sqrt(pressure_scale),
        divergence,
        slopes[0][0],
        slopes[1][0],
        slopes[2][0],
    ]
    entries = list(features)
    for left in range(8):
        for right in range(left, 8):
            entries.append(features[left] * features[right])
    for left in range(1, 5):
        entries.append(features[left] * features[left] * features[left])
    model = jnp.zeros_like(density)
    for k, entry in enumerate(entries):
        terms[k : k + 1, :] = entry
        model = model + coefficients[k] * entry
    residual = friction - model
    table = terms[...]
    gram_out[...] = (
        lax.dot_general(
            table,
            table,
            (((1,), (1,)), ((), ())),
            precision=lax.Precision.HIGHEST,
            preferred_element_type=F32,
        )
        / nodes
    )
    moment = lax.dot_general(
        jnp.broadcast_to(friction, (8, nodes)),
        table,
        (((1,), (1,)), ((), ())),
        precision=lax.Precision.HIGHEST,
        preferred_element_type=F32,
    )
    moment_out[...] = moment[0:1] / nodes
    down = lax.axis_index("down")
    cross = lax.axis_index("cross")
    depth = lax.axis_index("depth")
    b_rows = lax.broadcasted_iota(jnp.int32, (2, 1), 0)
    z_lanes = lax.broadcasted_iota(jnp.int32, (2, 2), 1)
    for a in range(2):
        mine = jnp.logical_and(node_x == down * 2 + a, node_y == cross * 2 + b_rows)
        column = [
            jnp.sum(
                jnp.where(jnp.logical_and(mine, node_z == depth * 2 + z), residual, 0.0),
                axis=1,
                keepdims=True,
            )
            for z in range(2)
        ]
        residual_out[a] = jnp.where(z_lanes == 0, column[0], column[1])


def ring(axis, step):
    peers = lax.axis_size(axis)
    return [(i, (i + step) % peers) for i in range(peers)]


def exchange(own, inner, height):
    cross = lax.axis_size("cross")

    def cells(block, first, count):
        return block[first * height : (first + count) * height]

    depth_halo = lax.ppermute(inner, "depth", [(0, 1), (1, 0)])
    if cross == 2:
        side = lax.ppermute(own, "cross", [(0, 1), (1, 0)])
        diag = lax.ppermute(inner, ("cross", "depth"), [(i, 3 - i) for i in range(4)])
        sides = [side, diag]

        def lateral(x):
            return [
                cells(side, x * 4 + 2, 2),
                cells(side, x * 4, 2),
                cells(diag, x * 2 + 1, 1),
                cells(diag, x * 2, 1),
            ]

    else:
        pairs = [(i * 2 + j, ((i + 1) % cross) * 2 + 1 - j) for i in range(cross) for j in range(2)]
        back = [(i * 2 + j, ((i - 1) % cross) * 2 + 1 - j) for i in range(cross) for j in range(2)]
        last = jnp.concatenate([cells(own, 2, 2), cells(own, 6, 2)], axis=0)
        first = jnp.concatenate([cells(own, 0, 2), cells(own, 4, 2)], axis=0)
        last_inner = jnp.concatenate([cells(inner, 1, 1), cells(inner, 3, 1)], axis=0)
        first_inner = jnp.concatenate([cells(inner, 0, 1), cells(inner, 2, 1)], axis=0)
        before = lax.ppermute(last, "cross", ring("cross", 1))
        after = lax.ppermute(first, "cross", ring("cross", -1))
        diag_before = lax.ppermute(last_inner, ("cross", "depth"), pairs)
        diag_after = lax.ppermute(first_inner, ("cross", "depth"), back)
        sides = [before, after, diag_before, diag_after]

        def lateral(x):
            return [
                cells(before, x * 2, 2),
                cells(after, x * 2, 2),
                cells(diag_before, x, 1),
                cells(diag_after, x, 1),
            ]

    def face(x):
        return jnp.concatenate([cells(own, x * 4, 4), cells(depth_halo, x * 2, 2)] + lateral(x), axis=0)

    x_before = lax.ppermute(face(1), "down", ring("down", 1))
    x_after = lax.ppermute(face(0), "down", ring("down", -1))
    return [own, depth_halo] + sides + [x_before, x_after]


def body(positions, velocities, sphere_radii, counts, coefficients):
    down, cross, depth = (lax.axis_size(name) for name in ("down", "cross", "depth"))
    wide = cross != 2
    grid = (2 * down, 2 * cross, 2 * depth)
    nodes = grid[0] * grid[1] * grid[2]
    params = pltpu.CompilerParams(vmem_limit_bytes=VMEM_LIMIT)
    vector_shape = jax.ShapeDtypeStruct((3, 2, 2, 2, S), F32)

    def rows(count):
        return jax.ShapeDtypeStruct((count, S), F32)

    own, inner = pl.pallas_call(
        pack_kernel,
        out_shape=(rows(64), rows(32)),
        in_specs=[SMEM_SPEC] + [pl.BlockSpec(memory_space=pl.ANY)] * 3,
        out_specs=(VMEM_SPEC, VMEM_SPEC),
        scratch_shapes=[
            pltpu.VMEM((3, 2, 2, 2, S), F32),
            pltpu.VMEM((3, 2, 2, 2, S), F32),
            pltpu.VMEM((2, 2, 2, S), F32),
            pltpu.SemaphoreType.DMA((3,)),
        ],
        compiler_params=pltpu.CompilerParams(vmem_limit_bytes=60 * 1024 * 1024),
        name="pack",
    )(counts, positions, velocities, sphere_radii)
    pieces = exchange(own, inner, 8)
    velocity_new, own_speed, inner_speed = pl.pallas_call(
        functools.partial(step_kernel, wide),
        out_shape=(vector_shape, rows(32), rows(16)),
        in_specs=[VMEM_SPEC] * len(pieces),
        out_specs=(VMEM_SPEC,) * 3,
        scratch_shapes=contact_scratch(3),
        compiler_params=params,
        name="step",
    )(*pieces)
    speeds = exchange(own_speed, inner_speed, 4)
    force_next, partial = pl.pallas_call(
        functools.partial(field_kernel, wide, grid),
        out_shape=(vector_shape, jax.ShapeDtypeStruct((16, nodes), F32)),
        in_specs=[VMEM_SPEC] * (len(pieces) + len(speeds)),
        out_specs=(VMEM_SPEC,) * 2,
        scratch_shapes=[pltpu.VMEM((16, 8 * S), F32)] + contact_scratch(9),
        compiler_params=params,
        name="field",
    )(*pieces, *speeds)
    peers = down * cross * depth
    parts = lax.all_to_all(
        jnp.broadcast_to(partial, (peers, 16, nodes)), ("down", "cross", "depth"), 0, 0
    )
    residual_field, gram_matrix, moment = pl.pallas_call(
        functools.partial(library_kernel, grid),
        out_shape=(
            jax.ShapeDtypeStruct((2, 2, 2), F32),
            jax.ShapeDtypeStruct((TERMS, TERMS), F32),
            jax.ShapeDtypeStruct((1, TERMS), F32),
        ),
        in_specs=[SMEM_SPEC, VMEM_SPEC],
        out_specs=(VMEM_SPEC,) * 3,
        scratch_shapes=[pltpu.VMEM((TERMS, nodes), F32)],
        compiler_params=params,
        name="library",
    )(coefficients, parts)
    return (velocity_new, force_next, residual_field, gram_matrix, moment.reshape(TERMS))


def solution(mesh):
    return jax.shard_map(
        body,
        mesh=mesh,
        in_specs=(
            P(None, ("groups", "down"), "cross", "depth", None),
            P(None, ("groups", "down"), "cross", "depth", None),
            P(("groups", "down"), "cross", "depth", None),
            P(("groups", "down"), "cross", "depth"),
            P(),
        ),
        out_specs=(
            P(None, ("groups", "down"), "cross", "depth", None),
            P(None, ("groups", "down"), "cross", "depth", None),
            P(("groups", "down"), "cross", "depth"),
            P("groups", None),
            P("groups"),
        ),
        check_vma=False,
    )
```

```python
import functools

import jax
import jax.numpy as jnp
from jax import lax
from jax.experimental import pallas as pl
from jax.experimental.pallas import tpu as pltpu
from jax.sharding import PartitionSpec as P

STIFFNESS = 100.0
DAMPING = 20.0
TIME_STEP = 0.05
KERNEL_WIDTH = 0.4
KERNEL_NORM = 64.0
SOFTENING = 0.0001
RADIUS_REF = 0.1
MASS_SHIFT = 0.1
DEAD = -1000.0
TERMS = 48
S = 128
F32 = jnp.float32
BF16 = jnp.bfloat16
CELLS = tuple((a, b, z) for a in range(2) for b in range(2) for z in range(2))
PAIRS = ((0, 2), (4, 6), (1, 3), (5, 7))
PAIR_LIST = ((0, 0), (0, 1), (0, 2), (1, 1), (1, 2), (2, 2))
VMEM_SPEC = pl.BlockSpec(memory_space=pltpu.VMEM)
SMEM_SPEC = pl.BlockSpec(memory_space=pltpu.SMEM)
VMEM_LIMIT = 48 * 1024 * 1024


def row_ids(shape):
    return lax.broadcasted_iota(jnp.int32, shape, 0)


def lane_ids(shape):
    return lax.broadcasted_iota(jnp.int32, shape, 1)


def one_hot(condition):
    return jnp.where(condition, 1.0, 0.0).astype(BF16)


def split(value):
    high = value.astype(BF16)
    return high, value - high.astype(F32)


def matmul(left, right):
    return lax.dot_general(left, right, (((1,), (0,)), ((), ())), preferred_element_type=F32)


def matmul_turned(left, right):
    return lax.dot_general(left, right, (((1,), (1,)), ((), ())), preferred_element_type=F32)


def lane_gather(table, index):
    return jnp.take_along_axis(table, index, axis=1)


def pack_kernel(
    counts, positions_hbm, velocities_hbm, radii_hbm, own, positions, velocities, radii, arrived
):
    copies = [
        pltpu.make_async_copy(source, target, arrived.at[k])
        for k, (source, target) in enumerate(
            ((positions_hbm, positions), (velocities_hbm, velocities), (radii_hbm, radii))
        )
    ]
    for copy in copies:
        copy.start()
    for copy in copies:
        copy.wait()
    lanes = lane_ids((1, S))
    for c, (a, b, z) in enumerate(CELLS):
        for k in range(3):
            own[c * 8 + k : c * 8 + k + 1, :] = positions[k, a, b, z : z + 1, :]
            own[c * 8 + 3 + k : c * 8 + 4 + k, :] = velocities[k, a, b, z : z + 1, :]
        live = lanes < counts[a, b, z]
        own[c * 8 + 6 : c * 8 + 7, :] = jnp.where(live, radii[a, b, z : z + 1, :], DEAD)
        own[c * 8 + 7 : c * 8 + 8, :] = jnp.zeros((1, S), F32)


def local_state(raw, centre):
    rows = row_ids(raw.shape)
    shift = jnp.where(rows == 0, centre[0], jnp.where(rows == 1, centre[1], centre[2]))
    return jnp.where(rows < 3, raw + shift, raw)


def cell_reader(gathered, height):
    down, cross, depth = (lax.axis_index(name) for name in ("down", "cross", "depth"))
    downs, crosses = lax.axis_size("down"), lax.axis_size("cross")

    def cell(x, y, slot):
        down_at = lax.rem(down + (x + 1) // 2 - 1 + downs, downs)
        cross_at = lax.rem(cross + (y + 1) // 2 - 1 + crosses, crosses)
        device = (down_at * crosses + cross_at) * 2
        place = (1 - x % 2) * 4 + (1 - y % 2) * 2
        if slot < 2:
            start = (device + depth) * 8 + place + slot
        else:
            start = (device + 1 - depth) * 8 + place + depth
        return gathered[pl.ds(pl.multiple_of(start * height, height), height), :]

    return cell


def own_place(a, b, z):
    return ((a + 1) * 4 + b + 1) * 3 + z


def extended_cells(depth):
    halo_z = 1.5 - 3.0 * depth.astype(F32)
    for x in range(4):
        for y in range(4):
            for slot in range(3):
                centre = (x - 1.5, y - 1.5, slot - 0.5 if slot < 2 else halo_z)
                yield x, y, slot, ((x * 4 + y) * 3 + slot) * 8, centre


def contact_scratch(width):
    return [
        pltpu.VMEM((48 * 8, S), F32),
        pltpu.VMEM((8 * 48, S), jnp.int32),
        pltpu.VMEM((8 * 48, S), jnp.int32),
        pltpu.VMEM((8 * 48, S), jnp.int32),
        pltpu.VMEM((8 * 48, S), jnp.int32),
        pltpu.VMEM((8, 27, 8, S), F32),
        pltpu.VMEM((8, 7, S, S), F32),
        pltpu.VMEM((8, width, S, S), F32),
    ]


def contact_all(depth, width, scratch):
    local_ref, index_ref, base_ref, amount_ref, chosen_ref, list_ref, spread_ref, sum_ref = scratch
    inner = 1 - depth
    for c, (a, b, z) in enumerate(CELLS):
        start = own_place(a, b, z) * 8
        turned = jnp.transpose(local_ref[start : start + 8, :])
        for k in range(7):
            spread_ref[c, k] = jnp.broadcast_to(turned[:, k : k + 1], (S, S))

    place = [local_ref[pl.ds(k, 48, stride=8), :] for k in range(3)]
    radius = local_ref[pl.ds(6, 48, stride=8), :]
    rows = row_ids((48, S))
    row_x, row_y, row_slot = rows // 12, (rows // 3) % 4, rows % 3
    masks = []
    for a, b, z in CELLS:
        start = own_place(a, b, z) * 8
        mine = local_ref[start : start + 8, :]
        live = mine[6:7] > 0.0
        low = jnp.min(jnp.where(live, mine, 1e9), axis=1, keepdims=True)
        high = jnp.max(jnp.where(live, mine, -1e9), axis=1, keepdims=True)
        reach = radius + high[6:7]
        near = jnp.logical_and(
            jnp.logical_and(row_x >= a, row_x <= a + 2), jnp.logical_and(row_y >= b, row_y <= b + 2)
        )
        near = jnp.logical_and(near, jnp.logical_or(row_slot < 2, inner == z))
        for k in range(3):
            near = jnp.logical_and(near, place[k] + reach > low[k : k + 1])
            near = jnp.logical_and(near, place[k] - reach < high[k : k + 1])
        masks.append(jnp.where(near, 1.0, 0.0).astype(F32))
    mask = jnp.concatenate(masks, axis=0).astype(BF16)
    upper = one_hot(row_ids((S, 2 * S)) <= lane_ids((S, 2 * S)))
    sums = matmul(mask, upper)
    prefix, amount = sums[:, :S], sums[:, S:]
    before = one_hot(lane_ids((48, 48)) < row_ids((48, 48)))
    totals = []
    for c in range(8):
        part = amount[c * 48 : c * 48 + 48]
        base = matmul(before, part.astype(BF16))
        base_ref[c * 48 : c * 48 + 48, :] = base.astype(jnp.int32)
        totals.append((base[47:48, 0:1] + part[47:48, 0:1]).astype(jnp.int32)[0, 0])
    amount_ref[...] = amount.astype(jnp.int32)
    wanted = lane_ids((8 * 48, S)).astype(F32)
    index = jnp.zeros((8 * 48, S), jnp.int32)
    for step in (64, 32, 16, 8, 4, 2, 1):
        probe = lane_gather(prefix, index + (step - 1))
        index = jnp.where(probe <= wanted, index + step, index)
    index_ref[...] = index
    tiles = [(total + (S - 1)) // S for total in totals]
    most = tiles[0]
    for count in tiles[1:]:
        most = jnp.maximum(most, count)

    empty = jnp.where(row_ids((8, S)) == 6, DEAD, 0.0).astype(F32)

    def gather_tiles(t, carry):
        want = t * S + lane_ids((8 * 48, S)) - base_ref[...]
        valid = jnp.logical_and(want >= 0, want < amount_ref[...])
        source = lane_gather(index_ref[...], jnp.clip(want, 0, S - 1))
        chosen_ref[...] = jnp.where(valid, source, -1)
        for c, (a, b, z) in enumerate(CELLS):
            tile = empty
            for dx in range(3):
                for dy in range(3):
                    for slot in range(3):
                        n = ((a + dx) * 4 + b + dy) * 3 + slot
                        pick = jnp.broadcast_to(chosen_ref[c * 48 + n : c * 48 + n + 1, :], (8, S))
                        values = lane_gather(local_ref[n * 8 : n * 8 + 8, :], jnp.maximum(pick, 0))
                        tile = jnp.where(pick >= 0, values, tile)
            list_ref[c, t] = tile
        return carry

    gather_tiles(0, 0)
    lax.fori_loop(1, most, gather_tiles, 0)

    def pair_tile(c, t, first):
        tile = list_ref[c, t]
        other = [jnp.broadcast_to(tile[k : k + 1], (8, S)) for k in range(7)]
        for block in range(16):
            row = block * 8
            me = [spread_ref[c, k, row : row + 8, :] for k in range(7)]
            r = [me[k] - other[k] for k in range(3)]
            u = [me[3 + k] - other[3 + k] for k in range(3)]
            squared = r[0] * r[0] + r[1] * r[1] + r[2] * r[2] + SOFTENING
            inverse = lax.rsqrt(squared)
            along = u[0] * r[0] + u[1] * r[1] + u[2] * r[2]
            overlap = jnp.maximum((me[6] + other[6]) * inverse - 1.0, 0.0)
            weight = overlap * (STIFFNESS - (DAMPING * along) * inverse)
            terms = [weight * r[k] for k in range(3)]
            if width == 9:
                terms += [terms[left] * r[right] for left, right in PAIR_LIST]
            for k, term in enumerate(terms):
                if first:
                    sum_ref[c, k, row : row + 8, :] = term
                else:
                    sum_ref[c, k, row : row + 8, :] += term

    for c in range(8):
        pair_tile(c, 0, True)
    for group in PAIRS:

        def later_tile(t, carry):
            for c in group:
                pair_tile(c, t, False)
            return carry

        lax.fori_loop(1, jnp.maximum(tiles[group[0]], tiles[group[1]]), later_tile, 0)
    lanes = lane_ids((S, S))
    table = jnp.zeros((S, S), F32)
    for k in range(width):
        for c in range(8):
            column = jnp.sum(sum_ref[c, k], axis=1, keepdims=True)
            table = jnp.where(lanes == k * 8 + c, column, table)
    return jnp.transpose(table)[0 : width * 8]


def mass_of(radius):
    scaled = radius / RADIUS_REF
    return scaled * scaled * scaled


def step_kernel(own, gathered, velocity_out, own_out, *scratch):
    depth = lax.axis_index("depth")
    cell = cell_reader(gathered, 8)
    for x, y, slot, start, centre in extended_cells(depth):
        scratch[0][start : start + 8, :] = local_state(cell(x, y, slot), centre)
    sums = contact_all(depth, 3, scratch)
    radius = own[pl.ds(6, 8, stride=8), :]
    safe_mass = jnp.where(radius > 0.0, mass_of(radius), 1.0)
    for k in range(3):
        velocity = own[pl.ds(3 + k, 8, stride=8), :] + TIME_STEP * sums[k * 8 : k * 8 + 8] / safe_mass
        for c, (a, b, z) in enumerate(CELLS):
            own_out[c * 4 + k : c * 4 + k + 1, :] = velocity[c : c + 1]
            if z == 0:
                velocity_out[k, a, b, :, :] = velocity[c : c + 2]
    for c in range(8):
        own_out[c * 4 + 3 : c * 4 + 4, :] = jnp.zeros((1, S), F32)


def field_kernel(grid, own, gathered, own_speed, speeds, force_out, node_out, moment_ref, *scratch):
    local_ref = scratch[0]
    depth = lax.axis_index("depth")
    down = lax.axis_index("down")
    cross = lax.axis_index("cross")
    cell = cell_reader(gathered, 8)
    speed = cell_reader(speeds, 4)
    for x, y, slot, start, centre in extended_cells(depth):
        old = cell(x, y, slot)
        new = speed(x, y, slot)[0:3]
        shift = jnp.where(
            row_ids((3, S)) == 0, centre[0], jnp.where(row_ids((3, S)) == 1, centre[1], centre[2])
        )
        local_ref[start : start + 3, :] = (old[0:3] + TIME_STEP * new) + shift
        local_ref[start + 3 : start + 6, :] = new
        local_ref[start + 6 : start + 8, :] = old[6:8]
    sums = contact_all(depth, 9, scratch)
    radius = own[pl.ds(6, 8, stride=8), :]
    mass = jnp.where(radius > 0.0, mass_of(radius), 0.0)
    moments = [mass] + [mass * own_speed[pl.ds(k, 8, stride=4), :] for k in range(3)]
    moments += [0.5 * sums[k * 8 : k * 8 + 8] for k in range(3, 9)]
    moment_ref[...] = jnp.zeros((16, 8 * S), F32)
    for k in range(3):
        for c, (a, b, z) in enumerate(CELLS):
            if z == 0:
                force_out[k, a, b, :, :] = sums[k * 8 + c : k * 8 + c + 2]
    for m, moment in enumerate(moments):
        for c in range(8):
            moment_ref[m : m + 1, c * S : (c + 1) * S] = moment[c : c + 1]
    rows = row_ids((64, S))
    near_x, near_y, near_z = rows // 16 - 1, (rows // 4) % 4 - 1, rows % 4 - 1
    centres = [index.astype(F32) - 0.5 for index in (near_x, near_y, near_z)]
    kernels = []
    for a, b, z in CELLS:
        start = own_place(a, b, z) * 8
        squared = jnp.zeros((64, S), F32)
        for k in range(3):
            gap = local_ref[start + k : start + k + 1, :] - centres[k]
            squared = squared + gap * gap
        kernel = jnp.exp(squared * (-0.5 / (KERNEL_WIDTH * KERNEL_WIDTH))) / KERNEL_NORM
        beside = jnp.logical_and(
            jnp.logical_and(jnp.abs(near_x - a) <= 1, jnp.abs(near_y - b) <= 1),
            jnp.abs(near_z - z) <= 1,
        )
        kernels.append(jnp.where(beside, kernel, 0.0))
    kernel_high, kernel_low = split(jnp.concatenate(kernels, axis=1))
    moment_high, moment_low = split(moment_ref[...])
    wide_part = matmul_turned(
        jnp.concatenate([moment_high, moment_low.astype(BF16)], axis=0), kernel_high
    )
    near = wide_part[0:16] + wide_part[16:32] + matmul_turned(moment_high, kernel_low.astype(BF16))
    size_x, size_y, size_z = grid
    nodes = size_x * size_y * size_z
    lanes = lane_ids((64, nodes))
    row = row_ids((64, nodes))
    target_x = (down * 2 + row // 16 - 1 + size_x) % size_x
    target_y = (cross * 2 + (row // 4) % 4 - 1 + size_y) % size_y
    target_z = depth * 2 + row % 4 - 1
    inside = jnp.logical_and(target_z >= 0, target_z < size_z)
    target = (target_x * size_y + target_y) * size_z + target_z
    chosen = one_hot(jnp.logical_and(inside, lanes == target))
    near_high, rest = split(near)
    near_middle, near_low = split(rest)
    placed = matmul(
        jnp.concatenate([near_high, near_middle, near_low.astype(BF16)], axis=0), chosen
    )
    node_out[...] = placed[0:16] + placed[16:32] + placed[32:48]


def library_kernel(grid, coefficients, parts, residual_out, gram_out, moment_out, terms):
    fields = jnp.sum(parts[...], axis=0)
    size_x, size_y, size_z = grid
    nodes = size_x * size_y * size_z
    lanes = lax.broadcasted_iota(jnp.int32, (1, nodes), 1)
    node_x = lanes // (size_y * size_z)
    node_y = (lanes // size_z) % size_y
    node_z = lanes % size_z
    rows = row_ids((8, nodes))
    density = fields[0:1]
    values = jnp.where(rows == 0, fields[0:8], fields[0:8] / (density + MASS_SHIFT))

    def moved(value, step):
        return pltpu.roll(value, step % nodes, 1)

    plane = size_y * size_z
    slope_x = (moved(values, -plane) - moved(values, plane)) * 0.5
    after_y = jnp.where(
        node_y == size_y - 1, moved(values, (size_y - 1) * size_z), moved(values, -size_z)
    )
    before_y = jnp.where(
        node_y == 0, moved(values, -(size_y - 1) * size_z), moved(values, size_z)
    )
    slope_y = (after_y - before_y) * 0.5
    after_z = jnp.where(node_z == size_z - 1, 0.0, moved(values, -1))
    before_z = jnp.where(node_z == 0, 0.0, moved(values, 1))
    slope_z = (after_z - before_z) * 0.5
    slopes = [[table[k : k + 1] for k in range(4)] for table in (slope_x, slope_y, slope_z)]
    strain = [
        [0.5 * (slopes[left][1 + right] + slopes[right][1 + left]) for right in range(3)]
        for left in range(3)
    ]
    divergence = strain[0][0] + strain[1][1] + strain[2][2]
    rate_sum = jnp.zeros_like(density)
    for left in range(3):
        for right in range(3):
            entry = strain[left][right]
            if left == right:
                entry = entry - divergence / 3.0
            rate_sum = rate_sum + entry * entry
    shear_rate = jnp.sqrt(2.0 * rate_sum + 0.01)
    stress = [fields[4 + k : 5 + k] for k in range(6)]
    pressure = (stress[0] + stress[3] + stress[5]) / 3.0
    deviator = (
        (stress[0] - pressure) ** 2
        + (stress[3] - pressure) ** 2
        + (stress[5] - pressure) ** 2
        + 2.0 * (stress[1] ** 2 + stress[2] ** 2 + stress[4] ** 2)
    )
    shear_stress = jnp.sqrt(0.5 * deviator + 0.01)
    pressure_scale = jnp.sqrt(pressure * pressure + 1.0)
    friction = shear_stress / pressure_scale
    features = [
        density,
        pressure / pressure_scale,
        shear_rate,
        shear_rate / jnp.sqrt(pressure_scale),
        divergence,
        slopes[0][0],
        slopes[1][0],
        slopes[2][0],
    ]
    entries = list(features)
    for left in range(8):
        for right in range(left, 8):
            entries.append(features[left] * features[right])
    for left in range(1, 5):
        entries.append(features[left] * features[left] * features[left])
    model = jnp.zeros_like(density)
    for k, entry in enumerate(entries):
        terms[k : k + 1, :] = entry
        model = model + coefficients[k] * entry
    residual = friction - model
    table = terms[...]
    gram_out[...] = (
        lax.dot_general(
            table,
            table,
            (((1,), (1,)), ((), ())),
            precision=lax.Precision.HIGHEST,
            preferred_element_type=F32,
        )
        / nodes
    )
    moment = lax.dot_general(
        jnp.broadcast_to(friction, (8, nodes)),
        table,
        (((1,), (1,)), ((), ())),
        precision=lax.Precision.HIGHEST,
        preferred_element_type=F32,
    )
    moment_out[...] = moment[0:1] / nodes
    down = lax.axis_index("down")
    cross = lax.axis_index("cross")
    depth = lax.axis_index("depth")
    b_rows = lax.broadcasted_iota(jnp.int32, (2, 1), 0)
    z_lanes = lax.broadcasted_iota(jnp.int32, (2, 2), 1)
    for a in range(2):
        mine = jnp.logical_and(node_x == down * 2 + a, node_y == cross * 2 + b_rows)
        column = [
            jnp.sum(
                jnp.where(jnp.logical_and(mine, node_z == depth * 2 + z), residual, 0.0),
                axis=1,
                keepdims=True,
            )
            for z in range(2)
        ]
        residual_out[a] = jnp.where(z_lanes == 0, column[0], column[1])


def gather(value):
    return lax.all_gather(value, ("down", "cross", "depth"), tiled=True)


def body(positions, velocities, sphere_radii, counts, coefficients):
    down, cross, depth = (lax.axis_size(name) for name in ("down", "cross", "depth"))
    grid = (2 * down, 2 * cross, 2 * depth)
    nodes = grid[0] * grid[1] * grid[2]
    params = pltpu.CompilerParams(vmem_limit_bytes=VMEM_LIMIT)
    vector_shape = jax.ShapeDtypeStruct((3, 2, 2, 2, S), F32)

    def rows(count):
        return jax.ShapeDtypeStruct((count, S), F32)

    own = pl.pallas_call(
        pack_kernel,
        out_shape=rows(64),
        in_specs=[SMEM_SPEC] + [pl.BlockSpec(memory_space=pl.ANY)] * 3,
        out_specs=VMEM_SPEC,
        scratch_shapes=[
            pltpu.VMEM((3, 2, 2, 2, S), F32),
            pltpu.VMEM((3, 2, 2, 2, S), F32),
            pltpu.VMEM((2, 2, 2, S), F32),
            pltpu.SemaphoreType.DMA((3,)),
        ],
        compiler_params=pltpu.CompilerParams(vmem_limit_bytes=60 * 1024 * 1024),
        name="pack",
    )(counts, positions, velocities, sphere_radii)
    gathered = gather(own)
    velocity_new, own_speed = pl.pallas_call(
        step_kernel,
        out_shape=(vector_shape, rows(32)),
        in_specs=[VMEM_SPEC] * 2,
        out_specs=(VMEM_SPEC,) * 2,
        scratch_shapes=contact_scratch(3),
        compiler_params=params,
        name="step",
    )(own, gathered)
    speeds = gather(own_speed)
    force_next, partial = pl.pallas_call(
        functools.partial(field_kernel, grid),
        out_shape=(vector_shape, jax.ShapeDtypeStruct((16, nodes), F32)),
        in_specs=[VMEM_SPEC] * 4,
        out_specs=(VMEM_SPEC,) * 2,
        scratch_shapes=[pltpu.VMEM((16, 8 * S), F32)] + contact_scratch(9),
        compiler_params=params,
        name="field",
    )(own, gathered, own_speed, speeds)
    parts = gather(partial).reshape(down * cross * depth, 16, nodes)
    residual_field, gram_matrix, moment = pl.pallas_call(
        functools.partial(library_kernel, grid),
        out_shape=(
            jax.ShapeDtypeStruct((2, 2, 2), F32),
            jax.ShapeDtypeStruct((TERMS, TERMS), F32),
            jax.ShapeDtypeStruct((1, TERMS), F32),
        ),
        in_specs=[SMEM_SPEC, VMEM_SPEC],
        out_specs=(VMEM_SPEC,) * 3,
        scratch_shapes=[pltpu.VMEM((TERMS, nodes), F32)],
        compiler_params=params,
        name="library",
    )(coefficients, parts)
    return (velocity_new, force_next, residual_field, gram_matrix, moment.reshape(TERMS))


def solution(mesh):
    return jax.shard_map(
        body,
        mesh=mesh,
        in_specs=(
            P(None, ("groups", "down"), "cross", "depth", None),
            P(None, ("groups", "down"), "cross", "depth", None),
            P(("groups", "down"), "cross", "depth", None),
            P(("groups", "down"), "cross", "depth"),
            P(),
        ),
        out_specs=(
            P(None, ("groups", "down"), "cross", "depth", None),
            P(None, ("groups", "down"), "cross", "depth", None),
            P(("groups", "down"), "cross", "depth"),
            P("groups", None),
            P("groups"),
        ),
        check_vma=False,
    )
```

```python
import functools

import jax
import jax.numpy as jnp
from jax import lax
from jax.experimental import pallas as pl
from jax.experimental.pallas import tpu as pltpu
from jax.sharding import PartitionSpec as P

STIFFNESS = 100.0
DAMPING = 20.0
TIME_STEP = 0.05
KERNEL_WIDTH = 0.4
KERNEL_NORM = 64.0
SOFTENING = 0.0001
RADIUS_REF = 0.1
MASS_SHIFT = 0.1
DEAD = -1000.0
TERMS = 48
S = 128
F32 = jnp.float32
BF16 = jnp.bfloat16
CELLS = tuple((a, b, z) for a in range(2) for b in range(2) for z in range(2))
PAIRS = ((0, 2), (4, 6), (1, 3), (5, 7))
PAIR_LIST = ((0, 0), (0, 1), (0, 2), (1, 1), (1, 2), (2, 2))
VMEM_SPEC = pl.BlockSpec(memory_space=pltpu.VMEM)
SMEM_SPEC = pl.BlockSpec(memory_space=pltpu.SMEM)
VMEM_LIMIT = 48 * 1024 * 1024


def row_ids(shape):
    return lax.broadcasted_iota(jnp.int32, shape, 0)


def lane_ids(shape):
    return lax.broadcasted_iota(jnp.int32, shape, 1)


def one_hot(condition):
    return jnp.where(condition, 1.0, 0.0).astype(BF16)


def split(value):
    high = value.astype(BF16)
    return high, value - high.astype(F32)


def matmul(left, right):
    return lax.dot_general(left, right, (((1,), (0,)), ((), ())), preferred_element_type=F32)


def matmul_turned(left, right):
    return lax.dot_general(left, right, (((1,), (1,)), ((), ())), preferred_element_type=F32)


def lane_gather(table, index):
    return jnp.take_along_axis(table, index, axis=1)


def pack_kernel(
    counts, positions_hbm, velocities_hbm, radii_hbm, own, inner, positions, velocities, radii, arrived
):
    copies = [
        pltpu.make_async_copy(source, target, arrived.at[k])
        for k, (source, target) in enumerate(
            ((positions_hbm, positions), (velocities_hbm, velocities), (radii_hbm, radii))
        )
    ]
    for copy in copies:
        copy.start()
    for copy in copies:
        copy.wait()
    depth = lax.axis_index("depth")
    lanes = lane_ids((1, S))
    for c, (a, b, z) in enumerate(CELLS):
        for k in range(3):
            own[c * 8 + k : c * 8 + k + 1, :] = positions[k, a, b, z : z + 1, :]
            own[c * 8 + 3 + k : c * 8 + 4 + k, :] = velocities[k, a, b, z : z + 1, :]
        live = lanes < counts[a, b, z]
        own[c * 8 + 6 : c * 8 + 7, :] = jnp.where(live, radii[a, b, z : z + 1, :], DEAD)
        own[c * 8 + 7 : c * 8 + 8, :] = jnp.zeros((1, S), F32)
    for column in range(4):
        source = pl.multiple_of(column * 16 + (1 - depth) * 8, 8)
        inner[column * 8 : column * 8 + 8, :] = own[pl.ds(source, 8), :]


def local_state(raw, centre):
    rows = row_ids(raw.shape)
    shift = jnp.where(rows == 0, centre[0], jnp.where(rows == 1, centre[1], centre[2]))
    return jnp.where(rows < 3, raw + shift, raw)


def piece_reader(refs, wide, height):
    own, depth_halo = refs[0], refs[1]
    downs = lax.axis_size("down")
    x_before, x_after = refs[-2], refs[-1]

    def read(ref, cell):
        if isinstance(ref, int):
            peer = lax.rem(lax.axis_index("down") + ref + downs, downs)
            start = pl.multiple_of(peer * (12 * height) + cell * height, height)
            return refs[-1][pl.ds(start, height), :]
        return ref[cell * height : cell * height + height, :]

    def cell(x, y, slot):
        if x in (0, 3):
            face = x_before if x == 0 else x_after
            if downs in (3, 4):
                face = -1 if x == 0 else 1
            if y in (1, 2):
                return read(face, (y - 1) * 2 + slot if slot < 2 else 4 + y - 1)
            side = 0 if y == 0 else 1
            return read(face, 6 + side * 2 + slot if slot < 2 else 10 + side)
        a = x - 1
        if y in (1, 2):
            return read(own, a * 4 + (y - 1) * 2 + slot) if slot < 2 else read(depth_halo, a * 2 + y - 1)
        if wide:
            before, after, diag_before, diag_after = refs[2:6]
            if slot < 2:
                return read(before if y == 0 else after, a * 2 + slot)
            return read(diag_before if y == 0 else diag_after, a)
        side, diag = refs[2:4]
        b = 1 if y == 0 else 0
        return read(side, a * 4 + b * 2 + slot) if slot < 2 else read(diag, a * 2 + b)

    return cell


def own_place(a, b, z):
    return ((a + 1) * 4 + b + 1) * 3 + z


def extended_cells(depth):
    halo_z = 1.5 - 3.0 * depth.astype(F32)
    for x in range(4):
        for y in range(4):
            for slot in range(3):
                centre = (x - 1.5, y - 1.5, slot - 0.5 if slot < 2 else halo_z)
                yield x, y, slot, ((x * 4 + y) * 3 + slot) * 8, centre


def contact_scratch(width):
    return [
        pltpu.VMEM((48 * 8, S), F32),
        pltpu.VMEM((8 * 48, S), jnp.int32),
        pltpu.VMEM((8 * 48, S), jnp.int32),
        pltpu.VMEM((8 * 48, S), jnp.int32),
        pltpu.VMEM((8 * 48, S), jnp.int32),
        pltpu.VMEM((8, 27, 8, S), F32),
        pltpu.VMEM((8, 7, S, S), F32),
        pltpu.VMEM((8, width, S, S), F32),
    ]


def contact_all(depth, width, scratch):
    local_ref, index_ref, base_ref, amount_ref, chosen_ref, list_ref, spread_ref, sum_ref = scratch
    inner = 1 - depth
    for c, (a, b, z) in enumerate(CELLS):
        start = own_place(a, b, z) * 8
        turned = jnp.transpose(local_ref[start : start + 8, :])
        for k in range(7):
            spread_ref[c, k] = jnp.broadcast_to(turned[:, k : k + 1], (S, S))

    place = [local_ref[pl.ds(k, 48, stride=8), :] for k in range(3)]
    radius = local_ref[pl.ds(6, 48, stride=8), :]
    rows = row_ids((48, S))
    row_x, row_y, row_slot = rows // 12, (rows // 3) % 4, rows % 3
    masks = []
    for a, b, z in CELLS:
        start = own_place(a, b, z) * 8
        mine = local_ref[start : start + 8, :]
        live = mine[6:7] > 0.0
        low = jnp.min(jnp.where(live, mine, 1e9), axis=1, keepdims=True)
        high = jnp.max(jnp.where(live, mine, -1e9), axis=1, keepdims=True)
        reach = radius + high[6:7]
        near = jnp.logical_and(
            jnp.logical_and(row_x >= a, row_x <= a + 2), jnp.logical_and(row_y >= b, row_y <= b + 2)
        )
        near = jnp.logical_and(near, jnp.logical_or(row_slot < 2, inner == z))
        for k in range(3):
            near = jnp.logical_and(near, place[k] + reach > low[k : k + 1])
            near = jnp.logical_and(near, place[k] - reach < high[k : k + 1])
        masks.append(jnp.where(near, 1.0, 0.0).astype(F32))
    mask = jnp.concatenate(masks, axis=0).astype(BF16)
    upper = one_hot(row_ids((S, 2 * S)) <= lane_ids((S, 2 * S)))
    sums = matmul(mask, upper)
    prefix, amount = sums[:, :S], sums[:, S:]
    before = one_hot(lane_ids((48, 48)) < row_ids((48, 48)))
    totals = []
    for c in range(8):
        part = amount[c * 48 : c * 48 + 48]
        base = matmul(before, part.astype(BF16))
        base_ref[c * 48 : c * 48 + 48, :] = base.astype(jnp.int32)
        totals.append((base[47:48, 0:1] + part[47:48, 0:1]).astype(jnp.int32)[0, 0])
    amount_ref[...] = amount.astype(jnp.int32)
    wanted = lane_ids((8 * 48, S)).astype(F32)
    index = jnp.zeros((8 * 48, S), jnp.int32)
    for step in (64, 32, 16, 8, 4, 2, 1):
        probe = lane_gather(prefix, index + (step - 1))
        index = jnp.where(probe <= wanted, index + step, index)
    index_ref[...] = index
    tiles = [(total + (S - 1)) // S for total in totals]
    most = tiles[0]
    for count in tiles[1:]:
        most = jnp.maximum(most, count)

    empty = jnp.where(row_ids((8, S)) == 6, DEAD, 0.0).astype(F32)

    def gather_tiles(t, carry):
        want = t * S + lane_ids((8 * 48, S)) - base_ref[...]
        valid = jnp.logical_and(want >= 0, want < amount_ref[...])
        source = lane_gather(index_ref[...], jnp.clip(want, 0, S - 1))
        chosen_ref[...] = jnp.where(valid, source, -1)
        for c, (a, b, z) in enumerate(CELLS):
            tile = empty
            for dx in range(3):
                for dy in range(3):
                    for slot in range(3):
                        n = ((a + dx) * 4 + b + dy) * 3 + slot
                        pick = jnp.broadcast_to(chosen_ref[c * 48 + n : c * 48 + n + 1, :], (8, S))
                        values = lane_gather(local_ref[n * 8 : n * 8 + 8, :], jnp.maximum(pick, 0))
                        tile = jnp.where(pick >= 0, values, tile)
            list_ref[c, t] = tile
        return carry

    gather_tiles(0, 0)
    lax.fori_loop(1, most, gather_tiles, 0)

    def pair_tile(c, t, first):
        tile = list_ref[c, t]
        other = [jnp.broadcast_to(tile[k : k + 1], (8, S)) for k in range(7)]
        for block in range(16):
            row = block * 8
            me = [spread_ref[c, k, row : row + 8, :] for k in range(7)]
            r = [me[k] - other[k] for k in range(3)]
            u = [me[3 + k] - other[3 + k] for k in range(3)]
            squared = r[0] * r[0] + r[1] * r[1] + r[2] * r[2] + SOFTENING
            inverse = lax.rsqrt(squared)
            along = u[0] * r[0] + u[1] * r[1] + u[2] * r[2]
            overlap = jnp.maximum((me[6] + other[6]) * inverse - 1.0, 0.0)
            weight = overlap * (STIFFNESS - (DAMPING * along) * inverse)
            terms = [weight * r[k] for k in range(3)]
            if width == 9:
                terms += [terms[left] * r[right] for left, right in PAIR_LIST]
            for k, term in enumerate(terms):
                if first:
                    sum_ref[c, k, row : row + 8, :] = term
                else:
                    sum_ref[c, k, row : row + 8, :] += term

    for c in range(8):
        pair_tile(c, 0, True)
    for group in PAIRS:

        def later_tile(t, carry):
            for c in group:
                pair_tile(c, t, False)
            return carry

        lax.fori_loop(1, jnp.maximum(tiles[group[0]], tiles[group[1]]), later_tile, 0)
    lanes = lane_ids((S, S))
    table = jnp.zeros((S, S), F32)
    for k in range(width):
        for c in range(8):
            column = jnp.sum(sum_ref[c, k], axis=1, keepdims=True)
            table = jnp.where(lanes == k * 8 + c, column, table)
    return jnp.transpose(table)[0 : width * 8]


def mass_of(radius):
    scaled = radius / RADIUS_REF
    return scaled * scaled * scaled


def step_kernel(count, wide, *refs):
    pieces, (velocity_out, own_out, inner_out) = refs[:count], refs[count : count + 3]
    scratch = refs[count + 3 :]
    own = pieces[0]
    depth = lax.axis_index("depth")
    cell = piece_reader(pieces, wide, 8)
    for x, y, slot, start, centre in extended_cells(depth):
        scratch[0][start : start + 8, :] = local_state(cell(x, y, slot), centre)
    sums = contact_all(depth, 3, scratch)
    radius = own[pl.ds(6, 8, stride=8), :]
    safe_mass = jnp.where(radius > 0.0, mass_of(radius), 1.0)
    for k in range(3):
        velocity = own[pl.ds(3 + k, 8, stride=8), :] + TIME_STEP * sums[k * 8 : k * 8 + 8] / safe_mass
        for c, (a, b, z) in enumerate(CELLS):
            own_out[c * 4 + k : c * 4 + k + 1, :] = velocity[c : c + 1]
            if z == 0:
                velocity_out[k, a, b, :, :] = velocity[c : c + 2]
    for c in range(8):
        own_out[c * 4 + 3 : c * 4 + 4, :] = jnp.zeros((1, S), F32)
    for column in range(4):
        chosen = own_out[column * 8 : column * 8 + 8, :]
        inner_out[column * 4 : column * 4 + 4, :] = jnp.where(depth == 0, chosen[4:8], chosen[0:4])


def field_kernel(count, wide, grid, *refs):
    pieces, speeds = refs[:count], refs[count : 2 * count]
    force_out, node_out = refs[2 * count : 2 * count + 2]
    moment_ref = refs[2 * count + 2]
    scratch = refs[2 * count + 3 :]
    local_ref = scratch[0]
    depth = lax.axis_index("depth")
    down = lax.axis_index("down")
    cross = lax.axis_index("cross")
    cell = piece_reader(pieces, wide, 8)
    speed = piece_reader(speeds, wide, 4)
    for x, y, slot, start, centre in extended_cells(depth):
        old = cell(x, y, slot)
        new = speed(x, y, slot)[0:3]
        shift = jnp.where(
            row_ids((3, S)) == 0, centre[0], jnp.where(row_ids((3, S)) == 1, centre[1], centre[2])
        )
        local_ref[start : start + 3, :] = (old[0:3] + TIME_STEP * new) + shift
        local_ref[start + 3 : start + 6, :] = new
        local_ref[start + 6 : start + 8, :] = old[6:8]
    sums = contact_all(depth, 9, scratch)
    radius = pieces[0][pl.ds(6, 8, stride=8), :]
    mass = jnp.where(radius > 0.0, mass_of(radius), 0.0)
    moments = [mass] + [mass * speeds[0][pl.ds(k, 8, stride=4), :] for k in range(3)]
    moments += [0.5 * sums[k * 8 : k * 8 + 8] for k in range(3, 9)]
    moment_ref[...] = jnp.zeros((16, 8 * S), F32)
    for k in range(3):
        for c, (a, b, z) in enumerate(CELLS):
            if z == 0:
                force_out[k, a, b, :, :] = sums[k * 8 + c : k * 8 + c + 2]
    for m, moment in enumerate(moments):
        for c in range(8):
            moment_ref[m : m + 1, c * S : (c + 1) * S] = moment[c : c + 1]
    rows = row_ids((64, S))
    near_x, near_y, near_z = rows // 16 - 1, (rows // 4) % 4 - 1, rows % 4 - 1
    centres = [index.astype(F32) - 0.5 for index in (near_x, near_y, near_z)]
    kernels = []
    for a, b, z in CELLS:
        start = own_place(a, b, z) * 8
        squared = jnp.zeros((64, S), F32)
        for k in range(3):
            gap = local_ref[start + k : start + k + 1, :] - centres[k]
            squared = squared + gap * gap
        kernel = jnp.exp(squared * (-0.5 / (KERNEL_WIDTH * KERNEL_WIDTH))) / KERNEL_NORM
        beside = jnp.logical_and(
            jnp.logical_and(jnp.abs(near_x - a) <= 1, jnp.abs(near_y - b) <= 1),
            jnp.abs(near_z - z) <= 1,
        )
        kernels.append(jnp.where(beside, kernel, 0.0))
    kernel_high, kernel_low = split(jnp.concatenate(kernels, axis=1))
    moment_high, moment_low = split(moment_ref[...])
    wide_part = matmul_turned(
        jnp.concatenate([moment_high, moment_low.astype(BF16)], axis=0), kernel_high
    )
    near = wide_part[0:16] + wide_part[16:32] + matmul_turned(moment_high, kernel_low.astype(BF16))
    size_x, size_y, size_z = grid
    nodes = size_x * size_y * size_z
    lanes = lane_ids((64, nodes))
    row = row_ids((64, nodes))
    target_x = (down * 2 + row // 16 - 1 + size_x) % size_x
    target_y = (cross * 2 + (row // 4) % 4 - 1 + size_y) % size_y
    target_z = depth * 2 + row % 4 - 1
    inside = jnp.logical_and(target_z >= 0, target_z < size_z)
    target = (target_x * size_y + target_y) * size_z + target_z
    chosen = one_hot(jnp.logical_and(inside, lanes == target))
    near_high, rest = split(near)
    near_middle, near_low = split(rest)
    placed = matmul(
        jnp.concatenate([near_high, near_middle, near_low.astype(BF16)], axis=0), chosen
    )
    node_out[...] = placed[0:16] + placed[16:32] + placed[32:48]


def library_kernel(grid, coefficients, parts, residual_out, gram_out, moment_out, terms):
    fields = jnp.sum(parts[...], axis=0)
    size_x, size_y, size_z = grid
    nodes = size_x * size_y * size_z
    lanes = lax.broadcasted_iota(jnp.int32, (1, nodes), 1)
    node_x = lanes // (size_y * size_z)
    node_y = (lanes // size_z) % size_y
    node_z = lanes % size_z
    rows = row_ids((8, nodes))
    density = fields[0:1]
    values = jnp.where(rows == 0, fields[0:8], fields[0:8] / (density + MASS_SHIFT))

    def moved(value, step):
        return pltpu.roll(value, step % nodes, 1)

    plane = size_y * size_z
    slope_x = (moved(values, -plane) - moved(values, plane)) * 0.5
    after_y = jnp.where(
        node_y == size_y - 1, moved(values, (size_y - 1) * size_z), moved(values, -size_z)
    )
    before_y = jnp.where(
        node_y == 0, moved(values, -(size_y - 1) * size_z), moved(values, size_z)
    )
    slope_y = (after_y - before_y) * 0.5
    after_z = jnp.where(node_z == size_z - 1, 0.0, moved(values, -1))
    before_z = jnp.where(node_z == 0, 0.0, moved(values, 1))
    slope_z = (after_z - before_z) * 0.5
    slopes = [[table[k : k + 1] for k in range(4)] for table in (slope_x, slope_y, slope_z)]
    strain = [
        [0.5 * (slopes[left][1 + right] + slopes[right][1 + left]) for right in range(3)]
        for left in range(3)
    ]
    divergence = strain[0][0] + strain[1][1] + strain[2][2]
    rate_sum = jnp.zeros_like(density)
    for left in range(3):
        for right in range(3):
            entry = strain[left][right]
            if left == right:
                entry = entry - divergence / 3.0
            rate_sum = rate_sum + entry * entry
    shear_rate = jnp.sqrt(2.0 * rate_sum + 0.01)
    stress = [fields[4 + k : 5 + k] for k in range(6)]
    pressure = (stress[0] + stress[3] + stress[5]) / 3.0
    deviator = (
        (stress[0] - pressure) ** 2
        + (stress[3] - pressure) ** 2
        + (stress[5] - pressure) ** 2
        + 2.0 * (stress[1] ** 2 + stress[2] ** 2 + stress[4] ** 2)
    )
    shear_stress = jnp.sqrt(0.5 * deviator + 0.01)
    pressure_scale = jnp.sqrt(pressure * pressure + 1.0)
    friction = shear_stress / pressure_scale
    features = [
        density,
        pressure / pressure_scale,
        shear_rate,
        shear_rate / jnp.sqrt(pressure_scale),
        divergence,
        slopes[0][0],
        slopes[1][0],
        slopes[2][0],
    ]
    entries = list(features)
    for left in range(8):
        for right in range(left, 8):
            entries.append(features[left] * features[right])
    for left in range(1, 5):
        entries.append(features[left] * features[left] * features[left])
    model = jnp.zeros_like(density)
    for k, entry in enumerate(entries):
        terms[k : k + 1, :] = entry
        model = model + coefficients[k] * entry
    residual = friction - model
    table = terms[...]
    gram_out[...] = (
        lax.dot_general(
            table,
            table,
            (((1,), (1,)), ((), ())),
            precision=lax.Precision.HIGHEST,
            preferred_element_type=F32,
        )
        / nodes
    )
    moment = lax.dot_general(
        jnp.broadcast_to(friction, (8, nodes)),
        table,
        (((1,), (1,)), ((), ())),
        precision=lax.Precision.HIGHEST,
        preferred_element_type=F32,
    )
    moment_out[...] = moment[0:1] / nodes
    down = lax.axis_index("down")
    cross = lax.axis_index("cross")
    depth = lax.axis_index("depth")
    b_rows = lax.broadcasted_iota(jnp.int32, (2, 1), 0)
    z_lanes = lax.broadcasted_iota(jnp.int32, (2, 2), 1)
    for a in range(2):
        mine = jnp.logical_and(node_x == down * 2 + a, node_y == cross * 2 + b_rows)
        column = [
            jnp.sum(
                jnp.where(jnp.logical_and(mine, node_z == depth * 2 + z), residual, 0.0),
                axis=1,
                keepdims=True,
            )
            for z in range(2)
        ]
        residual_out[a] = jnp.where(z_lanes == 0, column[0], column[1])


def ring(axis, step):
    peers = lax.axis_size(axis)
    return [(i, (i + step) % peers) for i in range(peers)]


def spread_along_down(last, first):
    downs = lax.axis_size("down")
    me = lax.axis_index("down")
    chunks = [jnp.where(lax.rem(me + 1, downs) == k, last, first) for k in range(downs)]
    return lax.all_to_all(jnp.concatenate(chunks, axis=0), "down", 0, 0, tiled=True)


def exchange(own, inner, height):
    cross = lax.axis_size("cross")

    def cells(block, first, count):
        return block[first * height : (first + count) * height]

    depth_halo = lax.ppermute(inner, "depth", [(0, 1), (1, 0)])
    if cross == 2:
        side = lax.ppermute(own, "cross", [(0, 1), (1, 0)])
        diag = lax.ppermute(inner, ("cross", "depth"), [(i, 3 - i) for i in range(4)])
        sides = [side, diag]

        def lateral(x):
            return [
                cells(side, x * 4 + 2, 2),
                cells(side, x * 4, 2),
                cells(diag, x * 2 + 1, 1),
                cells(diag, x * 2, 1),
            ]

    else:
        pairs = [(i * 2 + j, ((i + 1) % cross) * 2 + 1 - j) for i in range(cross) for j in range(2)]
        back = [(i * 2 + j, ((i - 1) % cross) * 2 + 1 - j) for i in range(cross) for j in range(2)]
        last = jnp.concatenate([cells(own, 2, 2), cells(own, 6, 2)], axis=0)
        first = jnp.concatenate([cells(own, 0, 2), cells(own, 4, 2)], axis=0)
        last_inner = jnp.concatenate([cells(inner, 1, 1), cells(inner, 3, 1)], axis=0)
        first_inner = jnp.concatenate([cells(inner, 0, 1), cells(inner, 2, 1)], axis=0)
        before = lax.ppermute(last, "cross", ring("cross", 1))
        after = lax.ppermute(first, "cross", ring("cross", -1))
        diag_before = lax.ppermute(last_inner, ("cross", "depth"), pairs)
        diag_after = lax.ppermute(first_inner, ("cross", "depth"), back)
        sides = [before, after, diag_before, diag_after]

        def lateral(x):
            return [
                cells(before, x * 2, 2),
                cells(after, x * 2, 2),
                cells(diag_before, x, 1),
                cells(diag_after, x, 1),
            ]

    def face(x):
        return jnp.concatenate([cells(own, x * 4, 4), cells(depth_halo, x * 2, 2)] + lateral(x), axis=0)

    if lax.axis_size("down") in (3, 4):
        return [own, depth_halo] + sides + [spread_along_down(face(1), face(0))]
    x_before = lax.ppermute(face(1), "down", ring("down", 1))
    x_after = lax.ppermute(face(0), "down", ring("down", -1))
    return [own, depth_halo] + sides + [x_before, x_after]


def shared(value, axes, peers):
    return [value] + [
        lax.ppermute(value, axes, [(i, i ^ k) for i in range(peers)]) for k in range(1, peers)
    ]


def tree_sum(parts):
    while len(parts) > 1:
        parts = [parts[k] + parts[k + 1] for k in range(0, len(parts), 2)]
    return parts[0]


def body(positions, velocities, sphere_radii, counts, coefficients):
    down, cross, depth = (lax.axis_size(name) for name in ("down", "cross", "depth"))
    wide = cross != 2
    grid = (2 * down, 2 * cross, 2 * depth)
    nodes = grid[0] * grid[1] * grid[2]
    params = pltpu.CompilerParams(vmem_limit_bytes=VMEM_LIMIT)
    vector_shape = jax.ShapeDtypeStruct((3, 2, 2, 2, S), F32)

    def rows(count):
        return jax.ShapeDtypeStruct((count, S), F32)

    own, inner = pl.pallas_call(
        pack_kernel,
        out_shape=(rows(64), rows(32)),
        in_specs=[SMEM_SPEC] + [pl.BlockSpec(memory_space=pl.ANY)] * 3,
        out_specs=(VMEM_SPEC, VMEM_SPEC),
        scratch_shapes=[
            pltpu.VMEM((3, 2, 2, 2, S), F32),
            pltpu.VMEM((3, 2, 2, 2, S), F32),
            pltpu.VMEM((2, 2, 2, S), F32),
            pltpu.SemaphoreType.DMA((3,)),
        ],
        compiler_params=pltpu.CompilerParams(vmem_limit_bytes=60 * 1024 * 1024),
        name="pack",
    )(counts, positions, velocities, sphere_radii)
    pieces = exchange(own, inner, 8)
    velocity_new, own_speed, inner_speed = pl.pallas_call(
        functools.partial(step_kernel, len(pieces), wide),
        out_shape=(vector_shape, rows(32), rows(16)),
        in_specs=[VMEM_SPEC] * len(pieces),
        out_specs=(VMEM_SPEC,) * 3,
        scratch_shapes=contact_scratch(3),
        compiler_params=params,
        name="step",
    )(*pieces)
    speeds = exchange(own_speed, inner_speed, 4)
    force_next, partial = pl.pallas_call(
        functools.partial(field_kernel, len(pieces), wide, grid),
        out_shape=(vector_shape, jax.ShapeDtypeStruct((16, nodes), F32)),
        in_specs=[VMEM_SPEC] * (len(pieces) + len(speeds)),
        out_specs=(VMEM_SPEC,) * 2,
        scratch_shapes=[pltpu.VMEM((16, 8 * S), F32)] + contact_scratch(9),
        compiler_params=params,
        name="field",
    )(*pieces, *speeds)
    partial = tree_sum(shared(partial, ("cross", "depth"), cross * depth))
    parts = lax.all_to_all(jnp.broadcast_to(partial, (down, 16, nodes)), "down", 0, 0)
    residual_field, gram_matrix, moment = pl.pallas_call(
        functools.partial(library_kernel, grid),
        out_shape=(
            jax.ShapeDtypeStruct((2, 2, 2), F32),
            jax.ShapeDtypeStruct((TERMS, TERMS), F32),
            jax.ShapeDtypeStruct((1, TERMS), F32),
        ),
        in_specs=[SMEM_SPEC, VMEM_SPEC],
        out_specs=(VMEM_SPEC,) * 3,
        scratch_shapes=[pltpu.VMEM((TERMS, nodes), F32)],
        compiler_params=params,
        name="library",
    )(coefficients, parts)
    return (velocity_new, force_next, residual_field, gram_matrix, moment.reshape(TERMS))


def solution(mesh):
    return jax.shard_map(
        body,
        mesh=mesh,
        in_specs=(
            P(None, ("groups", "down"), "cross", "depth", None),
            P(None, ("groups", "down"), "cross", "depth", None),
            P(("groups", "down"), "cross", "depth", None),
            P(("groups", "down"), "cross", "depth"),
            P(),
        ),
        out_specs=(
            P(None, ("groups", "down"), "cross", "depth", None),
            P(None, ("groups", "down"), "cross", "depth", None),
            P(("groups", "down"), "cross", "depth"),
            P("groups", None),
            P("groups"),
        ),
        check_vma=False,
    )
```

```python
import functools

import jax
import jax.numpy as jnp
from jax import lax
from jax.experimental import pallas as pl
from jax.experimental.pallas import tpu as pltpu
from jax.sharding import PartitionSpec as P

STIFFNESS = 100.0
DAMPING = 20.0
TIME_STEP = 0.05
KERNEL_WIDTH = 0.4
KERNEL_NORM = 64.0
SOFTENING = 0.0001
RADIUS_REF = 0.1
MASS_SHIFT = 0.1
DEAD = -1000.0
TERMS = 48
S = 128
F32 = jnp.float32
BF16 = jnp.bfloat16
CELLS = tuple((a, b, z) for a in range(2) for b in range(2) for z in range(2))
PAIRS = ((0, 2), (4, 6), (1, 3), (5, 7))
PAIR_LIST = ((0, 0), (0, 1), (0, 2), (1, 1), (1, 2), (2, 2))
VMEM_SPEC = pl.BlockSpec(memory_space=pltpu.VMEM)
SMEM_SPEC = pl.BlockSpec(memory_space=pltpu.SMEM)
VMEM_LIMIT = 48 * 1024 * 1024


def row_ids(shape):
    return lax.broadcasted_iota(jnp.int32, shape, 0)


def lane_ids(shape):
    return lax.broadcasted_iota(jnp.int32, shape, 1)


def one_hot(condition):
    return jnp.where(condition, 1.0, 0.0).astype(BF16)


def split(value):
    high = value.astype(BF16)
    return high, value - high.astype(F32)


def matmul(left, right):
    return lax.dot_general(left, right, (((1,), (0,)), ((), ())), preferred_element_type=F32)


def matmul_turned(left, right):
    return lax.dot_general(left, right, (((1,), (1,)), ((), ())), preferred_element_type=F32)


def lane_gather(table, index):
    return jnp.take_along_axis(table, index, axis=1)


def pack_kernel(
    counts, positions_hbm, velocities_hbm, radii_hbm, own, inner, positions, velocities, radii, arrived
):
    copies = [
        pltpu.make_async_copy(source, target, arrived.at[k])
        for k, (source, target) in enumerate(
            ((positions_hbm, positions), (velocities_hbm, velocities), (radii_hbm, radii))
        )
    ]
    for copy in copies:
        copy.start()
    for copy in copies:
        copy.wait()
    depth = lax.axis_index("depth")
    lanes = lane_ids((1, S))
    for c, (a, b, z) in enumerate(CELLS):
        for k in range(3):
            own[c * 8 + k : c * 8 + k + 1, :] = positions[k, a, b, z : z + 1, :]
            own[c * 8 + 3 + k : c * 8 + 4 + k, :] = velocities[k, a, b, z : z + 1, :]
        live = lanes < counts[a, b, z]
        own[c * 8 + 6 : c * 8 + 7, :] = jnp.where(live, radii[a, b, z : z + 1, :], DEAD)
        own[c * 8 + 7 : c * 8 + 8, :] = jnp.zeros((1, S), F32)
    for column in range(4):
        source = pl.multiple_of(column * 16 + (1 - depth) * 8, 8)
        inner[column * 8 : column * 8 + 8, :] = own[pl.ds(source, 8), :]


def local_state(raw, centre):
    rows = row_ids(raw.shape)
    shift = jnp.where(rows == 0, centre[0], jnp.where(rows == 1, centre[1], centre[2]))
    return jnp.where(rows < 3, raw + shift, raw)


def piece_reader(refs, wide, height):
    own, depth_halo = refs[0], refs[1]
    even = lax.rem(lax.axis_index("down"), 2) == 0
    swapped = lax.axis_size("down") % 2 == 0
    x_before, x_after = refs[-2], refs[-1]

    def read(ref, cell):
        if isinstance(ref, tuple):
            return jnp.where(even, read(ref[0], cell), read(ref[1], cell))
        return ref[cell * height : cell * height + height, :]

    def cell(x, y, slot):
        if x in (0, 3):
            face = x_before if x == 0 else x_after
            if swapped:
                face = (x_after, x_before) if x == 0 else (x_before, x_after)
            if y in (1, 2):
                return read(face, (y - 1) * 2 + slot if slot < 2 else 4 + y - 1)
            side = 0 if y == 0 else 1
            return read(face, 6 + side * 2 + slot if slot < 2 else 10 + side)
        a = x - 1
        if y in (1, 2):
            return read(own, a * 4 + (y - 1) * 2 + slot) if slot < 2 else read(depth_halo, a * 2 + y - 1)
        if wide:
            before, after, diag_before, diag_after = refs[2:6]
            if slot < 2:
                return read(before if y == 0 else after, a * 2 + slot)
            return read(diag_before if y == 0 else diag_after, a)
        side, diag = refs[2:4]
        b = 1 if y == 0 else 0
        return read(side, a * 4 + b * 2 + slot) if slot < 2 else read(diag, a * 2 + b)

    return cell


def own_place(a, b, z):
    return ((a + 1) * 4 + b + 1) * 3 + z


def extended_cells(depth):
    halo_z = 1.5 - 3.0 * depth.astype(F32)
    for x in range(4):
        for y in range(4):
            for slot in range(3):
                centre = (x - 1.5, y - 1.5, slot - 0.5 if slot < 2 else halo_z)
                yield x, y, slot, ((x * 4 + y) * 3 + slot) * 8, centre


def contact_scratch(width):
    return [
        pltpu.VMEM((48 * 8, S), F32),
        pltpu.VMEM((8 * 48, S), jnp.int32),
        pltpu.VMEM((8 * 48, S), jnp.int32),
        pltpu.VMEM((8 * 48, S), jnp.int32),
        pltpu.VMEM((8 * 48, S), jnp.int32),
        pltpu.VMEM((8, 27, 8, S), F32),
        pltpu.VMEM((8, 7, S, S), F32),
        pltpu.VMEM((8, width, S, S), F32),
    ]


def contact_all(depth, width, scratch):
    local_ref, index_ref, base_ref, amount_ref, chosen_ref, list_ref, spread_ref, sum_ref = scratch
    inner = 1 - depth
    for c, (a, b, z) in enumerate(CELLS):
        start = own_place(a, b, z) * 8
        turned = jnp.transpose(local_ref[start : start + 8, :])
        for k in range(7):
            spread_ref[c, k] = jnp.broadcast_to(turned[:, k : k + 1], (S, S))

    place = [local_ref[pl.ds(k, 48, stride=8), :] for k in range(3)]
    radius = local_ref[pl.ds(6, 48, stride=8), :]
    rows = row_ids((48, S))
    row_x, row_y, row_slot = rows // 12, (rows // 3) % 4, rows % 3
    masks = []
    for a, b, z in CELLS:
        start = own_place(a, b, z) * 8
        mine = local_ref[start : start + 8, :]
        live = mine[6:7] > 0.0
        low = jnp.min(jnp.where(live, mine, 1e9), axis=1, keepdims=True)
        high = jnp.max(jnp.where(live, mine, -1e9), axis=1, keepdims=True)
        reach = radius + high[6:7]
        near = jnp.logical_and(
            jnp.logical_and(row_x >= a, row_x <= a + 2), jnp.logical_and(row_y >= b, row_y <= b + 2)
        )
        near = jnp.logical_and(near, jnp.logical_or(row_slot < 2, inner == z))
        for k in range(3):
            near = jnp.logical_and(near, place[k] + reach > low[k : k + 1])
            near = jnp.logical_and(near, place[k] - reach < high[k : k + 1])
        masks.append(jnp.where(near, 1.0, 0.0).astype(F32))
    mask = jnp.concatenate(masks, axis=0).astype(BF16)
    upper = one_hot(row_ids((S, 2 * S)) <= lane_ids((S, 2 * S)))
    sums = matmul(mask, upper)
    prefix, amount = sums[:, :S], sums[:, S:]
    before = one_hot(lane_ids((48, 48)) < row_ids((48, 48)))
    totals = []
    for c in range(8):
        part = amount[c * 48 : c * 48 + 48]
        base = matmul(before, part.astype(BF16))
        base_ref[c * 48 : c * 48 + 48, :] = base.astype(jnp.int32)
        totals.append((base[47:48, 0:1] + part[47:48, 0:1]).astype(jnp.int32)[0, 0])
    amount_ref[...] = amount.astype(jnp.int32)
    wanted = lane_ids((8 * 48, S)).astype(F32)
    index = jnp.zeros((8 * 48, S), jnp.int32)
    for step in (64, 32, 16, 8, 4, 2, 1):
        probe = lane_gather(prefix, index + (step - 1))
        index = jnp.where(probe <= wanted, index + step, index)
    index_ref[...] = index
    tiles = [(total + (S - 1)) // S for total in totals]
    most = tiles[0]
    for count in tiles[1:]:
        most = jnp.maximum(most, count)

    empty = jnp.where(row_ids((8, S)) == 6, DEAD, 0.0).astype(F32)

    def gather_tiles(t, carry):
        want = t * S + lane_ids((8 * 48, S)) - base_ref[...]
        valid = jnp.logical_and(want >= 0, want < amount_ref[...])
        source = lane_gather(index_ref[...], jnp.clip(want, 0, S - 1))
        chosen_ref[...] = jnp.where(valid, source, -1)
        for c, (a, b, z) in enumerate(CELLS):
            tile = empty
            for dx in range(3):
                for dy in range(3):
                    for slot in range(3):
                        n = ((a + dx) * 4 + b + dy) * 3 + slot
                        pick = jnp.broadcast_to(chosen_ref[c * 48 + n : c * 48 + n + 1, :], (8, S))
                        values = lane_gather(local_ref[n * 8 : n * 8 + 8, :], jnp.maximum(pick, 0))
                        tile = jnp.where(pick >= 0, values, tile)
            list_ref[c, t] = tile
        return carry

    gather_tiles(0, 0)
    lax.fori_loop(1, most, gather_tiles, 0)

    def pair_tile(c, t, first):
        tile = list_ref[c, t]
        other = [jnp.broadcast_to(tile[k : k + 1], (8, S)) for k in range(7)]
        for block in range(16):
            row = block * 8
            me = [spread_ref[c, k, row : row + 8, :] for k in range(7)]
            r = [me[k] - other[k] for k in range(3)]
            u = [me[3 + k] - other[3 + k] for k in range(3)]
            squared = r[0] * r[0] + r[1] * r[1] + r[2] * r[2] + SOFTENING
            inverse = lax.rsqrt(squared)
            along = u[0] * r[0] + u[1] * r[1] + u[2] * r[2]
            overlap = jnp.maximum((me[6] + other[6]) * inverse - 1.0, 0.0)
            weight = overlap * (STIFFNESS - (DAMPING * along) * inverse)
            terms = [weight * r[k] for k in range(3)]
            if width == 9:
                terms += [terms[left] * r[right] for left, right in PAIR_LIST]
            for k, term in enumerate(terms):
                if first:
                    sum_ref[c, k, row : row + 8, :] = term
                else:
                    sum_ref[c, k, row : row + 8, :] += term

    for c in range(8):
        pair_tile(c, 0, True)
    for group in PAIRS:

        def later_tile(t, carry):
            for c in group:
                pair_tile(c, t, False)
            return carry

        lax.fori_loop(1, jnp.maximum(tiles[group[0]], tiles[group[1]]), later_tile, 0)
    lanes = lane_ids((S, S))
    table = jnp.zeros((S, S), F32)
    for k in range(width):
        for c in range(8):
            column = jnp.sum(sum_ref[c, k], axis=1, keepdims=True)
            table = jnp.where(lanes == k * 8 + c, column, table)
    return jnp.transpose(table)[0 : width * 8]


def mass_of(radius):
    scaled = radius / RADIUS_REF
    return scaled * scaled * scaled


def step_kernel(wide, *refs):
    count = 8 if wide else 6
    pieces, (velocity_out, own_out, inner_out) = refs[:count], refs[count : count + 3]
    scratch = refs[count + 3 :]
    own = pieces[0]
    depth = lax.axis_index("depth")
    cell = piece_reader(pieces, wide, 8)
    for x, y, slot, start, centre in extended_cells(depth):
        scratch[0][start : start + 8, :] = local_state(cell(x, y, slot), centre)
    sums = contact_all(depth, 3, scratch)
    radius = own[pl.ds(6, 8, stride=8), :]
    safe_mass = jnp.where(radius > 0.0, mass_of(radius), 1.0)
    for k in range(3):
        velocity = own[pl.ds(3 + k, 8, stride=8), :] + TIME_STEP * sums[k * 8 : k * 8 + 8] / safe_mass
        for c, (a, b, z) in enumerate(CELLS):
            own_out[c * 4 + k : c * 4 + k + 1, :] = velocity[c : c + 1]
            if z == 0:
                velocity_out[k, a, b, :, :] = velocity[c : c + 2]
    for c in range(8):
        own_out[c * 4 + 3 : c * 4 + 4, :] = jnp.zeros((1, S), F32)
    for column in range(4):
        chosen = own_out[column * 8 : column * 8 + 8, :]
        inner_out[column * 4 : column * 4 + 4, :] = jnp.where(depth == 0, chosen[4:8], chosen[0:4])


def field_kernel(wide, grid, *refs):
    count = 8 if wide else 6
    pieces, speeds = refs[:count], refs[count : 2 * count]
    force_out, node_out = refs[2 * count : 2 * count + 2]
    moment_ref = refs[2 * count + 2]
    scratch = refs[2 * count + 3 :]
    local_ref = scratch[0]
    depth = lax.axis_index("depth")
    down = lax.axis_index("down")
    cross = lax.axis_index("cross")
    cell = piece_reader(pieces, wide, 8)
    speed = piece_reader(speeds, wide, 4)
    for x, y, slot, start, centre in extended_cells(depth):
        old = cell(x, y, slot)
        new = speed(x, y, slot)[0:3]
        shift = jnp.where(
            row_ids((3, S)) == 0, centre[0], jnp.where(row_ids((3, S)) == 1, centre[1], centre[2])
        )
        local_ref[start : start + 3, :] = (old[0:3] + TIME_STEP * new) + shift
        local_ref[start + 3 : start + 6, :] = new
        local_ref[start + 6 : start + 8, :] = old[6:8]
    sums = contact_all(depth, 9, scratch)
    radius = pieces[0][pl.ds(6, 8, stride=8), :]
    mass = jnp.where(radius > 0.0, mass_of(radius), 0.0)
    moments = [mass] + [mass * speeds[0][pl.ds(k, 8, stride=4), :] for k in range(3)]
    moments += [0.5 * sums[k * 8 : k * 8 + 8] for k in range(3, 9)]
    moment_ref[...] = jnp.zeros((16, 8 * S), F32)
    for k in range(3):
        for c, (a, b, z) in enumerate(CELLS):
            if z == 0:
                force_out[k, a, b, :, :] = sums[k * 8 + c : k * 8 + c + 2]
    for m, moment in enumerate(moments):
        for c in range(8):
            moment_ref[m : m + 1, c * S : (c + 1) * S] = moment[c : c + 1]
    rows = row_ids((64, S))
    near_x, near_y, near_z = rows // 16 - 1, (rows // 4) % 4 - 1, rows % 4 - 1
    centres = [index.astype(F32) - 0.5 for index in (near_x, near_y, near_z)]
    kernels = []
    for a, b, z in CELLS:
        start = own_place(a, b, z) * 8
        squared = jnp.zeros((64, S), F32)
        for k in range(3):
            gap = local_ref[start + k : start + k + 1, :] - centres[k]
            squared = squared + gap * gap
        kernel = jnp.exp(squared * (-0.5 / (KERNEL_WIDTH * KERNEL_WIDTH))) / KERNEL_NORM
        beside = jnp.logical_and(
            jnp.logical_and(jnp.abs(near_x - a) <= 1, jnp.abs(near_y - b) <= 1),
            jnp.abs(near_z - z) <= 1,
        )
        kernels.append(jnp.where(beside, kernel, 0.0))
    kernel_high, kernel_low = split(jnp.concatenate(kernels, axis=1))
    moment_high, moment_low = split(moment_ref[...])
    wide_part = matmul_turned(
        jnp.concatenate([moment_high, moment_low.astype(BF16)], axis=0), kernel_high
    )
    near = wide_part[0:16] + wide_part[16:32] + matmul_turned(moment_high, kernel_low.astype(BF16))
    size_x, size_y, size_z = grid
    nodes = size_x * size_y * size_z
    lanes = lane_ids((64, nodes))
    row = row_ids((64, nodes))
    target_x = (down * 2 + row // 16 - 1 + size_x) % size_x
    target_y = (cross * 2 + (row // 4) % 4 - 1 + size_y) % size_y
    target_z = depth * 2 + row % 4 - 1
    inside = jnp.logical_and(target_z >= 0, target_z < size_z)
    target = (target_x * size_y + target_y) * size_z + target_z
    chosen = one_hot(jnp.logical_and(inside, lanes == target))
    near_high, rest = split(near)
    near_middle, near_low = split(rest)
    placed = matmul(
        jnp.concatenate([near_high, near_middle, near_low.astype(BF16)], axis=0), chosen
    )
    node_out[...] = placed[0:16] + placed[16:32] + placed[32:48]


def library_kernel(grid, coefficients, mine, other, residual_out, gram_out, moment_out, terms):
    fields = mine[...] + other[...]
    size_x, size_y, size_z = grid
    nodes = size_x * size_y * size_z
    lanes = lax.broadcasted_iota(jnp.int32, (1, nodes), 1)
    node_x = lanes // (size_y * size_z)
    node_y = (lanes // size_z) % size_y
    node_z = lanes % size_z
    rows = row_ids((8, nodes))
    density = fields[0:1]
    values = jnp.where(rows == 0, fields[0:8], fields[0:8] / (density + MASS_SHIFT))

    def moved(value, step):
        return pltpu.roll(value, step % nodes, 1)

    plane = size_y * size_z
    slope_x = (moved(values, -plane) - moved(values, plane)) * 0.5
    after_y = jnp.where(
        node_y == size_y - 1, moved(values, (size_y - 1) * size_z), moved(values, -size_z)
    )
    before_y = jnp.where(
        node_y == 0, moved(values, -(size_y - 1) * size_z), moved(values, size_z)
    )
    slope_y = (after_y - before_y) * 0.5
    after_z = jnp.where(node_z == size_z - 1, 0.0, moved(values, -1))
    before_z = jnp.where(node_z == 0, 0.0, moved(values, 1))
    slope_z = (after_z - before_z) * 0.5
    slopes = [[table[k : k + 1] for k in range(4)] for table in (slope_x, slope_y, slope_z)]
    strain = [
        [0.5 * (slopes[left][1 + right] + slopes[right][1 + left]) for right in range(3)]
        for left in range(3)
    ]
    divergence = strain[0][0] + strain[1][1] + strain[2][2]
    rate_sum = jnp.zeros_like(density)
    for left in range(3):
        for right in range(3):
            entry = strain[left][right]
            if left == right:
                entry = entry - divergence / 3.0
            rate_sum = rate_sum + entry * entry
    shear_rate = jnp.sqrt(2.0 * rate_sum + 0.01)
    stress = [fields[4 + k : 5 + k] for k in range(6)]
    pressure = (stress[0] + stress[3] + stress[5]) / 3.0
    deviator = (
        (stress[0] - pressure) ** 2
        + (stress[3] - pressure) ** 2
        + (stress[5] - pressure) ** 2
        + 2.0 * (stress[1] ** 2 + stress[2] ** 2 + stress[4] ** 2)
    )
    shear_stress = jnp.sqrt(0.5 * deviator + 0.01)
    pressure_scale = jnp.sqrt(pressure * pressure + 1.0)
    friction = shear_stress / pressure_scale
    features = [
        density,
        pressure / pressure_scale,
        shear_rate,
        shear_rate / jnp.sqrt(pressure_scale),
        divergence,
        slopes[0][0],
        slopes[1][0],
        slopes[2][0],
    ]
    entries = list(features)
    for left in range(8):
        for right in range(left, 8):
            entries.append(features[left] * features[right])
    for left in range(1, 5):
        entries.append(features[left] * features[left] * features[left])
    model = jnp.zeros_like(density)
    for k, entry in enumerate(entries):
        terms[k : k + 1, :] = entry
        model = model + coefficients[k] * entry
    residual = friction - model
    table = terms[...]
    gram_out[...] = (
        lax.dot_general(
            table,
            table,
            (((1,), (1,)), ((), ())),
            precision=lax.Precision.HIGHEST,
            preferred_element_type=F32,
        )
        / nodes
    )
    moment = lax.dot_general(
        jnp.broadcast_to(friction, (8, nodes)),
        table,
        (((1,), (1,)), ((), ())),
        precision=lax.Precision.HIGHEST,
        preferred_element_type=F32,
    )
    moment_out[...] = moment[0:1] / nodes
    down = lax.axis_index("down")
    cross = lax.axis_index("cross")
    depth = lax.axis_index("depth")
    b_rows = lax.broadcasted_iota(jnp.int32, (2, 1), 0)
    z_lanes = lax.broadcasted_iota(jnp.int32, (2, 2), 1)
    for a in range(2):
        mine = jnp.logical_and(node_x == down * 2 + a, node_y == cross * 2 + b_rows)
        column = [
            jnp.sum(
                jnp.where(jnp.logical_and(mine, node_z == depth * 2 + z), residual, 0.0),
                axis=1,
                keepdims=True,
            )
            for z in range(2)
        ]
        residual_out[a] = jnp.where(z_lanes == 0, column[0], column[1])


def ring(axis, step):
    peers = lax.axis_size(axis)
    return [(i, (i + step) % peers) for i in range(peers)]


def exchange(own, inner, height):
    cross = lax.axis_size("cross")

    def cells(block, first, count):
        return block[first * height : (first + count) * height]

    depth_halo = lax.ppermute(inner, "depth", [(0, 1), (1, 0)])
    if cross == 2:
        side = lax.ppermute(own, "cross", [(0, 1), (1, 0)])
        diag = lax.ppermute(inner, ("cross", "depth"), [(i, 3 - i) for i in range(4)])
        sides = [side, diag]

        def lateral(x):
            return [
                cells(side, x * 4 + 2, 2),
                cells(side, x * 4, 2),
                cells(diag, x * 2 + 1, 1),
                cells(diag, x * 2, 1),
            ]

    else:
        pairs = [(i * 2 + j, ((i + 1) % cross) * 2 + 1 - j) for i in range(cross) for j in range(2)]
        back = [(i * 2 + j, ((i - 1) % cross) * 2 + 1 - j) for i in range(cross) for j in range(2)]
        last = jnp.concatenate([cells(own, 2, 2), cells(own, 6, 2)], axis=0)
        first = jnp.concatenate([cells(own, 0, 2), cells(own, 4, 2)], axis=0)
        last_inner = jnp.concatenate([cells(inner, 1, 1), cells(inner, 3, 1)], axis=0)
        first_inner = jnp.concatenate([cells(inner, 0, 1), cells(inner, 2, 1)], axis=0)
        before = lax.ppermute(last, "cross", ring("cross", 1))
        after = lax.ppermute(first, "cross", ring("cross", -1))
        diag_before = lax.ppermute(last_inner, ("cross", "depth"), pairs)
        diag_after = lax.ppermute(first_inner, ("cross", "depth"), back)
        sides = [before, after, diag_before, diag_after]

        def lateral(x):
            return [
                cells(before, x * 2, 2),
                cells(after, x * 2, 2),
                cells(diag_before, x, 1),
                cells(diag_after, x, 1),
            ]

    def face(x):
        return jnp.concatenate([cells(own, x * 4, 4), cells(depth_halo, x * 2, 2)] + lateral(x), axis=0)

    downs = lax.axis_size("down")
    if downs % 2 == 0:
        even = lax.rem(lax.axis_index("down"), 2) == 0
        last, first = face(1), face(0)
        near = [(i, i ^ 1) for i in range(downs)]
        far = [(i, (i - 1 + 2 * (i % 2)) % downs) for i in range(downs)]
        return [own, depth_halo] + sides + [
            lax.ppermute(jnp.where(even, last, first), "down", near),
            lax.ppermute(jnp.where(even, first, last), "down", far),
        ]
    x_before = lax.ppermute(face(1), "down", ring("down", 1))
    x_after = lax.ppermute(face(0), "down", ring("down", -1))
    return [own, depth_halo] + sides + [x_before, x_after]


def shared(value, axes, peers):
    return [value] + [
        lax.ppermute(value, axes, [(i, i ^ k) for i in range(peers)]) for k in range(1, peers)
    ]


def tree_sum(parts):
    while len(parts) > 1:
        parts = [parts[k] + parts[k + 1] for k in range(0, len(parts), 2)]
    return parts[0]


def body(positions, velocities, sphere_radii, counts, coefficients):
    down, cross, depth = (lax.axis_size(name) for name in ("down", "cross", "depth"))
    wide = cross != 2
    grid = (2 * down, 2 * cross, 2 * depth)
    nodes = grid[0] * grid[1] * grid[2]
    params = pltpu.CompilerParams(vmem_limit_bytes=VMEM_LIMIT)
    vector_shape = jax.ShapeDtypeStruct((3, 2, 2, 2, S), F32)

    def rows(count):
        return jax.ShapeDtypeStruct((count, S), F32)

    own, inner = pl.pallas_call(
        pack_kernel,
        out_shape=(rows(64), rows(32)),
        in_specs=[SMEM_SPEC] + [pl.BlockSpec(memory_space=pl.ANY)] * 3,
        out_specs=(VMEM_SPEC, VMEM_SPEC),
        scratch_shapes=[
            pltpu.VMEM((3, 2, 2, 2, S), F32),
            pltpu.VMEM((3, 2, 2, 2, S), F32),
            pltpu.VMEM((2, 2, 2, S), F32),
            pltpu.SemaphoreType.DMA((3,)),
        ],
        compiler_params=pltpu.CompilerParams(vmem_limit_bytes=60 * 1024 * 1024),
        name="pack",
    )(counts, positions, velocities, sphere_radii)
    pieces = exchange(own, inner, 8)
    velocity_new, own_speed, inner_speed = pl.pallas_call(
        functools.partial(step_kernel, wide),
        out_shape=(vector_shape, rows(32), rows(16)),
        in_specs=[VMEM_SPEC] * len(pieces),
        out_specs=(VMEM_SPEC,) * 3,
        scratch_shapes=contact_scratch(3),
        compiler_params=params,
        name="step",
    )(*pieces)
    speeds = exchange(own_speed, inner_speed, 4)
    force_next, partial = pl.pallas_call(
        functools.partial(field_kernel, wide, grid),
        out_shape=(vector_shape, jax.ShapeDtypeStruct((16, nodes), F32)),
        in_specs=[VMEM_SPEC] * (len(pieces) + len(speeds)),
        out_specs=(VMEM_SPEC,) * 2,
        scratch_shapes=[pltpu.VMEM((16, 8 * S), F32)] + contact_scratch(9),
        compiler_params=params,
        name="field",
    )(*pieces, *speeds)
    partial = tree_sum(shared(partial, ("cross", "depth"), cross * depth))
    distance = 1
    while distance < down:
        other = lax.ppermute(partial, "down", [(i, i ^ distance) for i in range(down)])
        distance = distance * 2
        if distance < down:
            partial = partial + other
    residual_field, gram_matrix, moment = pl.pallas_call(
        functools.partial(library_kernel, grid),
        out_shape=(
            jax.ShapeDtypeStruct((2, 2, 2), F32),
            jax.ShapeDtypeStruct((TERMS, TERMS), F32),
            jax.ShapeDtypeStruct((1, TERMS), F32),
        ),
        in_specs=[SMEM_SPEC, VMEM_SPEC, VMEM_SPEC],
        out_specs=(VMEM_SPEC,) * 3,
        scratch_shapes=[pltpu.VMEM((TERMS, nodes), F32)],
        compiler_params=params,
        name="library",
    )(coefficients, partial, other)
    return (velocity_new, force_next, residual_field, gram_matrix, moment.reshape(TERMS))


def solution(mesh):
    return jax.shard_map(
        body,
        mesh=mesh,
        in_specs=(
            P(None, ("groups", "down"), "cross", "depth", None),
            P(None, ("groups", "down"), "cross", "depth", None),
            P(("groups", "down"), "cross", "depth", None),
            P(("groups", "down"), "cross", "depth"),
            P(),
        ),
        out_specs=(
            P(None, ("groups", "down"), "cross", "depth", None),
            P(None, ("groups", "down"), "cross", "depth", None),
            P(("groups", "down"), "cross", "depth"),
            P("groups", None),
            P("groups"),
        ),
        check_vma=False,
    )
```

```python
import functools

import jax
import jax.numpy as jnp
from jax import lax
from jax.experimental import pallas as pl
from jax.experimental.pallas import tpu as pltpu
from jax.sharding import PartitionSpec as P

STIFFNESS = 100.0
DAMPING = 20.0
TIME_STEP = 0.05
KERNEL_WIDTH = 0.4
KERNEL_NORM = 64.0
SOFTENING = 0.0001
RADIUS_REF = 0.1
MASS_SHIFT = 0.1
DEAD = -1000.0
TERMS = 48
S = 128
F32 = jnp.float32
BF16 = jnp.bfloat16
CELLS = tuple((a, b, z) for a in range(2) for b in range(2) for z in range(2))
PAIRS = ((0, 2), (4, 6), (1, 3), (5, 7))
PAIR_LIST = ((0, 0), (0, 1), (0, 2), (1, 1), (1, 2), (2, 2))
VMEM_SPEC = pl.BlockSpec(memory_space=pltpu.VMEM)
SMEM_SPEC = pl.BlockSpec(memory_space=pltpu.SMEM)
VMEM_LIMIT = 48 * 1024 * 1024


def row_ids(shape):
    return lax.broadcasted_iota(jnp.int32, shape, 0)


def lane_ids(shape):
    return lax.broadcasted_iota(jnp.int32, shape, 1)


def one_hot(condition):
    return jnp.where(condition, 1.0, 0.0).astype(BF16)


def split(value):
    high = value.astype(BF16)
    return high, value - high.astype(F32)


def matmul(left, right):
    return lax.dot_general(left, right, (((1,), (0,)), ((), ())), preferred_element_type=F32)


def matmul_turned(left, right):
    return lax.dot_general(left, right, (((1,), (1,)), ((), ())), preferred_element_type=F32)


def lane_gather(table, index):
    return jnp.take_along_axis(table, index, axis=1)


def pack_kernel(
    counts_hbm, positions_hbm, velocities_hbm, radii_hbm, own, inner, counts, positions, velocities, radii, arrived
):
    copies = [
        pltpu.make_async_copy(source, target, arrived.at[k])
        for k, (source, target) in enumerate(
            (
                (counts_hbm, counts),
                (positions_hbm, positions),
                (velocities_hbm, velocities),
                (radii_hbm, radii),
            )
        )
    ]
    for copy in copies:
        copy.start()
    for copy in copies:
        copy.wait()
    depth = lax.axis_index("depth")
    lanes = lane_ids((1, S))

    def layer(ref, at, z):
        rows = ref[at]
        return jnp.where(depth == z, rows[0:1], rows[1:2])

    for c, (a, b, z) in enumerate(CELLS):
        for k in range(3):
            own[c * 8 + k : c * 8 + k + 1, :] = layer(positions, (k, a, b), z)
            own[c * 8 + 3 + k : c * 8 + 4 + k, :] = layer(velocities, (k, a, b), z)
        count = jnp.where(depth == z, counts[a, b, 0], counts[a, b, 1])
        own[c * 8 + 6 : c * 8 + 7, :] = jnp.where(lanes < count, layer(radii, (a, b), z), DEAD)
        own[c * 8 + 7 : c * 8 + 8, :] = jnp.zeros((1, S), F32)
    for column in range(4):
        inner[column * 8 : column * 8 + 8, :] = own[column * 16 + 8 : column * 16 + 16, :]


def local_state(raw, centre):
    rows = row_ids(raw.shape)
    shift = jnp.where(rows == 0, centre[0], jnp.where(rows == 1, centre[1], centre[2]))
    return jnp.where(rows < 3, raw + shift, raw)


def plane_reader(refs, height):
    own, depth_halo, sides = refs[0], refs[1], refs[2:]

    def read(ref, cell):
        return ref[cell * height : cell * height + height, :]

    def cell(x, y, slot):
        a = x - 1
        if y in (1, 2):
            return read(own, a * 4 + (y - 1) * 2 + slot) if slot < 2 else read(depth_halo, a * 2 + y - 1)
        if len(sides) == 4:
            before, after, diag_before, diag_after = sides
            if slot < 2:
                return read(before if y == 0 else after, a * 2 + slot)
            return read(diag_before if y == 0 else diag_after, a)
        side, diag = sides
        b = 1 if y == 0 else 0
        return read(side, a * 4 + b * 2 + slot) if slot < 2 else read(diag, a * 2 + b)

    return cell


def down_reader(refs, height):
    even = lax.rem(lax.axis_index("down"), 2) == 0
    swapped = lax.axis_size("down") % 2 == 0

    def cell(x, y, slot):
        if y in (1, 2):
            place = (y - 1) * 2 + slot if slot < 2 else 4 + y - 1
        else:
            side = 0 if y == 0 else 1
            place = 6 + side * 2 + slot if slot < 2 else 10 + side
        one, two = (ref[place * height : place * height + height, :] for ref in refs)
        if swapped:
            return jnp.where(even, two, one) if x == 0 else jnp.where(even, one, two)
        return one if x == 0 else two

    return cell


def centre_of(x, y, slot, depth):
    side = 0.5 - depth.astype(F32)
    return (x - 1.5, y - 1.5, (-1.0, 1.0, 3.0)[slot] * side)


def extended_cells(xs, depth):
    for k, x in enumerate(xs):
        for y in range(4):
            for slot in range(3):
                yield x, y, slot, ((k * 4 + y) * 3 + slot) * 8, centre_of(x, y, slot, depth)


def stepped_state(old, speed, centre):
    rows = row_ids((3, S))
    shift = jnp.where(rows == 0, centre[0], jnp.where(rows == 1, centre[1], centre[2]))
    return (old[0:3] + TIME_STEP * speed[0:3]) + shift, speed[0:3], old[6:8]


def contact_scratch(width):
    return [
        pltpu.VMEM((24 * 8, S), F32),
        pltpu.VMEM((8 * 8, S), F32),
        pltpu.VMEM((8 * 24, S), jnp.int32),
        pltpu.VMEM((8 * 24, S), jnp.int32),
        pltpu.VMEM((8 * 24, S), jnp.int32),
        pltpu.VMEM((8 * 24, S), jnp.int32),
        pltpu.VMEM((8, 18, 8, S), F32),
        pltpu.VMEM((8, 7, S, S), F32),
        pltpu.VMEM((8, width, S, S), F32),
    ]


def contact_sums(xs, width, scratch):
    local_ref, mine_ref, index_ref, base_ref, amount_ref, chosen_ref, list_ref, spread_ref, sum_ref = scratch
    for c in range(8):
        turned = jnp.transpose(mine_ref[c * 8 : c * 8 + 8, :])
        for k in range(7):
            spread_ref[c, k] = jnp.broadcast_to(turned[:, k : k + 1], (S, S))

    def beside(a, b, z):
        return [
            (k * 4 + y) * 3 + slot
            for k, x in enumerate(xs)
            if abs(x - 1 - a) <= 1
            for y in range(b, b + 3)
            for slot in range(3 if z == 1 else 2)
        ]

    place = [local_ref[pl.ds(k, 24, stride=8), :] for k in range(3)]
    radius = local_ref[pl.ds(6, 24, stride=8), :]
    rows = row_ids((24, S))
    row_x = jnp.where(rows < 12, xs[0], xs[1])
    row_y, row_slot = (rows // 3) % 4, rows % 3
    masks = []
    for c, (a, b, z) in enumerate(CELLS):
        mine = mine_ref[c * 8 : c * 8 + 8, :]
        live = mine[6:7] > 0.0
        low = jnp.min(jnp.where(live, mine, 1e9), axis=1, keepdims=True)
        high = jnp.max(jnp.where(live, mine, -1e9), axis=1, keepdims=True)
        reach = radius + high[6:7]
        near = jnp.logical_and(
            jnp.logical_and(row_x >= a, row_x <= a + 2), jnp.logical_and(row_y >= b, row_y <= b + 2)
        )
        if z == 0:
            near = jnp.logical_and(near, row_slot < 2)
        for k in range(3):
            near = jnp.logical_and(near, place[k] + reach > low[k : k + 1])
            near = jnp.logical_and(near, place[k] - reach < high[k : k + 1])
        masks.append(jnp.where(near, 1.0, 0.0).astype(F32))
    mask = jnp.concatenate(masks, axis=0).astype(BF16)
    upper = one_hot(row_ids((S, 2 * S)) <= lane_ids((S, 2 * S)))
    sums = matmul(mask, upper)
    prefix, amount = sums[:, :S], sums[:, S:]
    before = one_hot(lane_ids((24, 24)) < row_ids((24, 24)))
    totals = []
    for c in range(8):
        part = amount[c * 24 : c * 24 + 24]
        base = matmul(before, part.astype(BF16))
        base_ref[c * 24 : c * 24 + 24, :] = base.astype(jnp.int32)
        totals.append((base[23:24, 0:1] + part[23:24, 0:1]).astype(jnp.int32)[0, 0])
    amount_ref[...] = amount.astype(jnp.int32)
    wanted = lane_ids((8 * 24, S)).astype(F32)
    index = jnp.zeros((8 * 24, S), jnp.int32)
    for step in (64, 32, 16, 8, 4, 2, 1):
        probe = lane_gather(prefix, index + (step - 1))
        index = jnp.where(probe <= wanted, index + step, index)
    index_ref[...] = index
    tiles = [(total + (S - 1)) // S for total in totals]
    most = tiles[0]
    for count in tiles[1:]:
        most = jnp.maximum(most, count)

    empty = jnp.where(row_ids((8, S)) == 6, DEAD, 0.0).astype(F32)

    def gather_tiles(t, carry):
        want = t * S + lane_ids((8 * 24, S)) - base_ref[...]
        valid = jnp.logical_and(want >= 0, want < amount_ref[...])
        source = lane_gather(index_ref[...], jnp.clip(want, 0, S - 1))
        chosen_ref[...] = jnp.where(valid, source, -1)
        for c, (a, b, z) in enumerate(CELLS):
            tile = empty
            for n in beside(a, b, z):
                pick = jnp.broadcast_to(chosen_ref[c * 24 + n : c * 24 + n + 1, :], (8, S))
                values = lane_gather(local_ref[n * 8 : n * 8 + 8, :], jnp.maximum(pick, 0))
                tile = jnp.where(pick >= 0, values, tile)
            list_ref[c, t] = tile
        return carry

    gather_tiles(0, 0)
    lax.fori_loop(1, most, gather_tiles, 0)

    def pair_tile(c, t, first):
        tile = list_ref[c, t]
        other = [jnp.broadcast_to(tile[k : k + 1], (8, S)) for k in range(7)]
        for block in range(16):
            row = block * 8
            me = [spread_ref[c, k, row : row + 8, :] for k in range(7)]
            r = [me[k] - other[k] for k in range(3)]
            u = [me[3 + k] - other[3 + k] for k in range(3)]
            squared = r[0] * r[0] + r[1] * r[1] + r[2] * r[2] + SOFTENING
            inverse = lax.rsqrt(squared)
            along = u[0] * r[0] + u[1] * r[1] + u[2] * r[2]
            overlap = jnp.maximum((me[6] + other[6]) * inverse - 1.0, 0.0)
            weight = overlap * (STIFFNESS - (DAMPING * along) * inverse)
            terms = [weight * r[k] for k in range(3)]
            if width == 9:
                terms += [terms[left] * r[right] for left, right in PAIR_LIST]
            for k, term in enumerate(terms):
                if first:
                    sum_ref[c, k, row : row + 8, :] = term
                else:
                    sum_ref[c, k, row : row + 8, :] += term

    for c in range(8):
        pair_tile(c, 0, True)
    for group in PAIRS:

        def later_tile(t, carry):
            for c in group:
                pair_tile(c, t, False)
            return carry

        lax.fori_loop(1, jnp.maximum(tiles[group[0]], tiles[group[1]]), later_tile, 0)
    lanes = lane_ids((S, S))
    table = jnp.zeros((S, S), F32)
    for k in range(width):
        for c in range(8):
            column = jnp.sum(sum_ref[c, k], axis=1, keepdims=True)
            table = jnp.where(lanes == k * 8 + c, column, table)
    return jnp.transpose(table)[0 : width * 8]


def mass_of(radius):
    scaled = radius / RADIUS_REF
    return scaled * scaled * scaled


def step_inside(*refs):
    pieces, sums_out, scratch = refs[:-10], refs[-10], refs[-9:]
    depth = lax.axis_index("depth")
    cell = plane_reader(pieces, 8)
    for x, y, slot, start, centre in extended_cells((1, 2), depth):
        scratch[0][start : start + 8, :] = local_state(cell(x, y, slot), centre)
    for c, (a, b, z) in enumerate(CELLS):
        start = ((a * 4 + b + 1) * 3 + z) * 8
        scratch[1][c * 8 : c * 8 + 8, :] = scratch[0][start : start + 8, :]
    sums_out[...] = contact_sums((1, 2), 3, scratch)


def step_outside(own, sums_in, near, far, own_out, inner_out, *scratch):
    depth = lax.axis_index("depth")
    cell = down_reader((near, far), 8)
    for x, y, slot, start, centre in extended_cells((0, 3), depth):
        scratch[0][start : start + 8, :] = local_state(cell(x, y, slot), centre)
    for c, (a, b, z) in enumerate(CELLS):
        scratch[1][c * 8 : c * 8 + 8, :] = local_state(
            own[c * 8 : c * 8 + 8, :], centre_of(a + 1, b + 1, z, depth)
        )
    sums = sums_in[...] + contact_sums((0, 3), 3, scratch)
    radius = own[pl.ds(6, 8, stride=8), :]
    safe_mass = jnp.where(radius > 0.0, mass_of(radius), 1.0)
    for k in range(3):
        velocity = own[pl.ds(3 + k, 8, stride=8), :] + TIME_STEP * sums[k * 8 : k * 8 + 8] / safe_mass
        for c in range(8):
            own_out[c * 4 + k : c * 4 + k + 1, :] = velocity[c : c + 1]
    for c in range(8):
        own_out[c * 4 + 3 : c * 4 + 4, :] = jnp.zeros((1, S), F32)
    for column in range(4):
        inner_out[column * 4 : column * 4 + 4, :] = own_out[column * 8 + 4 : column * 8 + 8, :]


def place_state(ref, start, state):
    ref[start : start + 3, :] = state[0]
    ref[start + 3 : start + 6, :] = state[1]
    ref[start + 6 : start + 8, :] = state[2]


def field_inside(*refs):
    count = (len(refs) - 10) // 2
    pieces, speeds, sums_out, scratch = refs[:count], refs[count : 2 * count], refs[-10], refs[-9:]
    depth = lax.axis_index("depth")
    cell, speed = plane_reader(pieces, 8), plane_reader(speeds, 4)
    for x, y, slot, start, centre in extended_cells((1, 2), depth):
        place_state(scratch[0], start, stepped_state(cell(x, y, slot), speed(x, y, slot), centre))
    for c, (a, b, z) in enumerate(CELLS):
        start = ((a * 4 + b + 1) * 3 + z) * 8
        scratch[1][c * 8 : c * 8 + 8, :] = scratch[0][start : start + 8, :]
    sums_out[...] = contact_sums((1, 2), 9, scratch)


def field_outside(
    grid, own, own_speed, sums_in, near_old, far_old, near_speed, far_speed, force_out, node_out, moment_ref, *scratch
):
    depth = lax.axis_index("depth")
    down = lax.axis_index("down")
    cross = lax.axis_index("cross")
    mine_ref = scratch[1]
    cell, speed = down_reader((near_old, far_old), 8), down_reader((near_speed, far_speed), 4)
    for x, y, slot, start, centre in extended_cells((0, 3), depth):
        place_state(scratch[0], start, stepped_state(cell(x, y, slot), speed(x, y, slot), centre))
    for c, (a, b, z) in enumerate(CELLS):
        state = stepped_state(
            own[c * 8 : c * 8 + 8, :],
            own_speed[c * 4 : c * 4 + 4, :],
            centre_of(a + 1, b + 1, z, depth),
        )
        place_state(mine_ref, c * 8, state)
    sums = sums_in[...] + contact_sums((0, 3), 9, scratch)
    force_out[...] = sums[0:24]
    radius = own[pl.ds(6, 8, stride=8), :]
    mass = jnp.where(radius > 0.0, mass_of(radius), 0.0)
    moments = [mass] + [mass * own_speed[pl.ds(k, 8, stride=4), :] for k in range(3)]
    moments += [0.5 * sums[k * 8 : k * 8 + 8] for k in range(3, 9)]
    moment_ref[...] = jnp.zeros((16, 8 * S), F32)
    for m, moment in enumerate(moments):
        for c in range(8):
            moment_ref[m : m + 1, c * S : (c + 1) * S] = moment[c : c + 1]
    rows = row_ids((64, S))
    near_x, near_y, near_z = rows // 16 - 1, (rows // 4) % 4 - 1, rows % 4 - 1
    centres = [index.astype(F32) - 0.5 for index in (near_x, near_y, near_z)]
    kernels = []
    for c, (a, b, z) in enumerate(CELLS):
        squared = jnp.zeros((64, S), F32)
        for k in range(3):
            gap = mine_ref[c * 8 + k : c * 8 + k + 1, :] - centres[k]
            squared = squared + gap * gap
        kernel = jnp.exp(squared * (-0.5 / (KERNEL_WIDTH * KERNEL_WIDTH))) / KERNEL_NORM
        beside = jnp.logical_and(
            jnp.logical_and(jnp.abs(near_x - a) <= 1, jnp.abs(near_y - b) <= 1),
            jnp.abs(near_z - jnp.where(depth == z, 0, 1)) <= 1,
        )
        kernels.append(jnp.where(beside, kernel, 0.0))
    kernel_high, kernel_low = split(jnp.concatenate(kernels, axis=1))
    moment_high, moment_low = split(moment_ref[...])
    wide_part = matmul_turned(
        jnp.concatenate([moment_high, moment_low.astype(BF16)], axis=0), kernel_high
    )
    near = wide_part[0:16] + wide_part[16:32] + matmul_turned(moment_high, kernel_low.astype(BF16))
    size_x, size_y, size_z = grid
    nodes = size_x * size_y * size_z
    lanes = lane_ids((64, nodes))
    row = row_ids((64, nodes))
    target_x = (down * 2 + row // 16 - 1 + size_x) % size_x
    target_y = (cross * 2 + (row // 4) % 4 - 1 + size_y) % size_y
    target_z = depth * 2 + row % 4 - 1
    inside = jnp.logical_and(target_z >= 0, target_z < size_z)
    target = (target_x * size_y + target_y) * size_z + target_z
    chosen = one_hot(jnp.logical_and(inside, lanes == target))
    near_high, rest = split(near)
    near_middle, near_low = split(rest)
    placed = matmul(
        jnp.concatenate([near_high, near_middle, near_low.astype(BF16)], axis=0), chosen
    )
    node_out[...] = placed[0:16] + placed[16:32] + placed[32:48]


def library_kernel(
    grid, coefficients, mine, other, speed, force, velocity_out, force_out, residual_out, gram_out, moment_out, terms
):
    flat = lax.axis_index("depth") == 0
    for k in range(3):
        for a in range(2):
            for b in range(2):
                c = a * 4 + b * 2
                layers = [speed[(c + z) * 4 + k : (c + z) * 4 + k + 1, :] for z in range(2)]
                pulls = [force[k * 8 + c + z : k * 8 + c + z + 1, :] for z in range(2)]
                for z in range(2):
                    velocity_out[k, a, b, z : z + 1, :] = jnp.where(flat, layers[z], layers[1 - z])
                    force_out[k, a, b, z : z + 1, :] = jnp.where(flat, pulls[z], pulls[1 - z])
    fields = mine[...] + other[...]
    size_x, size_y, size_z = grid
    nodes = size_x * size_y * size_z
    lanes = lax.broadcasted_iota(jnp.int32, (1, nodes), 1)
    node_x = lanes // (size_y * size_z)
    node_y = (lanes // size_z) % size_y
    node_z = lanes % size_z
    rows = row_ids((8, nodes))
    density = fields[0:1]
    values = jnp.where(rows == 0, fields[0:8], fields[0:8] / (density + MASS_SHIFT))

    def moved(value, step):
        return pltpu.roll(value, step % nodes, 1)

    plane = size_y * size_z
    slope_x = (moved(values, -plane) - moved(values, plane)) * 0.5
    after_y = jnp.where(
        node_y == size_y - 1, moved(values, (size_y - 1) * size_z), moved(values, -size_z)
    )
    before_y = jnp.where(
        node_y == 0, moved(values, -(size_y - 1) * size_z), moved(values, size_z)
    )
    slope_y = (after_y - before_y) * 0.5
    after_z = jnp.where(node_z == size_z - 1, 0.0, moved(values, -1))
    before_z = jnp.where(node_z == 0, 0.0, moved(values, 1))
    slope_z = (after_z - before_z) * 0.5
    slopes = [[table[k : k + 1] for k in range(4)] for table in (slope_x, slope_y, slope_z)]
    strain = [
        [0.5 * (slopes[left][1 + right] + slopes[right][1 + left]) for right in range(3)]
        for left in range(3)
    ]
    divergence = strain[0][0] + strain[1][1] + strain[2][2]
    rate_sum = jnp.zeros_like(density)
    for left in range(3):
        for right in range(3):
            entry = strain[left][right]
            if left == right:
                entry = entry - divergence / 3.0
            rate_sum = rate_sum + entry * entry
    shear_rate = jnp.sqrt(2.0 * rate_sum + 0.01)
    stress = [fields[4 + k : 5 + k] for k in range(6)]
    pressure = (stress[0] + stress[3] + stress[5]) / 3.0
    deviator = (
        (stress[0] - pressure) ** 2
        + (stress[3] - pressure) ** 2
        + (stress[5] - pressure) ** 2
        + 2.0 * (stress[1] ** 2 + stress[2] ** 2 + stress[4] ** 2)
    )
    shear_stress = jnp.sqrt(0.5 * deviator + 0.01)
    pressure_scale = jnp.sqrt(pressure * pressure + 1.0)
    friction = shear_stress / pressure_scale
    features = [
        density,
        pressure / pressure_scale,
        shear_rate,
        shear_rate / jnp.sqrt(pressure_scale),
        divergence,
        slopes[0][0],
        slopes[1][0],
        slopes[2][0],
    ]
    entries = list(features)
    for left in range(8):
        for right in range(left, 8):
            entries.append(features[left] * features[right])
    for left in range(1, 5):
        entries.append(features[left] * features[left] * features[left])
    model = jnp.zeros_like(density)
    for k, entry in enumerate(entries):
        terms[k : k + 1, :] = entry
        model = model + coefficients[k] * entry
    residual = friction - model
    table = terms[...]
    gram_out[...] = (
        lax.dot_general(
            table,
            table,
            (((1,), (1,)), ((), ())),
            precision=lax.Precision.HIGHEST,
            preferred_element_type=F32,
        )
        / nodes
    )
    moment = lax.dot_general(
        jnp.broadcast_to(friction, (8, nodes)),
        table,
        (((1,), (1,)), ((), ())),
        precision=lax.Precision.HIGHEST,
        preferred_element_type=F32,
    )
    moment_out[...] = moment[0:1] / nodes
    down = lax.axis_index("down")
    cross = lax.axis_index("cross")
    depth = lax.axis_index("depth")
    b_rows = lax.broadcasted_iota(jnp.int32, (2, 1), 0)
    z_lanes = lax.broadcasted_iota(jnp.int32, (2, 2), 1)
    for a in range(2):
        mine = jnp.logical_and(node_x == down * 2 + a, node_y == cross * 2 + b_rows)
        column = [
            jnp.sum(
                jnp.where(jnp.logical_and(mine, node_z == depth * 2 + z), residual, 0.0),
                axis=1,
                keepdims=True,
            )
            for z in range(2)
        ]
        residual_out[a] = jnp.where(z_lanes == 0, column[0], column[1])


def ring(axis, step):
    peers = lax.axis_size(axis)
    return [(i, (i + step) % peers) for i in range(peers)]


def exchange(own, inner, height):
    cross = lax.axis_size("cross")

    def cells(block, first, count):
        return block[first * height : (first + count) * height]

    depth_halo = lax.ppermute(inner, "depth", [(0, 1), (1, 0)])
    if cross == 2:
        side = lax.ppermute(own, "cross", [(0, 1), (1, 0)])
        diag = lax.ppermute(inner, ("cross", "depth"), [(i, 3 - i) for i in range(4)])
        sides = [side, diag]

        def lateral(x):
            return [
                cells(side, x * 4 + 2, 2),
                cells(side, x * 4, 2),
                cells(diag, x * 2 + 1, 1),
                cells(diag, x * 2, 1),
            ]

    else:
        pairs = [(i * 2 + j, ((i + 1) % cross) * 2 + 1 - j) for i in range(cross) for j in range(2)]
        back = [(i * 2 + j, ((i - 1) % cross) * 2 + 1 - j) for i in range(cross) for j in range(2)]
        last = jnp.concatenate([cells(own, 2, 2), cells(own, 6, 2)], axis=0)
        first = jnp.concatenate([cells(own, 0, 2), cells(own, 4, 2)], axis=0)
        last_inner = jnp.concatenate([cells(inner, 1, 1), cells(inner, 3, 1)], axis=0)
        first_inner = jnp.concatenate([cells(inner, 0, 1), cells(inner, 2, 1)], axis=0)
        before = lax.ppermute(last, "cross", ring("cross", 1))
        after = lax.ppermute(first, "cross", ring("cross", -1))
        diag_before = lax.ppermute(last_inner, ("cross", "depth"), pairs)
        diag_after = lax.ppermute(first_inner, ("cross", "depth"), back)
        sides = [before, after, diag_before, diag_after]

        def lateral(x):
            return [
                cells(before, x * 2, 2),
                cells(after, x * 2, 2),
                cells(diag_before, x, 1),
                cells(diag_after, x, 1),
            ]

    def face(x):
        return jnp.concatenate([cells(own, x * 4, 4), cells(depth_halo, x * 2, 2)] + lateral(x), axis=0)

    downs = lax.axis_size("down")
    last, first = face(1), face(0)
    if downs % 2 == 0:
        even = lax.rem(lax.axis_index("down"), 2) == 0
        near = [(i, i ^ 1) for i in range(downs)]
        far = [(i, (i - 1 + 2 * (i % 2)) % downs) for i in range(downs)]
        outside = [
            lax.ppermute(jnp.where(even, last, first), "down", near),
            lax.ppermute(jnp.where(even, first, last), "down", far),
        ]
    else:
        outside = [
            lax.ppermute(last, "down", ring("down", 1)),
            lax.ppermute(first, "down", ring("down", -1)),
        ]
    return [own, depth_halo] + sides, outside


def shared(value, axes, peers):
    return [value] + [
        lax.ppermute(value, axes, [(i, i ^ k) for i in range(peers)]) for k in range(1, peers)
    ]


def tree_sum(parts):
    while len(parts) > 1:
        parts = [parts[k] + parts[k + 1] for k in range(0, len(parts), 2)]
    return parts[0]


def body(positions, velocities, sphere_radii, counts, coefficients):
    down, cross, depth = (lax.axis_size(name) for name in ("down", "cross", "depth"))
    grid = (2 * down, 2 * cross, 2 * depth)
    nodes = grid[0] * grid[1] * grid[2]
    params = pltpu.CompilerParams(vmem_limit_bytes=VMEM_LIMIT)
    vector_shape = jax.ShapeDtypeStruct((3, 2, 2, 2, S), F32)

    def rows(count):
        return jax.ShapeDtypeStruct((count, S), F32)

    def call(kernel, inputs, outputs, scratch, name, vectors=0):
        return pl.pallas_call(
            kernel,
            out_shape=outputs,
            in_specs=[VMEM_SPEC] * len(inputs),
            out_specs=jax.tree.map(lambda _: VMEM_SPEC, outputs),
            scratch_shapes=scratch,
            compiler_params=params,
            cost_estimate=pl.CostEstimate(flops=vectors, bytes_accessed=1 << 20, transcendentals=0),
            name=name,
        )(*inputs)

    own, inner = pl.pallas_call(
        pack_kernel,
        out_shape=(rows(64), rows(32)),
        in_specs=[pl.BlockSpec(memory_space=pl.ANY)] * 4,
        out_specs=(VMEM_SPEC, VMEM_SPEC),
        scratch_shapes=[
            pltpu.SMEM((2, 2, 2), jnp.int32),
            pltpu.VMEM((3, 2, 2, 2, S), F32),
            pltpu.VMEM((3, 2, 2, 2, S), F32),
            pltpu.VMEM((2, 2, 2, S), F32),
            pltpu.SemaphoreType.DMA((4,)),
        ],
        compiler_params=pltpu.CompilerParams(vmem_limit_bytes=60 * 1024 * 1024),
        name="pack",
    )(counts, positions, velocities, sphere_radii)
    inside, outside = exchange(own, inner, 8)
    sums = call(step_inside, inside, rows(24), contact_scratch(3), "step_inside", 1 << 31)
    own_speed, inner_speed = call(
        step_outside, [own, sums] + outside, (rows(32), rows(16)), contact_scratch(3), "step_outside", 1 << 30
    )
    inside_speed, outside_speed = exchange(own_speed, inner_speed, 4)
    sums = call(
        field_inside, inside + inside_speed, rows(72), contact_scratch(9), "field_inside", 1 << 31
    )
    force, partial = call(
        functools.partial(field_outside, grid),
        [own, own_speed, sums] + outside + outside_speed,
        (rows(24), jax.ShapeDtypeStruct((16, nodes), F32)),
        [pltpu.VMEM((16, 8 * S), F32)] + contact_scratch(9),
        "field_outside",
        1 << 30,
    )
    partial = tree_sum(shared(partial, ("cross", "depth"), cross * depth))
    distance = 1
    while distance < down:
        other = lax.ppermute(partial, "down", [(i, i ^ distance) for i in range(down)])
        distance = distance * 2
        if distance < down:
            partial = partial + other
    velocity_new, force_next, residual_field, gram_matrix, moment = pl.pallas_call(
        functools.partial(library_kernel, grid),
        out_shape=(
            vector_shape,
            vector_shape,
            jax.ShapeDtypeStruct((2, 2, 2), F32),
            jax.ShapeDtypeStruct((TERMS, TERMS), F32),
            jax.ShapeDtypeStruct((1, TERMS), F32),
        ),
        in_specs=[SMEM_SPEC] + [VMEM_SPEC] * 4,
        out_specs=(VMEM_SPEC,) * 5,
        scratch_shapes=[pltpu.VMEM((TERMS, nodes), F32)],
        compiler_params=params,
        name="library",
    )(coefficients, partial, other, own_speed, force)
    return (velocity_new, force_next, residual_field, gram_matrix, moment.reshape(TERMS))


def solution(mesh):
    return jax.shard_map(
        body,
        mesh=mesh,
        in_specs=(
            P(None, ("groups", "down"), "cross", "depth", None),
            P(None, ("groups", "down"), "cross", "depth", None),
            P(("groups", "down"), "cross", "depth", None),
            P(("groups", "down"), "cross", "depth"),
            P(),
        ),
        out_specs=(
            P(None, ("groups", "down"), "cross", "depth", None),
            P(None, ("groups", "down"), "cross", "depth", None),
            P(("groups", "down"), "cross", "depth"),
            P("groups", None),
            P("groups"),
        ),
        check_vma=False,
    )
```

```python
import functools

import jax
import jax.numpy as jnp
from jax import lax
from jax.experimental import pallas as pl
from jax.experimental.pallas import tpu as pltpu
from jax.sharding import PartitionSpec as P

STIFFNESS = 100.0
DAMPING = 20.0
TIME_STEP = 0.05
KERNEL_WIDTH = 0.4
KERNEL_NORM = 64.0
SOFTENING = 0.0001
RADIUS_REF = 0.1
MASS_SHIFT = 0.1
DEAD = -1000.0
TERMS = 48
S = 128
F32 = jnp.float32
BF16 = jnp.bfloat16
CELLS = tuple((a, b, z) for a in range(2) for b in range(2) for z in range(2))
PAIR_LIST = ((0, 0), (0, 1), (0, 2), (1, 1), (1, 2), (2, 2))
VMEM_SPEC = pl.BlockSpec(memory_space=pltpu.VMEM)
SMEM_SPEC = pl.BlockSpec(memory_space=pltpu.SMEM)
VMEM_LIMIT = 48 * 1024 * 1024


def row_ids(shape):
    return lax.broadcasted_iota(jnp.int32, shape, 0)


def lane_ids(shape):
    return lax.broadcasted_iota(jnp.int32, shape, 1)


def one_hot(condition):
    return jnp.where(condition, 1.0, 0.0).astype(BF16)


def split(value):
    high = value.astype(BF16)
    return high, value - high.astype(F32)


def matmul(left, right):
    return lax.dot_general(left, right, (((1,), (0,)), ((), ())), preferred_element_type=F32)


def matmul_turned(left, right):
    return lax.dot_general(left, right, (((1,), (1,)), ((), ())), preferred_element_type=F32)


def lane_gather(table, index):
    return jnp.take_along_axis(table, index, axis=1)


def pack_kernel(
    counts_hbm, positions_hbm, velocities_hbm, radii_hbm, own, inner, counts, positions, velocities, radii, arrived
):
    copies = [
        pltpu.make_async_copy(source, target, arrived.at[k])
        for k, (source, target) in enumerate(
            (
                (counts_hbm, counts),
                (positions_hbm, positions),
                (velocities_hbm, velocities),
                (radii_hbm, radii),
            )
        )
    ]
    for copy in copies:
        copy.start()
    for copy in copies:
        copy.wait()
    depth = lax.axis_index("depth")
    lanes = lane_ids((1, S))

    def layer(ref, at, z):
        rows = ref[at]
        return jnp.where(depth == z, rows[0:1], rows[1:2])

    for c, (a, b, z) in enumerate(CELLS):
        for k in range(3):
            own[c * 8 + k : c * 8 + k + 1, :] = layer(positions, (k, a, b), z)
            own[c * 8 + 3 + k : c * 8 + 4 + k, :] = layer(velocities, (k, a, b), z)
        count = jnp.where(depth == z, counts[a, b, 0], counts[a, b, 1])
        own[c * 8 + 6 : c * 8 + 7, :] = jnp.where(lanes < count, layer(radii, (a, b), z), DEAD)
        own[c * 8 + 7 : c * 8 + 8, :] = jnp.zeros((1, S), F32)
    for column in range(4):
        inner[column * 8 : column * 8 + 8, :] = own[column * 16 + 8 : column * 16 + 16, :]


def local_state(raw, centre):
    rows = row_ids(raw.shape)
    shift = jnp.where(rows == 0, centre[0], jnp.where(rows == 1, centre[1], centre[2]))
    return jnp.where(rows < 3, raw + shift, raw)


def plane_reader(refs, height):
    own, depth_halo, sides = refs[0], refs[1], refs[2:]

    def read(ref, cell):
        return ref[cell * height : cell * height + height, :]

    def cell(x, y, slot):
        a = x - 1
        if y in (1, 2):
            return read(own, a * 4 + (y - 1) * 2 + slot) if slot < 2 else read(depth_halo, a * 2 + y - 1)
        if len(sides) == 4:
            before, after, diag_before, diag_after = sides
            if slot < 2:
                return read(before if y == 0 else after, a * 2 + slot)
            return read(diag_before if y == 0 else diag_after, a)
        side, diag = sides
        b = 1 if y == 0 else 0
        return read(side, a * 4 + b * 2 + slot) if slot < 2 else read(diag, a * 2 + b)

    return cell


def down_reader(refs, height):
    even = lax.rem(lax.axis_index("down"), 2) == 0
    swapped = lax.axis_size("down") % 2 == 0

    def cell(x, y, slot):
        if y in (1, 2):
            place = (y - 1) * 2 + slot if slot < 2 else 4 + y - 1
        else:
            side = 0 if y == 0 else 1
            place = 6 + side * 2 + slot if slot < 2 else 10 + side
        one, two = (ref[place * height : place * height + height, :] for ref in refs)
        if swapped:
            return jnp.where(even, two, one) if x == 0 else jnp.where(even, one, two)
        return one if x == 0 else two

    return cell


def centre_of(x, y, slot, depth):
    side = 0.5 - depth.astype(F32)
    return (x - 1.5, y - 1.5, (-1.0, 1.0, 3.0)[slot] * side)


def extended_cells(xs, depth):
    for k, x in enumerate(xs):
        for y in range(4):
            for slot in range(3):
                yield x, y, slot, ((k * 4 + y) * 3 + slot) * 8, centre_of(x, y, slot, depth)


def stepped_state(old, speed, centre):
    rows = row_ids((3, S))
    shift = jnp.where(rows == 0, centre[0], jnp.where(rows == 1, centre[1], centre[2]))
    return (old[0:3] + TIME_STEP * speed[0:3]) + shift, speed[0:3], old[6:8]


def contact_scratch(width):
    return [
        pltpu.VMEM((24 * 8, S), F32),
        pltpu.VMEM((8 * 8, S), F32),
        pltpu.VMEM((8 * 24, S), jnp.int32),
        pltpu.VMEM((8 * 24, S), jnp.int32),
        pltpu.VMEM((8 * 24, S), jnp.int32),
        pltpu.VMEM((8 * 24, S), jnp.int32),
        pltpu.VMEM((8, 18 * S, 8), F32),
        pltpu.VMEM((width * 8 * 8, S), F32),
    ]


def contact_sums(xs, width, scratch):
    local_ref, mine_ref, index_ref, base_ref, amount_ref, chosen_ref, list_ref, sum_ref = scratch
    together = xs[1] - xs[0] == 1
    span = 24 if together else 16

    def first_row(a):
        return 0 if together or a == 0 else 8

    def beside(a, b, z):
        return [
            (k * 4 + y) * 3 + slot
            for k, x in enumerate(xs)
            if abs(x - 1 - a) <= 1
            for y in range(b, b + 3)
            for slot in range(3 if z == 1 else 2)
        ]

    sum_ref[...] = jnp.zeros((width * 64, S), F32)
    place = [local_ref[pl.ds(k, 24, stride=8), :] for k in range(3)]
    radius = local_ref[pl.ds(6, 24, stride=8), :]
    rows = row_ids((24, S))
    row_x = jnp.where(rows < 12, xs[0], xs[1])
    row_y, row_slot = (rows // 3) % 4, rows % 3
    masks = []
    for c, (a, b, z) in enumerate(CELLS):
        mine = mine_ref[c * 8 : c * 8 + 8, :]
        live = mine[6:7] > 0.0
        low = jnp.min(jnp.where(live, mine, 1e9), axis=1, keepdims=True)
        high = jnp.max(jnp.where(live, mine, -1e9), axis=1, keepdims=True)
        part = slice(first_row(a), first_row(a) + span)
        reach = radius[part] + high[6:7]
        near = jnp.logical_and(row_y[part] >= b, row_y[part] <= b + 2)
        if not together:
            near = jnp.logical_and(near, row_x[part] == xs[a])
        if z == 0:
            near = jnp.logical_and(near, row_slot[part] < 2)
        for k in range(3):
            near = jnp.logical_and(near, place[k][part] + reach > low[k : k + 1])
            near = jnp.logical_and(near, place[k][part] - reach < high[k : k + 1])
        masks.append(jnp.where(near, 1.0, 0.0).astype(F32))
    mask = jnp.concatenate(masks, axis=0).astype(BF16)
    upper = one_hot(row_ids((S, 2 * S)) <= lane_ids((S, 2 * S)))
    sums = matmul(mask, upper)
    prefix, amount = sums[:, :S], sums[:, S:]
    before = one_hot(lane_ids((span, span)) < row_ids((span, span)))
    total = None
    for c in range(8):
        part = amount[c * span : (c + 1) * span]
        base = matmul(before, part.astype(BF16))
        base_ref[c * span : (c + 1) * span, :] = base.astype(jnp.int32)
        count = base[span - 1 : span] + part[span - 1 : span]
        total = count if total is None else jnp.maximum(total, count)
    most = total.astype(jnp.int32)[0, 0]
    amount_ref[0 : 8 * span, :] = amount.astype(jnp.int32)
    wanted = lane_ids((8 * span, S)).astype(F32)
    index = jnp.zeros((8 * span, S), jnp.int32)
    for step in (64, 32, 16, 8, 4, 2, 1):
        probe = lane_gather(prefix, index + (step - 1))
        index = jnp.where(probe <= wanted, index + step, index)
    index_ref[0 : 8 * span, :] = index
    empty = jnp.where(row_ids((8, S)) == 6, DEAD, 0.0).astype(F32)

    def gather_tiles(t, carry):
        want = t * S + lane_ids((8 * span, S)) - base_ref[0 : 8 * span, :]
        valid = jnp.logical_and(want >= 0, want < amount_ref[0 : 8 * span, :])
        source = lane_gather(index_ref[0 : 8 * span, :], jnp.clip(want, 0, S - 1))
        chosen_ref[0 : 8 * span, :] = jnp.where(valid, source, -1)
        for c, (a, b, z) in enumerate(CELLS):
            tile = empty
            for n in beside(a, b, z):
                row = c * span + n - first_row(a)
                pick = jnp.broadcast_to(chosen_ref[row : row + 1, :], (8, S))
                values = lane_gather(local_ref[n * 8 : n * 8 + 8, :], jnp.maximum(pick, 0))
                tile = jnp.where(pick >= 0, values, tile)
            list_ref[c, pl.ds(pl.multiple_of(t * S, S), S), :] = jnp.transpose(tile)
        return carry

    gather_tiles(0, 0)
    lax.fori_loop(1, (most + (S - 1)) // S, gather_tiles, 0)

    def pair_step(step, carry):
        for c in range(8):
            listed = list_ref[c, pl.ds(pl.multiple_of(step * 32, 32), 32), :]
            me = [jnp.broadcast_to(mine_ref[c * 8 + k : c * 8 + k + 1, :], (8, S)) for k in range(7)]
            added = [None] * width
            for block in range(4):
                other = [
                    jnp.broadcast_to(listed[block * 8 : block * 8 + 8, k : k + 1], (8, S))
                    for k in range(7)
                ]
                r = [me[k] - other[k] for k in range(3)]
                u = [me[3 + k] - other[3 + k] for k in range(3)]
                squared = r[0] * r[0] + r[1] * r[1] + r[2] * r[2] + SOFTENING
                inverse = lax.rsqrt(squared)
                along = u[0] * r[0] + u[1] * r[1] + u[2] * r[2]
                overlap = jnp.maximum((me[6] + other[6]) * inverse - 1.0, 0.0)
                weight = overlap * (STIFFNESS - (DAMPING * along) * inverse)
                terms = [weight * r[k] for k in range(3)]
                if width == 9:
                    terms += [terms[left] * r[right] for left, right in PAIR_LIST]
                added = [
                    term if total is None else total + term for total, term in zip(added, terms)
                ]
            for k in range(width):
                row = (k * 8 + c) * 8
                sum_ref[row : row + 8, :] += added[k]
        return carry

    lax.fori_loop(0, (most + 31) // 32, pair_step, 0)
    out = []
    for k in range(width):
        parts = [sum_ref[pl.ds(k * 64 + sub, 8, stride=8), :] for sub in range(8)]
        while len(parts) > 1:
            parts = [parts[i] + parts[i + 1] for i in range(0, len(parts), 2)]
        out.append(parts[0])
    return jnp.concatenate(out, axis=0)


def mass_of(radius):
    scaled = radius / RADIUS_REF
    return scaled * scaled * scaled


def step_inside(*refs):
    pieces, sums_out, scratch = refs[:-9], refs[-9], refs[-8:]
    depth = lax.axis_index("depth")
    cell = plane_reader(pieces, 8)
    for x, y, slot, start, centre in extended_cells((1, 2), depth):
        scratch[0][start : start + 8, :] = local_state(cell(x, y, slot), centre)
    for c, (a, b, z) in enumerate(CELLS):
        start = ((a * 4 + b + 1) * 3 + z) * 8
        scratch[1][c * 8 : c * 8 + 8, :] = scratch[0][start : start + 8, :]
    sums_out[...] = contact_sums((1, 2), 3, scratch)


def step_outside(own, sums_in, near, far, own_out, inner_out, *scratch):
    depth = lax.axis_index("depth")
    cell = down_reader((near, far), 8)
    for x, y, slot, start, centre in extended_cells((0, 3), depth):
        scratch[0][start : start + 8, :] = local_state(cell(x, y, slot), centre)
    for c, (a, b, z) in enumerate(CELLS):
        scratch[1][c * 8 : c * 8 + 8, :] = local_state(
            own[c * 8 : c * 8 + 8, :], centre_of(a + 1, b + 1, z, depth)
        )
    sums = sums_in[...] + contact_sums((0, 3), 3, scratch)
    radius = own[pl.ds(6, 8, stride=8), :]
    safe_mass = jnp.where(radius > 0.0, mass_of(radius), 1.0)
    for k in range(3):
        velocity = own[pl.ds(3 + k, 8, stride=8), :] + TIME_STEP * sums[k * 8 : k * 8 + 8] / safe_mass
        for c in range(8):
            own_out[c * 4 + k : c * 4 + k + 1, :] = velocity[c : c + 1]
    for c in range(8):
        own_out[c * 4 + 3 : c * 4 + 4, :] = jnp.zeros((1, S), F32)
    for column in range(4):
        inner_out[column * 4 : column * 4 + 4, :] = own_out[column * 8 + 4 : column * 8 + 8, :]


def place_state(ref, start, state):
    ref[start : start + 3, :] = state[0]
    ref[start + 3 : start + 6, :] = state[1]
    ref[start + 6 : start + 8, :] = state[2]


def field_inside(*refs):
    count = (len(refs) - 9) // 2
    pieces, speeds, sums_out, scratch = refs[:count], refs[count : 2 * count], refs[-9], refs[-8:]
    depth = lax.axis_index("depth")
    cell, speed = plane_reader(pieces, 8), plane_reader(speeds, 4)
    for x, y, slot, start, centre in extended_cells((1, 2), depth):
        place_state(scratch[0], start, stepped_state(cell(x, y, slot), speed(x, y, slot), centre))
    for c, (a, b, z) in enumerate(CELLS):
        start = ((a * 4 + b + 1) * 3 + z) * 8
        scratch[1][c * 8 : c * 8 + 8, :] = scratch[0][start : start + 8, :]
    sums_out[...] = contact_sums((1, 2), 9, scratch)


def field_outside(
    grid, own, own_speed, sums_in, near_old, far_old, near_speed, far_speed, force_out, node_out, moment_ref, *scratch
):
    depth = lax.axis_index("depth")
    down = lax.axis_index("down")
    cross = lax.axis_index("cross")
    mine_ref = scratch[1]
    cell, speed = down_reader((near_old, far_old), 8), down_reader((near_speed, far_speed), 4)
    for x, y, slot, start, centre in extended_cells((0, 3), depth):
        place_state(scratch[0], start, stepped_state(cell(x, y, slot), speed(x, y, slot), centre))
    for c, (a, b, z) in enumerate(CELLS):
        state = stepped_state(
            own[c * 8 : c * 8 + 8, :],
            own_speed[c * 4 : c * 4 + 4, :],
            centre_of(a + 1, b + 1, z, depth),
        )
        place_state(mine_ref, c * 8, state)
    sums = sums_in[...] + contact_sums((0, 3), 9, scratch)
    force_out[...] = sums[0:24]
    radius = own[pl.ds(6, 8, stride=8), :]
    mass = jnp.where(radius > 0.0, mass_of(radius), 0.0)
    moments = [mass] + [mass * own_speed[pl.ds(k, 8, stride=4), :] for k in range(3)]
    moments += [0.5 * sums[k * 8 : k * 8 + 8] for k in range(3, 9)]
    moment_ref[...] = jnp.zeros((16, 8 * S), F32)
    for m, moment in enumerate(moments):
        for c in range(8):
            moment_ref[m : m + 1, c * S : (c + 1) * S] = moment[c : c + 1]
    rows = row_ids((64, S))
    near_x, near_y, near_z = rows // 16 - 1, (rows // 4) % 4 - 1, rows % 4 - 1
    centres = [index.astype(F32) - 0.5 for index in (near_x, near_y, near_z)]
    kernels = []
    for c, (a, b, z) in enumerate(CELLS):
        squared = jnp.zeros((64, S), F32)
        for k in range(3):
            gap = mine_ref[c * 8 + k : c * 8 + k + 1, :] - centres[k]
            squared = squared + gap * gap
        kernel = jnp.exp(squared * (-0.5 / (KERNEL_WIDTH * KERNEL_WIDTH))) / KERNEL_NORM
        beside = jnp.logical_and(
            jnp.logical_and(jnp.abs(near_x - a) <= 1, jnp.abs(near_y - b) <= 1),
            jnp.abs(near_z - jnp.where(depth == z, 0, 1)) <= 1,
        )
        kernels.append(jnp.where(beside, kernel, 0.0))
    kernel_high, kernel_low = split(jnp.concatenate(kernels, axis=1))
    moment_high, moment_low = split(moment_ref[...])
    wide_part = matmul_turned(
        jnp.concatenate([moment_high, moment_low.astype(BF16)], axis=0), kernel_high
    )
    near = wide_part[0:16] + wide_part[16:32] + matmul_turned(moment_high, kernel_low.astype(BF16))
    size_x, size_y, size_z = grid
    nodes = size_x * size_y * size_z
    lanes = lane_ids((64, nodes))
    row = row_ids((64, nodes))
    target_x = (down * 2 + row // 16 - 1 + size_x) % size_x
    target_y = (cross * 2 + (row // 4) % 4 - 1 + size_y) % size_y
    target_z = depth * 2 + row % 4 - 1
    inside = jnp.logical_and(target_z >= 0, target_z < size_z)
    target = (target_x * size_y + target_y) * size_z + target_z
    chosen = one_hot(jnp.logical_and(inside, lanes == target))
    near_high, rest = split(near)
    near_middle, near_low = split(rest)
    placed = matmul(
        jnp.concatenate([near_high, near_middle, near_low.astype(BF16)], axis=0), chosen
    )
    node_out[...] = placed[0:16] + placed[16:32] + placed[32:48]


def library_kernel(
    grid, coefficients, mine, other, speed, force, velocity_out, force_out, residual_out, gram_out, moment_out, terms
):
    flat = lax.axis_index("depth") == 0
    for k in range(3):
        for a in range(2):
            for b in range(2):
                c = a * 4 + b * 2
                layers = [speed[(c + z) * 4 + k : (c + z) * 4 + k + 1, :] for z in range(2)]
                pulls = [force[k * 8 + c + z : k * 8 + c + z + 1, :] for z in range(2)]
                for z in range(2):
                    velocity_out[k, a, b, z : z + 1, :] = jnp.where(flat, layers[z], layers[1 - z])
                    force_out[k, a, b, z : z + 1, :] = jnp.where(flat, pulls[z], pulls[1 - z])
    fields = mine[...] + other[...]
    size_x, size_y, size_z = grid
    nodes = size_x * size_y * size_z
    lanes = lax.broadcasted_iota(jnp.int32, (1, nodes), 1)
    node_x = lanes // (size_y * size_z)
    node_y = (lanes // size_z) % size_y
    node_z = lanes % size_z
    rows = row_ids((8, nodes))
    density = fields[0:1]
    values = jnp.where(rows == 0, fields[0:8], fields[0:8] / (density + MASS_SHIFT))

    def moved(value, step):
        return pltpu.roll(value, step % nodes, 1)

    plane = size_y * size_z
    slope_x = (moved(values, -plane) - moved(values, plane)) * 0.5
    after_y = jnp.where(
        node_y == size_y - 1, moved(values, (size_y - 1) * size_z), moved(values, -size_z)
    )
    before_y = jnp.where(
        node_y == 0, moved(values, -(size_y - 1) * size_z), moved(values, size_z)
    )
    slope_y = (after_y - before_y) * 0.5
    after_z = jnp.where(node_z == size_z - 1, 0.0, moved(values, -1))
    before_z = jnp.where(node_z == 0, 0.0, moved(values, 1))
    slope_z = (after_z - before_z) * 0.5
    slopes = [[table[k : k + 1] for k in range(4)] for table in (slope_x, slope_y, slope_z)]
    strain = [
        [0.5 * (slopes[left][1 + right] + slopes[right][1 + left]) for right in range(3)]
        for left in range(3)
    ]
    divergence = strain[0][0] + strain[1][1] + strain[2][2]
    rate_sum = jnp.zeros_like(density)
    for left in range(3):
        for right in range(3):
            entry = strain[left][right]
            if left == right:
                entry = entry - divergence / 3.0
            rate_sum = rate_sum + entry * entry
    shear_rate = jnp.sqrt(2.0 * rate_sum + 0.01)
    stress = [fields[4 + k : 5 + k] for k in range(6)]
    pressure = (stress[0] + stress[3] + stress[5]) / 3.0
    deviator = (
        (stress[0] - pressure) ** 2
        + (stress[3] - pressure) ** 2
        + (stress[5] - pressure) ** 2
        + 2.0 * (stress[1] ** 2 + stress[2] ** 2 + stress[4] ** 2)
    )
    shear_stress = jnp.sqrt(0.5 * deviator + 0.01)
    pressure_scale = jnp.sqrt(pressure * pressure + 1.0)
    friction = shear_stress / pressure_scale
    features = [
        density,
        pressure / pressure_scale,
        shear_rate,
        shear_rate / jnp.sqrt(pressure_scale),
        divergence,
        slopes[0][0],
        slopes[1][0],
        slopes[2][0],
    ]
    entries = list(features)
    for left in range(8):
        for right in range(left, 8):
            entries.append(features[left] * features[right])
    for left in range(1, 5):
        entries.append(features[left] * features[left] * features[left])
    model = jnp.zeros_like(density)
    for k, entry in enumerate(entries):
        terms[k : k + 1, :] = entry
        model = model + coefficients[k] * entry
    residual = friction - model
    table = terms[...]
    gram_out[...] = (
        lax.dot_general(
            table,
            table,
            (((1,), (1,)), ((), ())),
            precision=lax.Precision.HIGHEST,
            preferred_element_type=F32,
        )
        / nodes
    )
    moment = lax.dot_general(
        jnp.broadcast_to(friction, (8, nodes)),
        table,
        (((1,), (1,)), ((), ())),
        precision=lax.Precision.HIGHEST,
        preferred_element_type=F32,
    )
    moment_out[...] = moment[0:1] / nodes
    down = lax.axis_index("down")
    cross = lax.axis_index("cross")
    depth = lax.axis_index("depth")
    b_rows = lax.broadcasted_iota(jnp.int32, (2, 1), 0)
    z_lanes = lax.broadcasted_iota(jnp.int32, (2, 2), 1)
    for a in range(2):
        mine = jnp.logical_and(node_x == down * 2 + a, node_y == cross * 2 + b_rows)
        column = [
            jnp.sum(
                jnp.where(jnp.logical_and(mine, node_z == depth * 2 + z), residual, 0.0),
                axis=1,
                keepdims=True,
            )
            for z in range(2)
        ]
        residual_out[a] = jnp.where(z_lanes == 0, column[0], column[1])


def ring(axis, step):
    peers = lax.axis_size(axis)
    return [(i, (i + step) % peers) for i in range(peers)]


def exchange(own, inner, height):
    cross = lax.axis_size("cross")

    def cells(block, first, count):
        return block[first * height : (first + count) * height]

    depth_halo = lax.ppermute(inner, "depth", [(0, 1), (1, 0)])
    if cross == 2:
        side = lax.ppermute(own, "cross", [(0, 1), (1, 0)])
        diag = lax.ppermute(inner, ("cross", "depth"), [(i, 3 - i) for i in range(4)])
        sides = [side, diag]

        def lateral(x):
            return [
                cells(side, x * 4 + 2, 2),
                cells(side, x * 4, 2),
                cells(diag, x * 2 + 1, 1),
                cells(diag, x * 2, 1),
            ]

    else:
        pairs = [(i * 2 + j, ((i + 1) % cross) * 2 + 1 - j) for i in range(cross) for j in range(2)]
        back = [(i * 2 + j, ((i - 1) % cross) * 2 + 1 - j) for i in range(cross) for j in range(2)]
        last = jnp.concatenate([cells(own, 2, 2), cells(own, 6, 2)], axis=0)
        first = jnp.concatenate([cells(own, 0, 2), cells(own, 4, 2)], axis=0)
        last_inner = jnp.concatenate([cells(inner, 1, 1), cells(inner, 3, 1)], axis=0)
        first_inner = jnp.concatenate([cells(inner, 0, 1), cells(inner, 2, 1)], axis=0)
        before = lax.ppermute(last, "cross", ring("cross", 1))
        after = lax.ppermute(first, "cross", ring("cross", -1))
        diag_before = lax.ppermute(last_inner, ("cross", "depth"), pairs)
        diag_after = lax.ppermute(first_inner, ("cross", "depth"), back)
        sides = [before, after, diag_before, diag_after]

        def lateral(x):
            return [
                cells(before, x * 2, 2),
                cells(after, x * 2, 2),
                cells(diag_before, x, 1),
                cells(diag_after, x, 1),
            ]

    def face(x):
        return jnp.concatenate([cells(own, x * 4, 4), cells(depth_halo, x * 2, 2)] + lateral(x), axis=0)

    downs = lax.axis_size("down")
    last, first = face(1), face(0)
    if downs % 2 == 0:
        even = lax.rem(lax.axis_index("down"), 2) == 0
        near = [(i, i ^ 1) for i in range(downs)]
        far = [(i, (i - 1 + 2 * (i % 2)) % downs) for i in range(downs)]
        outside = [
            lax.ppermute(jnp.where(even, last, first), "down", near),
            lax.ppermute(jnp.where(even, first, last), "down", far),
        ]
    else:
        outside = [
            lax.ppermute(last, "down", ring("down", 1)),
            lax.ppermute(first, "down", ring("down", -1)),
        ]
    return [own, depth_halo] + sides, outside


def shared(value, axes, peers):
    return [value] + [
        lax.ppermute(value, axes, [(i, i ^ k) for i in range(peers)]) for k in range(1, peers)
    ]


def tree_sum(parts):
    while len(parts) > 1:
        parts = [parts[k] + parts[k + 1] for k in range(0, len(parts), 2)]
    return parts[0]


def body(positions, velocities, sphere_radii, counts, coefficients):
    down, cross, depth = (lax.axis_size(name) for name in ("down", "cross", "depth"))
    grid = (2 * down, 2 * cross, 2 * depth)
    nodes = grid[0] * grid[1] * grid[2]
    params = pltpu.CompilerParams(vmem_limit_bytes=VMEM_LIMIT)
    vector_shape = jax.ShapeDtypeStruct((3, 2, 2, 2, S), F32)

    def rows(count):
        return jax.ShapeDtypeStruct((count, S), F32)

    def call(kernel, inputs, outputs, scratch, name, vectors=0):
        return pl.pallas_call(
            kernel,
            out_shape=outputs,
            in_specs=[VMEM_SPEC] * len(inputs),
            out_specs=jax.tree.map(lambda _: VMEM_SPEC, outputs),
            scratch_shapes=scratch,
            compiler_params=params,
            cost_estimate=pl.CostEstimate(flops=vectors, bytes_accessed=1 << 20, transcendentals=0),
            name=name,
        )(*inputs)

    own, inner = pl.pallas_call(
        pack_kernel,
        out_shape=(rows(64), rows(32)),
        in_specs=[pl.BlockSpec(memory_space=pl.ANY)] * 4,
        out_specs=(VMEM_SPEC, VMEM_SPEC),
        scratch_shapes=[
            pltpu.SMEM((2, 2, 2), jnp.int32),
            pltpu.VMEM((3, 2, 2, 2, S), F32),
            pltpu.VMEM((3, 2, 2, 2, S), F32),
            pltpu.VMEM((2, 2, 2, S), F32),
            pltpu.SemaphoreType.DMA((4,)),
        ],
        compiler_params=pltpu.CompilerParams(vmem_limit_bytes=60 * 1024 * 1024),
        name="pack",
    )(counts, positions, velocities, sphere_radii)
    inside, outside = exchange(own, inner, 8)
    sums = call(step_inside, inside, rows(24), contact_scratch(3), "step_inside", 1 << 31)
    own_speed, inner_speed = call(
        step_outside, [own, sums] + outside, (rows(32), rows(16)), contact_scratch(3), "step_outside", 1 << 30
    )
    inside_speed, outside_speed = exchange(own_speed, inner_speed, 4)
    sums = call(
        field_inside, inside + inside_speed, rows(72), contact_scratch(9), "field_inside", 1 << 31
    )
    force, partial = call(
        functools.partial(field_outside, grid),
        [own, own_speed, sums] + outside + outside_speed,
        (rows(24), jax.ShapeDtypeStruct((16, nodes), F32)),
        [pltpu.VMEM((16, 8 * S), F32)] + contact_scratch(9),
        "field_outside",
        1 << 30,
    )
    partial = tree_sum(shared(partial, ("cross", "depth"), cross * depth))
    distance = 1
    while distance < down:
        other = lax.ppermute(partial, "down", [(i, i ^ distance) for i in range(down)])
        distance = distance * 2
        if distance < down:
            partial = partial + other
    velocity_new, force_next, residual_field, gram_matrix, moment = pl.pallas_call(
        functools.partial(library_kernel, grid),
        out_shape=(
            vector_shape,
            vector_shape,
            jax.ShapeDtypeStruct((2, 2, 2), F32),
            jax.ShapeDtypeStruct((TERMS, TERMS), F32),
            jax.ShapeDtypeStruct((1, TERMS), F32),
        ),
        in_specs=[SMEM_SPEC] + [VMEM_SPEC] * 4,
        out_specs=(VMEM_SPEC,) * 5,
        scratch_shapes=[pltpu.VMEM((TERMS, nodes), F32)],
        compiler_params=params,
        name="library",
    )(coefficients, partial, other, own_speed, force)
    return (velocity_new, force_next, residual_field, gram_matrix, moment.reshape(TERMS))


def solution(mesh):
    return jax.shard_map(
        body,
        mesh=mesh,
        in_specs=(
            P(None, ("groups", "down"), "cross", "depth", None),
            P(None, ("groups", "down"), "cross", "depth", None),
            P(("groups", "down"), "cross", "depth", None),
            P(("groups", "down"), "cross", "depth"),
            P(),
        ),
        out_specs=(
            P(None, ("groups", "down"), "cross", "depth", None),
            P(None, ("groups", "down"), "cross", "depth", None),
            P(("groups", "down"), "cross", "depth"),
            P("groups", None),
            P("groups"),
        ),
        check_vma=False,
    )
```

```python
import functools

import jax
import jax.numpy as jnp
from jax import lax
from jax.experimental import pallas as pl
from jax.experimental.pallas import tpu as pltpu
from jax.sharding import PartitionSpec as P

STIFFNESS = 100.0
DAMPING = 20.0
TIME_STEP = 0.05
KERNEL_WIDTH = 0.4
KERNEL_NORM = 64.0
SOFTENING = 0.0001
RADIUS_REF = 0.1
MASS_SHIFT = 0.1
DEAD = -1000.0
TERMS = 48
S = 128
SPREAD = 4
F32 = jnp.float32
BF16 = jnp.bfloat16
CELLS = tuple((a, b, z) for a in range(2) for b in range(2) for z in range(2))
PAIR_LIST = ((0, 0), (0, 1), (0, 2), (1, 1), (1, 2), (2, 2))
VMEM_SPEC = pl.BlockSpec(memory_space=pltpu.VMEM)
SMEM_SPEC = pl.BlockSpec(memory_space=pltpu.SMEM)
VMEM_LIMIT = 48 * 1024 * 1024


def row_ids(shape):
    return lax.broadcasted_iota(jnp.int32, shape, 0)


def lane_ids(shape):
    return lax.broadcasted_iota(jnp.int32, shape, 1)


def one_hot(condition):
    return jnp.where(condition, 1.0, 0.0).astype(BF16)


def split(value):
    high = value.astype(BF16)
    return high, value - high.astype(F32)


def matmul(left, right):
    return lax.dot_general(left, right, (((1,), (0,)), ((), ())), preferred_element_type=F32)


def matmul_turned(left, right):
    return lax.dot_general(left, right, (((1,), (1,)), ((), ())), preferred_element_type=F32)


def lane_gather(table, index):
    return jnp.take_along_axis(table, index, axis=1)


def pack_kernel(
    counts_hbm, positions_hbm, velocities_hbm, radii_hbm, own, inner, counts, positions, velocities, radii, arrived
):
    copies = [
        pltpu.make_async_copy(source, target, arrived.at[k])
        for k, (source, target) in enumerate(
            (
                (counts_hbm, counts),
                (positions_hbm, positions),
                (velocities_hbm, velocities),
                (radii_hbm, radii),
            )
        )
    ]
    for copy in copies:
        copy.start()
    for copy in copies:
        copy.wait()
    depth = lax.axis_index("depth")
    lanes = lane_ids((1, S))

    def layer(ref, at, z):
        rows = ref[at]
        return jnp.where(depth == z, rows[0:1], rows[1:2])

    for c, (a, b, z) in enumerate(CELLS):
        for k in range(3):
            own[c * 8 + k : c * 8 + k + 1, :] = layer(positions, (k, a, b), z)
            own[c * 8 + 3 + k : c * 8 + 4 + k, :] = layer(velocities, (k, a, b), z)
        count = jnp.where(depth == z, counts[a, b, 0], counts[a, b, 1])
        own[c * 8 + 6 : c * 8 + 7, :] = jnp.where(lanes < count, layer(radii, (a, b), z), DEAD)
        own[c * 8 + 7 : c * 8 + 8, :] = jnp.zeros((1, S), F32)
    for column in range(4):
        inner[column * 8 : column * 8 + 8, :] = own[column * 16 + 8 : column * 16 + 16, :]


def local_state(raw, centre):
    rows = row_ids(raw.shape)
    shift = jnp.where(rows == 0, centre[0], jnp.where(rows == 1, centre[1], centre[2]))
    return jnp.where(rows < 3, raw + shift, raw)


def plane_reader(refs, height):
    own, depth_halo, sides = refs[0], refs[1], refs[2:]

    def read(ref, cell):
        return ref[cell * height : cell * height + height, :]

    def cell(x, y, slot):
        a = x - 1
        if y in (1, 2):
            return read(own, a * 4 + (y - 1) * 2 + slot) if slot < 2 else read(depth_halo, a * 2 + y - 1)
        if len(sides) == 4:
            before, after, diag_before, diag_after = sides
            if slot < 2:
                return read(before if y == 0 else after, a * 2 + slot)
            return read(diag_before if y == 0 else diag_after, a)
        b = 1 if y == 0 else 0
        return read(sides[0], a * 4 + b * 2 + slot if slot < 2 else 8 + a * 2 + b)

    return cell


def down_reader(refs, height):
    even = lax.rem(lax.axis_index("down"), 2) == 0
    swapped = lax.axis_size("down") % 2 == 0

    def cell(x, y, slot):
        if y in (1, 2):
            place = (y - 1) * 2 + slot if slot < 2 else 4 + y - 1
        else:
            side = 0 if y == 0 else 1
            place = 6 + side * 2 + slot if slot < 2 else 10 + side
        one, two = (ref[place * height : place * height + height, :] for ref in refs)
        if swapped:
            return jnp.where(even, two, one) if x == 0 else jnp.where(even, one, two)
        return one if x == 0 else two

    return cell


def centre_of(x, y, slot, depth):
    side = 0.5 - depth.astype(F32)
    return (x - 1.5, y - 1.5, (-1.0, 1.0, 3.0)[slot] * side)


def extended_cells(xs, depth):
    for k, x in enumerate(xs):
        for y in range(4):
            for slot in range(3):
                yield x, y, slot, ((k * 4 + y) * 3 + slot) * 8, centre_of(x, y, slot, depth)


def stepped_state(old, speed, centre):
    rows = row_ids((3, S))
    shift = jnp.where(rows == 0, centre[0], jnp.where(rows == 1, centre[1], centre[2]))
    return (old[0:3] + TIME_STEP * speed[0:3]) + shift, speed[0:3], old[6:8]


def contact_scratch(width):
    return [
        pltpu.VMEM((24 * 8, S), F32),
        pltpu.VMEM((8 * 8, S), F32),
        pltpu.VMEM((8 * 24, S), jnp.int32),
        pltpu.VMEM((8 * 24, S), jnp.int32),
        pltpu.VMEM((8 * 24, S), jnp.int32),
        pltpu.VMEM((8 * 24, S), jnp.int32),
        pltpu.VMEM((18 * 8 * S, 32), F32),
        pltpu.VMEM((width * 8 * 8, S), F32),
    ]


def contact_sums(xs, width, scratch):
    local_ref, mine_ref, index_ref, base_ref, amount_ref, chosen_ref, list_ref, sum_ref = scratch
    together = xs[1] - xs[0] == 1
    span = 24 if together else 16

    def first_row(a):
        return 0 if together or a == 0 else 8

    def beside(a, b, z):
        return [
            (k * 4 + y) * 3 + slot
            for k, x in enumerate(xs)
            if abs(x - 1 - a) <= 1
            for y in range(b, b + 3)
            for slot in range(3 if z == 1 else 2)
        ]

    sum_ref[...] = jnp.zeros((width * 64, S), F32)
    place = [local_ref[pl.ds(k, 24, stride=8), :] for k in range(3)]
    radius = local_ref[pl.ds(6, 24, stride=8), :]
    rows = row_ids((24, S))
    row_x = jnp.where(rows < 12, xs[0], xs[1])
    row_y, row_slot = (rows // 3) % 4, rows % 3
    masks = []
    for c, (a, b, z) in enumerate(CELLS):
        mine = mine_ref[c * 8 : c * 8 + 8, :]
        live = mine[6:7] > 0.0
        low = jnp.min(jnp.where(live, mine, 1e9), axis=1, keepdims=True)
        high = jnp.max(jnp.where(live, mine, -1e9), axis=1, keepdims=True)
        part = slice(first_row(a), first_row(a) + span)
        reach = radius[part] + high[6:7]
        near = jnp.logical_and(row_y[part] >= b, row_y[part] <= b + 2)
        if not together:
            near = jnp.logical_and(near, row_x[part] == xs[a])
        if z == 0:
            near = jnp.logical_and(near, row_slot[part] < 2)
        for k in range(3):
            near = jnp.logical_and(near, place[k][part] + reach > low[k : k + 1])
            near = jnp.logical_and(near, place[k][part] - reach < high[k : k + 1])
        masks.append(jnp.where(near, 1.0, 0.0).astype(F32))
    mask = jnp.concatenate(masks, axis=0).astype(BF16)
    upper = one_hot(row_ids((S, 2 * S)) <= lane_ids((S, 2 * S)))
    sums = matmul(mask, upper)
    prefix, amount = sums[:, :S], sums[:, S:]
    before = one_hot(lane_ids((span, span)) < row_ids((span, span)))
    total = None
    for c in range(8):
        part = amount[c * span : (c + 1) * span]
        base = matmul(before, part.astype(BF16))
        base_ref[c * span : (c + 1) * span, :] = base.astype(jnp.int32)
        count = base[span - 1 : span] + part[span - 1 : span]
        total = count if total is None else jnp.maximum(total, count)
    most = total.astype(jnp.int32)[0, 0]
    amount_ref[0 : 8 * span, :] = amount.astype(jnp.int32)
    wanted = lane_ids((8 * span, S)).astype(F32)
    index = jnp.zeros((8 * span, S), jnp.int32)
    for step in (64, 32, 16, 8, 4, 2, 1):
        probe = lane_gather(prefix, index + (step - 1))
        index = jnp.where(probe <= wanted, index + step, index)
    index_ref[0 : 8 * span, :] = index
    empty = jnp.where(row_ids((8, S)) == 6, DEAD, 0.0).astype(F32)

    def gather_tiles(t, carry):
        want = t * S + lane_ids((8 * span, S)) - base_ref[0 : 8 * span, :]
        valid = jnp.logical_and(want >= 0, want < amount_ref[0 : 8 * span, :])
        source = lane_gather(index_ref[0 : 8 * span, :], jnp.clip(want, 0, S - 1))
        chosen_ref[0 : 8 * span, :] = jnp.where(valid, source, -1)
        for c, (a, b, z) in enumerate(CELLS):
            tile = empty
            for n in beside(a, b, z):
                row = c * span + n - first_row(a)
                pick = jnp.broadcast_to(chosen_ref[row : row + 1, :], (8, S))
                values = lane_gather(local_ref[n * 8 : n * 8 + 8, :], jnp.maximum(pick, 0))
                tile = jnp.where(pick >= 0, values, tile)
            high = tile.astype(BF16).astype(F32)
            rest = tile - high
            middle = rest.astype(BF16).astype(F32)
            turned = jnp.transpose(jnp.concatenate([high, middle, rest - middle, tile], axis=0))
            for part in range(4):
                start = pl.multiple_of(t * (8 * S) + (part * 8 + c) * 32, 32)
                list_ref[pl.ds(start, 32), :] = turned[part * 32 : part * 32 + 32]
        return carry

    gather_tiles(0, 0)
    lax.fori_loop(1, (most + (S - 1)) // S, gather_tiles, 0)

    selector = jnp.logical_and(
        row_ids((32, SPREAD * S)) % 8 == lane_ids((32, SPREAD * S)) // S, row_ids((32, SPREAD * S)) < 24
    )
    selector = one_hot(selector)

    def pair_step(step, carry):
        every = list_ref[pl.ds(pl.multiple_of(step * 256, 256), 256), :]
        spread = matmul(every.astype(BF16), selector)
        for c in range(8):
            listed = every[c * 32 : c * 32 + 32]
            me = [jnp.broadcast_to(mine_ref[c * 8 + k : c * 8 + k + 1, :], (8, S)) for k in range(7)]
            added = [None] * width
            for block in range(4):
                row = c * 32 + block * 8
                other = [spread[row : row + 8, k * S : (k + 1) * S] for k in range(SPREAD)]
                other += [
                    jnp.broadcast_to(listed[block * 8 : block * 8 + 8, 24 + k : 25 + k], (8, S))
                    for k in range(SPREAD, 7)
                ]
                r = [me[k] - other[k] for k in range(3)]
                u = [me[3 + k] - other[3 + k] for k in range(3)]
                squared = r[0] * r[0] + r[1] * r[1] + r[2] * r[2] + SOFTENING
                inverse = lax.rsqrt(squared)
                along = u[0] * r[0] + u[1] * r[1] + u[2] * r[2]
                overlap = jnp.maximum((me[6] + other[6]) * inverse - 1.0, 0.0)
                weight = overlap * (STIFFNESS - (DAMPING * along) * inverse)
                terms = [weight * r[k] for k in range(3)]
                if width == 9:
                    terms += [terms[left] * r[right] for left, right in PAIR_LIST]
                added = [
                    term if total is None else total + term for total, term in zip(added, terms)
                ]
            for k in range(width):
                row = (k * 8 + c) * 8
                sum_ref[row : row + 8, :] += added[k]
        return carry

    lax.fori_loop(0, (most + 31) // 32, pair_step, 0)
    out = []
    for k in range(width):
        parts = [sum_ref[pl.ds(k * 64 + sub, 8, stride=8), :] for sub in range(8)]
        while len(parts) > 1:
            parts = [parts[i] + parts[i + 1] for i in range(0, len(parts), 2)]
        out.append(parts[0])
    return jnp.concatenate(out, axis=0)


def mass_of(radius):
    scaled = radius / RADIUS_REF
    return scaled * scaled * scaled


def step_inside(*refs):
    pieces, sums_out, scratch = refs[:-9], refs[-9], refs[-8:]
    depth = lax.axis_index("depth")
    cell = plane_reader(pieces, 8)
    for x, y, slot, start, centre in extended_cells((1, 2), depth):
        scratch[0][start : start + 8, :] = local_state(cell(x, y, slot), centre)
    for c, (a, b, z) in enumerate(CELLS):
        start = ((a * 4 + b + 1) * 3 + z) * 8
        scratch[1][c * 8 : c * 8 + 8, :] = scratch[0][start : start + 8, :]
    sums_out[...] = contact_sums((1, 2), 3, scratch)


def step_outside(own, sums_in, near, far, own_out, inner_out, *scratch):
    depth = lax.axis_index("depth")
    cell = down_reader((near, far), 8)
    for x, y, slot, start, centre in extended_cells((0, 3), depth):
        scratch[0][start : start + 8, :] = local_state(cell(x, y, slot), centre)
    for c, (a, b, z) in enumerate(CELLS):
        scratch[1][c * 8 : c * 8 + 8, :] = local_state(
            own[c * 8 : c * 8 + 8, :], centre_of(a + 1, b + 1, z, depth)
        )
    sums = sums_in[...] + contact_sums((0, 3), 3, scratch)
    radius = own[pl.ds(6, 8, stride=8), :]
    safe_mass = jnp.where(radius > 0.0, mass_of(radius), 1.0)
    for k in range(3):
        velocity = own[pl.ds(3 + k, 8, stride=8), :] + TIME_STEP * sums[k * 8 : k * 8 + 8] / safe_mass
        for c in range(8):
            own_out[c * 4 + k : c * 4 + k + 1, :] = velocity[c : c + 1]
    for c in range(8):
        own_out[c * 4 + 3 : c * 4 + 4, :] = jnp.zeros((1, S), F32)
    for column in range(4):
        inner_out[column * 4 : column * 4 + 4, :] = own_out[column * 8 + 4 : column * 8 + 8, :]


def place_state(ref, start, state):
    ref[start : start + 3, :] = state[0]
    ref[start + 3 : start + 6, :] = state[1]
    ref[start + 6 : start + 8, :] = state[2]


def field_inside(*refs):
    count = (len(refs) - 9) // 2
    pieces, speeds, sums_out, scratch = refs[:count], refs[count : 2 * count], refs[-9], refs[-8:]
    depth = lax.axis_index("depth")
    cell, speed = plane_reader(pieces, 8), plane_reader(speeds, 4)
    for x, y, slot, start, centre in extended_cells((1, 2), depth):
        place_state(scratch[0], start, stepped_state(cell(x, y, slot), speed(x, y, slot), centre))
    for c, (a, b, z) in enumerate(CELLS):
        start = ((a * 4 + b + 1) * 3 + z) * 8
        scratch[1][c * 8 : c * 8 + 8, :] = scratch[0][start : start + 8, :]
    sums_out[...] = contact_sums((1, 2), 9, scratch)


def field_outside(
    grid, own, own_speed, sums_in, near_old, far_old, near_speed, far_speed, force_out, node_out, moment_ref, *scratch
):
    depth = lax.axis_index("depth")
    down = lax.axis_index("down")
    cross = lax.axis_index("cross")
    mine_ref = scratch[1]
    cell, speed = down_reader((near_old, far_old), 8), down_reader((near_speed, far_speed), 4)
    for x, y, slot, start, centre in extended_cells((0, 3), depth):
        place_state(scratch[0], start, stepped_state(cell(x, y, slot), speed(x, y, slot), centre))
    for c, (a, b, z) in enumerate(CELLS):
        state = stepped_state(
            own[c * 8 : c * 8 + 8, :],
            own_speed[c * 4 : c * 4 + 4, :],
            centre_of(a + 1, b + 1, z, depth),
        )
        place_state(mine_ref, c * 8, state)
    sums = sums_in[...] + contact_sums((0, 3), 9, scratch)
    force_out[...] = sums[0:24]
    radius = own[pl.ds(6, 8, stride=8), :]
    mass = jnp.where(radius > 0.0, mass_of(radius), 0.0)
    moments = [mass] + [mass * own_speed[pl.ds(k, 8, stride=4), :] for k in range(3)]
    moments += [0.5 * sums[k * 8 : k * 8 + 8] for k in range(3, 9)]
    moment_ref[...] = jnp.zeros((16, 8 * S), F32)
    for m, moment in enumerate(moments):
        for c in range(8):
            moment_ref[m : m + 1, c * S : (c + 1) * S] = moment[c : c + 1]
    rows = row_ids((64, S))
    near_x, near_y, near_z = rows // 16 - 1, (rows // 4) % 4 - 1, rows % 4 - 1
    centres = [index.astype(F32) - 0.5 for index in (near_x, near_y, near_z)]
    kernels = []
    for c, (a, b, z) in enumerate(CELLS):
        squared = jnp.zeros((64, S), F32)
        for k in range(3):
            gap = mine_ref[c * 8 + k : c * 8 + k + 1, :] - centres[k]
            squared = squared + gap * gap
        kernel = jnp.exp(squared * (-0.5 / (KERNEL_WIDTH * KERNEL_WIDTH))) / KERNEL_NORM
        beside = jnp.logical_and(
            jnp.logical_and(jnp.abs(near_x - a) <= 1, jnp.abs(near_y - b) <= 1),
            jnp.abs(near_z - jnp.where(depth == z, 0, 1)) <= 1,
        )
        kernels.append(jnp.where(beside, kernel, 0.0))
    kernel_high, kernel_low = split(jnp.concatenate(kernels, axis=1))
    moment_high, moment_low = split(moment_ref[...])
    wide_part = matmul_turned(
        jnp.concatenate([moment_high, moment_low.astype(BF16)], axis=0), kernel_high
    )
    near = wide_part[0:16] + wide_part[16:32] + matmul_turned(moment_high, kernel_low.astype(BF16))
    size_x, size_y, size_z = grid
    nodes = size_x * size_y * size_z
    lanes = lane_ids((64, nodes))
    row = row_ids((64, nodes))
    target_x = (down * 2 + row // 16 - 1 + size_x) % size_x
    target_y = (cross * 2 + (row // 4) % 4 - 1 + size_y) % size_y
    target_z = depth * 2 + row % 4 - 1
    inside = jnp.logical_and(target_z >= 0, target_z < size_z)
    target = (target_x * size_y + target_y) * size_z + target_z
    chosen = one_hot(jnp.logical_and(inside, lanes == target))
    near_high, rest = split(near)
    near_middle, near_low = split(rest)
    placed = matmul(
        jnp.concatenate([near_high, near_middle, near_low.astype(BF16)], axis=0), chosen
    )
    node_out[...] = placed[0:16] + placed[16:32] + placed[32:48]


def library_kernel(
    grid, coefficients, mine, other, speed, force, velocity_out, force_out, residual_out, gram_out, moment_out, terms
):
    flat = lax.axis_index("depth") == 0
    for k in range(3):
        for a in range(2):
            for b in range(2):
                c = a * 4 + b * 2
                layers = [speed[(c + z) * 4 + k : (c + z) * 4 + k + 1, :] for z in range(2)]
                pulls = [force[k * 8 + c + z : k * 8 + c + z + 1, :] for z in range(2)]
                for z in range(2):
                    velocity_out[k, a, b, z : z + 1, :] = jnp.where(flat, layers[z], layers[1 - z])
                    force_out[k, a, b, z : z + 1, :] = jnp.where(flat, pulls[z], pulls[1 - z])
    fields = mine[...] + other[...]
    size_x, size_y, size_z = grid
    nodes = size_x * size_y * size_z
    lanes = lax.broadcasted_iota(jnp.int32, (1, nodes), 1)
    node_x = lanes // (size_y * size_z)
    node_y = (lanes // size_z) % size_y
    node_z = lanes % size_z
    rows = row_ids((8, nodes))
    density = fields[0:1]
    values = jnp.where(rows == 0, fields[0:8], fields[0:8] / (density + MASS_SHIFT))

    def moved(value, step):
        return pltpu.roll(value, step % nodes, 1)

    plane = size_y * size_z
    slope_x = (moved(values, -plane) - moved(values, plane)) * 0.5
    after_y = jnp.where(
        node_y == size_y - 1, moved(values, (size_y - 1) * size_z), moved(values, -size_z)
    )
    before_y = jnp.where(
        node_y == 0, moved(values, -(size_y - 1) * size_z), moved(values, size_z)
    )
    slope_y = (after_y - before_y) * 0.5
    after_z = jnp.where(node_z == size_z - 1, 0.0, moved(values, -1))
    before_z = jnp.where(node_z == 0, 0.0, moved(values, 1))
    slope_z = (after_z - before_z) * 0.5
    slopes = [[table[k : k + 1] for k in range(4)] for table in (slope_x, slope_y, slope_z)]
    strain = [
        [0.5 * (slopes[left][1 + right] + slopes[right][1 + left]) for right in range(3)]
        for left in range(3)
    ]
    divergence = strain[0][0] + strain[1][1] + strain[2][2]
    rate_sum = jnp.zeros_like(density)
    for left in range(3):
        for right in range(3):
            entry = strain[left][right]
            if left == right:
                entry = entry - divergence / 3.0
            rate_sum = rate_sum + entry * entry
    shear_rate = jnp.sqrt(2.0 * rate_sum + 0.01)
    stress = [fields[4 + k : 5 + k] for k in range(6)]
    pressure = (stress[0] + stress[3] + stress[5]) / 3.0
    deviator = (
        (stress[0] - pressure) ** 2
        + (stress[3] - pressure) ** 2
        + (stress[5] - pressure) ** 2
        + 2.0 * (stress[1] ** 2 + stress[2] ** 2 + stress[4] ** 2)
    )
    shear_stress = jnp.sqrt(0.5 * deviator + 0.01)
    pressure_scale = jnp.sqrt(pressure * pressure + 1.0)
    friction = shear_stress / pressure_scale
    features = [
        density,
        pressure / pressure_scale,
        shear_rate,
        shear_rate / jnp.sqrt(pressure_scale),
        divergence,
        slopes[0][0],
        slopes[1][0],
        slopes[2][0],
    ]
    entries = list(features)
    for left in range(8):
        for right in range(left, 8):
            entries.append(features[left] * features[right])
    for left in range(1, 5):
        entries.append(features[left] * features[left] * features[left])
    model = jnp.zeros_like(density)
    for k, entry in enumerate(entries):
        terms[k : k + 1, :] = entry
        model = model + coefficients[k] * entry
    residual = friction - model
    table = terms[...]
    gram_out[...] = (
        lax.dot_general(
            table,
            table,
            (((1,), (1,)), ((), ())),
            precision=lax.Precision.HIGHEST,
            preferred_element_type=F32,
        )
        / nodes
    )
    moment = lax.dot_general(
        jnp.broadcast_to(friction, (8, nodes)),
        table,
        (((1,), (1,)), ((), ())),
        precision=lax.Precision.HIGHEST,
        preferred_element_type=F32,
    )
    moment_out[...] = moment[0:1] / nodes
    down = lax.axis_index("down")
    cross = lax.axis_index("cross")
    depth = lax.axis_index("depth")
    b_rows = lax.broadcasted_iota(jnp.int32, (2, 1), 0)
    z_lanes = lax.broadcasted_iota(jnp.int32, (2, 2), 1)
    for a in range(2):
        mine = jnp.logical_and(node_x == down * 2 + a, node_y == cross * 2 + b_rows)
        column = [
            jnp.sum(
                jnp.where(jnp.logical_and(mine, node_z == depth * 2 + z), residual, 0.0),
                axis=1,
                keepdims=True,
            )
            for z in range(2)
        ]
        residual_out[a] = jnp.where(z_lanes == 0, column[0], column[1])


def ring(axis, step):
    peers = lax.axis_size(axis)
    return [(i, (i + step) % peers) for i in range(peers)]


def exchange(own, inner, height):
    cross = lax.axis_size("cross")

    def cells(block, first, count):
        return block[first * height : (first + count) * height]

    depth_halo = lax.ppermute(inner, "depth", [(0, 1), (1, 0)])
    if cross == 2:
        side = lax.ppermute(
            jnp.concatenate([own, depth_halo], axis=0), "cross", [(0, 1), (1, 0)]
        )
        sides = [side]

        def lateral(x):
            return [
                cells(side, x * 4 + 2, 2),
                cells(side, x * 4, 2),
                cells(side, 8 + x * 2 + 1, 1),
                cells(side, 8 + x * 2, 1),
            ]

    else:
        pairs = [(i * 2 + j, ((i + 1) % cross) * 2 + 1 - j) for i in range(cross) for j in range(2)]
        back = [(i * 2 + j, ((i - 1) % cross) * 2 + 1 - j) for i in range(cross) for j in range(2)]
        last = jnp.concatenate([cells(own, 2, 2), cells(own, 6, 2)], axis=0)
        first = jnp.concatenate([cells(own, 0, 2), cells(own, 4, 2)], axis=0)
        last_inner = jnp.concatenate([cells(inner, 1, 1), cells(inner, 3, 1)], axis=0)
        first_inner = jnp.concatenate([cells(inner, 0, 1), cells(inner, 2, 1)], axis=0)
        before = lax.ppermute(last, "cross", ring("cross", 1))
        after = lax.ppermute(first, "cross", ring("cross", -1))
        diag_before = lax.ppermute(last_inner, ("cross", "depth"), pairs)
        diag_after = lax.ppermute(first_inner, ("cross", "depth"), back)
        sides = [before, after, diag_before, diag_after]

        def lateral(x):
            return [
                cells(before, x * 2, 2),
                cells(after, x * 2, 2),
                cells(diag_before, x, 1),
                cells(diag_after, x, 1),
            ]

    def face(x):
        return jnp.concatenate([cells(own, x * 4, 4), cells(depth_halo, x * 2, 2)] + lateral(x), axis=0)

    downs = lax.axis_size("down")
    last, first = face(1), face(0)
    if downs % 2 == 0:
        even = lax.rem(lax.axis_index("down"), 2) == 0
        near = [(i, i ^ 1) for i in range(downs)]
        far = [(i, (i - 1 + 2 * (i % 2)) % downs) for i in range(downs)]
        outside = [
            lax.ppermute(jnp.where(even, last, first), "down", near),
            lax.ppermute(jnp.where(even, first, last), "down", far),
        ]
    else:
        outside = [
            lax.ppermute(last, "down", ring("down", 1)),
            lax.ppermute(first, "down", ring("down", -1)),
        ]
    return [own, depth_halo] + sides, outside


def shared(value, axes, peers):
    return [value] + [
        lax.ppermute(value, axes, [(i, i ^ k) for i in range(peers)]) for k in range(1, peers)
    ]


def tree_sum(parts):
    while len(parts) > 1:
        parts = [parts[k] + parts[k + 1] for k in range(0, len(parts), 2)]
    return parts[0]


def body(positions, velocities, sphere_radii, counts, coefficients):
    down, cross, depth = (lax.axis_size(name) for name in ("down", "cross", "depth"))
    grid = (2 * down, 2 * cross, 2 * depth)
    nodes = grid[0] * grid[1] * grid[2]
    params = pltpu.CompilerParams(vmem_limit_bytes=VMEM_LIMIT)
    vector_shape = jax.ShapeDtypeStruct((3, 2, 2, 2, S), F32)

    def rows(count):
        return jax.ShapeDtypeStruct((count, S), F32)

    def call(kernel, inputs, outputs, scratch, name, vectors=0):
        return pl.pallas_call(
            kernel,
            out_shape=outputs,
            in_specs=[VMEM_SPEC] * len(inputs),
            out_specs=jax.tree.map(lambda _: VMEM_SPEC, outputs),
            scratch_shapes=scratch,
            compiler_params=params,
            cost_estimate=pl.CostEstimate(flops=vectors, bytes_accessed=1 << 20, transcendentals=0),
            name=name,
        )(*inputs)

    own, inner = pl.pallas_call(
        pack_kernel,
        out_shape=(rows(64), rows(32)),
        in_specs=[pl.BlockSpec(memory_space=pl.ANY)] * 4,
        out_specs=(VMEM_SPEC, VMEM_SPEC),
        scratch_shapes=[
            pltpu.SMEM((2, 2, 2), jnp.int32),
            pltpu.VMEM((3, 2, 2, 2, S), F32),
            pltpu.VMEM((3, 2, 2, 2, S), F32),
            pltpu.VMEM((2, 2, 2, S), F32),
            pltpu.SemaphoreType.DMA((4,)),
        ],
        compiler_params=pltpu.CompilerParams(vmem_limit_bytes=60 * 1024 * 1024),
        name="pack",
    )(counts, positions, velocities, sphere_radii)
    inside, outside = exchange(own, inner, 8)
    sums = call(step_inside, inside, rows(24), contact_scratch(3), "step_inside", 1 << 31)
    own_speed, inner_speed = call(
        step_outside, [own, sums] + outside, (rows(32), rows(16)), contact_scratch(3), "step_outside", 1 << 30
    )
    inside_speed, outside_speed = exchange(own_speed, inner_speed, 4)
    sums = call(
        field_inside, inside + inside_speed, rows(72), contact_scratch(9), "field_inside", 1 << 31
    )
    force, partial = call(
        functools.partial(field_outside, grid),
        [own, own_speed, sums] + outside + outside_speed,
        (rows(24), jax.ShapeDtypeStruct((16, nodes), F32)),
        [pltpu.VMEM((16, 8 * S), F32)] + contact_scratch(9),
        "field_outside",
        1 << 30,
    )
    for axis in ("depth", "cross"):
        partial = tree_sum(shared(partial, axis, lax.axis_size(axis)))
    distance = 1
    while distance < down:
        other = lax.ppermute(partial, "down", [(i, i ^ distance) for i in range(down)])
        distance = distance * 2
        if distance < down:
            partial = partial + other
    velocity_new, force_next, residual_field, gram_matrix, moment = pl.pallas_call(
        functools.partial(library_kernel, grid),
        out_shape=(
            vector_shape,
            vector_shape,
            jax.ShapeDtypeStruct((2, 2, 2), F32),
            jax.ShapeDtypeStruct((TERMS, TERMS), F32),
            jax.ShapeDtypeStruct((1, TERMS), F32),
        ),
        in_specs=[SMEM_SPEC] + [VMEM_SPEC] * 4,
        out_specs=(VMEM_SPEC,) * 5,
        scratch_shapes=[pltpu.VMEM((TERMS, nodes), F32)],
        compiler_params=params,
        name="library",
    )(coefficients, partial, other, own_speed, force)
    return (velocity_new, force_next, residual_field, gram_matrix, moment.reshape(TERMS))


def solution(mesh):
    return jax.shard_map(
        body,
        mesh=mesh,
        in_specs=(
            P(None, ("groups", "down"), "cross", "depth", None),
            P(None, ("groups", "down"), "cross", "depth", None),
            P(("groups", "down"), "cross", "depth", None),
            P(("groups", "down"), "cross", "depth"),
            P(),
        ),
        out_specs=(
            P(None, ("groups", "down"), "cross", "depth", None),
            P(None, ("groups", "down"), "cross", "depth", None),
            P(("groups", "down"), "cross", "depth"),
            P("groups", None),
            P("groups"),
        ),
        check_vma=False,
    )
```

```python
import functools

import jax
import jax.numpy as jnp
from jax import lax
from jax.experimental import pallas as pl
from jax.experimental.pallas import tpu as pltpu
from jax.sharding import PartitionSpec as P

STIFFNESS = 100.0
DAMPING = 20.0
TIME_STEP = 0.05
KERNEL_WIDTH = 0.4
KERNEL_NORM = 64.0
SOFTENING = 0.0001
RADIUS_REF = 0.1
MASS_SHIFT = 0.1
DEAD = -1000.0
TERMS = 48
S = 128
SPREAD = 4
F32 = jnp.float32
BF16 = jnp.bfloat16
CELLS = tuple((a, b, z) for a in range(2) for b in range(2) for z in range(2))
PAIR_LIST = ((0, 0), (0, 1), (0, 2), (1, 1), (1, 2), (2, 2))
VMEM_SPEC = pl.BlockSpec(memory_space=pltpu.VMEM)
SMEM_SPEC = pl.BlockSpec(memory_space=pltpu.SMEM)
VMEM_LIMIT = 48 * 1024 * 1024


def row_ids(shape):
    return lax.broadcasted_iota(jnp.int32, shape, 0)


def lane_ids(shape):
    return lax.broadcasted_iota(jnp.int32, shape, 1)


def one_hot(condition):
    return jnp.where(condition, 1.0, 0.0).astype(BF16)


def split(value):
    high = value.astype(BF16)
    return high, value - high.astype(F32)


def matmul(left, right):
    return lax.dot_general(left, right, (((1,), (0,)), ((), ())), preferred_element_type=F32)


def matmul_turned(left, right):
    return lax.dot_general(left, right, (((1,), (1,)), ((), ())), preferred_element_type=F32)


def lane_gather(table, index):
    return jnp.take_along_axis(table, index, axis=1)


def pack_kernel(
    counts_hbm, positions_hbm, velocities_hbm, radii_hbm, own, inner, counts, positions, velocities, radii, arrived
):
    copies = [
        pltpu.make_async_copy(source, target, arrived.at[k])
        for k, (source, target) in enumerate(
            (
                (counts_hbm, counts),
                (positions_hbm, positions),
                (velocities_hbm, velocities),
                (radii_hbm, radii),
            )
        )
    ]
    for copy in copies:
        copy.start()
    for copy in copies:
        copy.wait()
    depth = lax.axis_index("depth")
    lanes = lane_ids((1, S))

    def layer(ref, at, z):
        rows = ref[at]
        return jnp.where(depth == z, rows[0:1], rows[1:2])

    for c, (a, b, z) in enumerate(CELLS):
        for k in range(3):
            own[c * 8 + k : c * 8 + k + 1, :] = layer(positions, (k, a, b), z)
            own[c * 8 + 3 + k : c * 8 + 4 + k, :] = layer(velocities, (k, a, b), z)
        count = jnp.where(depth == z, counts[a, b, 0], counts[a, b, 1])
        own[c * 8 + 6 : c * 8 + 7, :] = jnp.where(lanes < count, layer(radii, (a, b), z), DEAD)
        own[c * 8 + 7 : c * 8 + 8, :] = jnp.zeros((1, S), F32)
    for column in range(4):
        inner[column * 8 : column * 8 + 8, :] = own[column * 16 + 8 : column * 16 + 16, :]


def local_state(raw, centre):
    rows = row_ids(raw.shape)
    shift = jnp.where(rows == 0, centre[0], jnp.where(rows == 1, centre[1], centre[2]))
    return jnp.where(rows < 3, raw + shift, raw)


def plane_reader(refs, height):
    own, depth_halo, sides = refs[0], refs[1], refs[2:]

    def read(ref, cell):
        return ref[cell * height : cell * height + height, :]

    def cell(x, y, slot):
        a = x - 1
        if y in (1, 2):
            return read(own, a * 4 + (y - 1) * 2 + slot) if slot < 2 else read(depth_halo, a * 2 + y - 1)
        if len(sides) == 4:
            before, after, diag_before, diag_after = sides
            if slot < 2:
                return read(before if y == 0 else after, a * 2 + slot)
            return read(diag_before if y == 0 else diag_after, a)
        b = 1 if y == 0 else 0
        if slot < 2:
            return read(sides[0], a * 4 + b * 2 + slot)
        return read(sides[0], 8 + a * 2 + b) if len(sides) == 1 else read(sides[1], a * 2 + b)

    return cell


def down_reader(refs, height):
    even = lax.rem(lax.axis_index("down"), 2) == 0
    swapped = lax.axis_size("down") % 2 == 0

    def cell(x, y, slot):
        if y in (1, 2):
            place = (y - 1) * 2 + slot if slot < 2 else 4 + y - 1
        else:
            side = 0 if y == 0 else 1
            place = 6 + side * 2 + slot if slot < 2 else 10 + side
        one, two = (ref[place * height : place * height + height, :] for ref in refs)
        if swapped:
            return jnp.where(even, two, one) if x == 0 else jnp.where(even, one, two)
        return one if x == 0 else two

    return cell


def centre_of(x, y, slot, depth):
    side = 0.5 - depth.astype(F32)
    return (x - 1.5, y - 1.5, (-1.0, 1.0, 3.0)[slot] * side)


BLOCK = tuple((x, y, slot) for x in (1, 2) for y in (1, 2) for slot in (0, 1))
PLANE = tuple(
    (x, y, slot) for x in (1, 2) for y in range(4) for slot in range(3) if (x, y, slot) not in BLOCK
)
INSIDE = tuple((x, y, slot) for x in (1, 2) for y in range(4) for slot in range(3))
OUTSIDE = tuple((x, y, slot) for x in (0, 3) for y in range(4) for slot in range(3))


def stepped_state(old, speed, centre):
    rows = row_ids((3, S))
    shift = jnp.where(rows == 0, centre[0], jnp.where(rows == 1, centre[1], centre[2]))
    return (old[0:3] + TIME_STEP * speed[0:3]) + shift, speed[0:3], old[6:8]


def contact_scratch(cells, width):
    rows = len(cells)
    return [
        pltpu.VMEM((rows * 8, S), F32),
        pltpu.VMEM((8 * 8, S), F32),
        pltpu.VMEM((8 * rows, S), jnp.int32),
        pltpu.VMEM((8 * rows, S), jnp.int32),
        pltpu.VMEM((8 * rows, S), jnp.int32),
        pltpu.VMEM((8 * rows, S), jnp.int32),
        pltpu.VMEM((18 * 8 * S, 32), F32),
        pltpu.VMEM((width * 8 * 8, S), F32),
    ]


def contact_sums(cells, width, chunk, scratch):
    local_ref, mine_ref, index_ref, base_ref, amount_ref, chosen_ref, list_ref, sum_ref = scratch
    count = len(cells)
    span = 16 if cells == OUTSIDE else count

    def first_row(a):
        return 8 if cells == OUTSIDE and a == 1 else 0

    def beside(a, b, z):
        return [
            n
            for n, (x, y, slot) in enumerate(cells)
            if abs(x - 1 - a) <= 1 and abs(y - 1 - b) <= 1 and abs(slot - z) <= 1
        ]

    sum_ref[...] = jnp.zeros((width * 64, S), F32)
    place = [local_ref[pl.ds(k, count, stride=8), :] for k in range(3)]
    radius = local_ref[pl.ds(6, count, stride=8), :]
    rows = row_ids((count, S))
    masks = []
    for c, (a, b, z) in enumerate(CELLS):
        mine = mine_ref[c * 8 : c * 8 + 8, :]
        live = mine[6:7] > 0.0
        low = jnp.min(jnp.where(live, mine, 1e9), axis=1, keepdims=True)
        high = jnp.max(jnp.where(live, mine, -1e9), axis=1, keepdims=True)
        part = slice(first_row(a), first_row(a) + span)
        reach = radius[part] + high[6:7]
        near = reach > 0.0
        inside = set(beside(a, b, z))
        for n in range(part.start, part.stop):
            if n not in inside:
                near = jnp.logical_and(near, rows[part] != n)
        for k in range(3):
            near = jnp.logical_and(near, place[k][part] + reach > low[k : k + 1])
            near = jnp.logical_and(near, place[k][part] - reach < high[k : k + 1])
        masks.append(jnp.where(near, 1.0, 0.0).astype(F32))
    mask = jnp.concatenate(masks, axis=0).astype(BF16)
    upper = one_hot(row_ids((S, 2 * S)) <= lane_ids((S, 2 * S)))
    sums = matmul(mask, upper)
    prefix, amount = sums[:, :S], sums[:, S:]
    before = one_hot(lane_ids((span, span)) < row_ids((span, span)))
    total = None
    for c in range(8):
        part = amount[c * span : (c + 1) * span]
        base = matmul(before, part.astype(BF16))
        base_ref[c * span : (c + 1) * span, :] = base.astype(jnp.int32)
        listed = base[span - 1 : span] + part[span - 1 : span]
        total = listed if total is None else jnp.maximum(total, listed)
    most = total.astype(jnp.int32)[0, 0]
    amount_ref[0 : 8 * span, :] = amount.astype(jnp.int32)
    wanted = lane_ids((8 * span, S)).astype(F32)
    index = jnp.zeros((8 * span, S), jnp.int32)
    for step in (64, 32, 16, 8, 4, 2, 1):
        probe = lane_gather(prefix, index + (step - 1))
        index = jnp.where(probe <= wanted, index + step, index)
    index_ref[0 : 8 * span, :] = index
    empty = jnp.where(row_ids((8, S)) == 6, DEAD, 0.0).astype(F32)

    def gather_tiles(t, carry):
        want = t * S + lane_ids((8 * span, S)) - base_ref[0 : 8 * span, :]
        valid = jnp.logical_and(want >= 0, want < amount_ref[0 : 8 * span, :])
        source = lane_gather(index_ref[0 : 8 * span, :], jnp.clip(want, 0, S - 1))
        chosen_ref[0 : 8 * span, :] = jnp.where(valid, source, -1)
        for c, (a, b, z) in enumerate(CELLS):
            tile = empty
            for n in beside(a, b, z):
                row = c * span + n - first_row(a)
                pick = jnp.broadcast_to(chosen_ref[row : row + 1, :], (8, S))
                values = lane_gather(local_ref[n * 8 : n * 8 + 8, :], jnp.maximum(pick, 0))
                tile = jnp.where(pick >= 0, values, tile)
            high = tile.astype(BF16).astype(F32)
            rest = tile - high
            middle = rest.astype(BF16).astype(F32)
            turned = jnp.transpose(jnp.concatenate([high, middle, rest - middle, tile], axis=0))
            for part in range(S // chunk):
                start = pl.multiple_of(t * (8 * S) + (part * 8 + c) * chunk, chunk)
                list_ref[pl.ds(start, chunk), :] = turned[part * chunk : (part + 1) * chunk]
        return carry

    gather_tiles(0, 0)
    lax.fori_loop(1, (most + (S - 1)) // S, gather_tiles, 0)

    selector = jnp.logical_and(
        row_ids((32, SPREAD * S)) % 8 == lane_ids((32, SPREAD * S)) // S, row_ids((32, SPREAD * S)) < 24
    )
    selector = one_hot(selector)

    def pair_step(step, carry):
        every = list_ref[pl.ds(pl.multiple_of(step * (8 * chunk), 8 * chunk), 8 * chunk), :]
        spread = matmul(every.astype(BF16), selector)
        for c in range(8):
            listed = every[c * chunk : (c + 1) * chunk]
            me = [jnp.broadcast_to(mine_ref[c * 8 + k : c * 8 + k + 1, :], (8, S)) for k in range(7)]
            added = [None] * width
            for block in range(chunk // 8):
                row = c * chunk + block * 8
                other = [spread[row : row + 8, k * S : (k + 1) * S] for k in range(SPREAD)]
                other += [
                    jnp.broadcast_to(listed[block * 8 : block * 8 + 8, 24 + k : 25 + k], (8, S))
                    for k in range(SPREAD, 7)
                ]
                r = [me[k] - other[k] for k in range(3)]
                u = [me[3 + k] - other[3 + k] for k in range(3)]
                squared = r[0] * r[0] + r[1] * r[1] + r[2] * r[2] + SOFTENING
                inverse = lax.rsqrt(squared)
                along = u[0] * r[0] + u[1] * r[1] + u[2] * r[2]
                overlap = jnp.maximum((me[6] + other[6]) * inverse - 1.0, 0.0)
                weight = overlap * (STIFFNESS - (DAMPING * along) * inverse)
                terms = [weight * r[k] for k in range(3)]
                if width == 9:
                    terms += [terms[left] * r[right] for left, right in PAIR_LIST]
                added = [
                    term if total is None else total + term for total, term in zip(added, terms)
                ]
            for k in range(width):
                row = (k * 8 + c) * 8
                sum_ref[row : row + 8, :] += added[k]
        return carry

    lax.fori_loop(0, (most + (chunk - 1)) // chunk, pair_step, 0)
    out = []
    for k in range(width):
        parts = [sum_ref[pl.ds(k * 64 + sub, 8, stride=8), :] for sub in range(8)]
        while len(parts) > 1:
            parts = [parts[i] + parts[i + 1] for i in range(0, len(parts), 2)]
        out.append(parts[0])
    return jnp.concatenate(out, axis=0)


def mass_of(radius):
    scaled = radius / RADIUS_REF
    return scaled * scaled * scaled


def fill_start(cells, read, own, depth, scratch):
    for n, (x, y, slot) in enumerate(cells):
        scratch[0][n * 8 : n * 8 + 8, :] = local_state(read(x, y, slot), centre_of(x, y, slot, depth))
    for c, (a, b, z) in enumerate(CELLS):
        scratch[1][c * 8 : c * 8 + 8, :] = local_state(
            own[c * 8 : c * 8 + 8, :], centre_of(a + 1, b + 1, z, depth)
        )


def place_state(ref, start, state):
    ref[start : start + 3, :] = state[0]
    ref[start + 3 : start + 6, :] = state[1]
    ref[start + 6 : start + 8, :] = state[2]


def fill_stepped(cells, read, speed, own, own_speed, depth, scratch):
    for n, (x, y, slot) in enumerate(cells):
        state = stepped_state(read(x, y, slot), speed(x, y, slot), centre_of(x, y, slot, depth))
        place_state(scratch[0], n * 8, state)
    for c, (a, b, z) in enumerate(CELLS):
        state = stepped_state(
            own[c * 8 : c * 8 + 8, :],
            own_speed[c * 4 : c * 4 + 4, :],
            centre_of(a + 1, b + 1, z, depth),
        )
        place_state(scratch[1], c * 8, state)


def step_inside(*refs):
    pieces, sums_out, scratch = refs[:-9], refs[-9], refs[-8:]
    fill_start(INSIDE, plane_reader(pieces, 8), pieces[0], lax.axis_index("depth"), scratch)
    sums_out[...] = contact_sums(INSIDE, 3, 64, scratch)


def step_outside(own, sums_in, near, far, own_out, inner_out, *scratch):
    fill_start(OUTSIDE, down_reader((near, far), 8), own, lax.axis_index("depth"), scratch)
    sums = sums_in[...] + contact_sums(OUTSIDE, 3, 32, scratch)
    radius = own[pl.ds(6, 8, stride=8), :]
    safe_mass = jnp.where(radius > 0.0, mass_of(radius), 1.0)
    for k in range(3):
        velocity = own[pl.ds(3 + k, 8, stride=8), :] + TIME_STEP * sums[k * 8 : k * 8 + 8] / safe_mass
        for c in range(8):
            own_out[c * 4 + k : c * 4 + k + 1, :] = velocity[c : c + 1]
    for c in range(8):
        own_out[c * 4 + 3 : c * 4 + 4, :] = jnp.zeros((1, S), F32)
    for column in range(4):
        inner_out[column * 4 : column * 4 + 4, :] = own_out[column * 8 + 4 : column * 8 + 8, :]


def field_block(own, own_speed, sums_out, *scratch):
    read, speed = plane_reader((own, None), 8), plane_reader((own_speed, None), 4)
    fill_stepped(BLOCK, read, speed, own, own_speed, lax.axis_index("depth"), scratch)
    sums_out[...] = contact_sums(BLOCK, 9, 64, scratch)


def field_plane(split_at, sums_in, *refs):
    pieces, speeds, sums_out, scratch = refs[:split_at], refs[split_at:-9], refs[-9], refs[-8:]
    read, speed = plane_reader(pieces, 8), plane_reader(speeds, 4)
    fill_stepped(PLANE, read, speed, pieces[0], speeds[0], lax.axis_index("depth"), scratch)
    sums_out[...] = sums_in[...] + contact_sums(PLANE, 9, 32, scratch)


def field_outside(
    grid, own, own_speed, sums_in, near_old, far_old, near_speed, far_speed, force_out, node_out, moment_ref, *scratch
):
    depth = lax.axis_index("depth")
    down = lax.axis_index("down")
    cross = lax.axis_index("cross")
    mine_ref = scratch[1]
    read, speed = down_reader((near_old, far_old), 8), down_reader((near_speed, far_speed), 4)
    fill_stepped(OUTSIDE, read, speed, own, own_speed, depth, scratch)
    sums = sums_in[...] + contact_sums(OUTSIDE, 9, 32, scratch)
    force_out[...] = sums[0:24]
    radius = own[pl.ds(6, 8, stride=8), :]
    mass = jnp.where(radius > 0.0, mass_of(radius), 0.0)
    moments = [mass] + [mass * own_speed[pl.ds(k, 8, stride=4), :] for k in range(3)]
    moments += [0.5 * sums[k * 8 : k * 8 + 8] for k in range(3, 9)]
    moment_ref[...] = jnp.zeros((16, 8 * S), F32)
    for m, moment in enumerate(moments):
        for c in range(8):
            moment_ref[m : m + 1, c * S : (c + 1) * S] = moment[c : c + 1]
    rows = row_ids((64, S))
    near_x, near_y, near_z = rows // 16 - 1, (rows // 4) % 4 - 1, rows % 4 - 1
    centres = [index.astype(F32) - 0.5 for index in (near_x, near_y, near_z)]
    kernels = []
    for c, (a, b, z) in enumerate(CELLS):
        squared = jnp.zeros((64, S), F32)
        for k in range(3):
            gap = mine_ref[c * 8 + k : c * 8 + k + 1, :] - centres[k]
            squared = squared + gap * gap
        kernel = jnp.exp(squared * (-0.5 / (KERNEL_WIDTH * KERNEL_WIDTH))) / KERNEL_NORM
        beside = jnp.logical_and(
            jnp.logical_and(jnp.abs(near_x - a) <= 1, jnp.abs(near_y - b) <= 1),
            jnp.abs(near_z - jnp.where(depth == z, 0, 1)) <= 1,
        )
        kernels.append(jnp.where(beside, kernel, 0.0))
    kernel_high, kernel_low = split(jnp.concatenate(kernels, axis=1))
    moment_high, moment_low = split(moment_ref[...])
    wide_part = matmul_turned(
        jnp.concatenate([moment_high, moment_low.astype(BF16)], axis=0), kernel_high
    )
    near = wide_part[0:16] + wide_part[16:32] + matmul_turned(moment_high, kernel_low.astype(BF16))
    size_x, size_y, size_z = grid
    nodes = size_x * size_y * size_z
    lanes = lane_ids((64, nodes))
    row = row_ids((64, nodes))
    target_x = (down * 2 + row // 16 - 1 + size_x) % size_x
    target_y = (cross * 2 + (row // 4) % 4 - 1 + size_y) % size_y
    target_z = depth * 2 + row % 4 - 1
    inside = jnp.logical_and(target_z >= 0, target_z < size_z)
    target = (target_x * size_y + target_y) * size_z + target_z
    chosen = one_hot(jnp.logical_and(inside, lanes == target))
    near_high, rest = split(near)
    near_middle, near_low = split(rest)
    placed = matmul(
        jnp.concatenate([near_high, near_middle, near_low.astype(BF16)], axis=0), chosen
    )
    node_out[...] = placed[0:16] + placed[16:32] + placed[32:48]


def library_kernel(
    grid, coefficients, mine, other, speed, force, velocity_out, force_out, residual_out, gram_out, moment_out, terms
):
    flat = lax.axis_index("depth") == 0
    for k in range(3):
        for a in range(2):
            for b in range(2):
                c = a * 4 + b * 2
                layers = [speed[(c + z) * 4 + k : (c + z) * 4 + k + 1, :] for z in range(2)]
                pulls = [force[k * 8 + c + z : k * 8 + c + z + 1, :] for z in range(2)]
                for z in range(2):
                    velocity_out[k, a, b, z : z + 1, :] = jnp.where(flat, layers[z], layers[1 - z])
                    force_out[k, a, b, z : z + 1, :] = jnp.where(flat, pulls[z], pulls[1 - z])
    fields = mine[...] + other[...]
    size_x, size_y, size_z = grid
    nodes = size_x * size_y * size_z
    lanes = lax.broadcasted_iota(jnp.int32, (1, nodes), 1)
    node_x = lanes // (size_y * size_z)
    node_y = (lanes // size_z) % size_y
    node_z = lanes % size_z
    rows = row_ids((8, nodes))
    density = fields[0:1]
    values = jnp.where(rows == 0, fields[0:8], fields[0:8] / (density + MASS_SHIFT))

    def moved(value, step):
        return pltpu.roll(value, step % nodes, 1)

    plane = size_y * size_z
    slope_x = (moved(values, -plane) - moved(values, plane)) * 0.5
    after_y = jnp.where(
        node_y == size_y - 1, moved(values, (size_y - 1) * size_z), moved(values, -size_z)
    )
    before_y = jnp.where(
        node_y == 0, moved(values, -(size_y - 1) * size_z), moved(values, size_z)
    )
    slope_y = (after_y - before_y) * 0.5
    after_z = jnp.where(node_z == size_z - 1, 0.0, moved(values, -1))
    before_z = jnp.where(node_z == 0, 0.0, moved(values, 1))
    slope_z = (after_z - before_z) * 0.5
    slopes = [[table[k : k + 1] for k in range(4)] for table in (slope_x, slope_y, slope_z)]
    strain = [
        [0.5 * (slopes[left][1 + right] + slopes[right][1 + left]) for right in range(3)]
        for left in range(3)
    ]
    divergence = strain[0][0] + strain[1][1] + strain[2][2]
    rate_sum = jnp.zeros_like(density)
    for left in range(3):
        for right in range(3):
            entry = strain[left][right]
            if left == right:
                entry = entry - divergence / 3.0
            rate_sum = rate_sum + entry * entry
    shear_rate = jnp.sqrt(2.0 * rate_sum + 0.01)
    stress = [fields[4 + k : 5 + k] for k in range(6)]
    pressure = (stress[0] + stress[3] + stress[5]) / 3.0
    deviator = (
        (stress[0] - pressure) ** 2
        + (stress[3] - pressure) ** 2
        + (stress[5] - pressure) ** 2
        + 2.0 * (stress[1] ** 2 + stress[2] ** 2 + stress[4] ** 2)
    )
    shear_stress = jnp.sqrt(0.5 * deviator + 0.01)
    pressure_scale = jnp.sqrt(pressure * pressure + 1.0)
    friction = shear_stress / pressure_scale
    features = [
        density,
        pressure / pressure_scale,
        shear_rate,
        shear_rate / jnp.sqrt(pressure_scale),
        divergence,
        slopes[0][0],
        slopes[1][0],
        slopes[2][0],
    ]
    entries = list(features)
    for left in range(8):
        for right in range(left, 8):
            entries.append(features[left] * features[right])
    for left in range(1, 5):
        entries.append(features[left] * features[left] * features[left])
    model = jnp.zeros_like(density)
    for k, entry in enumerate(entries):
        terms[k : k + 1, :] = entry
        model = model + coefficients[k] * entry
    residual = friction - model
    table = terms[...]
    gram_out[...] = (
        lax.dot_general(
            table,
            table,
            (((1,), (1,)), ((), ())),
            precision=lax.Precision.HIGHEST,
            preferred_element_type=F32,
        )
        / nodes
    )
    moment = lax.dot_general(
        jnp.broadcast_to(friction, (8, nodes)),
        table,
        (((1,), (1,)), ((), ())),
        precision=lax.Precision.HIGHEST,
        preferred_element_type=F32,
    )
    moment_out[...] = moment[0:1] / nodes
    down = lax.axis_index("down")
    cross = lax.axis_index("cross")
    depth = lax.axis_index("depth")
    b_rows = lax.broadcasted_iota(jnp.int32, (2, 1), 0)
    z_lanes = lax.broadcasted_iota(jnp.int32, (2, 2), 1)
    for a in range(2):
        mine = jnp.logical_and(node_x == down * 2 + a, node_y == cross * 2 + b_rows)
        column = [
            jnp.sum(
                jnp.where(jnp.logical_and(mine, node_z == depth * 2 + z), residual, 0.0),
                axis=1,
                keepdims=True,
            )
            for z in range(2)
        ]
        residual_out[a] = jnp.where(z_lanes == 0, column[0], column[1])


def ring(axis, step):
    peers = lax.axis_size(axis)
    return [(i, (i + step) % peers) for i in range(peers)]


def exchange(own, inner, height, joined, beside=None):
    cross = lax.axis_size("cross")

    def cells(block, first, count):
        return block[first * height : (first + count) * height]

    depth_halo = lax.ppermute(inner, "depth", [(0, 1), (1, 0)])
    if cross == 2:
        if joined:
            side = lax.ppermute(
                jnp.concatenate([own, depth_halo], axis=0), "cross", [(0, 1), (1, 0)]
            )
            diag = cells(side, 8, 4)
            sides = [side]
        else:
            side = lax.ppermute(own, "cross", [(0, 1), (1, 0)])
            diag = lax.ppermute(inner, ("cross", "depth"), [(i, 3 - i) for i in range(4)])
            sides = [side, diag]

        def lateral(x):
            return [
                cells(side, x * 4 + 2, 2),
                cells(side, x * 4, 2),
                cells(diag, x * 2 + 1, 1),
                cells(diag, x * 2, 1),
            ]

    else:
        pairs = [(i * 2 + j, ((i + 1) % cross) * 2 + 1 - j) for i in range(cross) for j in range(2)]
        back = [(i * 2 + j, ((i - 1) % cross) * 2 + 1 - j) for i in range(cross) for j in range(2)]
        last = jnp.concatenate([cells(own, 2, 2), cells(own, 6, 2)], axis=0)
        first = jnp.concatenate([cells(own, 0, 2), cells(own, 4, 2)], axis=0)
        last_inner = jnp.concatenate([cells(inner, 1, 1), cells(inner, 3, 1)], axis=0)
        first_inner = jnp.concatenate([cells(inner, 0, 1), cells(inner, 2, 1)], axis=0)
        before = lax.ppermute(last, "cross", ring("cross", 1))
        after = lax.ppermute(first, "cross", ring("cross", -1))
        diag_before = lax.ppermute(last_inner, ("cross", "depth"), pairs)
        diag_after = lax.ppermute(first_inner, ("cross", "depth"), back)
        sides = [before, after, diag_before, diag_after]

        def lateral(x):
            return [
                cells(before, x * 2, 2),
                cells(after, x * 2, 2),
                cells(diag_before, x, 1),
                cells(diag_after, x, 1),
            ]

    def face(x):
        return jnp.concatenate([cells(own, x * 4, 4), cells(depth_halo, x * 2, 2)] + lateral(x), axis=0)

    downs = lax.axis_size("down")
    last, first = face(1), face(0)
    if beside is not None:
        mine, depth_halo = lax.optimization_barrier((own, depth_halo))
        last, first, result = lax.optimization_barrier((last, first, beside(mine)))
    if downs % 2 == 0:
        even = lax.rem(lax.axis_index("down"), 2) == 0
        near = [(i, i ^ 1) for i in range(downs)]
        far = [(i, (i - 1 + 2 * (i % 2)) % downs) for i in range(downs)]
        outside = [
            lax.ppermute(jnp.where(even, last, first), "down", near),
            lax.ppermute(jnp.where(even, first, last), "down", far),
        ]
    else:
        outside = [
            lax.ppermute(last, "down", ring("down", 1)),
            lax.ppermute(first, "down", ring("down", -1)),
        ]
    if beside is not None:
        return [own, depth_halo] + sides, outside, result
    return [own, depth_halo] + sides, outside


def shared(value, axes, peers):
    return [value] + [
        lax.ppermute(value, axes, [(i, i ^ k) for i in range(peers)]) for k in range(1, peers)
    ]


def tree_sum(parts):
    while len(parts) > 1:
        parts = [parts[k] + parts[k + 1] for k in range(0, len(parts), 2)]
    return parts[0]


def body(positions, velocities, sphere_radii, counts, coefficients):
    down, cross, depth = (lax.axis_size(name) for name in ("down", "cross", "depth"))
    grid = (2 * down, 2 * cross, 2 * depth)
    nodes = grid[0] * grid[1] * grid[2]
    params = pltpu.CompilerParams(vmem_limit_bytes=VMEM_LIMIT)
    vector_shape = jax.ShapeDtypeStruct((3, 2, 2, 2, S), F32)

    def rows(count):
        return jax.ShapeDtypeStruct((count, S), F32)

    def call(kernel, inputs, outputs, scratch, name, vectors=0):
        return pl.pallas_call(
            kernel,
            out_shape=outputs,
            in_specs=[VMEM_SPEC] * len(inputs),
            out_specs=jax.tree.map(lambda _: VMEM_SPEC, outputs),
            scratch_shapes=scratch,
            compiler_params=params,
            cost_estimate=pl.CostEstimate(flops=vectors, bytes_accessed=1 << 20, transcendentals=0),
            name=name,
        )(*inputs)

    own, inner = pl.pallas_call(
        pack_kernel,
        out_shape=(rows(64), rows(32)),
        in_specs=[pl.BlockSpec(memory_space=pl.ANY)] * 4,
        out_specs=(VMEM_SPEC, VMEM_SPEC),
        scratch_shapes=[
            pltpu.SMEM((2, 2, 2), jnp.int32),
            pltpu.VMEM((3, 2, 2, 2, S), F32),
            pltpu.VMEM((3, 2, 2, 2, S), F32),
            pltpu.VMEM((2, 2, 2, S), F32),
            pltpu.SemaphoreType.DMA((4,)),
        ],
        compiler_params=pltpu.CompilerParams(vmem_limit_bytes=60 * 1024 * 1024),
        name="pack",
    )(counts, positions, velocities, sphere_radii)
    inside, outside = exchange(own, inner, 8, True)
    sums = call(step_inside, inside, rows(24), contact_scratch(INSIDE, 3), "step_inside", 1 << 31)
    own_speed, inner_speed = call(
        step_outside, [own, sums] + outside, (rows(32), rows(16)), contact_scratch(OUTSIDE, 3), "step_outside", 1 << 30
    )
    inside_speed, outside_speed, sums = exchange(
        own_speed,
        inner_speed,
        4,
        False,
        lambda speed: call(
            field_block, [own, speed], rows(72), contact_scratch(BLOCK, 9), "field_block", 1 << 31
        ),
    )
    sums = call(
        functools.partial(field_plane, len(inside)),
        [sums] + inside + inside_speed,
        rows(72),
        contact_scratch(PLANE, 9),
        "field_plane",
        1 << 31,
    )
    force, partial = call(
        functools.partial(field_outside, grid),
        [own, own_speed, sums] + outside + outside_speed,
        (rows(24), jax.ShapeDtypeStruct((16, nodes), F32)),
        [pltpu.VMEM((16, 8 * S), F32)] + contact_scratch(OUTSIDE, 9),
        "field_outside",
        1 << 30,
    )
    partial = tree_sum(shared(partial, ("cross", "depth"), cross * depth))
    distance = 1
    while distance < down:
        other = lax.ppermute(partial, "down", [(i, i ^ distance) for i in range(down)])
        distance = distance * 2
        if distance < down:
            partial = partial + other
    velocity_new, force_next, residual_field, gram_matrix, moment = pl.pallas_call(
        functools.partial(library_kernel, grid),
        out_shape=(
            vector_shape,
            vector_shape,
            jax.ShapeDtypeStruct((2, 2, 2), F32),
            jax.ShapeDtypeStruct((TERMS, TERMS), F32),
            jax.ShapeDtypeStruct((1, TERMS), F32),
        ),
        in_specs=[SMEM_SPEC] + [VMEM_SPEC] * 4,
        out_specs=(VMEM_SPEC,) * 5,
        scratch_shapes=[pltpu.VMEM((TERMS, nodes), F32)],
        compiler_params=params,
        name="library",
    )(coefficients, partial, other, own_speed, force)
    return (velocity_new, force_next, residual_field, gram_matrix, moment.reshape(TERMS))


def solution(mesh):
    return jax.shard_map(
        body,
        mesh=mesh,
        in_specs=(
            P(None, ("groups", "down"), "cross", "depth", None),
            P(None, ("groups", "down"), "cross", "depth", None),
            P(("groups", "down"), "cross", "depth", None),
            P(("groups", "down"), "cross", "depth"),
            P(),
        ),
        out_specs=(
            P(None, ("groups", "down"), "cross", "depth", None),
            P(None, ("groups", "down"), "cross", "depth", None),
            P(("groups", "down"), "cross", "depth"),
            P("groups", None),
            P("groups"),
        ),
        check_vma=False,
    )
```

```python
import functools

import jax
import jax.numpy as jnp
from jax import lax
from jax.experimental import pallas as pl
from jax.experimental.pallas import tpu as pltpu
from jax.sharding import PartitionSpec as P

STIFFNESS = 100.0
DAMPING = 20.0
TIME_STEP = 0.05
KERNEL_WIDTH = 0.4
KERNEL_NORM = 64.0
SOFTENING = 0.0001
RADIUS_REF = 0.1
MASS_SHIFT = 0.1
DEAD = -1000.0
TERMS = 48
S = 128
SPREAD = 4
F32 = jnp.float32
BF16 = jnp.bfloat16
CELLS = tuple((a, b, z) for a in range(2) for b in range(2) for z in range(2))
PAIR_LIST = ((0, 0), (0, 1), (0, 2), (1, 1), (1, 2), (2, 2))
VMEM_SPEC = pl.BlockSpec(memory_space=pltpu.VMEM)
SMEM_SPEC = pl.BlockSpec(memory_space=pltpu.SMEM)
VMEM_LIMIT = 48 * 1024 * 1024


def row_ids(shape):
    return lax.broadcasted_iota(jnp.int32, shape, 0)


def lane_ids(shape):
    return lax.broadcasted_iota(jnp.int32, shape, 1)


def one_hot(condition):
    return jnp.where(condition, 1.0, 0.0).astype(BF16)


def split(value):
    high = value.astype(BF16)
    return high, value - high.astype(F32)


def matmul(left, right):
    return lax.dot_general(left, right, (((1,), (0,)), ((), ())), preferred_element_type=F32)


def matmul_turned(left, right):
    return lax.dot_general(left, right, (((1,), (1,)), ((), ())), preferred_element_type=F32)


def lane_gather(table, index):
    return jnp.take_along_axis(table, index, axis=1)


def pack_kernel(
    counts_hbm, positions_hbm, velocities_hbm, radii_hbm, own, inner, counts, positions, velocities, radii, arrived
):
    copies = [
        pltpu.make_async_copy(source, target, arrived.at[k])
        for k, (source, target) in enumerate(
            (
                (counts_hbm, counts),
                (positions_hbm, positions),
                (velocities_hbm, velocities),
                (radii_hbm, radii),
            )
        )
    ]
    for copy in copies:
        copy.start()
    for copy in copies:
        copy.wait()
    depth = lax.axis_index("depth")
    lanes = lane_ids((1, S))

    def layer(ref, at, z):
        rows = ref[at]
        return jnp.where(depth == z, rows[0:1], rows[1:2])

    for c, (a, b, z) in enumerate(CELLS):
        for k in range(3):
            own[c * 8 + k : c * 8 + k + 1, :] = layer(positions, (k, a, b), z)
            own[c * 8 + 3 + k : c * 8 + 4 + k, :] = layer(velocities, (k, a, b), z)
        count = jnp.where(depth == z, counts[a, b, 0], counts[a, b, 1])
        own[c * 8 + 6 : c * 8 + 7, :] = jnp.where(lanes < count, layer(radii, (a, b), z), DEAD)
        own[c * 8 + 7 : c * 8 + 8, :] = jnp.zeros((1, S), F32)
    for column in range(4):
        inner[column * 8 : column * 8 + 8, :] = own[column * 16 + 8 : column * 16 + 16, :]


def local_state(raw, centre):
    rows = row_ids(raw.shape)
    shift = jnp.where(rows == 0, centre[0], jnp.where(rows == 1, centre[1], centre[2]))
    return jnp.where(rows < 3, raw + shift, raw)


def plane_reader(refs, height):
    own, depth_halo, sides = refs[0], refs[1], refs[2:]

    def read(ref, cell):
        return ref[cell * height : cell * height + height, :]

    def cell(x, y, slot):
        a = x - 1
        if y in (1, 2):
            return read(own, a * 4 + (y - 1) * 2 + slot) if slot < 2 else read(depth_halo, a * 2 + y - 1)
        if len(sides) == 4:
            before, after, diag_before, diag_after = sides
            if slot < 2:
                return read(before if y == 0 else after, a * 2 + slot)
            return read(diag_before if y == 0 else diag_after, a)
        b = 1 if y == 0 else 0
        if slot < 2:
            return read(sides[0], a * 4 + b * 2 + slot)
        return read(sides[0], 8 + a * 2 + b) if len(sides) == 1 else read(sides[1], a * 2 + b)

    return cell


def down_reader(refs, height):
    even = lax.rem(lax.axis_index("down"), 2) == 0
    swapped = lax.axis_size("down") % 2 == 0

    def cell(x, y, slot):
        if y in (1, 2):
            place = (y - 1) * 2 + slot if slot < 2 else 4 + y - 1
        else:
            side = 0 if y == 0 else 1
            place = 6 + side * 2 + slot if slot < 2 else 10 + side
        one, two = (ref[place * height : place * height + height, :] for ref in refs)
        if swapped:
            return jnp.where(even, two, one) if x == 0 else jnp.where(even, one, two)
        return one if x == 0 else two

    return cell


def centre_of(x, y, slot, depth):
    side = 0.5 - depth.astype(F32)
    return (x - 1.5, y - 1.5, (-1.0, 1.0, 3.0)[slot] * side)


BLOCK = tuple((x, y, slot) for x in (1, 2) for y in (1, 2) for slot in (0, 1))
PLANE = tuple(
    (x, y, slot) for x in (1, 2) for y in range(4) for slot in range(3) if (x, y, slot) not in BLOCK
)
INSIDE = tuple((x, y, slot) for x in (1, 2) for y in range(4) for slot in range(3))
OUTSIDE = tuple((x, y, slot) for x in (0, 3) for y in range(4) for slot in range(3))


def stepped_state(old, speed, centre):
    rows = row_ids((3, S))
    shift = jnp.where(rows == 0, centre[0], jnp.where(rows == 1, centre[1], centre[2]))
    return (old[0:3] + TIME_STEP * speed[0:3]) + shift, speed[0:3], old[6:8]


def contact_scratch(cells, width):
    rows = len(cells)
    return [
        pltpu.VMEM((rows * 8, S), F32),
        pltpu.VMEM((8 * 8, S), F32),
        pltpu.VMEM((8 * rows, S), jnp.int32),
        pltpu.VMEM((8 * rows, S), jnp.int32),
        pltpu.VMEM((8 * rows, S), jnp.int32),
        pltpu.VMEM((8 * rows, S), jnp.int32),
        pltpu.VMEM((18 * 8 * S, 32), F32),
        pltpu.VMEM((width * 8 * 8, S), F32),
    ]


def contact_sums(cells, width, chunk, scratch):
    local_ref, mine_ref, index_ref, base_ref, amount_ref, chosen_ref, list_ref, sum_ref = scratch
    count = len(cells)
    span = 16 if cells == OUTSIDE else count

    def first_row(a):
        return 8 if cells == OUTSIDE and a == 1 else 0

    def beside(a, b, z):
        return [
            n
            for n, (x, y, slot) in enumerate(cells)
            if abs(x - 1 - a) <= 1 and abs(y - 1 - b) <= 1 and abs(slot - z) <= 1
        ]

    sum_ref[...] = jnp.zeros((width * 64, S), F32)
    place = [local_ref[pl.ds(k, count, stride=8), :] for k in range(3)]
    radius = local_ref[pl.ds(6, count, stride=8), :]
    rows = row_ids((count, S))
    masks = []
    for c, (a, b, z) in enumerate(CELLS):
        mine = mine_ref[c * 8 : c * 8 + 8, :]
        live = mine[6:7] > 0.0
        low = jnp.min(jnp.where(live, mine, 1e9), axis=1, keepdims=True)
        high = jnp.max(jnp.where(live, mine, -1e9), axis=1, keepdims=True)
        part = slice(first_row(a), first_row(a) + span)
        reach = radius[part] + high[6:7]
        near = reach > 0.0
        inside = set(beside(a, b, z))
        for n in range(part.start, part.stop):
            if n not in inside:
                near = jnp.logical_and(near, rows[part] != n)
        for k in range(3):
            near = jnp.logical_and(near, place[k][part] + reach > low[k : k + 1])
            near = jnp.logical_and(near, place[k][part] - reach < high[k : k + 1])
        masks.append(jnp.where(near, 1.0, 0.0).astype(F32))
    mask = jnp.concatenate(masks, axis=0).astype(BF16)
    upper = one_hot(row_ids((S, 2 * S)) <= lane_ids((S, 2 * S)))
    sums = matmul(mask, upper)
    prefix, amount = sums[:, :S], sums[:, S:]
    before = one_hot(lane_ids((span, span)) < row_ids((span, span)))
    total = None
    for c in range(8):
        part = amount[c * span : (c + 1) * span]
        base = matmul(before, part.astype(BF16))
        base_ref[c * span : (c + 1) * span, :] = base.astype(jnp.int32)
        listed = base[span - 1 : span] + part[span - 1 : span]
        total = listed if total is None else jnp.maximum(total, listed)
    most = total.astype(jnp.int32)[0, 0]
    amount_ref[0 : 8 * span, :] = amount.astype(jnp.int32)
    wanted = lane_ids((8 * span, S)).astype(F32)
    index = jnp.zeros((8 * span, S), jnp.int32)
    for step in (64, 32, 16, 8, 4, 2, 1):
        probe = lane_gather(prefix, index + (step - 1))
        index = jnp.where(probe <= wanted, index + step, index)
    index_ref[0 : 8 * span, :] = index
    empty = jnp.where(row_ids((8, S)) == 6, DEAD, 0.0).astype(F32)

    def gather_tiles(t, carry):
        want = t * S + lane_ids((8 * span, S)) - base_ref[0 : 8 * span, :]
        valid = jnp.logical_and(want >= 0, want < amount_ref[0 : 8 * span, :])
        source = lane_gather(index_ref[0 : 8 * span, :], jnp.clip(want, 0, S - 1))
        chosen_ref[0 : 8 * span, :] = jnp.where(valid, source, -1)
        for c, (a, b, z) in enumerate(CELLS):
            tile = empty
            for n in beside(a, b, z):
                row = c * span + n - first_row(a)
                pick = jnp.broadcast_to(chosen_ref[row : row + 1, :], (8, S))
                values = lane_gather(local_ref[n * 8 : n * 8 + 8, :], jnp.maximum(pick, 0))
                tile = jnp.where(pick >= 0, values, tile)
            high = tile.astype(BF16).astype(F32)
            rest = tile - high
            middle = rest.astype(BF16).astype(F32)
            turned = jnp.transpose(jnp.concatenate([high, middle, rest - middle, tile], axis=0))
            for part in range(S // chunk):
                start = pl.multiple_of(t * (8 * S) + (part * 8 + c) * chunk, chunk)
                list_ref[pl.ds(start, chunk), :] = turned[part * chunk : (part + 1) * chunk]
        return carry

    gather_tiles(0, 0)
    lax.fori_loop(1, (most + (S - 1)) // S, gather_tiles, 0)

    selector = jnp.logical_and(
        row_ids((32, SPREAD * S)) % 8 == lane_ids((32, SPREAD * S)) // S, row_ids((32, SPREAD * S)) < 24
    )
    selector = one_hot(selector)

    def pair_step(step, carry):
        every = list_ref[pl.ds(pl.multiple_of(step * (8 * chunk), 8 * chunk), 8 * chunk), :]
        spread = matmul(every.astype(BF16), selector)
        for c in range(8):
            listed = every[c * chunk : (c + 1) * chunk]
            me = [jnp.broadcast_to(mine_ref[c * 8 + k : c * 8 + k + 1, :], (8, S)) for k in range(7)]
            added = [None] * width
            for block in range(chunk // 8):
                row = c * chunk + block * 8
                other = [spread[row : row + 8, k * S : (k + 1) * S] for k in range(SPREAD)]
                other += [
                    jnp.broadcast_to(listed[block * 8 : block * 8 + 8, 24 + k : 25 + k], (8, S))
                    for k in range(SPREAD, 7)
                ]
                r = [me[k] - other[k] for k in range(3)]
                u = [me[3 + k] - other[3 + k] for k in range(3)]
                squared = r[0] * r[0] + r[1] * r[1] + r[2] * r[2] + SOFTENING
                inverse = lax.rsqrt(squared)
                along = u[0] * r[0] + u[1] * r[1] + u[2] * r[2]
                overlap = jnp.maximum((me[6] + other[6]) * inverse - 1.0, 0.0)
                weight = overlap * (STIFFNESS - (DAMPING * along) * inverse)
                terms = [weight * r[k] for k in range(3)]
                if width == 9:
                    terms += [terms[left] * r[right] for left, right in PAIR_LIST]
                added = [
                    term if total is None else total + term for total, term in zip(added, terms)
                ]
            for k in range(width):
                row = (k * 8 + c) * 8
                sum_ref[row : row + 8, :] += added[k]
        return carry

    lax.fori_loop(0, (most + (chunk - 1)) // chunk, pair_step, 0)
    out = []
    for k in range(width):
        parts = [sum_ref[pl.ds(k * 64 + sub, 8, stride=8), :] for sub in range(8)]
        while len(parts) > 1:
            parts = [parts[i] + parts[i + 1] for i in range(0, len(parts), 2)]
        out.append(parts[0])
    return jnp.concatenate(out, axis=0)


def mass_of(radius):
    scaled = radius / RADIUS_REF
    return scaled * scaled * scaled


def fill_start(cells, read, own, depth, scratch):
    for n, (x, y, slot) in enumerate(cells):
        scratch[0][n * 8 : n * 8 + 8, :] = local_state(read(x, y, slot), centre_of(x, y, slot, depth))
    for c, (a, b, z) in enumerate(CELLS):
        scratch[1][c * 8 : c * 8 + 8, :] = local_state(
            own[c * 8 : c * 8 + 8, :], centre_of(a + 1, b + 1, z, depth)
        )


def place_state(ref, start, state):
    ref[start : start + 3, :] = state[0]
    ref[start + 3 : start + 6, :] = state[1]
    ref[start + 6 : start + 8, :] = state[2]


def fill_stepped(cells, read, speed, own, own_speed, depth, scratch):
    for n, (x, y, slot) in enumerate(cells):
        state = stepped_state(read(x, y, slot), speed(x, y, slot), centre_of(x, y, slot, depth))
        place_state(scratch[0], n * 8, state)
    for c, (a, b, z) in enumerate(CELLS):
        state = stepped_state(
            own[c * 8 : c * 8 + 8, :],
            own_speed[c * 4 : c * 4 + 4, :],
            centre_of(a + 1, b + 1, z, depth),
        )
        place_state(scratch[1], c * 8, state)


def step_inside(*refs):
    pieces, sums_out, scratch = refs[:-9], refs[-9], refs[-8:]
    fill_start(INSIDE, plane_reader(pieces, 8), pieces[0], lax.axis_index("depth"), scratch)
    sums_out[...] = contact_sums(INSIDE, 3, 64, scratch)


def step_outside(own, sums_in, near, far, own_out, inner_out, *scratch):
    fill_start(OUTSIDE, down_reader((near, far), 8), own, lax.axis_index("depth"), scratch)
    sums = sums_in[...] + contact_sums(OUTSIDE, 3, 32, scratch)
    radius = own[pl.ds(6, 8, stride=8), :]
    safe_mass = jnp.where(radius > 0.0, mass_of(radius), 1.0)
    for k in range(3):
        velocity = own[pl.ds(3 + k, 8, stride=8), :] + TIME_STEP * sums[k * 8 : k * 8 + 8] / safe_mass
        for c in range(8):
            own_out[c * 4 + k : c * 4 + k + 1, :] = velocity[c : c + 1]
    for c in range(8):
        own_out[c * 4 + 3 : c * 4 + 4, :] = jnp.zeros((1, S), F32)
    for column in range(4):
        inner_out[column * 4 : column * 4 + 4, :] = own_out[column * 8 + 4 : column * 8 + 8, :]


def field_weights(grid, own, own_speed, coefficients, high_out, low_out, chosen_out, model_out):
    model_out[...] = coefficients[...]
    depth = lax.axis_index("depth")
    down = lax.axis_index("down")
    cross = lax.axis_index("cross")
    rows = row_ids((64, S))
    near_x, near_y, near_z = rows // 16 - 1, (rows // 4) % 4 - 1, rows % 4 - 1
    centres = [index.astype(F32) - 0.5 for index in (near_x, near_y, near_z)]
    kernels = []
    for c, (a, b, z) in enumerate(CELLS):
        place = stepped_state(
            own[c * 8 : c * 8 + 8, :],
            own_speed[c * 4 : c * 4 + 4, :],
            centre_of(a + 1, b + 1, z, depth),
        )[0]
        squared = jnp.zeros((64, S), F32)
        for k in range(3):
            gap = place[k : k + 1] - centres[k]
            squared = squared + gap * gap
        kernel = jnp.exp(squared * (-0.5 / (KERNEL_WIDTH * KERNEL_WIDTH))) / KERNEL_NORM
        beside = jnp.logical_and(
            jnp.logical_and(jnp.abs(near_x - a) <= 1, jnp.abs(near_y - b) <= 1),
            jnp.abs(near_z - jnp.where(depth == z, 0, 1)) <= 1,
        )
        kernels.append(jnp.where(beside, kernel, 0.0))
    kernel_high, kernel_low = split(jnp.concatenate(kernels, axis=1))
    high_out[...] = kernel_high
    low_out[...] = kernel_low.astype(BF16)
    size_x, size_y, size_z = grid
    nodes = size_x * size_y * size_z
    lanes = lane_ids((64, nodes))
    row = row_ids((64, nodes))
    target_x = (down * 2 + row // 16 - 1 + size_x) % size_x
    target_y = (cross * 2 + (row // 4) % 4 - 1 + size_y) % size_y
    target_z = depth * 2 + row % 4 - 1
    inside = jnp.logical_and(target_z >= 0, target_z < size_z)
    target = (target_x * size_y + target_y) * size_z + target_z
    chosen_out[...] = one_hot(jnp.logical_and(inside, lanes == target))


def field_inside(*refs):
    split_at = (len(refs) - 9) // 2
    pieces, speeds, sums_out, scratch = refs[:split_at], refs[split_at:-9], refs[-9], refs[-8:]
    read, speed = plane_reader(pieces, 8), plane_reader(speeds, 4)
    fill_stepped(INSIDE, read, speed, pieces[0], speeds[0], lax.axis_index("depth"), scratch)
    sums_out[...] = contact_sums(INSIDE, 9, 64, scratch)


def field_outside(
    own, own_speed, sums_in, near_old, far_old, near_speed, far_speed, kernel_high, kernel_low, chosen,
    force_out, node_out, moment_ref, *scratch
):
    depth = lax.axis_index("depth")
    read, speed = down_reader((near_old, far_old), 8), down_reader((near_speed, far_speed), 4)
    fill_stepped(OUTSIDE, read, speed, own, own_speed, depth, scratch)
    sums = sums_in[...] + contact_sums(OUTSIDE, 9, 32, scratch)
    force_out[...] = sums[0:24]
    radius = own[pl.ds(6, 8, stride=8), :]
    mass = jnp.where(radius > 0.0, mass_of(radius), 0.0)
    moments = [mass] + [mass * own_speed[pl.ds(k, 8, stride=4), :] for k in range(3)]
    moments += [0.5 * sums[k * 8 : k * 8 + 8] for k in range(3, 9)]
    moment_ref[...] = jnp.zeros((16, 8 * S), F32)
    for m, moment in enumerate(moments):
        for c in range(8):
            moment_ref[m : m + 1, c * S : (c + 1) * S] = moment[c : c + 1]
    moment_high, moment_low = split(moment_ref[...])
    wide_part = matmul_turned(
        jnp.concatenate([moment_high, moment_low.astype(BF16)], axis=0), kernel_high[...]
    )
    near = wide_part[0:16] + wide_part[16:32] + matmul_turned(moment_high, kernel_low[...])
    near_high, rest = split(near)
    near_middle, near_low = split(rest)
    placed = matmul(
        jnp.concatenate([near_high, near_middle, near_low.astype(BF16)], axis=0), chosen[...]
    )
    node_out[...] = placed[0:16] + placed[16:32] + placed[32:48]


def library_kernel(
    grid, coefficients, mine, other, speed, force, velocity_out, force_out, residual_out, gram_out, moment_out, terms
):
    flat = lax.axis_index("depth") == 0
    for k in range(3):
        for a in range(2):
            for b in range(2):
                c = a * 4 + b * 2
                layers = [speed[(c + z) * 4 + k : (c + z) * 4 + k + 1, :] for z in range(2)]
                pulls = [force[k * 8 + c + z : k * 8 + c + z + 1, :] for z in range(2)]
                for z in range(2):
                    velocity_out[k, a, b, z : z + 1, :] = jnp.where(flat, layers[z], layers[1 - z])
                    force_out[k, a, b, z : z + 1, :] = jnp.where(flat, pulls[z], pulls[1 - z])
    fields = mine[...] + other[...]
    size_x, size_y, size_z = grid
    nodes = size_x * size_y * size_z
    lanes = lax.broadcasted_iota(jnp.int32, (1, nodes), 1)
    node_x = lanes // (size_y * size_z)
    node_y = (lanes // size_z) % size_y
    node_z = lanes % size_z
    rows = row_ids((8, nodes))
    density = fields[0:1]
    values = jnp.where(rows == 0, fields[0:8], fields[0:8] / (density + MASS_SHIFT))

    def moved(value, step):
        return pltpu.roll(value, step % nodes, 1)

    plane = size_y * size_z
    slope_x = (moved(values, -plane) - moved(values, plane)) * 0.5
    after_y = jnp.where(
        node_y == size_y - 1, moved(values, (size_y - 1) * size_z), moved(values, -size_z)
    )
    before_y = jnp.where(
        node_y == 0, moved(values, -(size_y - 1) * size_z), moved(values, size_z)
    )
    slope_y = (after_y - before_y) * 0.5
    after_z = jnp.where(node_z == size_z - 1, 0.0, moved(values, -1))
    before_z = jnp.where(node_z == 0, 0.0, moved(values, 1))
    slope_z = (after_z - before_z) * 0.5
    slopes = [[table[k : k + 1] for k in range(4)] for table in (slope_x, slope_y, slope_z)]
    strain = [
        [0.5 * (slopes[left][1 + right] + slopes[right][1 + left]) for right in range(3)]
        for left in range(3)
    ]
    divergence = strain[0][0] + strain[1][1] + strain[2][2]
    rate_sum = jnp.zeros_like(density)
    for left in range(3):
        for right in range(3):
            entry = strain[left][right]
            if left == right:
                entry = entry - divergence / 3.0
            rate_sum = rate_sum + entry * entry
    shear_rate = jnp.sqrt(2.0 * rate_sum + 0.01)
    stress = [fields[4 + k : 5 + k] for k in range(6)]
    pressure = (stress[0] + stress[3] + stress[5]) / 3.0
    deviator = (
        (stress[0] - pressure) ** 2
        + (stress[3] - pressure) ** 2
        + (stress[5] - pressure) ** 2
        + 2.0 * (stress[1] ** 2 + stress[2] ** 2 + stress[4] ** 2)
    )
    shear_stress = jnp.sqrt(0.5 * deviator + 0.01)
    pressure_scale = jnp.sqrt(pressure * pressure + 1.0)
    friction = shear_stress / pressure_scale
    features = [
        density,
        pressure / pressure_scale,
        shear_rate,
        shear_rate / jnp.sqrt(pressure_scale),
        divergence,
        slopes[0][0],
        slopes[1][0],
        slopes[2][0],
    ]
    entries = list(features)
    for left in range(8):
        for right in range(left, 8):
            entries.append(features[left] * features[right])
    for left in range(1, 5):
        entries.append(features[left] * features[left] * features[left])
    for k, entry in enumerate(entries):
        terms[k : k + 1, :] = entry
    table = terms[...]
    model = lax.dot_general(
        jnp.broadcast_to(coefficients[...], (8, TERMS)),
        table,
        (((1,), (0,)), ((), ())),
        precision=lax.Precision.HIGHEST,
        preferred_element_type=F32,
    )
    residual = friction - model[0:1]
    gram_out[...] = (
        lax.dot_general(
            table,
            table,
            (((1,), (1,)), ((), ())),
            precision=lax.Precision.HIGHEST,
            preferred_element_type=F32,
        )
        / nodes
    )
    moment = lax.dot_general(
        jnp.broadcast_to(friction, (8, nodes)),
        table,
        (((1,), (1,)), ((), ())),
        precision=lax.Precision.HIGHEST,
        preferred_element_type=F32,
    )
    moment_out[...] = moment[0:1] / nodes
    down = lax.axis_index("down")
    cross = lax.axis_index("cross")
    depth = lax.axis_index("depth")
    b_rows = lax.broadcasted_iota(jnp.int32, (2, 1), 0)
    z_lanes = lax.broadcasted_iota(jnp.int32, (2, 2), 1)
    for a in range(2):
        mine = jnp.logical_and(node_x == down * 2 + a, node_y == cross * 2 + b_rows)
        column = [
            jnp.sum(
                jnp.where(jnp.logical_and(mine, node_z == depth * 2 + z), residual, 0.0),
                axis=1,
                keepdims=True,
            )
            for z in range(2)
        ]
        residual_out[a] = jnp.where(z_lanes == 0, column[0], column[1])


def ring(axis, step):
    peers = lax.axis_size(axis)
    return [(i, (i + step) % peers) for i in range(peers)]


def exchange(own, inner, height, joined, beside=None):
    cross = lax.axis_size("cross")

    def cells(block, first, count):
        return block[first * height : (first + count) * height]

    depth_halo = lax.ppermute(inner, "depth", [(0, 1), (1, 0)])
    if cross == 2:
        if joined:
            side = lax.ppermute(
                jnp.concatenate([own, depth_halo], axis=0), "cross", [(0, 1), (1, 0)]
            )
            diag = cells(side, 8, 4)
            sides = [side]
        else:
            side = lax.ppermute(own, "cross", [(0, 1), (1, 0)])
            diag = lax.ppermute(inner, ("cross", "depth"), [(i, 3 - i) for i in range(4)])
            sides = [side, diag]

        def lateral(x):
            return [
                cells(side, x * 4 + 2, 2),
                cells(side, x * 4, 2),
                cells(diag, x * 2 + 1, 1),
                cells(diag, x * 2, 1),
            ]

    else:
        pairs = [(i * 2 + j, ((i + 1) % cross) * 2 + 1 - j) for i in range(cross) for j in range(2)]
        back = [(i * 2 + j, ((i - 1) % cross) * 2 + 1 - j) for i in range(cross) for j in range(2)]
        last = jnp.concatenate([cells(own, 2, 2), cells(own, 6, 2)], axis=0)
        first = jnp.concatenate([cells(own, 0, 2), cells(own, 4, 2)], axis=0)
        last_inner = jnp.concatenate([cells(inner, 1, 1), cells(inner, 3, 1)], axis=0)
        first_inner = jnp.concatenate([cells(inner, 0, 1), cells(inner, 2, 1)], axis=0)
        before = lax.ppermute(last, "cross", ring("cross", 1))
        after = lax.ppermute(first, "cross", ring("cross", -1))
        diag_before = lax.ppermute(last_inner, ("cross", "depth"), pairs)
        diag_after = lax.ppermute(first_inner, ("cross", "depth"), back)
        sides = [before, after, diag_before, diag_after]

        def lateral(x):
            return [
                cells(before, x * 2, 2),
                cells(after, x * 2, 2),
                cells(diag_before, x, 1),
                cells(diag_after, x, 1),
            ]

    def face(x):
        return jnp.concatenate([cells(own, x * 4, 4), cells(depth_halo, x * 2, 2)] + lateral(x), axis=0)

    downs = lax.axis_size("down")
    last, first = face(1), face(0)
    if beside is not None:
        mine, depth_halo = lax.optimization_barrier((own, depth_halo))
        last, first, result = lax.optimization_barrier((last, first, beside(mine)))
    if downs % 2 == 0:
        even = lax.rem(lax.axis_index("down"), 2) == 0
        near = [(i, i ^ 1) for i in range(downs)]
        far = [(i, (i - 1 + 2 * (i % 2)) % downs) for i in range(downs)]
        outside = [
            lax.ppermute(jnp.where(even, last, first), "down", near),
            lax.ppermute(jnp.where(even, first, last), "down", far),
        ]
    else:
        outside = [
            lax.ppermute(last, "down", ring("down", 1)),
            lax.ppermute(first, "down", ring("down", -1)),
        ]
    if beside is not None:
        return [own, depth_halo] + sides, outside, result
    return [own, depth_halo] + sides, outside


def shared(value, axes, peers):
    return [value] + [
        lax.ppermute(value, axes, [(i, i ^ k) for i in range(peers)]) for k in range(1, peers)
    ]


def tree_sum(parts):
    while len(parts) > 1:
        parts = [parts[k] + parts[k + 1] for k in range(0, len(parts), 2)]
    return parts[0]


def body(positions, velocities, sphere_radii, counts, coefficients):
    down, cross, depth = (lax.axis_size(name) for name in ("down", "cross", "depth"))
    grid = (2 * down, 2 * cross, 2 * depth)
    nodes = grid[0] * grid[1] * grid[2]
    params = pltpu.CompilerParams(vmem_limit_bytes=VMEM_LIMIT)
    vector_shape = jax.ShapeDtypeStruct((3, 2, 2, 2, S), F32)

    def rows(count):
        return jax.ShapeDtypeStruct((count, S), F32)

    def call(kernel, inputs, outputs, scratch, name, vectors=0):
        return pl.pallas_call(
            kernel,
            out_shape=outputs,
            in_specs=[VMEM_SPEC] * len(inputs),
            out_specs=jax.tree.map(lambda _: VMEM_SPEC, outputs),
            scratch_shapes=scratch,
            compiler_params=params,
            cost_estimate=pl.CostEstimate(flops=vectors, bytes_accessed=1 << 20, transcendentals=0),
            name=name,
        )(*inputs)

    own, inner = pl.pallas_call(
        pack_kernel,
        out_shape=(rows(64), rows(32)),
        in_specs=[pl.BlockSpec(memory_space=pl.ANY)] * 4,
        out_specs=(VMEM_SPEC, VMEM_SPEC),
        scratch_shapes=[
            pltpu.SMEM((2, 2, 2), jnp.int32),
            pltpu.VMEM((3, 2, 2, 2, S), F32),
            pltpu.VMEM((3, 2, 2, 2, S), F32),
            pltpu.VMEM((2, 2, 2, S), F32),
            pltpu.SemaphoreType.DMA((4,)),
        ],
        compiler_params=pltpu.CompilerParams(vmem_limit_bytes=60 * 1024 * 1024),
        name="pack",
    )(counts, positions, velocities, sphere_radii)
    inside, outside = exchange(own, inner, 8, True)
    sums = call(step_inside, inside, rows(24), contact_scratch(INSIDE, 3), "step_inside", 1 << 31)
    own_speed, inner_speed = call(
        step_outside, [own, sums] + outside, (rows(32), rows(16)), contact_scratch(OUTSIDE, 3), "step_outside", 1 << 30
    )
    table = jax.ShapeDtypeStruct((64, 8 * S), BF16)
    inside_speed, outside_speed, weights = exchange(
        own_speed,
        inner_speed,
        4,
        False,
        lambda speed: call(
            functools.partial(field_weights, grid),
            [own, speed, coefficients.reshape(1, TERMS)],
            (
                table,
                table,
                jax.ShapeDtypeStruct((64, nodes), BF16),
                jax.ShapeDtypeStruct((1, TERMS), F32),
            ),
            [],
            "field_weights",
            1 << 30,
        ),
    )
    sums = call(
        field_inside, inside + inside_speed, rows(72), contact_scratch(INSIDE, 9), "field_inside", 1 << 31
    )
    force, partial = call(
        field_outside,
        [own, own_speed, sums] + outside + outside_speed + list(weights[:3]),
        (rows(24), jax.ShapeDtypeStruct((16, nodes), F32)),
        [pltpu.VMEM((16, 8 * S), F32)] + contact_scratch(OUTSIDE, 9),
        "field_outside",
        1 << 30,
    )
    partial = tree_sum(shared(partial, ("cross", "depth"), cross * depth))
    distance = 1
    while distance < down:
        other = lax.ppermute(partial, "down", [(i, i ^ distance) for i in range(down)])
        distance = distance * 2
        if distance < down:
            partial = partial + other
    velocity_new, force_next, residual_field, gram_matrix, moment = pl.pallas_call(
        functools.partial(library_kernel, grid),
        out_shape=(
            vector_shape,
            vector_shape,
            jax.ShapeDtypeStruct((2, 2, 2), F32),
            jax.ShapeDtypeStruct((TERMS, TERMS), F32),
            jax.ShapeDtypeStruct((1, TERMS), F32),
        ),
        in_specs=[VMEM_SPEC] * 5,
        out_specs=(VMEM_SPEC,) * 5,
        scratch_shapes=[pltpu.VMEM((TERMS, nodes), F32)],
        compiler_params=params,
        name="library",
    )(weights[3], partial, other, own_speed, force)
    return (velocity_new, force_next, residual_field, gram_matrix, moment.reshape(TERMS))


def solution(mesh):
    return jax.shard_map(
        body,
        mesh=mesh,
        in_specs=(
            P(None, ("groups", "down"), "cross", "depth", None),
            P(None, ("groups", "down"), "cross", "depth", None),
            P(("groups", "down"), "cross", "depth", None),
            P(("groups", "down"), "cross", "depth"),
            P(),
        ),
        out_specs=(
            P(None, ("groups", "down"), "cross", "depth", None),
            P(None, ("groups", "down"), "cross", "depth", None),
            P(("groups", "down"), "cross", "depth"),
            P("groups", None),
            P("groups"),
        ),
        check_vma=False,
    )
```

```python
import functools

import jax
import jax.numpy as jnp
from jax import lax
from jax.experimental import pallas as pl
from jax.experimental.pallas import tpu as pltpu
from jax.sharding import PartitionSpec as P

STIFFNESS = 100.0
DAMPING = 20.0
TIME_STEP = 0.05
KERNEL_WIDTH = 0.4
KERNEL_NORM = 64.0
SOFTENING = 0.0001
RADIUS_REF = 0.1
MASS_SHIFT = 0.1
DEAD = -1000.0
TERMS = 48
S = 128
SPREAD = 4
F32 = jnp.float32
BF16 = jnp.bfloat16
CELLS = tuple((a, b, z) for a in range(2) for b in range(2) for z in range(2))
PAIR_LIST = ((0, 0), (0, 1), (0, 2), (1, 1), (1, 2), (2, 2))
VMEM_SPEC = pl.BlockSpec(memory_space=pltpu.VMEM)
SMEM_SPEC = pl.BlockSpec(memory_space=pltpu.SMEM)
VMEM_LIMIT = 48 * 1024 * 1024


def row_ids(shape):
    return lax.broadcasted_iota(jnp.int32, shape, 0)


def lane_ids(shape):
    return lax.broadcasted_iota(jnp.int32, shape, 1)


def one_hot(condition):
    return jnp.where(condition, 1.0, 0.0).astype(BF16)


def split(value):
    high = value.astype(BF16)
    return high, value - high.astype(F32)


def matmul(left, right):
    return lax.dot_general(left, right, (((1,), (0,)), ((), ())), preferred_element_type=F32)


def matmul_turned(left, right):
    return lax.dot_general(left, right, (((1,), (1,)), ((), ())), preferred_element_type=F32)


def lane_gather(table, index):
    return jnp.take_along_axis(table, index, axis=1)


def pack_kernel(
    counts_hbm, positions_hbm, velocities_hbm, radii_hbm, own, inner, counts, positions, velocities, radii, arrived
):
    copies = [
        pltpu.make_async_copy(source, target, arrived.at[k])
        for k, (source, target) in enumerate(
            (
                (counts_hbm, counts),
                (positions_hbm, positions),
                (velocities_hbm, velocities),
                (radii_hbm, radii),
            )
        )
    ]
    for copy in copies:
        copy.start()
    for copy in copies:
        copy.wait()
    depth = lax.axis_index("depth")
    lanes = lane_ids((1, S))

    def layer(ref, at, z):
        rows = ref[at]
        return jnp.where(depth == z, rows[0:1], rows[1:2])

    for c, (a, b, z) in enumerate(CELLS):
        for k in range(3):
            own[c * 8 + k : c * 8 + k + 1, :] = layer(positions, (k, a, b), z)
            own[c * 8 + 3 + k : c * 8 + 4 + k, :] = layer(velocities, (k, a, b), z)
        count = jnp.where(depth == z, counts[a, b, 0], counts[a, b, 1])
        own[c * 8 + 6 : c * 8 + 7, :] = jnp.where(lanes < count, layer(radii, (a, b), z), DEAD)
        own[c * 8 + 7 : c * 8 + 8, :] = jnp.zeros((1, S), F32)
    for column in range(4):
        inner[column * 8 : column * 8 + 8, :] = own[column * 16 + 8 : column * 16 + 16, :]


def local_state(raw, centre):
    rows = row_ids(raw.shape)
    shift = jnp.where(rows == 0, centre[0], jnp.where(rows == 1, centre[1], centre[2]))
    return jnp.where(rows < 3, raw + shift, raw)


def plane_reader(refs, height):
    own, depth_halo, sides = refs[0], refs[1], refs[2:]

    def read(ref, cell):
        return ref[cell * height : cell * height + height, :]

    def cell(x, y, slot):
        a = x - 1
        if y in (1, 2):
            return read(own, a * 4 + (y - 1) * 2 + slot) if slot < 2 else read(depth_halo, a * 2 + y - 1)
        if len(sides) == 4:
            before, after, diag_before, diag_after = sides
            if slot < 2:
                return read(before if y == 0 else after, a * 2 + slot)
            return read(diag_before if y == 0 else diag_after, a)
        b = 1 if y == 0 else 0
        if slot < 2:
            return read(sides[0], a * 4 + b * 2 + slot)
        return read(sides[0], 8 + a * 2 + b) if len(sides) == 1 else read(sides[1], a * 2 + b)

    return cell


def down_reader(refs, height):
    even = lax.rem(lax.axis_index("down"), 2) == 0
    swapped = lax.axis_size("down") % 2 == 0

    def cell(x, y, slot):
        if y in (1, 2):
            place = (y - 1) * 2 + slot if slot < 2 else 4 + y - 1
        else:
            side = 0 if y == 0 else 1
            place = 6 + side * 2 + slot if slot < 2 else 10 + side
        one, two = (ref[place * height : place * height + height, :] for ref in refs)
        if swapped:
            return jnp.where(even, two, one) if x == 0 else jnp.where(even, one, two)
        return one if x == 0 else two

    return cell


def centre_of(x, y, slot, depth):
    side = 0.5 - depth.astype(F32)
    return (x - 1.5, y - 1.5, (-1.0, 1.0, 3.0)[slot] * side)


BLOCK = tuple((x, y, slot) for x in (1, 2) for y in (1, 2) for slot in (0, 1))
PLANE = tuple(
    (x, y, slot) for x in (1, 2) for y in range(4) for slot in range(3) if (x, y, slot) not in BLOCK
)
INSIDE = tuple((x, y, slot) for x in (1, 2) for y in range(4) for slot in range(3))
OUTSIDE = tuple((x, y, slot) for x in (0, 3) for y in range(4) for slot in range(3))


def stepped_state(old, speed, centre):
    rows = row_ids((3, S))
    shift = jnp.where(rows == 0, centre[0], jnp.where(rows == 1, centre[1], centre[2]))
    return (old[0:3] + TIME_STEP * speed[0:3]) + shift, speed[0:3], old[6:8]


def contact_scratch(cells, width):
    rows = len(cells)
    return [
        pltpu.VMEM((rows * 8, S), F32),
        pltpu.VMEM((8 * 8, S), F32),
        pltpu.VMEM((8 * rows, S), jnp.int32),
        pltpu.VMEM((8 * rows, S), jnp.int32),
        pltpu.VMEM((8 * rows, S), jnp.int32),
        pltpu.VMEM((8 * rows, S), jnp.int32),
        pltpu.VMEM((18 * 8 * S, 32), F32),
        pltpu.VMEM((width * 8 * 8, S), F32),
    ]


def contact_sums(cells, width, chunk, scratch):
    local_ref, mine_ref, index_ref, base_ref, amount_ref, chosen_ref, list_ref, sum_ref = scratch
    count = len(cells)
    span = 16 if cells == OUTSIDE else count

    def first_row(a):
        return 8 if cells == OUTSIDE and a == 1 else 0

    def beside(a, b, z):
        return [
            n
            for n, (x, y, slot) in enumerate(cells)
            if abs(x - 1 - a) <= 1 and abs(y - 1 - b) <= 1 and abs(slot - z) <= 1
        ]

    sum_ref[...] = jnp.zeros((width * 64, S), F32)
    place = [local_ref[pl.ds(k, count, stride=8), :] for k in range(3)]
    radius = local_ref[pl.ds(6, count, stride=8), :]
    rows = row_ids((count, S))
    masks = []
    for c, (a, b, z) in enumerate(CELLS):
        mine = mine_ref[c * 8 : c * 8 + 8, :]
        live = mine[6:7] > 0.0
        low = jnp.min(jnp.where(live, mine, 1e9), axis=1, keepdims=True)
        high = jnp.max(jnp.where(live, mine, -1e9), axis=1, keepdims=True)
        part = slice(first_row(a), first_row(a) + span)
        reach = radius[part] + high[6:7]
        near = reach > 0.0
        inside = set(beside(a, b, z))
        for n in range(part.start, part.stop):
            if n not in inside:
                near = jnp.logical_and(near, rows[part] != n)
        for k in range(3):
            near = jnp.logical_and(near, place[k][part] + reach > low[k : k + 1])
            near = jnp.logical_and(near, place[k][part] - reach < high[k : k + 1])
        masks.append(jnp.where(near, 1.0, 0.0).astype(F32))
    mask = jnp.concatenate(masks, axis=0).astype(BF16)
    upper = one_hot(row_ids((S, 2 * S)) <= lane_ids((S, 2 * S)))
    sums = matmul(mask, upper)
    prefix, amount = sums[:, :S], sums[:, S:]
    before = one_hot(lane_ids((span, span)) < row_ids((span, span)))
    total = None
    for c in range(8):
        part = amount[c * span : (c + 1) * span]
        base = matmul(before, part.astype(BF16))
        base_ref[c * span : (c + 1) * span, :] = base.astype(jnp.int32)
        listed = base[span - 1 : span] + part[span - 1 : span]
        total = listed if total is None else jnp.maximum(total, listed)
    most = total.astype(jnp.int32)[0, 0]
    amount_ref[0 : 8 * span, :] = amount.astype(jnp.int32)
    wanted = lane_ids((8 * span, S)).astype(F32)
    index = jnp.zeros((8 * span, S), jnp.int32)
    for step in (64, 32, 16, 8, 4, 2, 1):
        probe = lane_gather(prefix, index + (step - 1))
        index = jnp.where(probe <= wanted, index + step, index)
    index_ref[0 : 8 * span, :] = index
    empty = jnp.where(row_ids((8, S)) == 6, DEAD, 0.0).astype(F32)

    def gather_tiles(t, carry):
        want = t * S + lane_ids((8 * span, S)) - base_ref[0 : 8 * span, :]
        valid = jnp.logical_and(want >= 0, want < amount_ref[0 : 8 * span, :])
        source = lane_gather(index_ref[0 : 8 * span, :], jnp.clip(want, 0, S - 1))
        chosen_ref[0 : 8 * span, :] = jnp.where(valid, source, -1)
        for c, (a, b, z) in enumerate(CELLS):
            tile = empty
            for n in beside(a, b, z):
                row = c * span + n - first_row(a)
                pick = jnp.broadcast_to(chosen_ref[row : row + 1, :], (8, S))
                values = lane_gather(local_ref[n * 8 : n * 8 + 8, :], jnp.maximum(pick, 0))
                tile = jnp.where(pick >= 0, values, tile)
            high = tile.astype(BF16).astype(F32)
            rest = tile - high
            middle = rest.astype(BF16).astype(F32)
            turned = jnp.transpose(jnp.concatenate([high, middle, rest - middle, tile], axis=0))
            for part in range(S // chunk):
                start = pl.multiple_of(t * (8 * S) + (part * 8 + c) * chunk, chunk)
                list_ref[pl.ds(start, chunk), :] = turned[part * chunk : (part + 1) * chunk]
        return carry

    gather_tiles(0, 0)
    lax.fori_loop(1, (most + (S - 1)) // S, gather_tiles, 0)

    selector = jnp.logical_and(
        row_ids((32, SPREAD * S)) % 8 == lane_ids((32, SPREAD * S)) // S, row_ids((32, SPREAD * S)) < 24
    )
    selector = one_hot(selector)

    def pair_step(step, carry):
        every = list_ref[pl.ds(pl.multiple_of(step * (8 * chunk), 8 * chunk), 8 * chunk), :]
        spread = matmul(every.astype(BF16), selector)
        for c in range(8):
            listed = every[c * chunk : (c + 1) * chunk]
            me = [jnp.broadcast_to(mine_ref[c * 8 + k : c * 8 + k + 1, :], (8, S)) for k in range(7)]
            added = [None] * width
            for block in range(chunk // 8):
                row = c * chunk + block * 8
                other = [spread[row : row + 8, k * S : (k + 1) * S] for k in range(SPREAD)]
                other += [
                    jnp.broadcast_to(listed[block * 8 : block * 8 + 8, 24 + k : 25 + k], (8, S))
                    for k in range(SPREAD, 7)
                ]
                r = [me[k] - other[k] for k in range(3)]
                u = [me[3 + k] - other[3 + k] for k in range(3)]
                squared = r[0] * r[0] + r[1] * r[1] + r[2] * r[2] + SOFTENING
                inverse = lax.rsqrt(squared)
                along = u[0] * r[0] + u[1] * r[1] + u[2] * r[2]
                overlap = jnp.maximum((me[6] + other[6]) * inverse - 1.0, 0.0)
                weight = overlap * (STIFFNESS - (DAMPING * along) * inverse)
                terms = [weight * r[k] for k in range(3)]
                if width == 9:
                    terms += [terms[left] * r[right] for left, right in PAIR_LIST]
                added = [
                    term if total is None else total + term for total, term in zip(added, terms)
                ]
            for k in range(width):
                row = (k * 8 + c) * 8
                sum_ref[row : row + 8, :] += added[k]
        return carry

    lax.fori_loop(0, (most + (chunk - 1)) // chunk, pair_step, 0)
    out = []
    for k in range(width):
        parts = [sum_ref[pl.ds(k * 64 + sub, 8, stride=8), :] for sub in range(8)]
        while len(parts) > 1:
            parts = [parts[i] + parts[i + 1] for i in range(0, len(parts), 2)]
        out.append(parts[0])
    return jnp.concatenate(out, axis=0)


def mass_of(radius):
    scaled = radius / RADIUS_REF
    return scaled * scaled * scaled


def fill_start(cells, read, own, depth, scratch):
    for n, (x, y, slot) in enumerate(cells):
        scratch[0][n * 8 : n * 8 + 8, :] = local_state(read(x, y, slot), centre_of(x, y, slot, depth))
    for c, (a, b, z) in enumerate(CELLS):
        scratch[1][c * 8 : c * 8 + 8, :] = local_state(
            own[c * 8 : c * 8 + 8, :], centre_of(a + 1, b + 1, z, depth)
        )


def place_state(ref, start, state):
    ref[start : start + 3, :] = state[0]
    ref[start + 3 : start + 6, :] = state[1]
    ref[start + 6 : start + 8, :] = state[2]


def fill_stepped(cells, read, speed, own, own_speed, depth, scratch):
    for n, (x, y, slot) in enumerate(cells):
        state = stepped_state(read(x, y, slot), speed(x, y, slot), centre_of(x, y, slot, depth))
        place_state(scratch[0], n * 8, state)
    for c, (a, b, z) in enumerate(CELLS):
        state = stepped_state(
            own[c * 8 : c * 8 + 8, :],
            own_speed[c * 4 : c * 4 + 4, :],
            centre_of(a + 1, b + 1, z, depth),
        )
        place_state(scratch[1], c * 8, state)


def step_inside(*refs):
    pieces, sums_out, scratch = refs[:-9], refs[-9], refs[-8:]
    fill_start(INSIDE, plane_reader(pieces, 8), pieces[0], lax.axis_index("depth"), scratch)
    sums_out[...] = contact_sums(INSIDE, 3, 64, scratch)


def step_outside(own, sums_in, near, far, own_out, inner_out, *scratch):
    fill_start(OUTSIDE, down_reader((near, far), 8), own, lax.axis_index("depth"), scratch)
    sums = sums_in[...] + contact_sums(OUTSIDE, 3, 32, scratch)
    radius = own[pl.ds(6, 8, stride=8), :]
    safe_mass = jnp.where(radius > 0.0, mass_of(radius), 1.0)
    for k in range(3):
        velocity = own[pl.ds(3 + k, 8, stride=8), :] + TIME_STEP * sums[k * 8 : k * 8 + 8] / safe_mass
        for c in range(8):
            own_out[c * 4 + k : c * 4 + k + 1, :] = velocity[c : c + 1]
    for c in range(8):
        own_out[c * 4 + 3 : c * 4 + 4, :] = jnp.zeros((1, S), F32)
    for column in range(4):
        inner_out[column * 4 : column * 4 + 4, :] = own_out[column * 8 + 4 : column * 8 + 8, :]


def field_weights(grid, own, own_speed, coefficients, high_out, low_out, chosen_out, model_out):
    model_out[...] = coefficients[...]
    depth = lax.axis_index("depth")
    down = lax.axis_index("down")
    cross = lax.axis_index("cross")
    rows = row_ids((64, S))
    near_x, near_y, near_z = rows // 16 - 1, (rows // 4) % 4 - 1, rows % 4 - 1
    centres = [index.astype(F32) - 0.5 for index in (near_x, near_y, near_z)]
    kernels = []
    for c, (a, b, z) in enumerate(CELLS):
        place = stepped_state(
            own[c * 8 : c * 8 + 8, :],
            own_speed[c * 4 : c * 4 + 4, :],
            centre_of(a + 1, b + 1, z, depth),
        )[0]
        squared = jnp.zeros((64, S), F32)
        for k in range(3):
            gap = place[k : k + 1] - centres[k]
            squared = squared + gap * gap
        kernel = jnp.exp(squared * (-0.5 / (KERNEL_WIDTH * KERNEL_WIDTH))) / KERNEL_NORM
        beside = jnp.logical_and(
            jnp.logical_and(jnp.abs(near_x - a) <= 1, jnp.abs(near_y - b) <= 1),
            jnp.abs(near_z - jnp.where(depth == z, 0, 1)) <= 1,
        )
        kernels.append(jnp.where(beside, kernel, 0.0))
    kernel_high, kernel_low = split(jnp.concatenate(kernels, axis=1))
    high_out[...] = kernel_high
    low_out[...] = kernel_low.astype(BF16)
    size_x, size_y, size_z = grid
    nodes = size_x * size_y * size_z
    lanes = lane_ids((64, nodes))
    row = row_ids((64, nodes))
    target_x = (down * 2 + row // 16 - 1 + size_x) % size_x
    target_y = (cross * 2 + (row // 4) % 4 - 1 + size_y) % size_y
    target_z = depth * 2 + row % 4 - 1
    inside = jnp.logical_and(target_z >= 0, target_z < size_z)
    target = (target_x * size_y + target_y) * size_z + target_z
    chosen_out[...] = one_hot(jnp.logical_and(inside, lanes == target))


def field_inside(*refs):
    split_at = (len(refs) - 9) // 2
    pieces, speeds, sums_out, scratch = refs[:split_at], refs[split_at:-9], refs[-9], refs[-8:]
    read, speed = plane_reader(pieces, 8), plane_reader(speeds, 4)
    fill_stepped(INSIDE, read, speed, pieces[0], speeds[0], lax.axis_index("depth"), scratch)
    sums_out[...] = contact_sums(INSIDE, 9, 64, scratch)


def field_outside(
    own, own_speed, sums_in, near_old, far_old, near_speed, far_speed, kernel_high, kernel_low, chosen,
    force_out, node_out, moment_ref, *scratch
):
    depth = lax.axis_index("depth")
    read, speed = down_reader((near_old, far_old), 8), down_reader((near_speed, far_speed), 4)
    fill_stepped(OUTSIDE, read, speed, own, own_speed, depth, scratch)
    sums = sums_in[...] + contact_sums(OUTSIDE, 9, 32, scratch)
    force_out[...] = sums[0:24]
    radius = own[pl.ds(6, 8, stride=8), :]
    mass = jnp.where(radius > 0.0, mass_of(radius), 0.0)
    moments = [mass] + [mass * own_speed[pl.ds(k, 8, stride=4), :] for k in range(3)]
    moments += [0.5 * sums[k * 8 : k * 8 + 8] for k in range(3, 9)]
    moment_ref[...] = jnp.zeros((16, 8 * S), F32)
    for m, moment in enumerate(moments):
        for c in range(8):
            moment_ref[m : m + 1, c * S : (c + 1) * S] = moment[c : c + 1]
    moment_high, moment_low = split(moment_ref[...])
    wide_part = matmul_turned(
        jnp.concatenate([moment_high, moment_low.astype(BF16)], axis=0), kernel_high[...]
    )
    near = wide_part[0:16] + wide_part[16:32] + matmul_turned(moment_high, kernel_low[...])
    near_high, rest = split(near)
    near_middle, near_low = split(rest)
    placed = matmul(
        jnp.concatenate([near_high, near_middle, near_low.astype(BF16)], axis=0), chosen[...]
    )
    node_out[...] = placed[0:16] + placed[16:32] + placed[32:48]


def library_kernel(
    grid, coefficients, parts, speed, force, velocity_out, force_out, residual_out, gram_out, moment_out, terms
):
    flat = lax.axis_index("depth") == 0
    for k in range(3):
        for a in range(2):
            for b in range(2):
                c = a * 4 + b * 2
                layers = [speed[(c + z) * 4 + k : (c + z) * 4 + k + 1, :] for z in range(2)]
                pulls = [force[k * 8 + c + z : k * 8 + c + z + 1, :] for z in range(2)]
                for z in range(2):
                    velocity_out[k, a, b, z : z + 1, :] = jnp.where(flat, layers[z], layers[1 - z])
                    force_out[k, a, b, z : z + 1, :] = jnp.where(flat, pulls[z], pulls[1 - z])
    fields = jnp.sum(parts[...], axis=0)
    size_x, size_y, size_z = grid
    nodes = size_x * size_y * size_z
    lanes = lax.broadcasted_iota(jnp.int32, (1, nodes), 1)
    node_x = lanes // (size_y * size_z)
    node_y = (lanes // size_z) % size_y
    node_z = lanes % size_z
    rows = row_ids((8, nodes))
    density = fields[0:1]
    values = jnp.where(rows == 0, fields[0:8], fields[0:8] / (density + MASS_SHIFT))

    def moved(value, step):
        return pltpu.roll(value, step % nodes, 1)

    plane = size_y * size_z
    slope_x = (moved(values, -plane) - moved(values, plane)) * 0.5
    after_y = jnp.where(
        node_y == size_y - 1, moved(values, (size_y - 1) * size_z), moved(values, -size_z)
    )
    before_y = jnp.where(
        node_y == 0, moved(values, -(size_y - 1) * size_z), moved(values, size_z)
    )
    slope_y = (after_y - before_y) * 0.5
    after_z = jnp.where(node_z == size_z - 1, 0.0, moved(values, -1))
    before_z = jnp.where(node_z == 0, 0.0, moved(values, 1))
    slope_z = (after_z - before_z) * 0.5
    slopes = [[table[k : k + 1] for k in range(4)] for table in (slope_x, slope_y, slope_z)]
    strain = [
        [0.5 * (slopes[left][1 + right] + slopes[right][1 + left]) for right in range(3)]
        for left in range(3)
    ]
    divergence = strain[0][0] + strain[1][1] + strain[2][2]
    rate_sum = jnp.zeros_like(density)
    for left in range(3):
        for right in range(3):
            entry = strain[left][right]
            if left == right:
                entry = entry - divergence / 3.0
            rate_sum = rate_sum + entry * entry
    shear_rate = jnp.sqrt(2.0 * rate_sum + 0.01)
    stress = [fields[4 + k : 5 + k] for k in range(6)]
    pressure = (stress[0] + stress[3] + stress[5]) / 3.0
    deviator = (
        (stress[0] - pressure) ** 2
        + (stress[3] - pressure) ** 2
        + (stress[5] - pressure) ** 2
        + 2.0 * (stress[1] ** 2 + stress[2] ** 2 + stress[4] ** 2)
    )
    shear_stress = jnp.sqrt(0.5 * deviator + 0.01)
    pressure_scale = jnp.sqrt(pressure * pressure + 1.0)
    friction = shear_stress / pressure_scale
    features = [
        density,
        pressure / pressure_scale,
        shear_rate,
        shear_rate / jnp.sqrt(pressure_scale),
        divergence,
        slopes[0][0],
        slopes[1][0],
        slopes[2][0],
    ]
    entries = list(features)
    for left in range(8):
        for right in range(left, 8):
            entries.append(features[left] * features[right])
    for left in range(1, 5):
        entries.append(features[left] * features[left] * features[left])
    for k, entry in enumerate(entries):
        terms[k : k + 1, :] = entry
    table = terms[...]
    model = lax.dot_general(
        jnp.broadcast_to(coefficients[...], (8, TERMS)),
        table,
        (((1,), (0,)), ((), ())),
        precision=lax.Precision.HIGHEST,
        preferred_element_type=F32,
    )
    residual = friction - model[0:1]
    gram_out[...] = (
        lax.dot_general(
            table,
            table,
            (((1,), (1,)), ((), ())),
            precision=lax.Precision.HIGHEST,
            preferred_element_type=F32,
        )
        / nodes
    )
    moment = lax.dot_general(
        jnp.broadcast_to(friction, (8, nodes)),
        table,
        (((1,), (1,)), ((), ())),
        precision=lax.Precision.HIGHEST,
        preferred_element_type=F32,
    )
    moment_out[...] = moment[0:1] / nodes
    down = lax.axis_index("down")
    cross = lax.axis_index("cross")
    depth = lax.axis_index("depth")
    b_rows = lax.broadcasted_iota(jnp.int32, (2, 1), 0)
    z_lanes = lax.broadcasted_iota(jnp.int32, (2, 2), 1)
    for a in range(2):
        mine = jnp.logical_and(node_x == down * 2 + a, node_y == cross * 2 + b_rows)
        column = [
            jnp.sum(
                jnp.where(jnp.logical_and(mine, node_z == depth * 2 + z), residual, 0.0),
                axis=1,
                keepdims=True,
            )
            for z in range(2)
        ]
        residual_out[a] = jnp.where(z_lanes == 0, column[0], column[1])


def ring(axis, step):
    peers = lax.axis_size(axis)
    return [(i, (i + step) % peers) for i in range(peers)]


def exchange(own, inner, height, joined, beside=None):
    cross = lax.axis_size("cross")

    def cells(block, first, count):
        return block[first * height : (first + count) * height]

    if cross == 2 and not joined:
        side = lax.ppermute(own, "cross", [(0, 1), (1, 0)])
    depth_halo = lax.ppermute(inner, "depth", [(0, 1), (1, 0)])
    if cross == 2:
        if joined:
            side = lax.ppermute(
                jnp.concatenate([own, depth_halo], axis=0), "cross", [(0, 1), (1, 0)]
            )
            diag = cells(side, 8, 4)
            sides = [side]
        else:
            diag = lax.ppermute(inner, ("cross", "depth"), [(i, 3 - i) for i in range(4)])
            sides = [side, diag]

        def lateral(x):
            return [
                cells(side, x * 4 + 2, 2),
                cells(side, x * 4, 2),
                cells(diag, x * 2 + 1, 1),
                cells(diag, x * 2, 1),
            ]

    else:
        pairs = [(i * 2 + j, ((i + 1) % cross) * 2 + 1 - j) for i in range(cross) for j in range(2)]
        back = [(i * 2 + j, ((i - 1) % cross) * 2 + 1 - j) for i in range(cross) for j in range(2)]
        last = jnp.concatenate([cells(own, 2, 2), cells(own, 6, 2)], axis=0)
        first = jnp.concatenate([cells(own, 0, 2), cells(own, 4, 2)], axis=0)
        last_inner = jnp.concatenate([cells(inner, 1, 1), cells(inner, 3, 1)], axis=0)
        first_inner = jnp.concatenate([cells(inner, 0, 1), cells(inner, 2, 1)], axis=0)
        before = lax.ppermute(last, "cross", ring("cross", 1))
        after = lax.ppermute(first, "cross", ring("cross", -1))
        diag_before = lax.ppermute(last_inner, ("cross", "depth"), pairs)
        diag_after = lax.ppermute(first_inner, ("cross", "depth"), back)
        sides = [before, after, diag_before, diag_after]

        def lateral(x):
            return [
                cells(before, x * 2, 2),
                cells(after, x * 2, 2),
                cells(diag_before, x, 1),
                cells(diag_after, x, 1),
            ]

    def face(x):
        return jnp.concatenate([cells(own, x * 4, 4), cells(depth_halo, x * 2, 2)] + lateral(x), axis=0)

    downs = lax.axis_size("down")
    last, first = face(1), face(0)
    if beside is not None:
        mine, depth_halo = lax.optimization_barrier((own, depth_halo))
        last, first, result = lax.optimization_barrier((last, first, beside(mine)))
    if downs % 2 == 0:
        even = lax.rem(lax.axis_index("down"), 2) == 0
        near = [(i, i ^ 1) for i in range(downs)]
        far = [(i, (i - 1 + 2 * (i % 2)) % downs) for i in range(downs)]
        outside = [
            lax.ppermute(jnp.where(even, last, first), "down", near),
            lax.ppermute(jnp.where(even, first, last), "down", far),
        ]
    else:
        outside = [
            lax.ppermute(last, "down", ring("down", 1)),
            lax.ppermute(first, "down", ring("down", -1)),
        ]
    if beside is not None:
        return [own, depth_halo] + sides, outside, result
    return [own, depth_halo] + sides, outside


def shared(value, axes, peers):
    return [value] + [
        lax.ppermute(value, axes, [(i, i ^ k) for i in range(peers)]) for k in range(1, peers)
    ]


def tree_sum(parts):
    while len(parts) > 1:
        parts = [parts[k] + parts[k + 1] for k in range(0, len(parts), 2)]
    return parts[0]


def body(positions, velocities, sphere_radii, counts, coefficients):
    down, cross, depth = (lax.axis_size(name) for name in ("down", "cross", "depth"))
    grid = (2 * down, 2 * cross, 2 * depth)
    nodes = grid[0] * grid[1] * grid[2]
    params = pltpu.CompilerParams(vmem_limit_bytes=VMEM_LIMIT)
    vector_shape = jax.ShapeDtypeStruct((3, 2, 2, 2, S), F32)

    def rows(count):
        return jax.ShapeDtypeStruct((count, S), F32)

    def call(kernel, inputs, outputs, scratch, name, vectors=0):
        return pl.pallas_call(
            kernel,
            out_shape=outputs,
            in_specs=[VMEM_SPEC] * len(inputs),
            out_specs=jax.tree.map(lambda _: VMEM_SPEC, outputs),
            scratch_shapes=scratch,
            compiler_params=params,
            cost_estimate=pl.CostEstimate(flops=vectors, bytes_accessed=1 << 20, transcendentals=0),
            name=name,
        )(*inputs)

    own, inner = pl.pallas_call(
        pack_kernel,
        out_shape=(rows(64), rows(32)),
        in_specs=[pl.BlockSpec(memory_space=pl.ANY)] * 4,
        out_specs=(VMEM_SPEC, VMEM_SPEC),
        scratch_shapes=[
            pltpu.SMEM((2, 2, 2), jnp.int32),
            pltpu.VMEM((3, 2, 2, 2, S), F32),
            pltpu.VMEM((3, 2, 2, 2, S), F32),
            pltpu.VMEM((2, 2, 2, S), F32),
            pltpu.SemaphoreType.DMA((4,)),
        ],
        compiler_params=pltpu.CompilerParams(vmem_limit_bytes=60 * 1024 * 1024),
        name="pack",
    )(counts, positions, velocities, sphere_radii)
    inside, outside = exchange(own, inner, 8, True)
    sums = call(step_inside, inside, rows(24), contact_scratch(INSIDE, 3), "step_inside", 1 << 31)
    own_speed, inner_speed = call(
        step_outside, [own, sums] + outside, (rows(32), rows(16)), contact_scratch(OUTSIDE, 3), "step_outside", 1 << 30
    )
    table = jax.ShapeDtypeStruct((64, 8 * S), BF16)
    inside_speed, outside_speed, weights = exchange(
        own_speed,
        inner_speed,
        4,
        False,
        lambda speed: call(
            functools.partial(field_weights, grid),
            [own, speed, coefficients.reshape(1, TERMS)],
            (
                table,
                table,
                jax.ShapeDtypeStruct((64, nodes), BF16),
                jax.ShapeDtypeStruct((1, TERMS), F32),
            ),
            [],
            "field_weights",
            1 << 30,
        ),
    )
    sums = call(
        field_inside, inside + inside_speed, rows(72), contact_scratch(INSIDE, 9), "field_inside", 1 << 31
    )
    force, partial = call(
        field_outside,
        [own, own_speed, sums] + outside + outside_speed + list(weights[:3]),
        (rows(24), jax.ShapeDtypeStruct((16, nodes), F32)),
        [pltpu.VMEM((16, 8 * S), F32)] + contact_scratch(OUTSIDE, 9),
        "field_outside",
        1 << 30,
    )
    partial = tree_sum(shared(partial, ("cross", "depth"), cross * depth))
    parts = lax.all_to_all(jnp.broadcast_to(partial, (down, 16, nodes)), "down", 0, 0)
    velocity_new, force_next, residual_field, gram_matrix, moment = pl.pallas_call(
        functools.partial(library_kernel, grid),
        out_shape=(
            vector_shape,
            vector_shape,
            jax.ShapeDtypeStruct((2, 2, 2), F32),
            jax.ShapeDtypeStruct((TERMS, TERMS), F32),
            jax.ShapeDtypeStruct((1, TERMS), F32),
        ),
        in_specs=[VMEM_SPEC] * 4,
        out_specs=(VMEM_SPEC,) * 5,
        scratch_shapes=[pltpu.VMEM((TERMS, nodes), F32)],
        compiler_params=params,
        name="library",
    )(weights[3], parts, own_speed, force)
    return (velocity_new, force_next, residual_field, gram_matrix, moment.reshape(TERMS))


def solution(mesh):
    return jax.shard_map(
        body,
        mesh=mesh,
        in_specs=(
            P(None, ("groups", "down"), "cross", "depth", None),
            P(None, ("groups", "down"), "cross", "depth", None),
            P(("groups", "down"), "cross", "depth", None),
            P(("groups", "down"), "cross", "depth"),
            P(),
        ),
        out_specs=(
            P(None, ("groups", "down"), "cross", "depth", None),
            P(None, ("groups", "down"), "cross", "depth", None),
            P(("groups", "down"), "cross", "depth"),
            P("groups", None),
            P("groups"),
        ),
        check_vma=False,
    )
```

```python
import functools

import jax
import jax.numpy as jnp
from jax import lax
from jax.experimental import pallas as pl
from jax.experimental.pallas import tpu as pltpu
from jax.sharding import PartitionSpec as P

STIFFNESS = 100.0
DAMPING = 20.0
TIME_STEP = 0.05
KERNEL_WIDTH = 0.4
KERNEL_NORM = 64.0
SOFTENING = 0.0001
RADIUS_REF = 0.1
MASS_SHIFT = 0.1
DEAD = -1000.0
TERMS = 48
S = 128
SPREAD = 4
F32 = jnp.float32
BF16 = jnp.bfloat16
CELLS = tuple((a, b, z) for a in range(2) for b in range(2) for z in range(2))
PAIR_LIST = ((0, 0), (0, 1), (0, 2), (1, 1), (1, 2), (2, 2))
VMEM_SPEC = pl.BlockSpec(memory_space=pltpu.VMEM)
SMEM_SPEC = pl.BlockSpec(memory_space=pltpu.SMEM)
VMEM_LIMIT = 48 * 1024 * 1024


def row_ids(shape):
    return lax.broadcasted_iota(jnp.int32, shape, 0)


def lane_ids(shape):
    return lax.broadcasted_iota(jnp.int32, shape, 1)


def one_hot(condition):
    return jnp.where(condition, 1.0, 0.0).astype(BF16)


def split(value):
    high = value.astype(BF16)
    return high, value - high.astype(F32)


def matmul(left, right):
    return lax.dot_general(left, right, (((1,), (0,)), ((), ())), preferred_element_type=F32)


def matmul_turned(left, right):
    return lax.dot_general(left, right, (((1,), (1,)), ((), ())), preferred_element_type=F32)


def lane_gather(table, index):
    return jnp.take_along_axis(table, index, axis=1)


def pack_kernel(
    counts_hbm, positions_hbm, velocities_hbm, radii_hbm, own, inner, counts, positions, velocities, radii, arrived
):
    copies = [
        pltpu.make_async_copy(source, target, arrived.at[k])
        for k, (source, target) in enumerate(
            (
                (counts_hbm, counts),
                (positions_hbm, positions),
                (velocities_hbm, velocities),
                (radii_hbm, radii),
            )
        )
    ]
    for copy in copies:
        copy.start()
    for copy in copies:
        copy.wait()
    depth = lax.axis_index("depth")
    lanes = lane_ids((1, S))

    def layer(ref, at, z):
        rows = ref[at]
        return jnp.where(depth == z, rows[0:1], rows[1:2])

    for c, (a, b, z) in enumerate(CELLS):
        for k in range(3):
            own[c * 8 + k : c * 8 + k + 1, :] = layer(positions, (k, a, b), z)
            own[c * 8 + 3 + k : c * 8 + 4 + k, :] = layer(velocities, (k, a, b), z)
        count = jnp.where(depth == z, counts[a, b, 0], counts[a, b, 1])
        own[c * 8 + 6 : c * 8 + 7, :] = jnp.where(lanes < count, layer(radii, (a, b), z), DEAD)
        own[c * 8 + 7 : c * 8 + 8, :] = jnp.zeros((1, S), F32)
    for column in range(4):
        inner[column * 8 : column * 8 + 8, :] = own[column * 16 + 8 : column * 16 + 16, :]


def local_state(raw, centre):
    rows = row_ids(raw.shape)
    shift = jnp.where(rows == 0, centre[0], jnp.where(rows == 1, centre[1], centre[2]))
    return jnp.where(rows < 3, raw + shift, jnp.where(rows < 6, DAMPING * raw, raw))


def plane_reader(refs, height):
    own, depth_halo, sides = refs[0], refs[1], refs[2:]

    def read(ref, cell):
        return ref[cell * height : cell * height + height, :]

    def cell(x, y, slot):
        a = x - 1
        if y in (1, 2):
            return read(own, a * 4 + (y - 1) * 2 + slot) if slot < 2 else read(depth_halo, a * 2 + y - 1)
        if len(sides) == 4:
            before, after, diag_before, diag_after = sides
            if slot < 2:
                return read(before if y == 0 else after, a * 2 + slot)
            return read(diag_before if y == 0 else diag_after, a)
        b = 1 if y == 0 else 0
        if slot < 2:
            return read(sides[0], a * 4 + b * 2 + slot)
        return read(sides[0], 8 + a * 2 + b) if len(sides) == 1 else read(sides[1], a * 2 + b)

    return cell


def down_reader(refs, height):
    even = lax.rem(lax.axis_index("down"), 2) == 0
    swapped = lax.axis_size("down") % 2 == 0

    def cell(x, y, slot):
        if y in (1, 2):
            place = (y - 1) * 2 + slot if slot < 2 else 4 + y - 1
        else:
            side = 0 if y == 0 else 1
            place = 6 + side * 2 + slot if slot < 2 else 10 + side
        one, two = (ref[place * height : place * height + height, :] for ref in refs)
        if swapped:
            return jnp.where(even, two, one) if x == 0 else jnp.where(even, one, two)
        return one if x == 0 else two

    return cell


def centre_of(x, y, slot, depth):
    side = 0.5 - depth.astype(F32)
    return (x - 1.5, y - 1.5, (-1.0, 1.0, 3.0)[slot] * side)


BLOCK = tuple((x, y, slot) for x in (1, 2) for y in (1, 2) for slot in (0, 1))
PLANE = tuple(
    (x, y, slot) for x in (1, 2) for y in range(4) for slot in range(3) if (x, y, slot) not in BLOCK
)
INSIDE = tuple((x, y, slot) for x in (1, 2) for y in range(4) for slot in range(3))
OUTSIDE = tuple((x, y, slot) for x in (0, 3) for y in range(4) for slot in range(3))


def stepped_state(old, speed, centre):
    rows = row_ids((3, S))
    shift = jnp.where(rows == 0, centre[0], jnp.where(rows == 1, centre[1], centre[2]))
    return (old[0:3] + TIME_STEP * speed[0:3]) + shift, DAMPING * speed[0:3], old[6:8]


def contact_scratch(cells, width):
    rows = len(cells)
    return [
        pltpu.VMEM((rows * 8, S), F32),
        pltpu.VMEM((8 * 8, S), F32),
        pltpu.VMEM((8 * rows, S), jnp.int32),
        pltpu.VMEM((8 * rows, S), jnp.int32),
        pltpu.VMEM((8 * rows, S), jnp.int32),
        pltpu.VMEM((8 * rows, S), jnp.int32),
        pltpu.VMEM((18 * 8 * S, 32), F32),
        pltpu.VMEM((width * 8 * 8, S), F32),
    ]


def store_listed(list_ref, t, c, chunk, tile):
    high = tile.astype(BF16).astype(F32)
    rest = tile - high
    middle = rest.astype(BF16).astype(F32)
    turned = jnp.transpose(jnp.concatenate([high, middle, rest - middle, tile], axis=0))
    for part in range(S // chunk):
        start = pl.multiple_of(t * (8 * S) + (part * 8 + c) * chunk, chunk)
        list_ref[pl.ds(start, chunk), :] = turned[part * chunk : (part + 1) * chunk]


def pair_step(width, chunk, mine_ref, list_ref, sum_ref):
    selector = jnp.logical_and(
        row_ids((32, SPREAD * S)) % 8 == lane_ids((32, SPREAD * S)) // S, row_ids((32, SPREAD * S)) < 24
    )
    selector = one_hot(selector)

    def one_step(step, carry):
        every = list_ref[pl.ds(pl.multiple_of(step * (8 * chunk), 8 * chunk), 8 * chunk), :]
        spread = matmul(every.astype(BF16), selector)
        for c in range(8):
            listed = every[c * chunk : (c + 1) * chunk]
            me = [jnp.broadcast_to(mine_ref[c * 8 + k : c * 8 + k + 1, :], (8, S)) for k in range(7)]
            added = [None] * width
            for block in range(chunk // 8):
                row = c * chunk + block * 8
                other = [spread[row : row + 8, k * S : (k + 1) * S] for k in range(SPREAD)]
                other += [
                    jnp.broadcast_to(listed[block * 8 : block * 8 + 8, 24 + k : 25 + k], (8, S))
                    for k in range(SPREAD, 7)
                ]
                r = [me[k] - other[k] for k in range(3)]
                u = [me[3 + k] - other[3 + k] for k in range(3)]
                squared = r[0] * r[0] + r[1] * r[1] + r[2] * r[2] + SOFTENING
                inverse = lax.rsqrt(squared)
                along = u[0] * r[0] + u[1] * r[1] + u[2] * r[2]
                overlap = jnp.maximum((me[6] + other[6]) * inverse - 1.0, 0.0)
                weight = overlap * (STIFFNESS - along * inverse)
                terms = [weight * r[k] for k in range(3)]
                if width == 9:
                    terms += [terms[left] * r[right] for left, right in PAIR_LIST]
                added = [
                    term if total is None else total + term for total, term in zip(added, terms)
                ]
            for k in range(width):
                row = (k * 8 + c) * 8
                sum_ref[row : row + 8, :] += added[k]
        return carry

    return one_step


def collected(width, sum_ref):
    out = []
    for k in range(width):
        parts = [sum_ref[pl.ds(k * 64 + sub, 8, stride=8), :] for sub in range(8)]
        while len(parts) > 1:
            parts = [parts[i] + parts[i + 1] for i in range(0, len(parts), 2)]
        out.append(parts[0])
    return jnp.concatenate(out, axis=0)


def contact_sums(cells, width, chunk, scratch, skip_own=False):
    local_ref, mine_ref, index_ref, base_ref, amount_ref, chosen_ref, list_ref, sum_ref = scratch
    count = len(cells)
    span = 16 if cells == OUTSIDE else count

    def first_row(a):
        return 8 if cells == OUTSIDE and a == 1 else 0

    def beside(a, b, z):
        return [
            n
            for n, (x, y, slot) in enumerate(cells)
            if abs(x - 1 - a) <= 1 and abs(y - 1 - b) <= 1 and abs(slot - z) <= 1
            and not (skip_own and (x, y, slot) == (a + 1, b + 1, z))
        ]

    sum_ref[...] = jnp.zeros((width * 64, S), F32)
    place = [local_ref[pl.ds(k, count, stride=8), :] for k in range(3)]
    radius = local_ref[pl.ds(6, count, stride=8), :]
    rows = row_ids((count, S))
    masks = []
    for c, (a, b, z) in enumerate(CELLS):
        mine = mine_ref[c * 8 : c * 8 + 8, :]
        live = mine[6:7] > 0.0
        low = jnp.min(jnp.where(live, mine, 1e9), axis=1, keepdims=True)
        high = jnp.max(jnp.where(live, mine, -1e9), axis=1, keepdims=True)
        part = slice(first_row(a), first_row(a) + span)
        reach = radius[part] + high[6:7]
        near = reach > 0.0
        inside = set(beside(a, b, z))
        for n in range(part.start, part.stop):
            if n not in inside:
                near = jnp.logical_and(near, rows[part] != n)
        for k in range(3):
            near = jnp.logical_and(near, place[k][part] + reach > low[k : k + 1])
            near = jnp.logical_and(near, place[k][part] - reach < high[k : k + 1])
        masks.append(jnp.where(near, 1.0, 0.0).astype(F32))
    mask = jnp.concatenate(masks, axis=0).astype(BF16)
    upper = one_hot(row_ids((S, 2 * S)) <= lane_ids((S, 2 * S)))
    sums = matmul(mask, upper)
    prefix, amount = sums[:, :S], sums[:, S:]
    before = one_hot(lane_ids((span, span)) < row_ids((span, span)))
    total = None
    for c in range(8):
        part = amount[c * span : (c + 1) * span]
        base = matmul(before, part.astype(BF16))
        base_ref[c * span : (c + 1) * span, :] = base.astype(jnp.int32)
        listed = base[span - 1 : span] + part[span - 1 : span]
        total = listed if total is None else jnp.maximum(total, listed)
    most = total.astype(jnp.int32)[0, 0]
    amount_ref[0 : 8 * span, :] = amount.astype(jnp.int32)
    wanted = lane_ids((8 * span, S)).astype(F32)
    index = jnp.zeros((8 * span, S), jnp.int32)
    for step in (64, 32, 16, 8, 4, 2, 1):
        probe = lane_gather(prefix, index + (step - 1))
        index = jnp.where(probe <= wanted, index + step, index)
    index_ref[0 : 8 * span, :] = index
    empty = jnp.where(row_ids((8, S)) == 6, DEAD, 0.0).astype(F32)

    def gather_tiles(t, carry):
        want = t * S + lane_ids((8 * span, S)) - base_ref[0 : 8 * span, :]
        valid = jnp.logical_and(want >= 0, want < amount_ref[0 : 8 * span, :])
        source = lane_gather(index_ref[0 : 8 * span, :], jnp.clip(want, 0, S - 1))
        chosen_ref[0 : 8 * span, :] = jnp.where(valid, source, -1)
        for c, (a, b, z) in enumerate(CELLS):
            tile = empty
            for n in beside(a, b, z):
                row = c * span + n - first_row(a)
                pick = jnp.broadcast_to(chosen_ref[row : row + 1, :], (8, S))
                values = lane_gather(local_ref[n * 8 : n * 8 + 8, :], jnp.maximum(pick, 0))
                tile = jnp.where(pick >= 0, values, tile)
            store_listed(list_ref, t, c, chunk, tile)
        return carry

    gather_tiles(0, 0)
    lax.fori_loop(1, (most + (S - 1)) // S, gather_tiles, 0)

    lax.fori_loop(
        0, (most + (chunk - 1)) // chunk, pair_step(width, chunk, mine_ref, list_ref, sum_ref), 0
    )
    return collected(width, sum_ref)


def own_sums(width, scratch):
    mine_ref, list_ref, sum_ref = scratch
    sum_ref[...] = jnp.zeros((width * 64, S), F32)
    for c in range(8):
        store_listed(list_ref, 0, c, 64, mine_ref[c * 8 : c * 8 + 8, :])
    step = pair_step(width, 64, mine_ref, list_ref, sum_ref)
    for part in range(2):
        step(part, 0)
    return collected(width, sum_ref)


def mass_of(radius):
    scaled = radius / RADIUS_REF
    return scaled * scaled * scaled


def fill_start(cells, read, own, depth, scratch):
    for n, (x, y, slot) in enumerate(cells):
        scratch[0][n * 8 : n * 8 + 8, :] = local_state(read(x, y, slot), centre_of(x, y, slot, depth))
    for c, (a, b, z) in enumerate(CELLS):
        scratch[1][c * 8 : c * 8 + 8, :] = local_state(
            own[c * 8 : c * 8 + 8, :], centre_of(a + 1, b + 1, z, depth)
        )


def place_state(ref, start, state):
    ref[start : start + 3, :] = state[0]
    ref[start + 3 : start + 6, :] = state[1]
    ref[start + 6 : start + 8, :] = state[2]


def fill_stepped(cells, read, speed, own, own_speed, depth, scratch):
    for n, (x, y, slot) in enumerate(cells):
        state = stepped_state(read(x, y, slot), speed(x, y, slot), centre_of(x, y, slot, depth))
        place_state(scratch[0], n * 8, state)
    for c, (a, b, z) in enumerate(CELLS):
        state = stepped_state(
            own[c * 8 : c * 8 + 8, :],
            own_speed[c * 4 : c * 4 + 4, :],
            centre_of(a + 1, b + 1, z, depth),
        )
        place_state(scratch[1], c * 8, state)


def step_inside(*refs):
    pieces, sums_out, scratch = refs[:-9], refs[-9], refs[-8:]
    fill_start(INSIDE, plane_reader(pieces, 8), pieces[0], lax.axis_index("depth"), scratch)
    sums_out[...] = contact_sums(INSIDE, 3, 64, scratch)


def step_outside(own, sums_in, near, far, own_out, inner_out, *scratch):
    fill_start(OUTSIDE, down_reader((near, far), 8), own, lax.axis_index("depth"), scratch)
    sums = sums_in[...] + contact_sums(OUTSIDE, 3, 32, scratch)
    radius = own[pl.ds(6, 8, stride=8), :]
    safe_mass = jnp.where(radius > 0.0, mass_of(radius), 1.0)
    for k in range(3):
        velocity = own[pl.ds(3 + k, 8, stride=8), :] + TIME_STEP * sums[k * 8 : k * 8 + 8] / safe_mass
        for c in range(8):
            own_out[c * 4 + k : c * 4 + k + 1, :] = velocity[c : c + 1]
    for c in range(8):
        own_out[c * 4 + 3 : c * 4 + 4, :] = jnp.zeros((1, S), F32)
    for column in range(4):
        inner_out[column * 4 : column * 4 + 4, :] = own_out[column * 8 + 4 : column * 8 + 8, :]


def field_own(
    grid, own, own_speed, coefficients, sums_out, high_out, low_out, chosen_out, model_out, *scratch
):
    model_out[...] = coefficients[...]
    depth = lax.axis_index("depth")
    down = lax.axis_index("down")
    cross = lax.axis_index("cross")
    rows = row_ids((64, S))
    near_x, near_y, near_z = rows // 16 - 1, (rows // 4) % 4 - 1, rows % 4 - 1
    centres = [index.astype(F32) - 0.5 for index in (near_x, near_y, near_z)]
    kernels = []
    for c, (a, b, z) in enumerate(CELLS):
        state = stepped_state(
            own[c * 8 : c * 8 + 8, :],
            own_speed[c * 4 : c * 4 + 4, :],
            centre_of(a + 1, b + 1, z, depth),
        )
        place = state[0]
        place_state(scratch[0], c * 8, state)
        squared = jnp.zeros((64, S), F32)
        for k in range(3):
            gap = place[k : k + 1] - centres[k]
            squared = squared + gap * gap
        kernel = jnp.exp(squared * (-0.5 / (KERNEL_WIDTH * KERNEL_WIDTH))) / KERNEL_NORM
        beside = jnp.logical_and(
            jnp.logical_and(jnp.abs(near_x - a) <= 1, jnp.abs(near_y - b) <= 1),
            jnp.abs(near_z - jnp.where(depth == z, 0, 1)) <= 1,
        )
        kernels.append(jnp.where(beside, kernel, 0.0))
    kernel_high, kernel_low = split(jnp.concatenate(kernels, axis=1))
    high_out[...] = kernel_high
    low_out[...] = kernel_low.astype(BF16)
    size_x, size_y, size_z = grid
    nodes = size_x * size_y * size_z
    lanes = lane_ids((64, nodes))
    row = row_ids((64, nodes))
    target_x = (down * 2 + row // 16 - 1 + size_x) % size_x
    target_y = (cross * 2 + (row // 4) % 4 - 1 + size_y) % size_y
    target_z = depth * 2 + row % 4 - 1
    inside = jnp.logical_and(target_z >= 0, target_z < size_z)
    target = (target_x * size_y + target_y) * size_z + target_z
    sums_out[...] = own_sums(9, scratch)
    chosen_out[...] = one_hot(jnp.logical_and(inside, lanes == target))


def field_inside(sums_in, *refs):
    split_at = (len(refs) - 9) // 2
    pieces, speeds, sums_out, scratch = refs[:split_at], refs[split_at:-9], refs[-9], refs[-8:]
    read, speed = plane_reader(pieces, 8), plane_reader(speeds, 4)
    fill_stepped(INSIDE, read, speed, pieces[0], speeds[0], lax.axis_index("depth"), scratch)
    sums_out[...] = sums_in[...] + contact_sums(INSIDE, 9, 64, scratch, True)


def field_outside(
    own, own_speed, sums_in, near_old, far_old, near_speed, far_speed, kernel_high, kernel_low, chosen,
    force_out, node_out, moment_ref, *scratch
):
    depth = lax.axis_index("depth")
    read, speed = down_reader((near_old, far_old), 8), down_reader((near_speed, far_speed), 4)
    fill_stepped(OUTSIDE, read, speed, own, own_speed, depth, scratch)
    sums = sums_in[...] + contact_sums(OUTSIDE, 9, 32, scratch)
    force_out[...] = sums[0:24]
    radius = own[pl.ds(6, 8, stride=8), :]
    mass = jnp.where(radius > 0.0, mass_of(radius), 0.0)
    moments = [mass] + [mass * own_speed[pl.ds(k, 8, stride=4), :] for k in range(3)]
    moments += [0.5 * sums[k * 8 : k * 8 + 8] for k in range(3, 9)]
    moment_ref[...] = jnp.zeros((16, 8 * S), F32)
    for m, moment in enumerate(moments):
        for c in range(8):
            moment_ref[m : m + 1, c * S : (c + 1) * S] = moment[c : c + 1]
    moment_high, moment_low = split(moment_ref[...])
    wide_part = matmul_turned(
        jnp.concatenate([moment_high, moment_low.astype(BF16)], axis=0), kernel_high[...]
    )
    near = wide_part[0:16] + wide_part[16:32] + matmul_turned(moment_high, kernel_low[...])
    near_high, rest = split(near)
    near_middle, near_low = split(rest)
    placed = matmul(
        jnp.concatenate([near_high, near_middle, near_low.astype(BF16)], axis=0), chosen[...]
    )
    node_out[...] = placed[0:16] + placed[16:32] + placed[32:48]


def library_kernel(
    grid, coefficients, parts, speed, force, velocity_out, force_out, residual_out, gram_out, moment_out, terms
):
    flat = lax.axis_index("depth") == 0
    for k in range(3):
        for a in range(2):
            for b in range(2):
                c = a * 4 + b * 2
                layers = [speed[(c + z) * 4 + k : (c + z) * 4 + k + 1, :] for z in range(2)]
                pulls = [force[k * 8 + c + z : k * 8 + c + z + 1, :] for z in range(2)]
                for z in range(2):
                    velocity_out[k, a, b, z : z + 1, :] = jnp.where(flat, layers[z], layers[1 - z])
                    force_out[k, a, b, z : z + 1, :] = jnp.where(flat, pulls[z], pulls[1 - z])
    fields = jnp.sum(parts[...], axis=0)
    size_x, size_y, size_z = grid
    nodes = size_x * size_y * size_z
    lanes = lax.broadcasted_iota(jnp.int32, (1, nodes), 1)
    node_x = lanes // (size_y * size_z)
    node_y = (lanes // size_z) % size_y
    node_z = lanes % size_z
    rows = row_ids((8, nodes))
    density = fields[0:1]
    values = jnp.where(rows == 0, fields[0:8], fields[0:8] / (density + MASS_SHIFT))

    def moved(value, step):
        return pltpu.roll(value, step % nodes, 1)

    plane = size_y * size_z
    slope_x = (moved(values, -plane) - moved(values, plane)) * 0.5
    after_y = jnp.where(
        node_y == size_y - 1, moved(values, (size_y - 1) * size_z), moved(values, -size_z)
    )
    before_y = jnp.where(
        node_y == 0, moved(values, -(size_y - 1) * size_z), moved(values, size_z)
    )
    slope_y = (after_y - before_y) * 0.5
    after_z = jnp.where(node_z == size_z - 1, 0.0, moved(values, -1))
    before_z = jnp.where(node_z == 0, 0.0, moved(values, 1))
    slope_z = (after_z - before_z) * 0.5
    slopes = [[table[k : k + 1] for k in range(4)] for table in (slope_x, slope_y, slope_z)]
    strain = [
        [0.5 * (slopes[left][1 + right] + slopes[right][1 + left]) for right in range(3)]
        for left in range(3)
    ]
    divergence = strain[0][0] + strain[1][1] + strain[2][2]
    rate_sum = jnp.zeros_like(density)
    for left in range(3):
        for right in range(3):
            entry = strain[left][right]
            if left == right:
                entry = entry - divergence / 3.0
            rate_sum = rate_sum + entry * entry
    shear_rate = jnp.sqrt(2.0 * rate_sum + 0.01)
    stress = [fields[4 + k : 5 + k] for k in range(6)]
    pressure = (stress[0] + stress[3] + stress[5]) / 3.0
    deviator = (
        (stress[0] - pressure) ** 2
        + (stress[3] - pressure) ** 2
        + (stress[5] - pressure) ** 2
        + 2.0 * (stress[1] ** 2 + stress[2] ** 2 + stress[4] ** 2)
    )
    shear_stress = jnp.sqrt(0.5 * deviator + 0.01)
    pressure_scale = jnp.sqrt(pressure * pressure + 1.0)
    friction = shear_stress / pressure_scale
    features = [
        density,
        pressure / pressure_scale,
        shear_rate,
        shear_rate / jnp.sqrt(pressure_scale),
        divergence,
        slopes[0][0],
        slopes[1][0],
        slopes[2][0],
    ]
    entries = list(features)
    for left in range(8):
        for right in range(left, 8):
            entries.append(features[left] * features[right])
    for left in range(1, 5):
        entries.append(features[left] * features[left] * features[left])
    for k, entry in enumerate(entries):
        terms[k : k + 1, :] = entry
    table = terms[...]
    model = lax.dot_general(
        jnp.broadcast_to(coefficients[...], (8, TERMS)),
        table,
        (((1,), (0,)), ((), ())),
        precision=lax.Precision.HIGHEST,
        preferred_element_type=F32,
    )
    residual = friction - model[0:1]
    gram_out[...] = (
        lax.dot_general(
            table,
            table,
            (((1,), (1,)), ((), ())),
            precision=lax.Precision.HIGHEST,
            preferred_element_type=F32,
        )
        / nodes
    )
    moment = lax.dot_general(
        jnp.broadcast_to(friction, (8, nodes)),
        table,
        (((1,), (1,)), ((), ())),
        precision=lax.Precision.HIGHEST,
        preferred_element_type=F32,
    )
    moment_out[...] = moment[0:1] / nodes
    down = lax.axis_index("down")
    cross = lax.axis_index("cross")
    depth = lax.axis_index("depth")
    b_rows = lax.broadcasted_iota(jnp.int32, (2, 1), 0)
    z_lanes = lax.broadcasted_iota(jnp.int32, (2, 2), 1)
    for a in range(2):
        mine = jnp.logical_and(node_x == down * 2 + a, node_y == cross * 2 + b_rows)
        column = [
            jnp.sum(
                jnp.where(jnp.logical_and(mine, node_z == depth * 2 + z), residual, 0.0),
                axis=1,
                keepdims=True,
            )
            for z in range(2)
        ]
        residual_out[a] = jnp.where(z_lanes == 0, column[0], column[1])


def ring(axis, step):
    peers = lax.axis_size(axis)
    return [(i, (i + step) % peers) for i in range(peers)]


def exchange(own, inner, height, joined, beside=None):
    cross = lax.axis_size("cross")

    def cells(block, first, count):
        return block[first * height : (first + count) * height]

    if cross == 2 and not joined:
        side = lax.ppermute(own, "cross", [(0, 1), (1, 0)])
    depth_halo = lax.ppermute(inner, "depth", [(0, 1), (1, 0)])
    if cross == 2:
        if joined:
            side = lax.ppermute(
                jnp.concatenate([own, depth_halo], axis=0), "cross", [(0, 1), (1, 0)]
            )
            diag = cells(side, 8, 4)
            sides = [side]
        else:
            diag = lax.ppermute(inner, ("cross", "depth"), [(i, 3 - i) for i in range(4)])
            sides = [side, diag]

        def lateral(x):
            return [
                cells(side, x * 4 + 2, 2),
                cells(side, x * 4, 2),
                cells(diag, x * 2 + 1, 1),
                cells(diag, x * 2, 1),
            ]

    else:
        pairs = [(i * 2 + j, ((i + 1) % cross) * 2 + 1 - j) for i in range(cross) for j in range(2)]
        back = [(i * 2 + j, ((i - 1) % cross) * 2 + 1 - j) for i in range(cross) for j in range(2)]
        last = jnp.concatenate([cells(own, 2, 2), cells(own, 6, 2)], axis=0)
        first = jnp.concatenate([cells(own, 0, 2), cells(own, 4, 2)], axis=0)
        last_inner = jnp.concatenate([cells(inner, 1, 1), cells(inner, 3, 1)], axis=0)
        first_inner = jnp.concatenate([cells(inner, 0, 1), cells(inner, 2, 1)], axis=0)
        before = lax.ppermute(last, "cross", ring("cross", 1))
        after = lax.ppermute(first, "cross", ring("cross", -1))
        diag_before = lax.ppermute(last_inner, ("cross", "depth"), pairs)
        diag_after = lax.ppermute(first_inner, ("cross", "depth"), back)
        sides = [before, after, diag_before, diag_after]

        def lateral(x):
            return [
                cells(before, x * 2, 2),
                cells(after, x * 2, 2),
                cells(diag_before, x, 1),
                cells(diag_after, x, 1),
            ]

    def face(x):
        return jnp.concatenate([cells(own, x * 4, 4), cells(depth_halo, x * 2, 2)] + lateral(x), axis=0)

    downs = lax.axis_size("down")
    last, first = face(1), face(0)
    if beside is not None:
        mine, depth_halo = lax.optimization_barrier((own, depth_halo))
        last, first, result = lax.optimization_barrier((last, first, beside(mine)))
    if downs % 2 == 0:
        even = lax.rem(lax.axis_index("down"), 2) == 0
        near = [(i, i ^ 1) for i in range(downs)]
        far = [(i, (i - 1 + 2 * (i % 2)) % downs) for i in range(downs)]
        outside = [
            lax.ppermute(jnp.where(even, last, first), "down", near),
            lax.ppermute(jnp.where(even, first, last), "down", far),
        ]
    else:
        outside = [
            lax.ppermute(last, "down", ring("down", 1)),
            lax.ppermute(first, "down", ring("down", -1)),
        ]
    if beside is not None:
        return [own, depth_halo] + sides, outside, result
    return [own, depth_halo] + sides, outside


def shared(value, axes, peers):
    return [value] + [
        lax.ppermute(value, axes, [(i, i ^ k) for i in range(peers)]) for k in range(1, peers)
    ]


def tree_sum(parts):
    while len(parts) > 1:
        parts = [parts[k] + parts[k + 1] for k in range(0, len(parts), 2)]
    return parts[0]


def body(positions, velocities, sphere_radii, counts, coefficients):
    down, cross, depth = (lax.axis_size(name) for name in ("down", "cross", "depth"))
    grid = (2 * down, 2 * cross, 2 * depth)
    nodes = grid[0] * grid[1] * grid[2]
    params = pltpu.CompilerParams(vmem_limit_bytes=VMEM_LIMIT)
    vector_shape = jax.ShapeDtypeStruct((3, 2, 2, 2, S), F32)

    def rows(count):
        return jax.ShapeDtypeStruct((count, S), F32)

    def call(kernel, inputs, outputs, scratch, name, vectors=0):
        return pl.pallas_call(
            kernel,
            out_shape=outputs,
            in_specs=[VMEM_SPEC] * len(inputs),
            out_specs=jax.tree.map(lambda _: VMEM_SPEC, outputs),
            scratch_shapes=scratch,
            compiler_params=params,
            cost_estimate=pl.CostEstimate(flops=vectors, bytes_accessed=1 << 20, transcendentals=0),
            name=name,
        )(*inputs)

    own, inner = pl.pallas_call(
        pack_kernel,
        out_shape=(rows(64), rows(32)),
        in_specs=[pl.BlockSpec(memory_space=pl.ANY)] * 4,
        out_specs=(VMEM_SPEC, VMEM_SPEC),
        scratch_shapes=[
            pltpu.SMEM((2, 2, 2), jnp.int32),
            pltpu.VMEM((3, 2, 2, 2, S), F32),
            pltpu.VMEM((3, 2, 2, 2, S), F32),
            pltpu.VMEM((2, 2, 2, S), F32),
            pltpu.SemaphoreType.DMA((4,)),
        ],
        compiler_params=pltpu.CompilerParams(vmem_limit_bytes=60 * 1024 * 1024),
        name="pack",
    )(counts, positions, velocities, sphere_radii)
    inside, outside = exchange(own, inner, 8, True)
    sums = call(step_inside, inside, rows(24), contact_scratch(INSIDE, 3), "step_inside", 1 << 31)
    own_speed, inner_speed = call(
        step_outside, [own, sums] + outside, (rows(32), rows(16)), contact_scratch(OUTSIDE, 3), "step_outside", 1 << 30
    )
    table = jax.ShapeDtypeStruct((64, 8 * S), BF16)
    inside_speed, outside_speed, weights = exchange(
        own_speed,
        inner_speed,
        4,
        False,
        lambda speed: call(
            functools.partial(field_own, grid),
            [own, speed, coefficients.reshape(1, TERMS)],
            (
                rows(72),
                table,
                table,
                jax.ShapeDtypeStruct((64, nodes), BF16),
                jax.ShapeDtypeStruct((1, TERMS), F32),
            ),
            [
                pltpu.VMEM((8 * 8, S), F32),
                pltpu.VMEM((8 * S, 32), F32),
                pltpu.VMEM((9 * 8 * 8, S), F32),
            ],
            "field_own",
            1 << 30,
        ),
    )
    sums = call(
        field_inside, [weights[0]] + inside + inside_speed, rows(72), contact_scratch(INSIDE, 9), "field_inside", 1 << 31
    )
    force, partial = call(
        field_outside,
        [own, own_speed, sums] + outside + outside_speed + list(weights[1:4]),
        (rows(24), jax.ShapeDtypeStruct((16, nodes), F32)),
        [pltpu.VMEM((16, 8 * S), F32)] + contact_scratch(OUTSIDE, 9),
        "field_outside",
        1 << 30,
    )
    partial = tree_sum(shared(partial, ("cross", "depth"), cross * depth))
    parts = lax.all_to_all(jnp.broadcast_to(partial, (down, 16, nodes)), "down", 0, 0)
    velocity_new, force_next, residual_field, gram_matrix, moment = pl.pallas_call(
        functools.partial(library_kernel, grid),
        out_shape=(
            vector_shape,
            vector_shape,
            jax.ShapeDtypeStruct((2, 2, 2), F32),
            jax.ShapeDtypeStruct((TERMS, TERMS), F32),
            jax.ShapeDtypeStruct((1, TERMS), F32),
        ),
        in_specs=[VMEM_SPEC] * 4,
        out_specs=(VMEM_SPEC,) * 5,
        scratch_shapes=[pltpu.VMEM((TERMS, nodes), F32)],
        compiler_params=params,
        name="library",
    )(weights[4], parts, own_speed, force)
    return (velocity_new, force_next, residual_field, gram_matrix, moment.reshape(TERMS))


def solution(mesh):
    return jax.shard_map(
        body,
        mesh=mesh,
        in_specs=(
            P(None, ("groups", "down"), "cross", "depth", None),
            P(None, ("groups", "down"), "cross", "depth", None),
            P(("groups", "down"), "cross", "depth", None),
            P(("groups", "down"), "cross", "depth"),
            P(),
        ),
        out_specs=(
            P(None, ("groups", "down"), "cross", "depth", None),
            P(None, ("groups", "down"), "cross", "depth", None),
            P(("groups", "down"), "cross", "depth"),
            P("groups", None),
            P("groups"),
        ),
        check_vma=False,
    )
```

```python
import functools

import jax
import jax.numpy as jnp
from jax import lax
from jax.experimental import pallas as pl
from jax.experimental.pallas import tpu as pltpu
from jax.sharding import PartitionSpec as P

STIFFNESS = 100.0
DAMPING = 20.0
TIME_STEP = 0.05
KERNEL_WIDTH = 0.4
KERNEL_NORM = 64.0
SOFTENING = 0.0001
RADIUS_REF = 0.1
MASS_SHIFT = 0.1
DEAD = -1000.0
TERMS = 48
S = 128
SPREAD = 4
F32 = jnp.float32
BF16 = jnp.bfloat16
CELLS = tuple((a, b, z) for a in range(2) for b in range(2) for z in range(2))
PAIR_LIST = ((0, 0), (0, 1), (0, 2), (1, 1), (1, 2), (2, 2))
VMEM_SPEC = pl.BlockSpec(memory_space=pltpu.VMEM)
SMEM_SPEC = pl.BlockSpec(memory_space=pltpu.SMEM)
VMEM_LIMIT = 48 * 1024 * 1024


def row_ids(shape):
    return lax.broadcasted_iota(jnp.int32, shape, 0)


def lane_ids(shape):
    return lax.broadcasted_iota(jnp.int32, shape, 1)


def one_hot(condition):
    return jnp.where(condition, 1.0, 0.0).astype(BF16)


def split(value):
    high = value.astype(BF16)
    return high, value - high.astype(F32)


def matmul(left, right):
    return lax.dot_general(left, right, (((1,), (0,)), ((), ())), preferred_element_type=F32)


def matmul_turned(left, right):
    return lax.dot_general(left, right, (((1,), (1,)), ((), ())), preferred_element_type=F32)


def lane_gather(table, index):
    return jnp.take_along_axis(table, index, axis=1)


def pack_kernel(
    counts_hbm, positions_hbm, velocities_hbm, radii_hbm, own, inner, counts, positions, velocities, radii, arrived
):
    copies = [
        pltpu.make_async_copy(source, target, arrived.at[k])
        for k, (source, target) in enumerate(
            (
                (counts_hbm, counts),
                (positions_hbm, positions),
                (velocities_hbm, velocities),
                (radii_hbm, radii),
            )
        )
    ]
    for copy in copies:
        copy.start()
    for copy in copies:
        copy.wait()
    depth = lax.axis_index("depth")
    lanes = lane_ids((1, S))

    def layer(ref, at, z):
        rows = ref[at]
        return jnp.where(depth == z, rows[0:1], rows[1:2])

    for c, (a, b, z) in enumerate(CELLS):
        for k in range(3):
            own[c * 8 + k : c * 8 + k + 1, :] = layer(positions, (k, a, b), z)
            own[c * 8 + 3 + k : c * 8 + 4 + k, :] = layer(velocities, (k, a, b), z)
        count = jnp.where(depth == z, counts[a, b, 0], counts[a, b, 1])
        own[c * 8 + 6 : c * 8 + 7, :] = jnp.where(lanes < count, layer(radii, (a, b), z), DEAD)
        own[c * 8 + 7 : c * 8 + 8, :] = jnp.zeros((1, S), F32)
    for column in range(4):
        inner[column * 8 : column * 8 + 8, :] = own[column * 16 + 8 : column * 16 + 16, :]


def local_state(raw, centre):
    rows = row_ids(raw.shape)
    shift = jnp.where(rows == 0, centre[0], jnp.where(rows == 1, centre[1], centre[2]))
    return jnp.where(rows < 3, raw + shift, jnp.where(rows < 6, DAMPING * raw, raw))


def plane_reader(refs, height):
    own, depth_halo, sides = refs[0], refs[1], refs[2:]

    def read(ref, cell):
        return ref[cell * height : cell * height + height, :]

    def cell(x, y, slot):
        a = x - 1
        if y in (1, 2):
            return read(own, a * 4 + (y - 1) * 2 + slot) if slot < 2 else read(depth_halo, a * 2 + y - 1)
        if len(sides) == 4:
            before, after, diag_before, diag_after = sides
            if slot < 2:
                return read(before if y == 0 else after, a * 2 + slot)
            return read(diag_before if y == 0 else diag_after, a)
        b = 1 if y == 0 else 0
        if slot < 2:
            return read(sides[0], a * 4 + b * 2 + slot)
        return read(sides[0], 8 + a * 2 + b) if len(sides) == 1 else read(sides[1], a * 2 + b)

    return cell


def down_reader(refs, height):
    even = lax.rem(lax.axis_index("down"), 2) == 0
    swapped = lax.axis_size("down") % 2 == 0

    def cell(x, y, slot):
        if y in (1, 2):
            place = (y - 1) * 2 + slot if slot < 2 else 4 + y - 1
        else:
            side = 0 if y == 0 else 1
            place = 6 + side * 2 + slot if slot < 2 else 10 + side
        one, two = (ref[place * height : place * height + height, :] for ref in refs)
        if swapped:
            return jnp.where(even, one, two) if x == 0 else jnp.where(even, two, one)
        return one if x == 0 else two

    return cell


def centre_of(x, y, slot, depth):
    side = 0.5 - depth.astype(F32)
    return (x - 1.5, y - 1.5, (-1.0, 1.0, 3.0)[slot] * side)


BLOCK = tuple((x, y, slot) for x in (1, 2) for y in (1, 2) for slot in (0, 1))
PLANE = tuple(
    (x, y, slot) for x in (1, 2) for y in range(4) for slot in range(3) if (x, y, slot) not in BLOCK
)
INSIDE = tuple((x, y, slot) for x in (1, 2) for y in range(4) for slot in range(3))
OUTSIDE = tuple((x, y, slot) for x in (0, 3) for y in range(4) for slot in range(3))


def stepped_state(old, speed, centre):
    rows = row_ids((3, S))
    shift = jnp.where(rows == 0, centre[0], jnp.where(rows == 1, centre[1], centre[2]))
    return (old[0:3] + TIME_STEP * speed[0:3]) + shift, DAMPING * speed[0:3], old[6:8]


def contact_scratch(cells, width):
    rows = len(cells)
    return [
        pltpu.VMEM((rows * 8, S), F32),
        pltpu.VMEM((8 * 8, S), F32),
        pltpu.VMEM((8 * rows, S), jnp.int32),
        pltpu.VMEM((8 * rows, S), jnp.int32),
        pltpu.VMEM((8 * rows, S), jnp.int32),
        pltpu.VMEM((8 * rows, S), jnp.int32),
        pltpu.VMEM((18 * 8 * S, 32), F32),
        pltpu.VMEM((width * 8 * 8, S), F32),
    ]


def store_listed(list_ref, t, c, chunk, tile):
    high = tile.astype(BF16).astype(F32)
    rest = tile - high
    middle = rest.astype(BF16).astype(F32)
    turned = jnp.transpose(jnp.concatenate([high, middle, rest - middle, tile], axis=0))
    for part in range(S // chunk):
        start = pl.multiple_of(t * (8 * S) + (part * 8 + c) * chunk, chunk)
        list_ref[pl.ds(start, chunk), :] = turned[part * chunk : (part + 1) * chunk]


def pair_step(width, chunk, mine_ref, list_ref, sum_ref):
    selector = jnp.logical_and(
        row_ids((32, SPREAD * S)) % 8 == lane_ids((32, SPREAD * S)) // S, row_ids((32, SPREAD * S)) < 24
    )
    selector = one_hot(selector)

    def one_step(step, carry):
        every = list_ref[pl.ds(pl.multiple_of(step * (8 * chunk), 8 * chunk), 8 * chunk), :]
        spread = matmul(every.astype(BF16), selector)
        for c in range(8):
            listed = every[c * chunk : (c + 1) * chunk]
            me = [jnp.broadcast_to(mine_ref[c * 8 + k : c * 8 + k + 1, :], (8, S)) for k in range(7)]
            added = [None] * width
            for block in range(chunk // 8):
                row = c * chunk + block * 8
                other = [spread[row : row + 8, k * S : (k + 1) * S] for k in range(SPREAD)]
                other += [
                    jnp.broadcast_to(listed[block * 8 : block * 8 + 8, 24 + k : 25 + k], (8, S))
                    for k in range(SPREAD, 7)
                ]
                r = [me[k] - other[k] for k in range(3)]
                u = [me[3 + k] - other[3 + k] for k in range(3)]
                squared = r[0] * r[0] + r[1] * r[1] + r[2] * r[2] + SOFTENING
                inverse = lax.rsqrt(squared)
                along = u[0] * r[0] + u[1] * r[1] + u[2] * r[2]
                overlap = jnp.maximum((me[6] + other[6]) * inverse - 1.0, 0.0)
                weight = overlap * (STIFFNESS - along * inverse)
                terms = [weight * r[k] for k in range(3)]
                if width == 9:
                    terms += [terms[left] * r[right] for left, right in PAIR_LIST]
                added = [
                    term if total is None else total + term for total, term in zip(added, terms)
                ]
            for k in range(width):
                row = (k * 8 + c) * 8
                sum_ref[row : row + 8, :] += added[k]
        return carry

    return one_step


def collected(width, sum_ref):
    out = []
    for k in range(width):
        parts = [sum_ref[pl.ds(k * 64 + sub, 8, stride=8), :] for sub in range(8)]
        while len(parts) > 1:
            parts = [parts[i] + parts[i + 1] for i in range(0, len(parts), 2)]
        out.append(parts[0])
    return jnp.concatenate(out, axis=0)


def contact_sums(cells, width, chunk, scratch, skip_own=False):
    local_ref, mine_ref, index_ref, base_ref, amount_ref, chosen_ref, list_ref, sum_ref = scratch
    count = len(cells)
    span = 16 if cells == OUTSIDE else count

    def first_row(a):
        return 8 if cells == OUTSIDE and a == 1 else 0

    def beside(a, b, z):
        return [
            n
            for n, (x, y, slot) in enumerate(cells)
            if abs(x - 1 - a) <= 1 and abs(y - 1 - b) <= 1 and abs(slot - z) <= 1
            and not (skip_own and (x, y, slot) == (a + 1, b + 1, z))
        ]

    sum_ref[...] = jnp.zeros((width * 64, S), F32)
    place = [local_ref[pl.ds(k, count, stride=8), :] for k in range(3)]
    radius = local_ref[pl.ds(6, count, stride=8), :]
    rows = row_ids((count, S))
    masks = []
    for c, (a, b, z) in enumerate(CELLS):
        mine = mine_ref[c * 8 : c * 8 + 8, :]
        live = mine[6:7] > 0.0
        low = jnp.min(jnp.where(live, mine, 1e9), axis=1, keepdims=True)
        high = jnp.max(jnp.where(live, mine, -1e9), axis=1, keepdims=True)
        part = slice(first_row(a), first_row(a) + span)
        reach = radius[part] + high[6:7]
        near = reach > 0.0
        inside = set(beside(a, b, z))
        for n in range(part.start, part.stop):
            if n not in inside:
                near = jnp.logical_and(near, rows[part] != n)
        for k in range(3):
            near = jnp.logical_and(near, place[k][part] + reach > low[k : k + 1])
            near = jnp.logical_and(near, place[k][part] - reach < high[k : k + 1])
        masks.append(jnp.where(near, 1.0, 0.0).astype(F32))
    mask = jnp.concatenate(masks, axis=0).astype(BF16)
    upper = one_hot(row_ids((S, 2 * S)) <= lane_ids((S, 2 * S)))
    sums = matmul(mask, upper)
    prefix, amount = sums[:, :S], sums[:, S:]
    before = one_hot(lane_ids((span, span)) < row_ids((span, span)))
    total = None
    for c in range(8):
        part = amount[c * span : (c + 1) * span]
        base = matmul(before, part.astype(BF16))
        base_ref[c * span : (c + 1) * span, :] = base.astype(jnp.int32)
        listed = base[span - 1 : span] + part[span - 1 : span]
        total = listed if total is None else jnp.maximum(total, listed)
    most = total.astype(jnp.int32)[0, 0]
    amount_ref[0 : 8 * span, :] = amount.astype(jnp.int32)
    wanted = lane_ids((8 * span, S)).astype(F32)
    index = jnp.zeros((8 * span, S), jnp.int32)
    for step in (64, 32, 16, 8, 4, 2, 1):
        probe = lane_gather(prefix, index + (step - 1))
        index = jnp.where(probe <= wanted, index + step, index)
    index_ref[0 : 8 * span, :] = index
    empty = jnp.where(row_ids((8, S)) == 6, DEAD, 0.0).astype(F32)

    def gather_tiles(t, carry):
        want = t * S + lane_ids((8 * span, S)) - base_ref[0 : 8 * span, :]
        valid = jnp.logical_and(want >= 0, want < amount_ref[0 : 8 * span, :])
        source = lane_gather(index_ref[0 : 8 * span, :], jnp.clip(want, 0, S - 1))
        chosen_ref[0 : 8 * span, :] = jnp.where(valid, source, -1)
        for c, (a, b, z) in enumerate(CELLS):
            tile = empty
            for n in beside(a, b, z):
                row = c * span + n - first_row(a)
                pick = jnp.broadcast_to(chosen_ref[row : row + 1, :], (8, S))
                values = lane_gather(local_ref[n * 8 : n * 8 + 8, :], jnp.maximum(pick, 0))
                tile = jnp.where(pick >= 0, values, tile)
            store_listed(list_ref, t, c, chunk, tile)
        return carry

    gather_tiles(0, 0)
    lax.fori_loop(1, (most + (S - 1)) // S, gather_tiles, 0)

    lax.fori_loop(
        0, (most + (chunk - 1)) // chunk, pair_step(width, chunk, mine_ref, list_ref, sum_ref), 0
    )
    return collected(width, sum_ref)


def own_sums(width, scratch):
    mine_ref, list_ref, sum_ref = scratch
    sum_ref[...] = jnp.zeros((width * 64, S), F32)
    for c in range(8):
        store_listed(list_ref, 0, c, 64, mine_ref[c * 8 : c * 8 + 8, :])
    step = pair_step(width, 64, mine_ref, list_ref, sum_ref)
    for part in range(2):
        step(part, 0)
    return collected(width, sum_ref)


def mass_of(radius):
    scaled = radius / RADIUS_REF
    return scaled * scaled * scaled


def fill_start(cells, read, own, depth, scratch):
    for n, (x, y, slot) in enumerate(cells):
        scratch[0][n * 8 : n * 8 + 8, :] = local_state(read(x, y, slot), centre_of(x, y, slot, depth))
    for c, (a, b, z) in enumerate(CELLS):
        scratch[1][c * 8 : c * 8 + 8, :] = local_state(
            own[c * 8 : c * 8 + 8, :], centre_of(a + 1, b + 1, z, depth)
        )


def place_state(ref, start, state):
    ref[start : start + 3, :] = state[0]
    ref[start + 3 : start + 6, :] = state[1]
    ref[start + 6 : start + 8, :] = state[2]


def fill_stepped(cells, read, speed, own, own_speed, depth, scratch):
    for n, (x, y, slot) in enumerate(cells):
        state = stepped_state(read(x, y, slot), speed(x, y, slot), centre_of(x, y, slot, depth))
        place_state(scratch[0], n * 8, state)
    for c, (a, b, z) in enumerate(CELLS):
        state = stepped_state(
            own[c * 8 : c * 8 + 8, :],
            own_speed[c * 4 : c * 4 + 4, :],
            centre_of(a + 1, b + 1, z, depth),
        )
        place_state(scratch[1], c * 8, state)


def step_inside(*refs):
    pieces, sums_out, scratch = refs[:-9], refs[-9], refs[-8:]
    fill_start(INSIDE, plane_reader(pieces, 8), pieces[0], lax.axis_index("depth"), scratch)
    sums_out[...] = contact_sums(INSIDE, 3, 64, scratch)


def step_outside(own, sums_in, far, near, own_out, inner_out, *scratch):
    fill_start(OUTSIDE, down_reader((far, near), 8), own, lax.axis_index("depth"), scratch)
    sums = sums_in[...] + contact_sums(OUTSIDE, 3, 32, scratch)
    radius = own[pl.ds(6, 8, stride=8), :]
    safe_mass = jnp.where(radius > 0.0, mass_of(radius), 1.0)
    for k in range(3):
        velocity = own[pl.ds(3 + k, 8, stride=8), :] + TIME_STEP * sums[k * 8 : k * 8 + 8] / safe_mass
        for c in range(8):
            own_out[c * 4 + k : c * 4 + k + 1, :] = velocity[c : c + 1]
    for c in range(8):
        own_out[c * 4 + 3 : c * 4 + 4, :] = jnp.zeros((1, S), F32)
    for column in range(4):
        inner_out[column * 4 : column * 4 + 4, :] = own_out[column * 8 + 4 : column * 8 + 8, :]


def field_own(
    grid, own, own_speed, coefficients, sums_out, high_out, low_out, chosen_out, model_out, *scratch
):
    model_out[...] = coefficients[...]
    depth = lax.axis_index("depth")
    down = lax.axis_index("down")
    cross = lax.axis_index("cross")
    rows = row_ids((64, S))
    near_x, near_y, near_z = rows // 16 - 1, (rows // 4) % 4 - 1, rows % 4 - 1
    centres = [index.astype(F32) - 0.5 for index in (near_x, near_y, near_z)]
    kernels = []
    for c, (a, b, z) in enumerate(CELLS):
        state = stepped_state(
            own[c * 8 : c * 8 + 8, :],
            own_speed[c * 4 : c * 4 + 4, :],
            centre_of(a + 1, b + 1, z, depth),
        )
        place = state[0]
        place_state(scratch[0], c * 8, state)
        squared = jnp.zeros((64, S), F32)
        for k in range(3):
            gap = place[k : k + 1] - centres[k]
            squared = squared + gap * gap
        kernel = jnp.exp(squared * (-0.5 / (KERNEL_WIDTH * KERNEL_WIDTH))) / KERNEL_NORM
        beside = jnp.logical_and(
            jnp.logical_and(jnp.abs(near_x - a) <= 1, jnp.abs(near_y - b) <= 1),
            jnp.abs(near_z - jnp.where(depth == z, 0, 1)) <= 1,
        )
        kernels.append(jnp.where(beside, kernel, 0.0))
    kernel_high, kernel_low = split(jnp.concatenate(kernels, axis=1))
    high_out[...] = kernel_high
    low_out[...] = kernel_low.astype(BF16)
    size_x, size_y, size_z = grid
    nodes = size_x * size_y * size_z
    lanes = lane_ids((64, nodes))
    row = row_ids((64, nodes))
    target_x = (down * 2 + row // 16 - 1 + size_x) % size_x
    target_y = (cross * 2 + (row // 4) % 4 - 1 + size_y) % size_y
    target_z = depth * 2 + row % 4 - 1
    inside = jnp.logical_and(target_z >= 0, target_z < size_z)
    target = (target_x * size_y + target_y) * size_z + target_z
    sums_out[...] = own_sums(9, scratch)
    chosen_out[...] = one_hot(jnp.logical_and(inside, lanes == target))


def field_inside(sums_in, *refs):
    split_at = (len(refs) - 9) // 2
    pieces, speeds, sums_out, scratch = refs[:split_at], refs[split_at:-9], refs[-9], refs[-8:]
    read, speed = plane_reader(pieces, 8), plane_reader(speeds, 4)
    fill_stepped(INSIDE, read, speed, pieces[0], speeds[0], lax.axis_index("depth"), scratch)
    sums_out[...] = sums_in[...] + contact_sums(INSIDE, 9, 64, scratch, True)


def field_outside(
    own, own_speed, sums_in, far_old, near_old, far_speed, near_speed, kernel_high, kernel_low, chosen,
    force_out, node_out, moment_ref, *scratch
):
    depth = lax.axis_index("depth")
    read, speed = down_reader((far_old, near_old), 8), down_reader((far_speed, near_speed), 4)
    fill_stepped(OUTSIDE, read, speed, own, own_speed, depth, scratch)
    sums = sums_in[...] + contact_sums(OUTSIDE, 9, 32, scratch)
    force_out[...] = sums[0:24]
    radius = own[pl.ds(6, 8, stride=8), :]
    mass = jnp.where(radius > 0.0, mass_of(radius), 0.0)
    moments = [mass] + [mass * own_speed[pl.ds(k, 8, stride=4), :] for k in range(3)]
    moments += [0.5 * sums[k * 8 : k * 8 + 8] for k in range(3, 9)]
    moment_ref[...] = jnp.zeros((16, 8 * S), F32)
    for m, moment in enumerate(moments):
        for c in range(8):
            moment_ref[m : m + 1, c * S : (c + 1) * S] = moment[c : c + 1]
    moment_high, moment_low = split(moment_ref[...])
    wide_part = matmul_turned(
        jnp.concatenate([moment_high, moment_low.astype(BF16)], axis=0), kernel_high[...]
    )
    near = wide_part[0:16] + wide_part[16:32] + matmul_turned(moment_high, kernel_low[...])
    near_high, rest = split(near)
    near_middle, near_low = split(rest)
    placed = matmul(
        jnp.concatenate([near_high, near_middle, near_low.astype(BF16)], axis=0), chosen[...]
    )
    node_out[...] = placed[0:16] + placed[16:32] + placed[32:48]


def library_kernel(
    grid, coefficients, mine, other, speed, force, velocity_out, force_out, residual_out, gram_out, moment_out, terms
):
    flat = lax.axis_index("depth") == 0
    for k in range(3):
        for a in range(2):
            for b in range(2):
                c = a * 4 + b * 2
                layers = [speed[(c + z) * 4 + k : (c + z) * 4 + k + 1, :] for z in range(2)]
                pulls = [force[k * 8 + c + z : k * 8 + c + z + 1, :] for z in range(2)]
                for z in range(2):
                    velocity_out[k, a, b, z : z + 1, :] = jnp.where(flat, layers[z], layers[1 - z])
                    force_out[k, a, b, z : z + 1, :] = jnp.where(flat, pulls[z], pulls[1 - z])
    fields = mine[...] + other[...]
    size_x, size_y, size_z = grid
    nodes = size_x * size_y * size_z
    lanes = lax.broadcasted_iota(jnp.int32, (1, nodes), 1)
    node_x = lanes // (size_y * size_z)
    node_y = (lanes // size_z) % size_y
    node_z = lanes % size_z
    rows = row_ids((8, nodes))
    density = fields[0:1]
    values = jnp.where(rows == 0, fields[0:8], fields[0:8] / (density + MASS_SHIFT))

    def moved(value, step):
        return pltpu.roll(value, step % nodes, 1)

    plane = size_y * size_z
    slope_x = (moved(values, -plane) - moved(values, plane)) * 0.5
    after_y = jnp.where(
        node_y == size_y - 1, moved(values, (size_y - 1) * size_z), moved(values, -size_z)
    )
    before_y = jnp.where(
        node_y == 0, moved(values, -(size_y - 1) * size_z), moved(values, size_z)
    )
    slope_y = (after_y - before_y) * 0.5
    after_z = jnp.where(node_z == size_z - 1, 0.0, moved(values, -1))
    before_z = jnp.where(node_z == 0, 0.0, moved(values, 1))
    slope_z = (after_z - before_z) * 0.5
    slopes = [[table[k : k + 1] for k in range(4)] for table in (slope_x, slope_y, slope_z)]
    strain = [
        [0.5 * (slopes[left][1 + right] + slopes[right][1 + left]) for right in range(3)]
        for left in range(3)
    ]
    divergence = strain[0][0] + strain[1][1] + strain[2][2]
    rate_sum = jnp.zeros_like(density)
    for left in range(3):
        for right in range(3):
            entry = strain[left][right]
            if left == right:
                entry = entry - divergence / 3.0
            rate_sum = rate_sum + entry * entry
    shear_rate = jnp.sqrt(2.0 * rate_sum + 0.01)
    stress = [fields[4 + k : 5 + k] for k in range(6)]
    pressure = (stress[0] + stress[3] + stress[5]) / 3.0
    deviator = (
        (stress[0] - pressure) ** 2
        + (stress[3] - pressure) ** 2
        + (stress[5] - pressure) ** 2
        + 2.0 * (stress[1] ** 2 + stress[2] ** 2 + stress[4] ** 2)
    )
    shear_stress = jnp.sqrt(0.5 * deviator + 0.01)
    pressure_scale = jnp.sqrt(pressure * pressure + 1.0)
    friction = shear_stress / pressure_scale
    features = [
        density,
        pressure / pressure_scale,
        shear_rate,
        shear_rate / jnp.sqrt(pressure_scale),
        divergence,
        slopes[0][0],
        slopes[1][0],
        slopes[2][0],
    ]
    entries = list(features)
    for left in range(8):
        for right in range(left, 8):
            entries.append(features[left] * features[right])
    for left in range(1, 5):
        entries.append(features[left] * features[left] * features[left])
    for k, entry in enumerate(entries):
        terms[k : k + 1, :] = entry
    table = terms[...]
    model = lax.dot_general(
        jnp.broadcast_to(coefficients[...], (8, TERMS)),
        table,
        (((1,), (0,)), ((), ())),
        precision=lax.Precision.HIGHEST,
        preferred_element_type=F32,
    )
    residual = friction - model[0:1]
    gram_out[...] = (
        lax.dot_general(
            table,
            table,
            (((1,), (1,)), ((), ())),
            precision=lax.Precision.HIGHEST,
            preferred_element_type=F32,
        )
        / nodes
    )
    moment = lax.dot_general(
        jnp.broadcast_to(friction, (8, nodes)),
        table,
        (((1,), (1,)), ((), ())),
        precision=lax.Precision.HIGHEST,
        preferred_element_type=F32,
    )
    moment_out[...] = moment[0:1] / nodes
    down = lax.axis_index("down")
    cross = lax.axis_index("cross")
    depth = lax.axis_index("depth")
    b_rows = lax.broadcasted_iota(jnp.int32, (2, 1), 0)
    z_lanes = lax.broadcasted_iota(jnp.int32, (2, 2), 1)
    for a in range(2):
        mine = jnp.logical_and(node_x == down * 2 + a, node_y == cross * 2 + b_rows)
        column = [
            jnp.sum(
                jnp.where(jnp.logical_and(mine, node_z == depth * 2 + z), residual, 0.0),
                axis=1,
                keepdims=True,
            )
            for z in range(2)
        ]
        residual_out[a] = jnp.where(z_lanes == 0, column[0], column[1])


def ring(axis, step):
    peers = lax.axis_size(axis)
    return [(i, (i + step) % peers) for i in range(peers)]


def exchange(own, inner, height, joined, beside=None):
    cross = lax.axis_size("cross")

    def cells(block, first, count):
        return block[first * height : (first + count) * height]

    if cross == 2 and not joined:
        side = lax.ppermute(own, "cross", [(0, 1), (1, 0)])
    depth_halo = lax.ppermute(inner, "depth", [(0, 1), (1, 0)])
    if cross == 2:
        if joined:
            side = lax.ppermute(
                jnp.concatenate([own, depth_halo], axis=0), "cross", [(0, 1), (1, 0)]
            )
            diag = cells(side, 8, 4)
            sides = [side]
        else:
            diag = lax.ppermute(inner, ("cross", "depth"), [(i, 3 - i) for i in range(4)])
            sides = [side, diag]

        def lateral(x):
            return [
                cells(side, x * 4 + 2, 2),
                cells(side, x * 4, 2),
                cells(diag, x * 2 + 1, 1),
                cells(diag, x * 2, 1),
            ]

    else:
        pairs = [(i * 2 + j, ((i + 1) % cross) * 2 + 1 - j) for i in range(cross) for j in range(2)]
        back = [(i * 2 + j, ((i - 1) % cross) * 2 + 1 - j) for i in range(cross) for j in range(2)]
        last = jnp.concatenate([cells(own, 2, 2), cells(own, 6, 2)], axis=0)
        first = jnp.concatenate([cells(own, 0, 2), cells(own, 4, 2)], axis=0)
        last_inner = jnp.concatenate([cells(inner, 1, 1), cells(inner, 3, 1)], axis=0)
        first_inner = jnp.concatenate([cells(inner, 0, 1), cells(inner, 2, 1)], axis=0)
        before = lax.ppermute(last, "cross", ring("cross", 1))
        after = lax.ppermute(first, "cross", ring("cross", -1))
        diag_before = lax.ppermute(last_inner, ("cross", "depth"), pairs)
        diag_after = lax.ppermute(first_inner, ("cross", "depth"), back)
        sides = [before, after, diag_before, diag_after]

        def lateral(x):
            return [
                cells(before, x * 2, 2),
                cells(after, x * 2, 2),
                cells(diag_before, x, 1),
                cells(diag_after, x, 1),
            ]

    def face(x):
        return jnp.concatenate([cells(own, x * 4, 4), cells(depth_halo, x * 2, 2)] + lateral(x), axis=0)

    downs = lax.axis_size("down")
    last, first = face(1), face(0)
    if beside is not None:
        mine, depth_halo = lax.optimization_barrier((own, depth_halo))
        last, first, result = lax.optimization_barrier((last, first, beside(mine)))
    if downs % 2 == 0:
        even = lax.rem(lax.axis_index("down"), 2) == 0
        near = [(i, i ^ 1) for i in range(downs)]
        far = [(i, (i - 1 + 2 * (i % 2)) % downs) for i in range(downs)]
        outside = [
            lax.ppermute(jnp.where(even, first, last), "down", far),
            lax.ppermute(jnp.where(even, last, first), "down", near),
        ]
    else:
        outside = [
            lax.ppermute(last, "down", ring("down", 1)),
            lax.ppermute(first, "down", ring("down", -1)),
        ]
    if beside is not None:
        return [own, depth_halo] + sides, outside, result
    return [own, depth_halo] + sides, outside


def shared(value, axes, peers):
    return [value] + [
        lax.ppermute(value, axes, [(i, i ^ k) for i in range(peers)]) for k in range(1, peers)
    ]


def tree_sum(parts):
    while len(parts) > 1:
        parts = [parts[k] + parts[k + 1] for k in range(0, len(parts), 2)]
    return parts[0]


def body(positions, velocities, sphere_radii, counts, coefficients):
    down, cross, depth = (lax.axis_size(name) for name in ("down", "cross", "depth"))
    grid = (2 * down, 2 * cross, 2 * depth)
    nodes = grid[0] * grid[1] * grid[2]
    params = pltpu.CompilerParams(vmem_limit_bytes=VMEM_LIMIT)
    vector_shape = jax.ShapeDtypeStruct((3, 2, 2, 2, S), F32)

    def rows(count):
        return jax.ShapeDtypeStruct((count, S), F32)

    def call(kernel, inputs, outputs, scratch, name, vectors=0):
        return pl.pallas_call(
            kernel,
            out_shape=outputs,
            in_specs=[VMEM_SPEC] * len(inputs),
            out_specs=jax.tree.map(lambda _: VMEM_SPEC, outputs),
            scratch_shapes=scratch,
            compiler_params=params,
            cost_estimate=pl.CostEstimate(flops=vectors, bytes_accessed=1 << 20, transcendentals=0),
            name=name,
        )(*inputs)

    own, inner = pl.pallas_call(
        pack_kernel,
        out_shape=(rows(64), rows(32)),
        in_specs=[pl.BlockSpec(memory_space=pl.ANY)] * 4,
        out_specs=(VMEM_SPEC, VMEM_SPEC),
        scratch_shapes=[
            pltpu.SMEM((2, 2, 2), jnp.int32),
            pltpu.VMEM((3, 2, 2, 2, S), F32),
            pltpu.VMEM((3, 2, 2, 2, S), F32),
            pltpu.VMEM((2, 2, 2, S), F32),
            pltpu.SemaphoreType.DMA((4,)),
        ],
        compiler_params=pltpu.CompilerParams(vmem_limit_bytes=60 * 1024 * 1024),
        name="pack",
    )(counts, positions, velocities, sphere_radii)
    inside, outside = exchange(own, inner, 8, True)
    sums = call(step_inside, inside, rows(24), contact_scratch(INSIDE, 3), "step_inside", 1 << 31)
    own_speed, inner_speed = call(
        step_outside, [own, sums] + outside, (rows(32), rows(16)), contact_scratch(OUTSIDE, 3), "step_outside", 1 << 30
    )
    table = jax.ShapeDtypeStruct((64, 8 * S), BF16)
    inside_speed, outside_speed, weights = exchange(
        own_speed,
        inner_speed,
        4,
        False,
        lambda speed: call(
            functools.partial(field_own, grid),
            [own, speed, coefficients.reshape(1, TERMS)],
            (
                rows(72),
                table,
                table,
                jax.ShapeDtypeStruct((64, nodes), BF16),
                jax.ShapeDtypeStruct((1, TERMS), F32),
            ),
            [
                pltpu.VMEM((8 * 8, S), F32),
                pltpu.VMEM((8 * S, 32), F32),
                pltpu.VMEM((9 * 8 * 8, S), F32),
            ],
            "field_own",
            1 << 30,
        ),
    )
    sums = call(
        field_inside, [weights[0]] + inside + inside_speed, rows(72), contact_scratch(INSIDE, 9), "field_inside", 1 << 31
    )
    force, partial = call(
        field_outside,
        [own, own_speed, sums] + outside + outside_speed + list(weights[1:4]),
        (rows(24), jax.ShapeDtypeStruct((16, nodes), F32)),
        [pltpu.VMEM((16, 8 * S), F32)] + contact_scratch(OUTSIDE, 9),
        "field_outside",
        1 << 30,
    )
    partial = tree_sum(shared(partial, ("cross", "depth"), cross * depth))
    distance = 1
    while distance < down:
        other = lax.ppermute(partial, "down", [(i, i ^ distance) for i in range(down)])
        distance = distance * 2
        if distance < down:
            partial = partial + other
    velocity_new, force_next, residual_field, gram_matrix, moment = pl.pallas_call(
        functools.partial(library_kernel, grid),
        out_shape=(
            vector_shape,
            vector_shape,
            jax.ShapeDtypeStruct((2, 2, 2), F32),
            jax.ShapeDtypeStruct((TERMS, TERMS), F32),
            jax.ShapeDtypeStruct((1, TERMS), F32),
        ),
        in_specs=[VMEM_SPEC] * 5,
        out_specs=(VMEM_SPEC,) * 5,
        scratch_shapes=[pltpu.VMEM((TERMS, nodes), F32)],
        compiler_params=params,
        name="library",
    )(weights[4], partial, other, own_speed, force)
    return (velocity_new, force_next, residual_field, gram_matrix, moment.reshape(TERMS))


def solution(mesh):
    return jax.shard_map(
        body,
        mesh=mesh,
        in_specs=(
            P(None, ("groups", "down"), "cross", "depth", None),
            P(None, ("groups", "down"), "cross", "depth", None),
            P(("groups", "down"), "cross", "depth", None),
            P(("groups", "down"), "cross", "depth"),
            P(),
        ),
        out_specs=(
            P(None, ("groups", "down"), "cross", "depth", None),
            P(None, ("groups", "down"), "cross", "depth", None),
            P(("groups", "down"), "cross", "depth"),
            P("groups", None),
            P("groups"),
        ),
        check_vma=False,
    )
```

```python
import functools

import jax
import jax.numpy as jnp
from jax import lax
from jax.experimental import pallas as pl
from jax.experimental.pallas import tpu as pltpu
from jax.sharding import PartitionSpec as P

STIFFNESS = 100.0
DAMPING = 20.0
TIME_STEP = 0.05
KERNEL_WIDTH = 0.4
KERNEL_NORM = 64.0
SOFTENING = 0.0001
RADIUS_REF = 0.1
MASS_SHIFT = 0.1
DEAD = -1000.0
TERMS = 48
S = 128
SPREAD = 4
F32 = jnp.float32
BF16 = jnp.bfloat16
CELLS = tuple((a, b, z) for a in range(2) for b in range(2) for z in range(2))
PAIR_LIST = ((0, 0), (0, 1), (0, 2), (1, 1), (1, 2), (2, 2))
VMEM_SPEC = pl.BlockSpec(memory_space=pltpu.VMEM)
SMEM_SPEC = pl.BlockSpec(memory_space=pltpu.SMEM)
VMEM_LIMIT = 48 * 1024 * 1024


def row_ids(shape):
    return lax.broadcasted_iota(jnp.int32, shape, 0)


def lane_ids(shape):
    return lax.broadcasted_iota(jnp.int32, shape, 1)


def one_hot(condition):
    return jnp.where(condition, 1.0, 0.0).astype(BF16)


def split(value):
    high = value.astype(BF16)
    return high, value - high.astype(F32)


def matmul(left, right):
    return lax.dot_general(left, right, (((1,), (0,)), ((), ())), preferred_element_type=F32)


def matmul_turned(left, right):
    return lax.dot_general(left, right, (((1,), (1,)), ((), ())), preferred_element_type=F32)


def lane_gather(table, index):
    return jnp.take_along_axis(table, index, axis=1)


def pack_kernel(
    counts_hbm, positions_hbm, velocities_hbm, radii_hbm, own, inner, counts, positions, velocities, radii, arrived
):
    copies = [
        pltpu.make_async_copy(source, target, arrived.at[k])
        for k, (source, target) in enumerate(
            (
                (counts_hbm, counts),
                (positions_hbm, positions),
                (velocities_hbm, velocities),
                (radii_hbm, radii),
            )
        )
    ]
    for copy in copies:
        copy.start()
    for copy in copies:
        copy.wait()
    depth = lax.axis_index("depth")
    lanes = lane_ids((1, S))

    def layer(ref, at, z):
        rows = ref[at]
        return jnp.where(depth == z, rows[0:1], rows[1:2])

    for c, (a, b, z) in enumerate(CELLS):
        for k in range(3):
            own[c * 8 + k : c * 8 + k + 1, :] = layer(positions, (k, a, b), z)
            own[c * 8 + 3 + k : c * 8 + 4 + k, :] = layer(velocities, (k, a, b), z)
        count = jnp.where(depth == z, counts[a, b, 0], counts[a, b, 1])
        own[c * 8 + 6 : c * 8 + 7, :] = jnp.where(lanes < count, layer(radii, (a, b), z), DEAD)
        own[c * 8 + 7 : c * 8 + 8, :] = jnp.zeros((1, S), F32)
    for column in range(4):
        inner[column * 8 : column * 8 + 8, :] = own[column * 16 + 8 : column * 16 + 16, :]


def local_state(raw, centre):
    rows = row_ids(raw.shape)
    shift = jnp.where(rows == 0, centre[0], jnp.where(rows == 1, centre[1], centre[2]))
    return jnp.where(rows < 3, raw + shift, jnp.where(rows < 6, DAMPING * raw, raw))


def plane_reader(refs, height):
    own, depth_halo, sides = refs[0], refs[1], refs[2:]

    def read(ref, cell):
        return ref[cell * height : cell * height + height, :]

    def cell(x, y, slot):
        a = x - 1
        if y in (1, 2):
            return read(own, a * 4 + (y - 1) * 2 + slot) if slot < 2 else read(depth_halo, a * 2 + y - 1)
        if len(sides) == 4:
            before, after, diag_before, diag_after = sides
            if slot < 2:
                return read(before if y == 0 else after, a * 2 + slot)
            return read(diag_before if y == 0 else diag_after, a)
        b = 1 if y == 0 else 0
        if slot < 2:
            return read(sides[0], a * 4 + b * 2 + slot)
        return read(sides[0], 8 + a * 2 + b) if len(sides) == 1 else read(sides[1], a * 2 + b)

    return cell


def down_reader(refs, height):
    even = lax.rem(lax.axis_index("down"), 2) == 0
    swapped = lax.axis_size("down") % 2 == 0

    def cell(x, y, slot):
        if y in (1, 2):
            place = (y - 1) * 2 + slot if slot < 2 else 4 + y - 1
        else:
            side = 0 if y == 0 else 1
            place = 6 + side * 2 + slot if slot < 2 else 10 + side
        one, two = (ref[place * height : place * height + height, :] for ref in refs)
        if swapped:
            return jnp.where(even, one, two) if x == 0 else jnp.where(even, two, one)
        return one if x == 0 else two

    return cell


def centre_of(x, y, slot, depth):
    side = 0.5 - depth.astype(F32)
    return (x - 1.5, y - 1.5, (-1.0, 1.0, 3.0)[slot] * side)


BLOCK = tuple((x, y, slot) for x in (1, 2) for y in (1, 2) for slot in (0, 1))
PLANE = tuple(
    (x, y, slot) for x in (1, 2) for y in range(4) for slot in range(3) if (x, y, slot) not in BLOCK
)
INSIDE = tuple((x, y, slot) for x in (1, 2) for y in range(4) for slot in range(3))
OUTSIDE = tuple((x, y, slot) for x in (0, 3) for y in range(4) for slot in range(3))


def stepped_state(old, speed, centre):
    rows = row_ids((3, S))
    shift = jnp.where(rows == 0, centre[0], jnp.where(rows == 1, centre[1], centre[2]))
    return (old[0:3] + TIME_STEP * speed[0:3]) + shift, DAMPING * speed[0:3], old[6:8]


def contact_scratch(cells, width):
    rows = len(cells)
    return [
        pltpu.VMEM((rows * 8, S), F32),
        pltpu.VMEM((8 * 8, S), F32),
        pltpu.VMEM((8 * rows, S), jnp.int32),
        pltpu.VMEM((8 * rows, S), jnp.int32),
        pltpu.VMEM((8 * rows, S), jnp.int32),
        pltpu.VMEM((8 * rows, S), jnp.int32),
        pltpu.VMEM((18 * 8 * S, 32), F32),
        pltpu.VMEM((width * 8 * 8, S), F32),
    ]


def store_listed(list_ref, t, c, chunk, tile):
    high = tile.astype(BF16).astype(F32)
    rest = tile - high
    middle = rest.astype(BF16).astype(F32)
    turned = jnp.transpose(jnp.concatenate([high, middle, rest - middle, tile], axis=0))
    for part in range(S // chunk):
        start = pl.multiple_of(t * (8 * S) + (part * 8 + c) * chunk, chunk)
        list_ref[pl.ds(start, chunk), :] = turned[part * chunk : (part + 1) * chunk]


def pair_step(width, chunk, mine_ref, list_ref, sum_ref):
    selector = jnp.logical_and(
        row_ids((32, SPREAD * S)) % 8 == lane_ids((32, SPREAD * S)) // S, row_ids((32, SPREAD * S)) < 24
    )
    selector = one_hot(selector)

    def one_step(step, carry):
        every = list_ref[pl.ds(pl.multiple_of(step * (8 * chunk), 8 * chunk), 8 * chunk), :]
        spread = matmul(every.astype(BF16), selector)
        for c in range(8):
            listed = every[c * chunk : (c + 1) * chunk]
            me = [jnp.broadcast_to(mine_ref[c * 8 + k : c * 8 + k + 1, :], (8, S)) for k in range(7)]
            added = [None] * width
            for block in range(chunk // 8):
                row = c * chunk + block * 8
                other = [spread[row : row + 8, k * S : (k + 1) * S] for k in range(SPREAD)]
                other += [
                    jnp.broadcast_to(listed[block * 8 : block * 8 + 8, 24 + k : 25 + k], (8, S))
                    for k in range(SPREAD, 7)
                ]
                r = [me[k] - other[k] for k in range(3)]
                u = [me[3 + k] - other[3 + k] for k in range(3)]
                squared = r[0] * r[0] + r[1] * r[1] + r[2] * r[2] + SOFTENING
                inverse = lax.rsqrt(squared)
                along = u[0] * r[0] + u[1] * r[1] + u[2] * r[2]
                overlap = jnp.maximum((me[6] + other[6]) * inverse - 1.0, 0.0)
                weight = overlap * (STIFFNESS - along * inverse)
                terms = [weight * r[k] for k in range(3)]
                if width == 9:
                    terms += [terms[left] * r[right] for left, right in PAIR_LIST]
                added = [
                    term if total is None else total + term for total, term in zip(added, terms)
                ]
            for k in range(width):
                row = (k * 8 + c) * 8
                sum_ref[row : row + 8, :] += added[k]
        return carry

    return one_step


def collected(width, sum_ref):
    out = []
    for k in range(width):
        parts = [sum_ref[pl.ds(k * 64 + sub, 8, stride=8), :] for sub in range(8)]
        while len(parts) > 1:
            parts = [parts[i] + parts[i + 1] for i in range(0, len(parts), 2)]
        out.append(parts[0])
    return jnp.concatenate(out, axis=0)


def contact_sums(cells, width, chunk, scratch, skip_own=False):
    local_ref, mine_ref, index_ref, base_ref, amount_ref, chosen_ref, list_ref, sum_ref = scratch
    count = len(cells)
    span = 16 if cells == OUTSIDE else count

    def first_row(a):
        return 8 if cells == OUTSIDE and a == 1 else 0

    def beside(a, b, z):
        return [
            n
            for n, (x, y, slot) in enumerate(cells)
            if abs(x - 1 - a) <= 1 and abs(y - 1 - b) <= 1 and abs(slot - z) <= 1
            and not (skip_own and (x, y, slot) == (a + 1, b + 1, z))
        ]

    sum_ref[...] = jnp.zeros((width * 64, S), F32)
    place = [local_ref[pl.ds(k, count, stride=8), :] for k in range(3)]
    radius = local_ref[pl.ds(6, count, stride=8), :]
    rows = row_ids((count, S))
    masks = []
    for c, (a, b, z) in enumerate(CELLS):
        mine = mine_ref[c * 8 : c * 8 + 8, :]
        live = mine[6:7] > 0.0
        low = jnp.min(jnp.where(live, mine, 1e9), axis=1, keepdims=True)
        high = jnp.max(jnp.where(live, mine, -1e9), axis=1, keepdims=True)
        part = slice(first_row(a), first_row(a) + span)
        reach = radius[part] + high[6:7]
        near = reach > 0.0
        inside = set(beside(a, b, z))
        for n in range(part.start, part.stop):
            if n not in inside:
                near = jnp.logical_and(near, rows[part] != n)
        for k in range(3):
            near = jnp.logical_and(near, place[k][part] + reach > low[k : k + 1])
            near = jnp.logical_and(near, place[k][part] - reach < high[k : k + 1])
        masks.append(jnp.where(near, 1.0, 0.0).astype(F32))
    mask = jnp.concatenate(masks, axis=0).astype(BF16)
    upper = one_hot(row_ids((S, 2 * S)) <= lane_ids((S, 2 * S)))
    sums = matmul(mask, upper)
    prefix, amount = sums[:, :S], sums[:, S:]
    before = one_hot(lane_ids((span, span)) < row_ids((span, span)))
    total = None
    for c in range(8):
        part = amount[c * span : (c + 1) * span]
        base = matmul(before, part.astype(BF16))
        base_ref[c * span : (c + 1) * span, :] = base.astype(jnp.int32)
        listed = base[span - 1 : span] + part[span - 1 : span]
        total = listed if total is None else jnp.maximum(total, listed)
    most = total.astype(jnp.int32)[0, 0]
    amount_ref[0 : 8 * span, :] = amount.astype(jnp.int32)
    wanted = lane_ids((8 * span, S)).astype(F32)
    index = jnp.zeros((8 * span, S), jnp.int32)
    for step in (64, 32, 16, 8, 4, 2, 1):
        probe = lane_gather(prefix, index + (step - 1))
        index = jnp.where(probe <= wanted, index + step, index)
    index_ref[0 : 8 * span, :] = index
    empty = jnp.where(row_ids((8, S)) == 6, DEAD, 0.0).astype(F32)

    def gather_tiles(t, carry):
        want = t * S + lane_ids((8 * span, S)) - base_ref[0 : 8 * span, :]
        valid = jnp.logical_and(want >= 0, want < amount_ref[0 : 8 * span, :])
        source = lane_gather(index_ref[0 : 8 * span, :], jnp.clip(want, 0, S - 1))
        chosen_ref[0 : 8 * span, :] = jnp.where(valid, source, -1)
        for c, (a, b, z) in enumerate(CELLS):
            tile = empty
            for n in beside(a, b, z):
                row = c * span + n - first_row(a)
                pick = jnp.broadcast_to(chosen_ref[row : row + 1, :], (8, S))
                values = lane_gather(local_ref[n * 8 : n * 8 + 8, :], jnp.maximum(pick, 0))
                tile = jnp.where(pick >= 0, values, tile)
            store_listed(list_ref, t, c, chunk, tile)
        return carry

    gather_tiles(0, 0)
    lax.fori_loop(1, (most + (S - 1)) // S, gather_tiles, 0)

    lax.fori_loop(
        0, (most + (chunk - 1)) // chunk, pair_step(width, chunk, mine_ref, list_ref, sum_ref), 0
    )
    return collected(width, sum_ref)


def own_sums(width, scratch):
    mine_ref, list_ref, sum_ref = scratch
    sum_ref[...] = jnp.zeros((width * 64, S), F32)
    for c in range(8):
        store_listed(list_ref, 0, c, 64, mine_ref[c * 8 : c * 8 + 8, :])
    step = pair_step(width, 64, mine_ref, list_ref, sum_ref)
    for part in range(2):
        step(part, 0)
    return collected(width, sum_ref)


def mass_of(radius):
    scaled = radius / RADIUS_REF
    return scaled * scaled * scaled


def fill_start(cells, read, own, depth, scratch):
    for n, (x, y, slot) in enumerate(cells):
        scratch[0][n * 8 : n * 8 + 8, :] = local_state(read(x, y, slot), centre_of(x, y, slot, depth))
    for c, (a, b, z) in enumerate(CELLS):
        scratch[1][c * 8 : c * 8 + 8, :] = local_state(
            own[c * 8 : c * 8 + 8, :], centre_of(a + 1, b + 1, z, depth)
        )


def place_state(ref, start, state):
    ref[start : start + 3, :] = state[0]
    ref[start + 3 : start + 6, :] = state[1]
    ref[start + 6 : start + 8, :] = state[2]


def fill_stepped(cells, read, speed, own, own_speed, depth, scratch):
    for n, (x, y, slot) in enumerate(cells):
        state = stepped_state(read(x, y, slot), speed(x, y, slot), centre_of(x, y, slot, depth))
        place_state(scratch[0], n * 8, state)
    for c, (a, b, z) in enumerate(CELLS):
        state = stepped_state(
            own[c * 8 : c * 8 + 8, :],
            own_speed[c * 4 : c * 4 + 4, :],
            centre_of(a + 1, b + 1, z, depth),
        )
        place_state(scratch[1], c * 8, state)


def step_inside(*refs):
    pieces, sums_out, scratch = refs[:-9], refs[-9], refs[-8:]
    fill_start(INSIDE, plane_reader(pieces, 8), pieces[0], lax.axis_index("depth"), scratch)
    sums_out[...] = contact_sums(INSIDE, 3, 64, scratch)


def step_outside(own, sums_in, far, near, own_out, inner_out, *scratch):
    fill_start(OUTSIDE, down_reader((far, near), 8), own, lax.axis_index("depth"), scratch)
    sums = sums_in[...] + contact_sums(OUTSIDE, 3, 32, scratch)
    radius = own[pl.ds(6, 8, stride=8), :]
    safe_mass = jnp.where(radius > 0.0, mass_of(radius), 1.0)
    for k in range(3):
        velocity = own[pl.ds(3 + k, 8, stride=8), :] + TIME_STEP * sums[k * 8 : k * 8 + 8] / safe_mass
        for c in range(8):
            own_out[c * 4 + k : c * 4 + k + 1, :] = velocity[c : c + 1]
    for c in range(8):
        own_out[c * 4 + 3 : c * 4 + 4, :] = jnp.zeros((1, S), F32)
    for column in range(4):
        inner_out[column * 4 : column * 4 + 4, :] = own_out[column * 8 + 4 : column * 8 + 8, :]


def field_own(
    grid, own, own_speed, sums_out, high_out, low_out, chosen_out, *scratch
):
    depth = lax.axis_index("depth")
    down = lax.axis_index("down")
    cross = lax.axis_index("cross")
    rows = row_ids((64, S))
    near_x, near_y, near_z = rows // 16 - 1, (rows // 4) % 4 - 1, rows % 4 - 1
    centres = [index.astype(F32) - 0.5 for index in (near_x, near_y, near_z)]
    kernels = []
    for c, (a, b, z) in enumerate(CELLS):
        state = stepped_state(
            own[c * 8 : c * 8 + 8, :],
            own_speed[c * 4 : c * 4 + 4, :],
            centre_of(a + 1, b + 1, z, depth),
        )
        place = state[0]
        place_state(scratch[0], c * 8, state)
        squared = jnp.zeros((64, S), F32)
        for k in range(3):
            gap = place[k : k + 1] - centres[k]
            squared = squared + gap * gap
        kernel = jnp.exp(squared * (-0.5 / (KERNEL_WIDTH * KERNEL_WIDTH))) / KERNEL_NORM
        beside = jnp.logical_and(
            jnp.logical_and(jnp.abs(near_x - a) <= 1, jnp.abs(near_y - b) <= 1),
            jnp.abs(near_z - jnp.where(depth == z, 0, 1)) <= 1,
        )
        kernels.append(jnp.where(beside, kernel, 0.0))
    kernel_high, kernel_low = split(jnp.concatenate(kernels, axis=1))
    high_out[...] = kernel_high
    low_out[...] = kernel_low.astype(BF16)
    size_x, size_y, size_z = grid
    nodes = size_x * size_y * size_z
    lanes = lane_ids((64, nodes))
    row = row_ids((64, nodes))
    target_x = (down * 2 + row // 16 - 1 + size_x) % size_x
    target_y = (cross * 2 + (row // 4) % 4 - 1 + size_y) % size_y
    target_z = depth * 2 + row % 4 - 1
    inside = jnp.logical_and(target_z >= 0, target_z < size_z)
    target = (target_x * size_y + target_y) * size_z + target_z
    sums_out[...] = own_sums(9, scratch)
    chosen_out[...] = one_hot(jnp.logical_and(inside, lanes == target))


def field_inside(sums_in, coefficients, *refs):
    split_at = (len(refs) - 10) // 2
    pieces, speeds, scratch = refs[:split_at], refs[split_at:-10], refs[-8:]
    sums_out, model_out = refs[-10:-8]
    model_out[...] = coefficients[...]
    read, speed = plane_reader(pieces, 8), plane_reader(speeds, 4)
    fill_stepped(INSIDE, read, speed, pieces[0], speeds[0], lax.axis_index("depth"), scratch)
    sums_out[...] = sums_in[...] + contact_sums(INSIDE, 9, 64, scratch, True)


def field_outside(
    own, own_speed, sums_in, far_old, near_old, far_speed, near_speed, kernel_high, kernel_low, chosen,
    force_out, node_out, moment_ref, *scratch
):
    depth = lax.axis_index("depth")
    read, speed = down_reader((far_old, near_old), 8), down_reader((far_speed, near_speed), 4)
    fill_stepped(OUTSIDE, read, speed, own, own_speed, depth, scratch)
    sums = sums_in[...] + contact_sums(OUTSIDE, 9, 32, scratch)
    force_out[...] = sums[0:24]
    radius = own[pl.ds(6, 8, stride=8), :]
    mass = jnp.where(radius > 0.0, mass_of(radius), 0.0)
    moments = [mass] + [mass * own_speed[pl.ds(k, 8, stride=4), :] for k in range(3)]
    moments += [0.5 * sums[k * 8 : k * 8 + 8] for k in range(3, 9)]
    moment_ref[...] = jnp.zeros((16, 8 * S), F32)
    for m, moment in enumerate(moments):
        for c in range(8):
            moment_ref[m : m + 1, c * S : (c + 1) * S] = moment[c : c + 1]
    moment_high, moment_low = split(moment_ref[...])
    wide_part = matmul_turned(
        jnp.concatenate([moment_high, moment_low.astype(BF16)], axis=0), kernel_high[...]
    )
    near = wide_part[0:16] + wide_part[16:32] + matmul_turned(moment_high, kernel_low[...])
    near_high, rest = split(near)
    near_middle, near_low = split(rest)
    placed = matmul(
        jnp.concatenate([near_high, near_middle, near_low.astype(BF16)], axis=0), chosen[...]
    )
    node_out[...] = placed[0:16] + placed[16:32] + placed[32:48]


def library_kernel(grid, coefficients, *refs):
    fields = tree_sum([ref[...] for ref in refs[:-8]])
    speed, force, velocity_out, force_out, residual_out, gram_out, moment_out, terms = refs[-8:]
    flat = lax.axis_index("depth") == 0
    for k in range(3):
        for a in range(2):
            for b in range(2):
                c = a * 4 + b * 2
                layers = [speed[(c + z) * 4 + k : (c + z) * 4 + k + 1, :] for z in range(2)]
                pulls = [force[k * 8 + c + z : k * 8 + c + z + 1, :] for z in range(2)]
                for z in range(2):
                    velocity_out[k, a, b, z : z + 1, :] = jnp.where(flat, layers[z], layers[1 - z])
                    force_out[k, a, b, z : z + 1, :] = jnp.where(flat, pulls[z], pulls[1 - z])
    size_x, size_y, size_z = grid
    nodes = size_x * size_y * size_z
    lanes = lax.broadcasted_iota(jnp.int32, (1, nodes), 1)
    node_x = lanes // (size_y * size_z)
    node_y = (lanes // size_z) % size_y
    node_z = lanes % size_z
    rows = row_ids((8, nodes))
    density = fields[0:1]
    values = jnp.where(rows == 0, fields[0:8], fields[0:8] / (density + MASS_SHIFT))

    def moved(value, step):
        return pltpu.roll(value, step % nodes, 1)

    plane = size_y * size_z
    slope_x = (moved(values, -plane) - moved(values, plane)) * 0.5
    after_y = jnp.where(
        node_y == size_y - 1, moved(values, (size_y - 1) * size_z), moved(values, -size_z)
    )
    before_y = jnp.where(
        node_y == 0, moved(values, -(size_y - 1) * size_z), moved(values, size_z)
    )
    slope_y = (after_y - before_y) * 0.5
    after_z = jnp.where(node_z == size_z - 1, 0.0, moved(values, -1))
    before_z = jnp.where(node_z == 0, 0.0, moved(values, 1))
    slope_z = (after_z - before_z) * 0.5
    slopes = [[table[k : k + 1] for k in range(4)] for table in (slope_x, slope_y, slope_z)]
    strain = [
        [0.5 * (slopes[left][1 + right] + slopes[right][1 + left]) for right in range(3)]
        for left in range(3)
    ]
    divergence = strain[0][0] + strain[1][1] + strain[2][2]
    rate_sum = jnp.zeros_like(density)
    for left in range(3):
        for right in range(3):
            entry = strain[left][right]
            if left == right:
                entry = entry - divergence / 3.0
            rate_sum = rate_sum + entry * entry
    shear_rate = jnp.sqrt(2.0 * rate_sum + 0.01)
    stress = [fields[4 + k : 5 + k] for k in range(6)]
    pressure = (stress[0] + stress[3] + stress[5]) / 3.0
    deviator = (
        (stress[0] - pressure) ** 2
        + (stress[3] - pressure) ** 2
        + (stress[5] - pressure) ** 2
        + 2.0 * (stress[1] ** 2 + stress[2] ** 2 + stress[4] ** 2)
    )
    shear_stress = jnp.sqrt(0.5 * deviator + 0.01)
    pressure_scale = jnp.sqrt(pressure * pressure + 1.0)
    friction = shear_stress / pressure_scale
    features = [
        density,
        pressure / pressure_scale,
        shear_rate,
        shear_rate / jnp.sqrt(pressure_scale),
        divergence,
        slopes[0][0],
        slopes[1][0],
        slopes[2][0],
    ]
    entries = list(features)
    for left in range(8):
        for right in range(left, 8):
            entries.append(features[left] * features[right])
    for left in range(1, 5):
        entries.append(features[left] * features[left] * features[left])
    for k, entry in enumerate(entries):
        terms[k : k + 1, :] = entry
    table = terms[...]
    model = lax.dot_general(
        jnp.broadcast_to(coefficients[...], (8, TERMS)),
        table,
        (((1,), (0,)), ((), ())),
        precision=lax.Precision.HIGHEST,
        preferred_element_type=F32,
    )
    residual = friction - model[0:1]
    gram_out[...] = (
        lax.dot_general(
            table,
            table,
            (((1,), (1,)), ((), ())),
            precision=lax.Precision.HIGHEST,
            preferred_element_type=F32,
        )
        / nodes
    )
    moment = lax.dot_general(
        jnp.broadcast_to(friction, (8, nodes)),
        table,
        (((1,), (1,)), ((), ())),
        precision=lax.Precision.HIGHEST,
        preferred_element_type=F32,
    )
    moment_out[...] = moment[0:1] / nodes
    down = lax.axis_index("down")
    cross = lax.axis_index("cross")
    depth = lax.axis_index("depth")
    b_rows = lax.broadcasted_iota(jnp.int32, (2, 1), 0)
    z_lanes = lax.broadcasted_iota(jnp.int32, (2, 2), 1)
    for a in range(2):
        mine = jnp.logical_and(node_x == down * 2 + a, node_y == cross * 2 + b_rows)
        column = [
            jnp.sum(
                jnp.where(jnp.logical_and(mine, node_z == depth * 2 + z), residual, 0.0),
                axis=1,
                keepdims=True,
            )
            for z in range(2)
        ]
        residual_out[a] = jnp.where(z_lanes == 0, column[0], column[1])


def ring(axis, step):
    peers = lax.axis_size(axis)
    return [(i, (i + step) % peers) for i in range(peers)]


def exchange(own, inner, height, joined, beside=None):
    cross = lax.axis_size("cross")

    def cells(block, first, count):
        return block[first * height : (first + count) * height]

    if cross == 2 and not joined:
        side = lax.ppermute(own, "cross", [(0, 1), (1, 0)])
    depth_halo = lax.ppermute(inner, "depth", [(0, 1), (1, 0)])
    if cross == 2:
        if joined:
            side = lax.ppermute(
                jnp.concatenate([own, depth_halo], axis=0), "cross", [(0, 1), (1, 0)]
            )
            diag = cells(side, 8, 4)
            sides = [side]
        else:
            diag = lax.ppermute(inner, ("cross", "depth"), [(i, 3 - i) for i in range(4)])
            sides = [side, diag]

        def lateral(x):
            return [
                cells(side, x * 4 + 2, 2),
                cells(side, x * 4, 2),
                cells(diag, x * 2 + 1, 1),
                cells(diag, x * 2, 1),
            ]

    else:
        pairs = [(i * 2 + j, ((i + 1) % cross) * 2 + 1 - j) for i in range(cross) for j in range(2)]
        back = [(i * 2 + j, ((i - 1) % cross) * 2 + 1 - j) for i in range(cross) for j in range(2)]
        last = jnp.concatenate([cells(own, 2, 2), cells(own, 6, 2)], axis=0)
        first = jnp.concatenate([cells(own, 0, 2), cells(own, 4, 2)], axis=0)
        last_inner = jnp.concatenate([cells(inner, 1, 1), cells(inner, 3, 1)], axis=0)
        first_inner = jnp.concatenate([cells(inner, 0, 1), cells(inner, 2, 1)], axis=0)
        before = lax.ppermute(last, "cross", ring("cross", 1))
        after = lax.ppermute(first, "cross", ring("cross", -1))
        diag_before = lax.ppermute(last_inner, ("cross", "depth"), pairs)
        diag_after = lax.ppermute(first_inner, ("cross", "depth"), back)
        sides = [before, after, diag_before, diag_after]

        def lateral(x):
            return [
                cells(before, x * 2, 2),
                cells(after, x * 2, 2),
                cells(diag_before, x, 1),
                cells(diag_after, x, 1),
            ]

    def face(x):
        return jnp.concatenate([cells(own, x * 4, 4), cells(depth_halo, x * 2, 2)] + lateral(x), axis=0)

    downs = lax.axis_size("down")
    last, first = face(1), face(0)
    if beside is not None:
        mine, depth_halo = lax.optimization_barrier((own, depth_halo))
        last, first, result = lax.optimization_barrier((last, first, beside(mine)))
    if downs % 2 == 0:
        even = lax.rem(lax.axis_index("down"), 2) == 0
        near = [(i, i ^ 1) for i in range(downs)]
        far = [(i, (i - 1 + 2 * (i % 2)) % downs) for i in range(downs)]
        outside = [
            lax.ppermute(jnp.where(even, first, last), "down", far),
            lax.ppermute(jnp.where(even, last, first), "down", near),
        ]
    else:
        outside = [
            lax.ppermute(last, "down", ring("down", 1)),
            lax.ppermute(first, "down", ring("down", -1)),
        ]
    if beside is not None:
        return [own, depth_halo] + sides, outside, result
    return [own, depth_halo] + sides, outside


def summed_parts(value, fast, slow):
    total = fast * slow
    near = [1 << k for k in range(fast.bit_length() - 1)]
    far = [fast << k for k in range(slow.bit_length() - 1)]
    if 1 << (len(near) + len(far)) != total:
        return [lax.psum(value, ("down", "cross", "depth"))]
    parts = [value]
    for k in range(max(len(near), len(far))):
        value = tree_sum(parts)
        masks = near[k : k + 1] + far[k : k + 1]
        if len(masks) == 2:
            masks.append(masks[0] ^ masks[1])
        parts = [value] + [
            lax.ppermute(value, ("down", "cross", "depth"), [(i, i ^ mask) for i in range(total)])
            for mask in masks
        ]
    return parts


def tree_sum(parts):
    while len(parts) > 1:
        parts = [parts[k] + parts[k + 1] for k in range(0, len(parts), 2)]
    return parts[0]


def body(positions, velocities, sphere_radii, counts, coefficients):
    down, cross, depth = (lax.axis_size(name) for name in ("down", "cross", "depth"))
    grid = (2 * down, 2 * cross, 2 * depth)
    nodes = grid[0] * grid[1] * grid[2]
    params = pltpu.CompilerParams(vmem_limit_bytes=VMEM_LIMIT)
    vector_shape = jax.ShapeDtypeStruct((3, 2, 2, 2, S), F32)

    def rows(count):
        return jax.ShapeDtypeStruct((count, S), F32)

    def call(kernel, inputs, outputs, scratch, name, vectors=0):
        return pl.pallas_call(
            kernel,
            out_shape=outputs,
            in_specs=[VMEM_SPEC] * len(inputs),
            out_specs=jax.tree.map(lambda _: VMEM_SPEC, outputs),
            scratch_shapes=scratch,
            compiler_params=params,
            cost_estimate=pl.CostEstimate(flops=vectors, bytes_accessed=1 << 20, transcendentals=0),
            name=name,
        )(*inputs)

    own, inner = pl.pallas_call(
        pack_kernel,
        out_shape=(rows(64), rows(32)),
        in_specs=[pl.BlockSpec(memory_space=pl.ANY)] * 4,
        out_specs=(VMEM_SPEC, VMEM_SPEC),
        scratch_shapes=[
            pltpu.SMEM((2, 2, 2), jnp.int32),
            pltpu.VMEM((3, 2, 2, 2, S), F32),
            pltpu.VMEM((3, 2, 2, 2, S), F32),
            pltpu.VMEM((2, 2, 2, S), F32),
            pltpu.SemaphoreType.DMA((4,)),
        ],
        compiler_params=pltpu.CompilerParams(vmem_limit_bytes=60 * 1024 * 1024),
        name="pack",
    )(counts, positions, velocities, sphere_radii)
    inside, outside = exchange(own, inner, 8, True)
    sums = call(step_inside, inside, rows(24), contact_scratch(INSIDE, 3), "step_inside", 1 << 31)
    own_speed, inner_speed = call(
        step_outside, [own, sums] + outside, (rows(32), rows(16)), contact_scratch(OUTSIDE, 3), "step_outside", 1 << 30
    )
    table = jax.ShapeDtypeStruct((64, 8 * S), BF16)
    inside_speed, outside_speed, weights = exchange(
        own_speed,
        inner_speed,
        4,
        False,
        lambda speed: call(
            functools.partial(field_own, grid),
            [own, speed],
            (
                rows(72),
                table,
                table,
                jax.ShapeDtypeStruct((64, nodes), BF16),
            ),
            [
                pltpu.VMEM((8 * 8, S), F32),
                pltpu.VMEM((8 * S, 32), F32),
                pltpu.VMEM((9 * 8 * 8, S), F32),
            ],
            "field_own",
            1 << 30,
        ),
    )
    sums, model = call(
        field_inside,
        [weights[0], coefficients.reshape(1, TERMS)] + inside + inside_speed,
        (rows(72), jax.ShapeDtypeStruct((1, TERMS), F32)),
        contact_scratch(INSIDE, 9),
        "field_inside",
        1 << 31,
    )
    force, partial = call(
        field_outside,
        [own, own_speed, sums] + outside + outside_speed + list(weights[1:4]),
        (rows(24), jax.ShapeDtypeStruct((16, nodes), F32)),
        [pltpu.VMEM((16, 8 * S), F32)] + contact_scratch(OUTSIDE, 9),
        "field_outside",
        1 << 30,
    )
    parts = summed_parts(partial, depth * cross, down)
    velocity_new, force_next, residual_field, gram_matrix, moment = pl.pallas_call(
        functools.partial(library_kernel, grid),
        out_shape=(
            vector_shape,
            vector_shape,
            jax.ShapeDtypeStruct((2, 2, 2), F32),
            jax.ShapeDtypeStruct((TERMS, TERMS), F32),
            jax.ShapeDtypeStruct((1, TERMS), F32),
        ),
        in_specs=[VMEM_SPEC] * (3 + len(parts)),
        out_specs=(VMEM_SPEC,) * 5,
        scratch_shapes=[pltpu.VMEM((TERMS, nodes), F32)],
        compiler_params=params,
        name="library",
    )(model, *parts, own_speed, force)
    return (velocity_new, force_next, residual_field, gram_matrix, moment.reshape(TERMS))


def solution(mesh):
    return jax.shard_map(
        body,
        mesh=mesh,
        in_specs=(
            P(None, ("groups", "down"), "cross", "depth", None),
            P(None, ("groups", "down"), "cross", "depth", None),
            P(("groups", "down"), "cross", "depth", None),
            P(("groups", "down"), "cross", "depth"),
            P(),
        ),
        out_specs=(
            P(None, ("groups", "down"), "cross", "depth", None),
            P(None, ("groups", "down"), "cross", "depth", None),
            P(("groups", "down"), "cross", "depth"),
            P("groups", None),
            P("groups"),
        ),
        check_vma=False,
    )
```

```python
import functools

import jax
import jax.numpy as jnp
from jax import lax
from jax.experimental import pallas as pl
from jax.experimental.pallas import tpu as pltpu
from jax.sharding import PartitionSpec as P

STIFFNESS = 100.0
DAMPING = 20.0
TIME_STEP = 0.05
KERNEL_WIDTH = 0.4
KERNEL_NORM = 64.0
SOFTENING = 0.0001
RADIUS_REF = 0.1
MASS_SHIFT = 0.1
DEAD = -1000.0
TERMS = 48
S = 128
SPREAD = 4
F32 = jnp.float32
BF16 = jnp.bfloat16
CELLS = tuple((a, b, z) for a in range(2) for b in range(2) for z in range(2))
PAIR_LIST = ((0, 0), (0, 1), (0, 2), (1, 1), (1, 2), (2, 2))
VMEM_SPEC = pl.BlockSpec(memory_space=pltpu.VMEM)
SMEM_SPEC = pl.BlockSpec(memory_space=pltpu.SMEM)
VMEM_LIMIT = 48 * 1024 * 1024


def row_ids(shape):
    return lax.broadcasted_iota(jnp.int32, shape, 0)


def lane_ids(shape):
    return lax.broadcasted_iota(jnp.int32, shape, 1)


def one_hot(condition):
    return jnp.where(condition, 1.0, 0.0).astype(BF16)


def split(value):
    high = value.astype(BF16)
    return high, value - high.astype(F32)


def matmul(left, right):
    return lax.dot_general(left, right, (((1,), (0,)), ((), ())), preferred_element_type=F32)


def matmul_turned(left, right):
    return lax.dot_general(left, right, (((1,), (1,)), ((), ())), preferred_element_type=F32)


def lane_gather(table, index):
    return jnp.take_along_axis(table, index, axis=1)


def pack_kernel(
    counts_hbm, positions_hbm, velocities_hbm, radii_hbm, own, inner, counts, positions, velocities, radii, arrived
):
    copies = [
        pltpu.make_async_copy(source, target, arrived.at[k])
        for k, (source, target) in enumerate(
            (
                (counts_hbm, counts),
                (positions_hbm, positions),
                (velocities_hbm, velocities),
                (radii_hbm, radii),
            )
        )
    ]
    for copy in copies:
        copy.start()
    for copy in copies:
        copy.wait()
    depth = lax.axis_index("depth")
    lanes = lane_ids((1, S))

    def layer(ref, at, z):
        rows = ref[at]
        return jnp.where(depth == z, rows[0:1], rows[1:2])

    for c, (a, b, z) in enumerate(CELLS):
        for k in range(3):
            own[c * 8 + k : c * 8 + k + 1, :] = layer(positions, (k, a, b), z)
            own[c * 8 + 3 + k : c * 8 + 4 + k, :] = layer(velocities, (k, a, b), z)
        count = jnp.where(depth == z, counts[a, b, 0], counts[a, b, 1])
        own[c * 8 + 6 : c * 8 + 7, :] = jnp.where(lanes < count, layer(radii, (a, b), z), DEAD)
        own[c * 8 + 7 : c * 8 + 8, :] = jnp.zeros((1, S), F32)
    for column in range(4):
        inner[column * 8 : column * 8 + 8, :] = own[column * 16 + 8 : column * 16 + 16, :]


def local_state(raw, centre):
    rows = row_ids(raw.shape)
    shift = jnp.where(rows == 0, centre[0], jnp.where(rows == 1, centre[1], centre[2]))
    return jnp.where(rows < 3, raw + shift, jnp.where(rows < 6, DAMPING * raw, raw))


def plane_reader(refs, height):
    own, depth_halo, sides = refs[0], refs[1], refs[2:]

    def read(ref, cell):
        return ref[cell * height : cell * height + height, :]

    def cell(x, y, slot):
        a = x - 1
        if y in (1, 2):
            return read(own, a * 4 + (y - 1) * 2 + slot) if slot < 2 else read(depth_halo, a * 2 + y - 1)
        if len(sides) == 4:
            before, after, diag_before, diag_after = sides
            if slot < 2:
                return read(before if y == 0 else after, a * 2 + slot)
            return read(diag_before if y == 0 else diag_after, a)
        b = 1 if y == 0 else 0
        if slot < 2:
            return read(sides[0], a * 4 + b * 2 + slot)
        return read(sides[0], 8 + a * 2 + b) if len(sides) == 1 else read(sides[1], a * 2 + b)

    return cell


def down_reader(refs, height):
    even = lax.rem(lax.axis_index("down"), 2) == 0
    swapped = lax.axis_size("down") % 2 == 0

    def cell(x, y, slot):
        if y in (1, 2):
            place = (y - 1) * 2 + slot if slot < 2 else 4 + y - 1
        else:
            side = 0 if y == 0 else 1
            place = 6 + side * 2 + slot if slot < 2 else 10 + side
        one, two = (ref[place * height : place * height + height, :] for ref in refs)
        if swapped:
            return jnp.where(even, one, two) if x == 0 else jnp.where(even, two, one)
        return one if x == 0 else two

    return cell


def centre_of(x, y, slot, depth):
    side = 0.5 - depth.astype(F32)
    return (x - 1.5, y - 1.5, (-1.0, 1.0, 3.0)[slot] * side)


BLOCK = tuple((x, y, slot) for x in (1, 2) for y in (1, 2) for slot in (0, 1))
PLANE = tuple(
    (x, y, slot) for x in (1, 2) for y in range(4) for slot in range(3) if (x, y, slot) not in BLOCK
)
INSIDE = tuple((x, y, slot) for x in (1, 2) for y in range(4) for slot in range(3))
OUTSIDE = tuple((x, y, slot) for x in (0, 3) for y in range(4) for slot in range(3))


def stepped_state(old, speed, centre):
    rows = row_ids((3, S))
    shift = jnp.where(rows == 0, centre[0], jnp.where(rows == 1, centre[1], centre[2]))
    return (old[0:3] + TIME_STEP * speed[0:3]) + shift, DAMPING * speed[0:3], old[6:8]


def contact_scratch(cells, width):
    rows = len(cells)
    return [
        pltpu.VMEM((rows * 8, S), F32),
        pltpu.VMEM((8 * 8, S), F32),
        pltpu.VMEM((8 * rows, S), jnp.int32),
        pltpu.VMEM((8 * rows, S), jnp.int32),
        pltpu.VMEM((8 * rows, S), jnp.int32),
        pltpu.VMEM((8 * rows, S), jnp.int32),
        pltpu.VMEM((18 * 8 * S, 32), F32),
        pltpu.VMEM((width * 8 * 8, S), F32),
    ]


def store_listed(list_ref, t, c, chunk, tile):
    high = tile.astype(BF16).astype(F32)
    rest = tile - high
    middle = rest.astype(BF16).astype(F32)
    turned = jnp.transpose(jnp.concatenate([high, middle, rest - middle, tile], axis=0))
    for part in range(S // chunk):
        start = pl.multiple_of(t * (8 * S) + (part * 8 + c) * chunk, chunk)
        list_ref[pl.ds(start, chunk), :] = turned[part * chunk : (part + 1) * chunk]


def pair_step(width, chunk, mine_ref, list_ref, sum_ref):
    selector = jnp.logical_and(
        row_ids((32, SPREAD * S)) % 8 == lane_ids((32, SPREAD * S)) // S, row_ids((32, SPREAD * S)) < 24
    )
    selector = one_hot(selector)

    def one_step(step, carry):
        every = list_ref[pl.ds(pl.multiple_of(step * (8 * chunk), 8 * chunk), 8 * chunk), :]
        spread = matmul(every.astype(BF16), selector)
        for c in range(8):
            listed = every[c * chunk : (c + 1) * chunk]
            me = [jnp.broadcast_to(mine_ref[c * 8 + k : c * 8 + k + 1, :], (8, S)) for k in range(7)]
            added = [None] * width
            for block in range(chunk // 8):
                row = c * chunk + block * 8
                other = [spread[row : row + 8, k * S : (k + 1) * S] for k in range(SPREAD)]
                other += [
                    jnp.broadcast_to(listed[block * 8 : block * 8 + 8, 24 + k : 25 + k], (8, S))
                    for k in range(SPREAD, 7)
                ]
                r = [me[k] - other[k] for k in range(3)]
                u = [me[3 + k] - other[3 + k] for k in range(3)]
                squared = r[0] * r[0] + r[1] * r[1] + r[2] * r[2] + SOFTENING
                inverse = lax.rsqrt(squared)
                along = u[0] * r[0] + u[1] * r[1] + u[2] * r[2]
                overlap = jnp.maximum((me[6] + other[6]) * inverse - 1.0, 0.0)
                weight = overlap * (STIFFNESS - along * inverse)
                terms = [weight * r[k] for k in range(3)]
                if width == 9:
                    terms += [terms[left] * r[right] for left, right in PAIR_LIST]
                added = [
                    term if total is None else total + term for total, term in zip(added, terms)
                ]
            for k in range(width):
                row = (k * 8 + c) * 8
                sum_ref[row : row + 8, :] += added[k]
        return carry

    return one_step


def collected(width, sum_ref):
    out = []
    for k in range(width):
        parts = [sum_ref[pl.ds(k * 64 + sub, 8, stride=8), :] for sub in range(8)]
        while len(parts) > 1:
            parts = [parts[i] + parts[i + 1] for i in range(0, len(parts), 2)]
        out.append(parts[0])
    return jnp.concatenate(out, axis=0)


def contact_sums(cells, width, chunk, scratch, skip_own=False):
    local_ref, mine_ref, index_ref, base_ref, amount_ref, chosen_ref, list_ref, sum_ref = scratch
    count = len(cells)
    span = 16 if cells == OUTSIDE else count

    def first_row(a):
        return 8 if cells == OUTSIDE and a == 1 else 0

    def beside(a, b, z):
        return [
            n
            for n, (x, y, slot) in enumerate(cells)
            if abs(x - 1 - a) <= 1 and abs(y - 1 - b) <= 1 and abs(slot - z) <= 1
            and not (skip_own and (x, y, slot) == (a + 1, b + 1, z))
        ]

    sum_ref[...] = jnp.zeros((width * 64, S), F32)
    place = [local_ref[pl.ds(k, count, stride=8), :] for k in range(3)]
    radius = local_ref[pl.ds(6, count, stride=8), :]
    rows = row_ids((count, S))
    masks = []
    for c, (a, b, z) in enumerate(CELLS):
        mine = mine_ref[c * 8 : c * 8 + 8, :]
        live = mine[6:7] > 0.0
        low = jnp.min(jnp.where(live, mine, 1e9), axis=1, keepdims=True)
        high = jnp.max(jnp.where(live, mine, -1e9), axis=1, keepdims=True)
        part = slice(first_row(a), first_row(a) + span)
        reach = radius[part] + high[6:7]
        near = reach > 0.0
        inside = set(beside(a, b, z))
        for n in range(part.start, part.stop):
            if n not in inside:
                near = jnp.logical_and(near, rows[part] != n)
        for k in range(3):
            near = jnp.logical_and(near, place[k][part] + reach > low[k : k + 1])
            near = jnp.logical_and(near, place[k][part] - reach < high[k : k + 1])
        masks.append(jnp.where(near, 1.0, 0.0).astype(F32))
    mask = jnp.concatenate(masks, axis=0).astype(BF16)
    upper = one_hot(row_ids((S, 2 * S)) <= lane_ids((S, 2 * S)))
    sums = matmul(mask, upper)
    prefix, amount = sums[:, :S], sums[:, S:]
    before = one_hot(lane_ids((span, span)) < row_ids((span, span)))
    total = None
    for c in range(8):
        part = amount[c * span : (c + 1) * span]
        base = matmul(before, part.astype(BF16))
        base_ref[c * span : (c + 1) * span, :] = base.astype(jnp.int32)
        listed = base[span - 1 : span] + part[span - 1 : span]
        total = listed if total is None else jnp.maximum(total, listed)
    most = total.astype(jnp.int32)[0, 0]
    amount_ref[0 : 8 * span, :] = amount.astype(jnp.int32)
    wanted = lane_ids((8 * span, S)).astype(F32)
    index = jnp.zeros((8 * span, S), jnp.int32)
    for step in (64, 32, 16, 8, 4, 2, 1):
        probe = lane_gather(prefix, index + (step - 1))
        index = jnp.where(probe <= wanted, index + step, index)
    index_ref[0 : 8 * span, :] = index
    empty = jnp.where(row_ids((8, S)) == 6, DEAD, 0.0).astype(F32)

    def gather_tiles(t, carry):
        want = t * S + lane_ids((8 * span, S)) - base_ref[0 : 8 * span, :]
        valid = jnp.logical_and(want >= 0, want < amount_ref[0 : 8 * span, :])
        source = lane_gather(index_ref[0 : 8 * span, :], jnp.clip(want, 0, S - 1))
        chosen_ref[0 : 8 * span, :] = jnp.where(valid, source, -1)
        for c, (a, b, z) in enumerate(CELLS):
            tile = empty
            for n in beside(a, b, z):
                row = c * span + n - first_row(a)
                pick = jnp.broadcast_to(chosen_ref[row : row + 1, :], (8, S))
                values = lane_gather(local_ref[n * 8 : n * 8 + 8, :], jnp.maximum(pick, 0))
                tile = jnp.where(pick >= 0, values, tile)
            store_listed(list_ref, t, c, chunk, tile)
        return carry

    gather_tiles(0, 0)
    lax.fori_loop(1, (most + (S - 1)) // S, gather_tiles, 0)

    lax.fori_loop(
        0, (most + (chunk - 1)) // chunk, pair_step(width, chunk, mine_ref, list_ref, sum_ref), 0
    )
    return collected(width, sum_ref)


def own_sums(width, scratch):
    mine_ref, list_ref, sum_ref = scratch
    sum_ref[...] = jnp.zeros((width * 64, S), F32)
    for c in range(8):
        store_listed(list_ref, 0, c, 64, mine_ref[c * 8 : c * 8 + 8, :])
    step = pair_step(width, 64, mine_ref, list_ref, sum_ref)
    for part in range(2):
        step(part, 0)
    return collected(width, sum_ref)


def mass_of(radius):
    scaled = radius / RADIUS_REF
    return scaled * scaled * scaled


def fill_start(cells, read, own, depth, scratch):
    for n, (x, y, slot) in enumerate(cells):
        scratch[0][n * 8 : n * 8 + 8, :] = local_state(read(x, y, slot), centre_of(x, y, slot, depth))
    for c, (a, b, z) in enumerate(CELLS):
        scratch[1][c * 8 : c * 8 + 8, :] = local_state(
            own[c * 8 : c * 8 + 8, :], centre_of(a + 1, b + 1, z, depth)
        )


def place_state(ref, start, state):
    ref[start : start + 3, :] = state[0]
    ref[start + 3 : start + 6, :] = state[1]
    ref[start + 6 : start + 8, :] = state[2]


def fill_stepped(cells, read, speed, own, own_speed, depth, scratch):
    for n, (x, y, slot) in enumerate(cells):
        state = stepped_state(read(x, y, slot), speed(x, y, slot), centre_of(x, y, slot, depth))
        place_state(scratch[0], n * 8, state)
    for c, (a, b, z) in enumerate(CELLS):
        state = stepped_state(
            own[c * 8 : c * 8 + 8, :],
            own_speed[c * 4 : c * 4 + 4, :],
            centre_of(a + 1, b + 1, z, depth),
        )
        place_state(scratch[1], c * 8, state)


def step_inside(*refs):
    pieces, sums_out, scratch = refs[:-9], refs[-9], refs[-8:]
    fill_start(INSIDE, plane_reader(pieces, 8), pieces[0], lax.axis_index("depth"), scratch)
    sums_out[...] = contact_sums(INSIDE, 3, 64, scratch)


def step_outside(own, sums_in, far, near, own_out, inner_out, *scratch):
    fill_start(OUTSIDE, down_reader((far, near), 8), own, lax.axis_index("depth"), scratch)
    sums = sums_in[...] + contact_sums(OUTSIDE, 3, 32, scratch)
    radius = own[pl.ds(6, 8, stride=8), :]
    safe_mass = jnp.where(radius > 0.0, mass_of(radius), 1.0)
    for k in range(3):
        velocity = own[pl.ds(3 + k, 8, stride=8), :] + TIME_STEP * sums[k * 8 : k * 8 + 8] / safe_mass
        for c in range(8):
            own_out[c * 4 + k : c * 4 + k + 1, :] = velocity[c : c + 1]
    for c in range(8):
        own_out[c * 4 + 3 : c * 4 + 4, :] = jnp.zeros((1, S), F32)
    for column in range(4):
        inner_out[column * 4 : column * 4 + 4, :] = own_out[column * 8 + 4 : column * 8 + 8, :]


def field_own(
    grid, own, own_speed, sums_out, high_out, low_out, chosen_out, *scratch
):
    depth = lax.axis_index("depth")
    down = lax.axis_index("down")
    cross = lax.axis_index("cross")
    rows = row_ids((64, S))
    near_x, near_y, near_z = rows // 16 - 1, (rows // 4) % 4 - 1, rows % 4 - 1
    centres = [index.astype(F32) - 0.5 for index in (near_x, near_y, near_z)]
    kernels = []
    for c, (a, b, z) in enumerate(CELLS):
        state = stepped_state(
            own[c * 8 : c * 8 + 8, :],
            own_speed[c * 4 : c * 4 + 4, :],
            centre_of(a + 1, b + 1, z, depth),
        )
        place = state[0]
        place_state(scratch[0], c * 8, state)
        squared = jnp.zeros((64, S), F32)
        for k in range(3):
            gap = place[k : k + 1] - centres[k]
            squared = squared + gap * gap
        kernel = jnp.exp(squared * (-0.5 / (KERNEL_WIDTH * KERNEL_WIDTH))) / KERNEL_NORM
        beside = jnp.logical_and(
            jnp.logical_and(jnp.abs(near_x - a) <= 1, jnp.abs(near_y - b) <= 1),
            jnp.abs(near_z - jnp.where(depth == z, 0, 1)) <= 1,
        )
        kernels.append(jnp.where(beside, kernel, 0.0))
    kernel_high, kernel_low = split(jnp.concatenate(kernels, axis=1))
    high_out[...] = kernel_high
    low_out[...] = kernel_low.astype(BF16)
    size_x, size_y, size_z = grid
    nodes = size_x * size_y * size_z
    lanes = lane_ids((64, nodes))
    row = row_ids((64, nodes))
    target_x = (down * 2 + row // 16 - 1 + size_x) % size_x
    target_y = (cross * 2 + (row // 4) % 4 - 1 + size_y) % size_y
    target_z = depth * 2 + row % 4 - 1
    inside = jnp.logical_and(target_z >= 0, target_z < size_z)
    target = (target_x * size_y + target_y) * size_z + target_z
    sums_out[...] = own_sums(9, scratch)
    chosen_out[...] = one_hot(jnp.logical_and(inside, lanes == target))


def field_inside(sums_in, coefficients, *refs):
    split_at = (len(refs) - 10) // 2
    pieces, speeds, scratch = refs[:split_at], refs[split_at:-10], refs[-8:]
    sums_out, model_out = refs[-10:-8]
    model_out[...] = coefficients[...]
    read, speed = plane_reader(pieces, 8), plane_reader(speeds, 4)
    fill_stepped(INSIDE, read, speed, pieces[0], speeds[0], lax.axis_index("depth"), scratch)
    sums_out[...] = sums_in[...] + contact_sums(INSIDE, 9, 64, scratch, True)


def field_outside(
    own, own_speed, sums_in, far_old, near_old, far_speed, near_speed, kernel_high, kernel_low, chosen,
    force_out, node_out, moment_ref, *scratch
):
    depth = lax.axis_index("depth")
    read, speed = down_reader((far_old, near_old), 8), down_reader((far_speed, near_speed), 4)
    fill_stepped(OUTSIDE, read, speed, own, own_speed, depth, scratch)
    sums = sums_in[...] + contact_sums(OUTSIDE, 9, 64, scratch)
    force_out[...] = sums[0:24]
    radius = own[pl.ds(6, 8, stride=8), :]
    mass = jnp.where(radius > 0.0, mass_of(radius), 0.0)
    moments = [mass] + [mass * own_speed[pl.ds(k, 8, stride=4), :] for k in range(3)]
    moments += [0.5 * sums[k * 8 : k * 8 + 8] for k in range(3, 9)]
    moment_ref[...] = jnp.zeros((16, 8 * S), F32)
    for m, moment in enumerate(moments):
        for c in range(8):
            moment_ref[m : m + 1, c * S : (c + 1) * S] = moment[c : c + 1]
    moment_high, moment_low = split(moment_ref[...])
    wide_part = matmul_turned(
        jnp.concatenate([moment_high, moment_low.astype(BF16)], axis=0), kernel_high[...]
    )
    near = wide_part[0:16] + wide_part[16:32] + matmul_turned(moment_high, kernel_low[...])
    near_high, rest = split(near)
    near_middle, near_low = split(rest)
    placed = matmul(
        jnp.concatenate([near_high, near_middle, near_low.astype(BF16)], axis=0), chosen[...]
    )
    node_out[...] = placed[0:16] + placed[16:32] + placed[32:48]


def library_kernel(grid, coefficients, *refs):
    fields = tree_sum([ref[...] for ref in refs[:-8]])
    speed, force, velocity_out, force_out, residual_out, gram_out, moment_out, terms = refs[-8:]
    flat = lax.axis_index("depth") == 0
    for k in range(3):
        for a in range(2):
            for b in range(2):
                c = a * 4 + b * 2
                layers = [speed[(c + z) * 4 + k : (c + z) * 4 + k + 1, :] for z in range(2)]
                pulls = [force[k * 8 + c + z : k * 8 + c + z + 1, :] for z in range(2)]
                for z in range(2):
                    velocity_out[k, a, b, z : z + 1, :] = jnp.where(flat, layers[z], layers[1 - z])
                    force_out[k, a, b, z : z + 1, :] = jnp.where(flat, pulls[z], pulls[1 - z])
    size_x, size_y, size_z = grid
    nodes = size_x * size_y * size_z
    lanes = lax.broadcasted_iota(jnp.int32, (1, nodes), 1)
    node_x = lanes // (size_y * size_z)
    node_y = (lanes // size_z) % size_y
    node_z = lanes % size_z
    rows = row_ids((8, nodes))
    density = fields[0:1]
    values = jnp.where(rows == 0, fields[0:8], fields[0:8] / (density + MASS_SHIFT))

    def moved(value, step):
        return pltpu.roll(value, step % nodes, 1)

    plane = size_y * size_z
    slope_x = (moved(values, -plane) - moved(values, plane)) * 0.5
    after_y = jnp.where(
        node_y == size_y - 1, moved(values, (size_y - 1) * size_z), moved(values, -size_z)
    )
    before_y = jnp.where(
        node_y == 0, moved(values, -(size_y - 1) * size_z), moved(values, size_z)
    )
    slope_y = (after_y - before_y) * 0.5
    after_z = jnp.where(node_z == size_z - 1, 0.0, moved(values, -1))
    before_z = jnp.where(node_z == 0, 0.0, moved(values, 1))
    slope_z = (after_z - before_z) * 0.5
    slopes = [[table[k : k + 1] for k in range(4)] for table in (slope_x, slope_y, slope_z)]
    strain = [
        [0.5 * (slopes[left][1 + right] + slopes[right][1 + left]) for right in range(3)]
        for left in range(3)
    ]
    divergence = strain[0][0] + strain[1][1] + strain[2][2]
    rate_sum = jnp.zeros_like(density)
    for left in range(3):
        for right in range(3):
            entry = strain[left][right]
            if left == right:
                entry = entry - divergence / 3.0
            rate_sum = rate_sum + entry * entry
    shear_rate = jnp.sqrt(2.0 * rate_sum + 0.01)
    stress = [fields[4 + k : 5 + k] for k in range(6)]
    pressure = (stress[0] + stress[3] + stress[5]) / 3.0
    deviator = (
        (stress[0] - pressure) ** 2
        + (stress[3] - pressure) ** 2
        + (stress[5] - pressure) ** 2
        + 2.0 * (stress[1] ** 2 + stress[2] ** 2 + stress[4] ** 2)
    )
    shear_stress = jnp.sqrt(0.5 * deviator + 0.01)
    pressure_scale = jnp.sqrt(pressure * pressure + 1.0)
    friction = shear_stress / pressure_scale
    features = [
        density,
        pressure / pressure_scale,
        shear_rate,
        shear_rate / jnp.sqrt(pressure_scale),
        divergence,
        slopes[0][0],
        slopes[1][0],
        slopes[2][0],
    ]
    entries = list(features)
    for left in range(8):
        for right in range(left, 8):
            entries.append(features[left] * features[right])
    for left in range(1, 5):
        entries.append(features[left] * features[left] * features[left])
    for k, entry in enumerate(entries):
        terms[k : k + 1, :] = entry
    table = terms[...]
    model = lax.dot_general(
        jnp.broadcast_to(coefficients[...], (8, TERMS)),
        table,
        (((1,), (0,)), ((), ())),
        precision=lax.Precision.HIGHEST,
        preferred_element_type=F32,
    )
    residual = friction - model[0:1]
    gram_out[...] = (
        lax.dot_general(
            table,
            table,
            (((1,), (1,)), ((), ())),
            precision=lax.Precision.HIGHEST,
            preferred_element_type=F32,
        )
        / nodes
    )
    moment = lax.dot_general(
        jnp.broadcast_to(friction, (8, nodes)),
        table,
        (((1,), (1,)), ((), ())),
        precision=lax.Precision.HIGHEST,
        preferred_element_type=F32,
    )
    moment_out[...] = moment[0:1] / nodes
    down = lax.axis_index("down")
    cross = lax.axis_index("cross")
    depth = lax.axis_index("depth")
    b_rows = lax.broadcasted_iota(jnp.int32, (2, 1), 0)
    z_lanes = lax.broadcasted_iota(jnp.int32, (2, 2), 1)
    for a in range(2):
        mine = jnp.logical_and(node_x == down * 2 + a, node_y == cross * 2 + b_rows)
        column = [
            jnp.sum(
                jnp.where(jnp.logical_and(mine, node_z == depth * 2 + z), residual, 0.0),
                axis=1,
                keepdims=True,
            )
            for z in range(2)
        ]
        residual_out[a] = jnp.where(z_lanes == 0, column[0], column[1])


def ring(axis, step):
    peers = lax.axis_size(axis)
    return [(i, (i + step) % peers) for i in range(peers)]


def exchange(own, inner, height, joined, beside=None):
    cross = lax.axis_size("cross")

    def cells(block, first, count):
        return block[first * height : (first + count) * height]

    if cross == 2 and not joined:
        side = lax.ppermute(own, "cross", [(0, 1), (1, 0)])
    depth_halo = lax.ppermute(inner, "depth", [(0, 1), (1, 0)])
    if cross == 2:
        if joined:
            side = lax.ppermute(
                jnp.concatenate([own, depth_halo], axis=0), "cross", [(0, 1), (1, 0)]
            )
            diag = cells(side, 8, 4)
            sides = [side]
        else:
            diag = lax.ppermute(inner, ("cross", "depth"), [(i, 3 - i) for i in range(4)])
            sides = [side, diag]

        def lateral(x):
            return [
                cells(side, x * 4 + 2, 2),
                cells(side, x * 4, 2),
                cells(diag, x * 2 + 1, 1),
                cells(diag, x * 2, 1),
            ]

    else:
        pairs = [(i * 2 + j, ((i + 1) % cross) * 2 + 1 - j) for i in range(cross) for j in range(2)]
        back = [(i * 2 + j, ((i - 1) % cross) * 2 + 1 - j) for i in range(cross) for j in range(2)]
        last = jnp.concatenate([cells(own, 2, 2), cells(own, 6, 2)], axis=0)
        first = jnp.concatenate([cells(own, 0, 2), cells(own, 4, 2)], axis=0)
        last_inner = jnp.concatenate([cells(inner, 1, 1), cells(inner, 3, 1)], axis=0)
        first_inner = jnp.concatenate([cells(inner, 0, 1), cells(inner, 2, 1)], axis=0)
        before = lax.ppermute(last, "cross", ring("cross", 1))
        after = lax.ppermute(first, "cross", ring("cross", -1))
        diag_before = lax.ppermute(last_inner, ("cross", "depth"), pairs)
        diag_after = lax.ppermute(first_inner, ("cross", "depth"), back)
        sides = [before, after, diag_before, diag_after]

        def lateral(x):
            return [
                cells(before, x * 2, 2),
                cells(after, x * 2, 2),
                cells(diag_before, x, 1),
                cells(diag_after, x, 1),
            ]

    def face(x):
        return jnp.concatenate([cells(own, x * 4, 4), cells(depth_halo, x * 2, 2)] + lateral(x), axis=0)

    downs = lax.axis_size("down")
    last, first = face(1), face(0)
    if beside is not None:
        mine, depth_halo = lax.optimization_barrier((own, depth_halo))
        last, first, result = lax.optimization_barrier((last, first, beside(mine)))
    if downs % 2 == 0:
        even = lax.rem(lax.axis_index("down"), 2) == 0
        near = [(i, i ^ 1) for i in range(downs)]
        far = [(i, (i - 1 + 2 * (i % 2)) % downs) for i in range(downs)]
        outside = [
            lax.ppermute(jnp.where(even, first, last), "down", far),
            lax.ppermute(jnp.where(even, last, first), "down", near),
        ]
    else:
        outside = [
            lax.ppermute(last, "down", ring("down", 1)),
            lax.ppermute(first, "down", ring("down", -1)),
        ]
    if beside is not None:
        return [own, depth_halo] + sides, outside, result
    return [own, depth_halo] + sides, outside


def summed_parts(value, fast, slow):
    total = fast * slow
    near = [1 << k for k in range(fast.bit_length() - 1)][::-1]
    far = [fast << k for k in range(slow.bit_length() - 1)]
    if 1 << (len(near) + len(far)) != total:
        return [lax.psum(value, ("down", "cross", "depth"))]
    parts = [value]
    for k in range(max(len(near), len(far))):
        value = tree_sum(parts)
        masks = near[k : k + 1] + far[k : k + 1]
        if len(masks) == 2:
            masks.append(masks[0] ^ masks[1])
        parts = [value] + [
            lax.ppermute(value, ("down", "cross", "depth"), [(i, i ^ mask) for i in range(total)])
            for mask in masks
        ]
    return parts


def tree_sum(parts):
    while len(parts) > 1:
        parts = [parts[k] + parts[k + 1] for k in range(0, len(parts), 2)]
    return parts[0]


def body(positions, velocities, sphere_radii, counts, coefficients):
    down, cross, depth = (lax.axis_size(name) for name in ("down", "cross", "depth"))
    grid = (2 * down, 2 * cross, 2 * depth)
    nodes = grid[0] * grid[1] * grid[2]
    params = pltpu.CompilerParams(vmem_limit_bytes=VMEM_LIMIT)
    vector_shape = jax.ShapeDtypeStruct((3, 2, 2, 2, S), F32)

    def rows(count):
        return jax.ShapeDtypeStruct((count, S), F32)

    def call(kernel, inputs, outputs, scratch, name, vectors=0):
        return pl.pallas_call(
            kernel,
            out_shape=outputs,
            in_specs=[VMEM_SPEC] * len(inputs),
            out_specs=jax.tree.map(lambda _: VMEM_SPEC, outputs),
            scratch_shapes=scratch,
            compiler_params=params,
            cost_estimate=pl.CostEstimate(flops=vectors, bytes_accessed=1 << 20, transcendentals=0),
            name=name,
        )(*inputs)

    own, inner = pl.pallas_call(
        pack_kernel,
        out_shape=(rows(64), rows(32)),
        in_specs=[pl.BlockSpec(memory_space=pl.ANY)] * 4,
        out_specs=(VMEM_SPEC, VMEM_SPEC),
        scratch_shapes=[
            pltpu.SMEM((2, 2, 2), jnp.int32),
            pltpu.VMEM((3, 2, 2, 2, S), F32),
            pltpu.VMEM((3, 2, 2, 2, S), F32),
            pltpu.VMEM((2, 2, 2, S), F32),
            pltpu.SemaphoreType.DMA((4,)),
        ],
        compiler_params=pltpu.CompilerParams(vmem_limit_bytes=60 * 1024 * 1024),
        name="pack",
    )(counts, positions, velocities, sphere_radii)
    inside, outside = exchange(own, inner, 8, True)
    sums = call(step_inside, inside, rows(24), contact_scratch(INSIDE, 3), "step_inside", 1 << 31)
    own_speed, inner_speed = call(
        step_outside, [own, sums] + outside, (rows(32), rows(16)), contact_scratch(OUTSIDE, 3), "step_outside", 1 << 30
    )
    table = jax.ShapeDtypeStruct((64, 8 * S), BF16)
    inside_speed, outside_speed, weights = exchange(
        own_speed,
        inner_speed,
        4,
        False,
        lambda speed: call(
            functools.partial(field_own, grid),
            [own, speed],
            (
                rows(72),
                table,
                table,
                jax.ShapeDtypeStruct((64, nodes), BF16),
            ),
            [
                pltpu.VMEM((8 * 8, S), F32),
                pltpu.VMEM((8 * S, 32), F32),
                pltpu.VMEM((9 * 8 * 8, S), F32),
            ],
            "field_own",
            1 << 30,
        ),
    )
    sums, model = call(
        field_inside,
        [weights[0], coefficients.reshape(1, TERMS)] + inside + inside_speed,
        (rows(72), jax.ShapeDtypeStruct((1, TERMS), F32)),
        contact_scratch(INSIDE, 9),
        "field_inside",
        1 << 31,
    )
    force, partial = call(
        field_outside,
        [own, own_speed, sums] + outside + outside_speed + list(weights[1:4]),
        (rows(24), jax.ShapeDtypeStruct((16, nodes), F32)),
        [pltpu.VMEM((16, 8 * S), F32)] + contact_scratch(OUTSIDE, 9),
        "field_outside",
        1 << 30,
    )
    parts = summed_parts(partial, depth * cross, down)
    velocity_new, force_next, residual_field, gram_matrix, moment = pl.pallas_call(
        functools.partial(library_kernel, grid),
        out_shape=(
            vector_shape,
            vector_shape,
            jax.ShapeDtypeStruct((2, 2, 2), F32),
            jax.ShapeDtypeStruct((TERMS, TERMS), F32),
            jax.ShapeDtypeStruct((1, TERMS), F32),
        ),
        in_specs=[VMEM_SPEC] * (3 + len(parts)),
        out_specs=(VMEM_SPEC,) * 5,
        scratch_shapes=[pltpu.VMEM((TERMS, nodes), F32)],
        compiler_params=params,
        name="library",
    )(model, *parts, own_speed, force)
    return (velocity_new, force_next, residual_field, gram_matrix, moment.reshape(TERMS))


def solution(mesh):
    return jax.shard_map(
        body,
        mesh=mesh,
        in_specs=(
            P(None, ("groups", "down"), "cross", "depth", None),
            P(None, ("groups", "down"), "cross", "depth", None),
            P(("groups", "down"), "cross", "depth", None),
            P(("groups", "down"), "cross", "depth"),
            P(),
        ),
        out_specs=(
            P(None, ("groups", "down"), "cross", "depth", None),
            P(None, ("groups", "down"), "cross", "depth", None),
            P(("groups", "down"), "cross", "depth"),
            P("groups", None),
            P("groups"),
        ),
        check_vma=False,
    )
```

```python
import functools

import jax
import jax.numpy as jnp
from jax import lax
from jax.experimental import pallas as pl
from jax.experimental.pallas import tpu as pltpu
from jax.sharding import PartitionSpec as P

STIFFNESS = 100.0
DAMPING = 20.0
TIME_STEP = 0.05
KERNEL_WIDTH = 0.4
KERNEL_NORM = 64.0
SOFTENING = 0.0001
RADIUS_REF = 0.1
MASS_SHIFT = 0.1
DEAD = -1000.0
TERMS = 48
S = 128
SPREAD = 4
F32 = jnp.float32
BF16 = jnp.bfloat16
CELLS = tuple((a, b, z) for a in range(2) for b in range(2) for z in range(2))
PAIR_LIST = ((0, 0), (0, 1), (0, 2), (1, 1), (1, 2), (2, 2))
VMEM_SPEC = pl.BlockSpec(memory_space=pltpu.VMEM)
SMEM_SPEC = pl.BlockSpec(memory_space=pltpu.SMEM)
VMEM_LIMIT = 48 * 1024 * 1024


def row_ids(shape):
    return lax.broadcasted_iota(jnp.int32, shape, 0)


def lane_ids(shape):
    return lax.broadcasted_iota(jnp.int32, shape, 1)


def one_hot(condition):
    return jnp.where(condition, 1.0, 0.0).astype(BF16)


def split(value):
    high = value.astype(BF16)
    return high, value - high.astype(F32)


def matmul(left, right):
    return lax.dot_general(left, right, (((1,), (0,)), ((), ())), preferred_element_type=F32)


def matmul_turned(left, right):
    return lax.dot_general(left, right, (((1,), (1,)), ((), ())), preferred_element_type=F32)


def lane_gather(table, index):
    return jnp.take_along_axis(table, index, axis=1)


def pack_kernel(
    counts_hbm, positions_hbm, velocities_hbm, radii_hbm, own, inner, counts, positions, velocities, radii, arrived
):
    copies = [
        pltpu.make_async_copy(source, target, arrived.at[k])
        for k, (source, target) in enumerate(
            (
                (counts_hbm, counts),
                (positions_hbm, positions),
                (velocities_hbm, velocities),
                (radii_hbm, radii),
            )
        )
    ]
    for copy in copies:
        copy.start()
    for copy in copies:
        copy.wait()
    depth = lax.axis_index("depth")
    lanes = lane_ids((1, S))

    def layer(ref, at, z):
        rows = ref[at]
        return jnp.where(depth == z, rows[0:1], rows[1:2])

    for c, (a, b, z) in enumerate(CELLS):
        for k in range(3):
            own[c * 8 + k : c * 8 + k + 1, :] = layer(positions, (k, a, b), z)
            own[c * 8 + 3 + k : c * 8 + 4 + k, :] = layer(velocities, (k, a, b), z)
        count = jnp.where(depth == z, counts[a, b, 0], counts[a, b, 1])
        own[c * 8 + 6 : c * 8 + 7, :] = jnp.where(lanes < count, layer(radii, (a, b), z), DEAD)
        own[c * 8 + 7 : c * 8 + 8, :] = jnp.zeros((1, S), F32)
    for column in range(4):
        inner[column * 8 : column * 8 + 8, :] = own[column * 16 + 8 : column * 16 + 16, :]


def local_state(raw, centre):
    rows = row_ids(raw.shape)
    shift = jnp.where(rows == 0, centre[0], jnp.where(rows == 1, centre[1], centre[2]))
    return jnp.where(rows < 3, raw + shift, jnp.where(rows < 6, DAMPING * raw, raw))


def plane_reader(refs, height):
    own, depth_halo, sides = refs[0], refs[1], refs[2:]

    def read(ref, cell):
        return ref[cell * height : cell * height + height, :]

    def cell(x, y, slot):
        a = x - 1
        if y in (1, 2):
            return read(own, a * 4 + (y - 1) * 2 + slot) if slot < 2 else read(depth_halo, a * 2 + y - 1)
        if len(sides) == 4:
            before, after, diag_before, diag_after = sides
            if slot < 2:
                return read(before if y == 0 else after, a * 2 + slot)
            return read(diag_before if y == 0 else diag_after, a)
        b = 1 if y == 0 else 0
        if slot < 2:
            return read(sides[0], a * 4 + b * 2 + slot)
        return read(sides[0], 8 + a * 2 + b) if len(sides) == 1 else read(sides[1], a * 2 + b)

    return cell


def down_reader(refs, height):
    even = lax.rem(lax.axis_index("down"), 2) == 0
    swapped = lax.axis_size("down") % 2 == 0

    def cell(x, y, slot):
        if y in (1, 2):
            place = (y - 1) * 2 + slot if slot < 2 else 4 + y - 1
        else:
            side = 0 if y == 0 else 1
            place = 6 + side * 2 + slot if slot < 2 else 10 + side
        one, two = (ref[place * height : place * height + height, :] for ref in refs)
        if swapped:
            return jnp.where(even, one, two) if x == 0 else jnp.where(even, two, one)
        return one if x == 0 else two

    return cell


def centre_of(x, y, slot, depth):
    side = 0.5 - depth.astype(F32)
    return (x - 1.5, y - 1.5, (-1.0, 1.0, 3.0)[slot] * side)


BLOCK = tuple((x, y, slot) for x in (1, 2) for y in (1, 2) for slot in (0, 1))
PLANE = tuple(
    (x, y, slot) for x in (1, 2) for y in range(4) for slot in range(3) if (x, y, slot) not in BLOCK
)
INSIDE = tuple((x, y, slot) for x in (1, 2) for y in range(4) for slot in range(3))
OUTSIDE = tuple((x, y, slot) for x in (0, 3) for y in range(4) for slot in range(3))


def stepped_state(old, speed, centre):
    rows = row_ids((3, S))
    shift = jnp.where(rows == 0, centre[0], jnp.where(rows == 1, centre[1], centre[2]))
    return (old[0:3] + TIME_STEP * speed[0:3]) + shift, DAMPING * speed[0:3], old[6:8]


def contact_scratch(cells, width):
    rows = len(cells)
    return [
        pltpu.VMEM((rows * 8, S), F32),
        pltpu.VMEM((8 * 8, S), F32),
        pltpu.VMEM((8 * rows, S), jnp.int32),
        pltpu.VMEM((8 * rows, S), jnp.int32),
        pltpu.VMEM((8 * rows, S), jnp.int32),
        pltpu.VMEM((8 * rows, S), jnp.int32),
        pltpu.VMEM((18 * 8 * S, 32), F32),
        pltpu.VMEM((width * 8 * 8, S), F32),
    ]


def store_listed(list_ref, t, c, chunk, tile):
    high = tile.astype(BF16).astype(F32)
    rest = tile - high
    middle = rest.astype(BF16).astype(F32)
    turned = jnp.transpose(jnp.concatenate([high, middle, rest - middle, tile], axis=0))
    for part in range(S // chunk):
        start = pl.multiple_of(t * (8 * S) + (part * 8 + c) * chunk, chunk)
        list_ref[pl.ds(start, chunk), :] = turned[part * chunk : (part + 1) * chunk]


def pair_step(width, chunk, mine_ref, list_ref, sum_ref):
    selector = jnp.logical_and(
        row_ids((32, SPREAD * S)) % 8 == lane_ids((32, SPREAD * S)) // S, row_ids((32, SPREAD * S)) < 24
    )
    selector = one_hot(selector)

    def one_step(step, carry):
        every = list_ref[pl.ds(pl.multiple_of(step * (8 * chunk), 8 * chunk), 8 * chunk), :]
        spread = matmul(every.astype(BF16), selector)
        for c in range(8):
            listed = every[c * chunk : (c + 1) * chunk]
            me = [jnp.broadcast_to(mine_ref[c * 8 + k : c * 8 + k + 1, :], (8, S)) for k in range(7)]
            added = [None] * width
            for block in range(chunk // 8):
                row = c * chunk + block * 8
                other = [spread[row : row + 8, k * S : (k + 1) * S] for k in range(SPREAD)]
                other += [
                    jnp.broadcast_to(listed[block * 8 : block * 8 + 8, 24 + k : 25 + k], (8, S))
                    for k in range(SPREAD, 7)
                ]
                r = [me[k] - other[k] for k in range(3)]
                u = [me[3 + k] - other[3 + k] for k in range(3)]
                squared = r[0] * r[0] + r[1] * r[1] + r[2] * r[2] + SOFTENING
                inverse = lax.rsqrt(squared)
                along = u[0] * r[0] + u[1] * r[1] + u[2] * r[2]
                overlap = jnp.maximum((me[6] + other[6]) * inverse - 1.0, 0.0)
                weight = overlap * (STIFFNESS - along * inverse)
                terms = [weight * r[k] for k in range(3)]
                if width == 9:
                    terms += [terms[left] * r[right] for left, right in PAIR_LIST]
                added = [
                    term if total is None else total + term for total, term in zip(added, terms)
                ]
            for k in range(width):
                row = (k * 8 + c) * 8
                sum_ref[row : row + 8, :] += added[k]
        return carry

    return one_step


def collected(width, sum_ref):
    out = []
    for k in range(width):
        parts = [sum_ref[pl.ds(k * 64 + sub, 8, stride=8), :] for sub in range(8)]
        while len(parts) > 1:
            parts = [parts[i] + parts[i + 1] for i in range(0, len(parts), 2)]
        out.append(parts[0])
    return jnp.concatenate(out, axis=0)


def contact_sums(cells, width, chunk, scratch, skip_own=False):
    local_ref, mine_ref, index_ref, base_ref, amount_ref, chosen_ref, list_ref, sum_ref = scratch
    count = len(cells)
    span = 16 if cells == OUTSIDE else count

    def first_row(a):
        return 8 if cells == OUTSIDE and a == 1 else 0

    def beside(a, b, z):
        return [
            n
            for n, (x, y, slot) in enumerate(cells)
            if abs(x - 1 - a) <= 1 and abs(y - 1 - b) <= 1 and abs(slot - z) <= 1
            and not (skip_own and (x, y, slot) == (a + 1, b + 1, z))
        ]

    sum_ref[...] = jnp.zeros((width * 64, S), F32)
    place = [local_ref[pl.ds(k, count, stride=8), :] for k in range(3)]
    radius = local_ref[pl.ds(6, count, stride=8), :]
    rows = row_ids((count, S))
    masks = []
    for c, (a, b, z) in enumerate(CELLS):
        mine = mine_ref[c * 8 : c * 8 + 8, :]
        live = mine[6:7] > 0.0
        low = jnp.min(jnp.where(live, mine, 1e9), axis=1, keepdims=True)
        high = jnp.max(jnp.where(live, mine, -1e9), axis=1, keepdims=True)
        part = slice(first_row(a), first_row(a) + span)
        reach = radius[part] + high[6:7]
        near = reach > 0.0
        inside = set(beside(a, b, z))
        for n in range(part.start, part.stop):
            if n not in inside:
                near = jnp.logical_and(near, rows[part] != n)
        for k in range(3):
            near = jnp.logical_and(near, place[k][part] + reach > low[k : k + 1])
            near = jnp.logical_and(near, place[k][part] - reach < high[k : k + 1])
        masks.append(jnp.where(near, 1.0, 0.0).astype(F32))
    mask = jnp.concatenate(masks, axis=0).astype(BF16)
    upper = one_hot(row_ids((S, 2 * S)) <= lane_ids((S, 2 * S)))
    sums = matmul(mask, upper)
    prefix, amount = sums[:, :S], sums[:, S:]
    before = one_hot(lane_ids((span, span)) < row_ids((span, span)))
    total = None
    for c in range(8):
        part = amount[c * span : (c + 1) * span]
        base = matmul(before, part.astype(BF16))
        base_ref[c * span : (c + 1) * span, :] = base.astype(jnp.int32)
        listed = base[span - 1 : span] + part[span - 1 : span]
        total = listed if total is None else jnp.maximum(total, listed)
    most = total.astype(jnp.int32)[0, 0]
    amount_ref[0 : 8 * span, :] = amount.astype(jnp.int32)
    wanted = lane_ids((8 * span, S)).astype(F32)
    index = jnp.zeros((8 * span, S), jnp.int32)
    for step in (64, 32, 16, 8, 4, 2, 1):
        probe = lane_gather(prefix, index + (step - 1))
        index = jnp.where(probe <= wanted, index + step, index)
    index_ref[0 : 8 * span, :] = index
    empty = jnp.where(row_ids((8, S)) == 6, DEAD, 0.0).astype(F32)

    def gather_tiles(t, carry):
        want = t * S + lane_ids((8 * span, S)) - base_ref[0 : 8 * span, :]
        valid = jnp.logical_and(want >= 0, want < amount_ref[0 : 8 * span, :])
        source = lane_gather(index_ref[0 : 8 * span, :], jnp.clip(want, 0, S - 1))
        chosen_ref[0 : 8 * span, :] = jnp.where(valid, source, -1)
        for c, (a, b, z) in enumerate(CELLS):
            tile = empty
            for n in beside(a, b, z):
                row = c * span + n - first_row(a)
                pick = jnp.broadcast_to(chosen_ref[row : row + 1, :], (8, S))
                values = lane_gather(local_ref[n * 8 : n * 8 + 8, :], jnp.maximum(pick, 0))
                tile = jnp.where(pick >= 0, values, tile)
            store_listed(list_ref, t, c, chunk, tile)
        return carry

    gather_tiles(0, 0)
    lax.fori_loop(1, (most + (S - 1)) // S, gather_tiles, 0)

    lax.fori_loop(
        0, (most + (chunk - 1)) // chunk, pair_step(width, chunk, mine_ref, list_ref, sum_ref), 0
    )
    return collected(width, sum_ref)


def own_sums(width, scratch):
    mine_ref, list_ref, sum_ref = scratch
    sum_ref[...] = jnp.zeros((width * 64, S), F32)
    for c in range(8):
        store_listed(list_ref, 0, c, 64, mine_ref[c * 8 : c * 8 + 8, :])
    step = pair_step(width, 64, mine_ref, list_ref, sum_ref)
    for part in range(2):
        step(part, 0)
    return collected(width, sum_ref)


def mass_of(radius):
    scaled = radius / RADIUS_REF
    return scaled * scaled * scaled


def fill_start(cells, read, own, depth, scratch):
    for n, (x, y, slot) in enumerate(cells):
        scratch[0][n * 8 : n * 8 + 8, :] = local_state(read(x, y, slot), centre_of(x, y, slot, depth))
    for c, (a, b, z) in enumerate(CELLS):
        scratch[1][c * 8 : c * 8 + 8, :] = local_state(
            own[c * 8 : c * 8 + 8, :], centre_of(a + 1, b + 1, z, depth)
        )


def place_state(ref, start, state):
    ref[start : start + 3, :] = state[0]
    ref[start + 3 : start + 6, :] = state[1]
    ref[start + 6 : start + 8, :] = state[2]


def fill_stepped(cells, read, speed, own, own_speed, depth, scratch):
    for n, (x, y, slot) in enumerate(cells):
        state = stepped_state(read(x, y, slot), speed(x, y, slot), centre_of(x, y, slot, depth))
        place_state(scratch[0], n * 8, state)
    for c, (a, b, z) in enumerate(CELLS):
        state = stepped_state(
            own[c * 8 : c * 8 + 8, :],
            own_speed[c * 4 : c * 4 + 4, :],
            centre_of(a + 1, b + 1, z, depth),
        )
        place_state(scratch[1], c * 8, state)


def step_own(own, sums_out, *scratch):
    depth = lax.axis_index("depth")
    for c, (a, b, z) in enumerate(CELLS):
        scratch[0][c * 8 : c * 8 + 8, :] = local_state(
            own[c * 8 : c * 8 + 8, :], centre_of(a + 1, b + 1, z, depth)
        )
    sums_out[...] = own_sums(3, scratch)


def step_inside(sums_in, *refs):
    pieces, sums_out, scratch = refs[:-9], refs[-9], refs[-8:]
    fill_start(INSIDE, plane_reader(pieces, 8), pieces[0], lax.axis_index("depth"), scratch)
    sums_out[...] = sums_in[...] + contact_sums(INSIDE, 3, 64, scratch, True)


def step_outside(own, sums_in, far, near, own_out, inner_out, *scratch):
    fill_start(OUTSIDE, down_reader((far, near), 8), own, lax.axis_index("depth"), scratch)
    sums = sums_in[...] + contact_sums(OUTSIDE, 3, 32, scratch)
    radius = own[pl.ds(6, 8, stride=8), :]
    safe_mass = jnp.where(radius > 0.0, mass_of(radius), 1.0)
    for k in range(3):
        velocity = own[pl.ds(3 + k, 8, stride=8), :] + TIME_STEP * sums[k * 8 : k * 8 + 8] / safe_mass
        for c in range(8):
            own_out[c * 4 + k : c * 4 + k + 1, :] = velocity[c : c + 1]
    for c in range(8):
        own_out[c * 4 + 3 : c * 4 + 4, :] = jnp.zeros((1, S), F32)
    for column in range(4):
        inner_out[column * 4 : column * 4 + 4, :] = own_out[column * 8 + 4 : column * 8 + 8, :]


def field_own(
    grid, own, own_speed, sums_out, high_out, low_out, chosen_out, *scratch
):
    depth = lax.axis_index("depth")
    down = lax.axis_index("down")
    cross = lax.axis_index("cross")
    rows = row_ids((64, S))
    near_x, near_y, near_z = rows // 16 - 1, (rows // 4) % 4 - 1, rows % 4 - 1
    centres = [index.astype(F32) - 0.5 for index in (near_x, near_y, near_z)]
    kernels = []
    for c, (a, b, z) in enumerate(CELLS):
        state = stepped_state(
            own[c * 8 : c * 8 + 8, :],
            own_speed[c * 4 : c * 4 + 4, :],
            centre_of(a + 1, b + 1, z, depth),
        )
        place = state[0]
        place_state(scratch[0], c * 8, state)
        squared = jnp.zeros((64, S), F32)
        for k in range(3):
            gap = place[k : k + 1] - centres[k]
            squared = squared + gap * gap
        kernel = jnp.exp(squared * (-0.5 / (KERNEL_WIDTH * KERNEL_WIDTH))) / KERNEL_NORM
        beside = jnp.logical_and(
            jnp.logical_and(jnp.abs(near_x - a) <= 1, jnp.abs(near_y - b) <= 1),
            jnp.abs(near_z - jnp.where(depth == z, 0, 1)) <= 1,
        )
        kernels.append(jnp.where(beside, kernel, 0.0))
    kernel_high, kernel_low = split(jnp.concatenate(kernels, axis=1))
    high_out[...] = kernel_high
    low_out[...] = kernel_low.astype(BF16)
    size_x, size_y, size_z = grid
    nodes = size_x * size_y * size_z
    lanes = lane_ids((64, nodes))
    row = row_ids((64, nodes))
    target_x = (down * 2 + row // 16 - 1 + size_x) % size_x
    target_y = (cross * 2 + (row // 4) % 4 - 1 + size_y) % size_y
    target_z = depth * 2 + row % 4 - 1
    inside = jnp.logical_and(target_z >= 0, target_z < size_z)
    target = (target_x * size_y + target_y) * size_z + target_z
    sums_out[...] = own_sums(9, scratch)
    chosen_out[...] = one_hot(jnp.logical_and(inside, lanes == target))


def field_inside(sums_in, coefficients, *refs):
    split_at = (len(refs) - 10) // 2
    pieces, speeds, scratch = refs[:split_at], refs[split_at:-10], refs[-8:]
    sums_out, model_out = refs[-10:-8]
    model_out[...] = coefficients[...]
    read, speed = plane_reader(pieces, 8), plane_reader(speeds, 4)
    fill_stepped(INSIDE, read, speed, pieces[0], speeds[0], lax.axis_index("depth"), scratch)
    sums_out[...] = sums_in[...] + contact_sums(INSIDE, 9, 64, scratch, True)


def field_outside(
    own, own_speed, sums_in, far_old, near_old, far_speed, near_speed, kernel_high, kernel_low, chosen,
    force_out, node_out, moment_ref, *scratch
):
    depth = lax.axis_index("depth")
    read, speed = down_reader((far_old, near_old), 8), down_reader((far_speed, near_speed), 4)
    fill_stepped(OUTSIDE, read, speed, own, own_speed, depth, scratch)
    sums = sums_in[...] + contact_sums(OUTSIDE, 9, 64, scratch)
    force_out[...] = sums[0:24]
    radius = own[pl.ds(6, 8, stride=8), :]
    mass = jnp.where(radius > 0.0, mass_of(radius), 0.0)
    moments = [mass] + [mass * own_speed[pl.ds(k, 8, stride=4), :] for k in range(3)]
    moments += [0.5 * sums[k * 8 : k * 8 + 8] for k in range(3, 9)]
    moment_ref[...] = jnp.zeros((16, 8 * S), F32)
    for m, moment in enumerate(moments):
        for c in range(8):
            moment_ref[m : m + 1, c * S : (c + 1) * S] = moment[c : c + 1]
    moment_high, moment_low = split(moment_ref[...])
    wide_part = matmul_turned(
        jnp.concatenate([moment_high, moment_low.astype(BF16)], axis=0), kernel_high[...]
    )
    near = wide_part[0:16] + wide_part[16:32] + matmul_turned(moment_high, kernel_low[...])
    near_high, rest = split(near)
    near_middle, near_low = split(rest)
    placed = matmul(
        jnp.concatenate([near_high, near_middle, near_low.astype(BF16)], axis=0), chosen[...]
    )
    node_out[...] = placed[0:16] + placed[16:32] + placed[32:48]


def library_kernel(grid, coefficients, *refs):
    fields = tree_sum([ref[...] for ref in refs[:-8]])
    speed, force, velocity_out, force_out, residual_out, gram_out, moment_out, terms = refs[-8:]
    flat = lax.axis_index("depth") == 0
    for k in range(3):
        for a in range(2):
            for b in range(2):
                c = a * 4 + b * 2
                layers = [speed[(c + z) * 4 + k : (c + z) * 4 + k + 1, :] for z in range(2)]
                pulls = [force[k * 8 + c + z : k * 8 + c + z + 1, :] for z in range(2)]
                for z in range(2):
                    velocity_out[k, a, b, z : z + 1, :] = jnp.where(flat, layers[z], layers[1 - z])
                    force_out[k, a, b, z : z + 1, :] = jnp.where(flat, pulls[z], pulls[1 - z])
    size_x, size_y, size_z = grid
    nodes = size_x * size_y * size_z
    lanes = lax.broadcasted_iota(jnp.int32, (1, nodes), 1)
    node_x = lanes // (size_y * size_z)
    node_y = (lanes // size_z) % size_y
    node_z = lanes % size_z
    rows = row_ids((8, nodes))
    density = fields[0:1]
    values = jnp.where(rows == 0, fields[0:8], fields[0:8] / (density + MASS_SHIFT))

    def moved(value, step):
        return pltpu.roll(value, step % nodes, 1)

    plane = size_y * size_z
    slope_x = (moved(values, -plane) - moved(values, plane)) * 0.5
    after_y = jnp.where(
        node_y == size_y - 1, moved(values, (size_y - 1) * size_z), moved(values, -size_z)
    )
    before_y = jnp.where(
        node_y == 0, moved(values, -(size_y - 1) * size_z), moved(values, size_z)
    )
    slope_y = (after_y - before_y) * 0.5
    after_z = jnp.where(node_z == size_z - 1, 0.0, moved(values, -1))
    before_z = jnp.where(node_z == 0, 0.0, moved(values, 1))
    slope_z = (after_z - before_z) * 0.5
    slopes = [[table[k : k + 1] for k in range(4)] for table in (slope_x, slope_y, slope_z)]
    strain = [
        [0.5 * (slopes[left][1 + right] + slopes[right][1 + left]) for right in range(3)]
        for left in range(3)
    ]
    divergence = strain[0][0] + strain[1][1] + strain[2][2]
    rate_sum = jnp.zeros_like(density)
    for left in range(3):
        for right in range(3):
            entry = strain[left][right]
            if left == right:
                entry = entry - divergence / 3.0
            rate_sum = rate_sum + entry * entry
    shear_rate = jnp.sqrt(2.0 * rate_sum + 0.01)
    stress = [fields[4 + k : 5 + k] for k in range(6)]
    pressure = (stress[0] + stress[3] + stress[5]) / 3.0
    deviator = (
        (stress[0] - pressure) ** 2
        + (stress[3] - pressure) ** 2
        + (stress[5] - pressure) ** 2
        + 2.0 * (stress[1] ** 2 + stress[2] ** 2 + stress[4] ** 2)
    )
    shear_stress = jnp.sqrt(0.5 * deviator + 0.01)
    pressure_scale = jnp.sqrt(pressure * pressure + 1.0)
    friction = shear_stress / pressure_scale
    features = [
        density,
        pressure / pressure_scale,
        shear_rate,
        shear_rate / jnp.sqrt(pressure_scale),
        divergence,
        slopes[0][0],
        slopes[1][0],
        slopes[2][0],
    ]
    entries = list(features)
    for left in range(8):
        for right in range(left, 8):
            entries.append(features[left] * features[right])
    for left in range(1, 5):
        entries.append(features[left] * features[left] * features[left])
    for k, entry in enumerate(entries):
        terms[k : k + 1, :] = entry
    table = terms[...]
    model = lax.dot_general(
        jnp.broadcast_to(coefficients[...], (8, TERMS)),
        table,
        (((1,), (0,)), ((), ())),
        precision=lax.Precision.HIGHEST,
        preferred_element_type=F32,
    )
    residual = friction - model[0:1]
    gram_out[...] = (
        lax.dot_general(
            table,
            table,
            (((1,), (1,)), ((), ())),
            precision=lax.Precision.HIGHEST,
            preferred_element_type=F32,
        )
        / nodes
    )
    moment = lax.dot_general(
        jnp.broadcast_to(friction, (8, nodes)),
        table,
        (((1,), (1,)), ((), ())),
        precision=lax.Precision.HIGHEST,
        preferred_element_type=F32,
    )
    moment_out[...] = moment[0:1] / nodes
    down = lax.axis_index("down")
    cross = lax.axis_index("cross")
    depth = lax.axis_index("depth")
    b_rows = lax.broadcasted_iota(jnp.int32, (2, 1), 0)
    z_lanes = lax.broadcasted_iota(jnp.int32, (2, 2), 1)
    for a in range(2):
        mine = jnp.logical_and(node_x == down * 2 + a, node_y == cross * 2 + b_rows)
        column = [
            jnp.sum(
                jnp.where(jnp.logical_and(mine, node_z == depth * 2 + z), residual, 0.0),
                axis=1,
                keepdims=True,
            )
            for z in range(2)
        ]
        residual_out[a] = jnp.where(z_lanes == 0, column[0], column[1])


def ring(axis, step):
    peers = lax.axis_size(axis)
    return [(i, (i + step) % peers) for i in range(peers)]


def exchange(own, inner, height, joined, beside=None):
    cross = lax.axis_size("cross")

    def cells(block, first, count):
        return block[first * height : (first + count) * height]

    if cross == 2 and not joined:
        side = lax.ppermute(own, "cross", [(0, 1), (1, 0)])
    depth_halo = lax.ppermute(inner, "depth", [(0, 1), (1, 0)])
    if cross == 2:
        if joined:
            side = lax.ppermute(
                jnp.concatenate([own, depth_halo], axis=0), "cross", [(0, 1), (1, 0)]
            )
            diag = cells(side, 8, 4)
            sides = [side]
        else:
            diag = lax.ppermute(inner, ("cross", "depth"), [(i, 3 - i) for i in range(4)])
            sides = [side, diag]

        def lateral(x):
            return [
                cells(side, x * 4 + 2, 2),
                cells(side, x * 4, 2),
                cells(diag, x * 2 + 1, 1),
                cells(diag, x * 2, 1),
            ]

    else:
        pairs = [(i * 2 + j, ((i + 1) % cross) * 2 + 1 - j) for i in range(cross) for j in range(2)]
        back = [(i * 2 + j, ((i - 1) % cross) * 2 + 1 - j) for i in range(cross) for j in range(2)]
        last = jnp.concatenate([cells(own, 2, 2), cells(own, 6, 2)], axis=0)
        first = jnp.concatenate([cells(own, 0, 2), cells(own, 4, 2)], axis=0)
        last_inner = jnp.concatenate([cells(inner, 1, 1), cells(inner, 3, 1)], axis=0)
        first_inner = jnp.concatenate([cells(inner, 0, 1), cells(inner, 2, 1)], axis=0)
        before = lax.ppermute(last, "cross", ring("cross", 1))
        after = lax.ppermute(first, "cross", ring("cross", -1))
        diag_before = lax.ppermute(last_inner, ("cross", "depth"), pairs)
        diag_after = lax.ppermute(first_inner, ("cross", "depth"), back)
        sides = [before, after, diag_before, diag_after]

        def lateral(x):
            return [
                cells(before, x * 2, 2),
                cells(after, x * 2, 2),
                cells(diag_before, x, 1),
                cells(diag_after, x, 1),
            ]

    def face(x):
        return jnp.concatenate([cells(own, x * 4, 4), cells(depth_halo, x * 2, 2)] + lateral(x), axis=0)

    downs = lax.axis_size("down")
    last, first = face(1), face(0)
    if beside is not None:
        mine, depth_halo = lax.optimization_barrier((own, depth_halo))
        last, first, result = lax.optimization_barrier((last, first, beside(mine)))
    if downs % 2 == 0:
        even = lax.rem(lax.axis_index("down"), 2) == 0
        near = [(i, i ^ 1) for i in range(downs)]
        far = [(i, (i - 1 + 2 * (i % 2)) % downs) for i in range(downs)]
        outside = [
            lax.ppermute(jnp.where(even, first, last), "down", far),
            lax.ppermute(jnp.where(even, last, first), "down", near),
        ]
    else:
        outside = [
            lax.ppermute(last, "down", ring("down", 1)),
            lax.ppermute(first, "down", ring("down", -1)),
        ]
    if beside is not None:
        return [own, depth_halo] + sides, outside, result
    return [own, depth_halo] + sides, outside


def summed_parts(value, fast, slow):
    total = fast * slow
    near = [1 << k for k in range(fast.bit_length() - 1)][::-1]
    far = [fast << k for k in range(slow.bit_length() - 1)]
    if 1 << (len(near) + len(far)) != total:
        return [lax.psum(value, ("down", "cross", "depth"))]
    parts = [value]
    for k in range(max(len(near), len(far))):
        value = tree_sum(parts)
        masks = near[k : k + 1] + far[k : k + 1]
        if len(masks) == 2:
            masks.append(masks[0] ^ masks[1])
        parts = [value] + [
            lax.ppermute(value, ("down", "cross", "depth"), [(i, i ^ mask) for i in range(total)])
            for mask in masks
        ]
    return parts


def tree_sum(parts):
    while len(parts) > 1:
        parts = [parts[k] + parts[k + 1] for k in range(0, len(parts), 2)]
    return parts[0]


def body(positions, velocities, sphere_radii, counts, coefficients):
    down, cross, depth = (lax.axis_size(name) for name in ("down", "cross", "depth"))
    grid = (2 * down, 2 * cross, 2 * depth)
    nodes = grid[0] * grid[1] * grid[2]
    params = pltpu.CompilerParams(vmem_limit_bytes=VMEM_LIMIT)
    vector_shape = jax.ShapeDtypeStruct((3, 2, 2, 2, S), F32)

    def rows(count):
        return jax.ShapeDtypeStruct((count, S), F32)

    def call(kernel, inputs, outputs, scratch, name, vectors=0):
        return pl.pallas_call(
            kernel,
            out_shape=outputs,
            in_specs=[VMEM_SPEC] * len(inputs),
            out_specs=jax.tree.map(lambda _: VMEM_SPEC, outputs),
            scratch_shapes=scratch,
            compiler_params=params,
            cost_estimate=pl.CostEstimate(flops=vectors, bytes_accessed=1 << 20, transcendentals=0),
            name=name,
        )(*inputs)

    own, inner = pl.pallas_call(
        pack_kernel,
        out_shape=(rows(64), rows(32)),
        in_specs=[pl.BlockSpec(memory_space=pl.ANY)] * 4,
        out_specs=(VMEM_SPEC, VMEM_SPEC),
        scratch_shapes=[
            pltpu.SMEM((2, 2, 2), jnp.int32),
            pltpu.VMEM((3, 2, 2, 2, S), F32),
            pltpu.VMEM((3, 2, 2, 2, S), F32),
            pltpu.VMEM((2, 2, 2, S), F32),
            pltpu.SemaphoreType.DMA((4,)),
        ],
        compiler_params=pltpu.CompilerParams(vmem_limit_bytes=60 * 1024 * 1024),
        name="pack",
    )(counts, positions, velocities, sphere_radii)
    def own_scratch(width):
        return [
            pltpu.VMEM((8 * 8, S), F32),
            pltpu.VMEM((8 * S, 32), F32),
            pltpu.VMEM((width * 8 * 8, S), F32),
        ]

    inside, outside, sums = exchange(
        own,
        inner,
        8,
        True,
        lambda mine: call(step_own, [mine], rows(24), own_scratch(3), "step_own", 1 << 30),
    )
    sums = call(
        step_inside, [sums] + inside, rows(24), contact_scratch(INSIDE, 3), "step_inside", 1 << 31
    )
    own_speed, inner_speed = call(
        step_outside, [own, sums] + outside, (rows(32), rows(16)), contact_scratch(OUTSIDE, 3), "step_outside", 1 << 30
    )
    table = jax.ShapeDtypeStruct((64, 8 * S), BF16)
    inside_speed, outside_speed, weights = exchange(
        own_speed,
        inner_speed,
        4,
        False,
        lambda speed: call(
            functools.partial(field_own, grid),
            [own, speed],
            (
                rows(72),
                table,
                table,
                jax.ShapeDtypeStruct((64, nodes), BF16),
            ),
            own_scratch(9),
            "field_own",
            1 << 30,
        ),
    )
    sums, model = call(
        field_inside,
        [weights[0], coefficients.reshape(1, TERMS)] + inside + inside_speed,
        (rows(72), jax.ShapeDtypeStruct((1, TERMS), F32)),
        contact_scratch(INSIDE, 9),
        "field_inside",
        1 << 31,
    )
    force, partial = call(
        field_outside,
        [own, own_speed, sums] + outside + outside_speed + list(weights[1:4]),
        (rows(24), jax.ShapeDtypeStruct((16, nodes), F32)),
        [pltpu.VMEM((16, 8 * S), F32)] + contact_scratch(OUTSIDE, 9),
        "field_outside",
        1 << 30,
    )
    parts = summed_parts(partial, depth * cross, down)
    velocity_new, force_next, residual_field, gram_matrix, moment = pl.pallas_call(
        functools.partial(library_kernel, grid),
        out_shape=(
            vector_shape,
            vector_shape,
            jax.ShapeDtypeStruct((2, 2, 2), F32),
            jax.ShapeDtypeStruct((TERMS, TERMS), F32),
            jax.ShapeDtypeStruct((1, TERMS), F32),
        ),
        in_specs=[VMEM_SPEC] * (3 + len(parts)),
        out_specs=(VMEM_SPEC,) * 5,
        scratch_shapes=[pltpu.VMEM((TERMS, nodes), F32)],
        compiler_params=params,
        name="library",
    )(model, *parts, own_speed, force)
    return (velocity_new, force_next, residual_field, gram_matrix, moment.reshape(TERMS))


def solution(mesh):
    return jax.shard_map(
        body,
        mesh=mesh,
        in_specs=(
            P(None, ("groups", "down"), "cross", "depth", None),
            P(None, ("groups", "down"), "cross", "depth", None),
            P(("groups", "down"), "cross", "depth", None),
            P(("groups", "down"), "cross", "depth"),
            P(),
        ),
        out_specs=(
            P(None, ("groups", "down"), "cross", "depth", None),
            P(None, ("groups", "down"), "cross", "depth", None),
            P(("groups", "down"), "cross", "depth"),
            P("groups", None),
            P("groups"),
        ),
        check_vma=False,
    )
```

```python
import functools

import jax
import jax.numpy as jnp
from jax import lax
from jax.experimental import pallas as pl
from jax.experimental.pallas import tpu as pltpu
from jax.sharding import PartitionSpec as P

STIFFNESS = 100.0
DAMPING = 20.0
TIME_STEP = 0.05
KERNEL_WIDTH = 0.4
KERNEL_NORM = 64.0
SOFTENING = 0.0001
RADIUS_REF = 0.1
MASS_SHIFT = 0.1
DEAD = -1000.0
TERMS = 48
S = 128
SPREAD = 4
F32 = jnp.float32
BF16 = jnp.bfloat16
CELLS = tuple((a, b, z) for a in range(2) for b in range(2) for z in range(2))
PAIR_LIST = ((0, 0), (0, 1), (0, 2), (1, 1), (1, 2), (2, 2))
VMEM_SPEC = pl.BlockSpec(memory_space=pltpu.VMEM)
SMEM_SPEC = pl.BlockSpec(memory_space=pltpu.SMEM)
VMEM_LIMIT = 48 * 1024 * 1024


def row_ids(shape):
    return lax.broadcasted_iota(jnp.int32, shape, 0)


def lane_ids(shape):
    return lax.broadcasted_iota(jnp.int32, shape, 1)


def one_hot(condition):
    return jnp.where(condition, 1.0, 0.0).astype(BF16)


def split(value):
    high = value.astype(BF16)
    return high, value - high.astype(F32)


def matmul(left, right):
    return lax.dot_general(left, right, (((1,), (0,)), ((), ())), preferred_element_type=F32)


def matmul_turned(left, right):
    return lax.dot_general(left, right, (((1,), (1,)), ((), ())), preferred_element_type=F32)


def lane_gather(table, index):
    return jnp.take_along_axis(table, index, axis=1)


def pack_kernel(
    counts_hbm, positions_hbm, velocities_hbm, radii_hbm, own, inner, counts, positions, velocities, radii, arrived
):
    copies = [
        pltpu.make_async_copy(source, target, arrived.at[k])
        for k, (source, target) in enumerate(
            (
                (counts_hbm, counts),
                (positions_hbm, positions),
                (velocities_hbm, velocities),
                (radii_hbm, radii),
            )
        )
    ]
    for copy in copies:
        copy.start()
    for copy in copies:
        copy.wait()
    depth = lax.axis_index("depth")
    lanes = lane_ids((1, S))

    def layer(ref, at, z):
        rows = ref[at]
        return jnp.where(depth == z, rows[0:1], rows[1:2])

    for c, (a, b, z) in enumerate(CELLS):
        for k in range(3):
            own[c * 8 + k : c * 8 + k + 1, :] = layer(positions, (k, a, b), z)
            own[c * 8 + 3 + k : c * 8 + 4 + k, :] = layer(velocities, (k, a, b), z)
        count = jnp.where(depth == z, counts[a, b, 0], counts[a, b, 1])
        own[c * 8 + 6 : c * 8 + 7, :] = jnp.where(lanes < count, layer(radii, (a, b), z), DEAD)
        own[c * 8 + 7 : c * 8 + 8, :] = jnp.zeros((1, S), F32)
    for column in range(4):
        inner[column * 8 : column * 8 + 8, :] = own[column * 16 + 8 : column * 16 + 16, :]


def local_state(raw, centre):
    rows = row_ids(raw.shape)
    shift = jnp.where(rows == 0, centre[0], jnp.where(rows == 1, centre[1], centre[2]))
    return jnp.where(rows < 3, raw + shift, jnp.where(rows < 6, DAMPING * raw, raw))


def plane_reader(refs, height):
    own, depth_halo, sides = refs[0], refs[1], refs[2:]

    def read(ref, cell):
        return ref[cell * height : cell * height + height, :]

    def cell(x, y, slot):
        a = x - 1
        if y in (1, 2):
            return read(own, a * 4 + (y - 1) * 2 + slot) if slot < 2 else read(depth_halo, a * 2 + y - 1)
        if len(sides) == 4:
            before, after, diag_before, diag_after = sides
            if slot < 2:
                return read(before if y == 0 else after, a * 2 + slot)
            return read(diag_before if y == 0 else diag_after, a)
        b = 1 if y == 0 else 0
        if slot < 2:
            return read(sides[0], a * 4 + b * 2 + slot)
        return read(sides[0], 8 + a * 2 + b) if len(sides) == 1 else read(sides[1], a * 2 + b)

    return cell


def down_reader(refs, height):
    even = lax.rem(lax.axis_index("down"), 2) == 0
    swapped = lax.axis_size("down") % 2 == 0

    def cell(x, y, slot):
        if y in (1, 2):
            place = (y - 1) * 2 + slot if slot < 2 else 4 + y - 1
        else:
            side = 0 if y == 0 else 1
            place = 6 + side * 2 + slot if slot < 2 else 10 + side
        one, two = (ref[place * height : place * height + height, :] for ref in refs)
        if swapped:
            return jnp.where(even, one, two) if x == 0 else jnp.where(even, two, one)
        return one if x == 0 else two

    return cell


def centre_of(x, y, slot, depth):
    side = 0.5 - depth.astype(F32)
    return (x - 1.5, y - 1.5, (-1.0, 1.0, 3.0)[slot] * side)


BLOCK = tuple((x, y, slot) for x in (1, 2) for y in (1, 2) for slot in (0, 1))
PLANE = tuple(
    (x, y, slot) for x in (1, 2) for y in range(4) for slot in range(3) if (x, y, slot) not in BLOCK
)
INSIDE = tuple((x, y, slot) for x in (1, 2) for y in range(4) for slot in range(3))
OUTSIDE = tuple((x, y, slot) for x in (0, 3) for y in range(4) for slot in range(3))


def stepped_state(old, speed, centre):
    rows = row_ids((3, S))
    shift = jnp.where(rows == 0, centre[0], jnp.where(rows == 1, centre[1], centre[2]))
    return (old[0:3] + TIME_STEP * speed[0:3]) + shift, DAMPING * speed[0:3], old[6:8]


def contact_scratch(cells, width):
    rows = len(cells)
    return [
        pltpu.VMEM((rows * 8, S), F32),
        pltpu.VMEM((8 * 8, S), F32),
        pltpu.VMEM((8 * rows, S), jnp.int32),
        pltpu.VMEM((8 * rows, S), jnp.int32),
        pltpu.VMEM((8 * rows, S), jnp.int32),
        pltpu.VMEM((8 * rows, S), jnp.int32),
        pltpu.VMEM((18 * 8 * S, 32), F32),
        pltpu.VMEM((width * 8 * 8, S), F32),
    ]


def store_listed(list_ref, t, c, chunk, tile):
    high = tile.astype(BF16).astype(F32)
    rest = tile - high
    middle = rest.astype(BF16).astype(F32)
    turned = jnp.transpose(jnp.concatenate([high, middle, rest - middle, tile], axis=0))
    for part in range(S // chunk):
        start = pl.multiple_of(t * (8 * S) + (part * 8 + c) * chunk, chunk)
        list_ref[pl.ds(start, chunk), :] = turned[part * chunk : (part + 1) * chunk]


def pair_step(width, chunk, mine_ref, list_ref, sum_ref):
    selector = jnp.logical_and(
        row_ids((32, SPREAD * S)) % 8 == lane_ids((32, SPREAD * S)) // S, row_ids((32, SPREAD * S)) < 24
    )
    selector = one_hot(selector)

    def one_step(step, carry):
        every = list_ref[pl.ds(pl.multiple_of(step * (8 * chunk), 8 * chunk), 8 * chunk), :]
        spread = matmul(every.astype(BF16), selector)
        for c in range(8):
            listed = every[c * chunk : (c + 1) * chunk]
            me = [jnp.broadcast_to(mine_ref[c * 8 + k : c * 8 + k + 1, :], (8, S)) for k in range(7)]
            added = [None] * width
            for block in range(chunk // 8):
                row = c * chunk + block * 8
                other = [spread[row : row + 8, k * S : (k + 1) * S] for k in range(SPREAD)]
                other += [
                    jnp.broadcast_to(listed[block * 8 : block * 8 + 8, 24 + k : 25 + k], (8, S))
                    for k in range(SPREAD, 7)
                ]
                r = [me[k] - other[k] for k in range(3)]
                u = [me[3 + k] - other[3 + k] for k in range(3)]
                squared = r[0] * r[0] + r[1] * r[1] + r[2] * r[2] + SOFTENING
                inverse = lax.rsqrt(squared)
                along = u[0] * r[0] + u[1] * r[1] + u[2] * r[2]
                overlap = jnp.maximum((me[6] + other[6]) * inverse - 1.0, 0.0)
                weight = overlap * (STIFFNESS - along * inverse)
                terms = [weight * r[k] for k in range(3)]
                if width == 9:
                    terms += [terms[left] * r[right] for left, right in PAIR_LIST]
                added = [
                    term if total is None else total + term for total, term in zip(added, terms)
                ]
            for k in range(width):
                row = (k * 8 + c) * 8
                sum_ref[row : row + 8, :] += added[k]
        return carry

    return one_step


def collected(width, sum_ref):
    out = []
    for k in range(width):
        parts = [sum_ref[pl.ds(k * 64 + sub, 8, stride=8), :] for sub in range(8)]
        while len(parts) > 1:
            parts = [parts[i] + parts[i + 1] for i in range(0, len(parts), 2)]
        out.append(parts[0])
    return jnp.concatenate(out, axis=0)


def contact_sums(cells, width, chunk, scratch, skip_own=False):
    local_ref, mine_ref, index_ref, base_ref, amount_ref, chosen_ref, list_ref, sum_ref = scratch
    count = len(cells)
    span = 16 if cells == OUTSIDE else count

    def first_row(a):
        return 8 if cells == OUTSIDE and a == 1 else 0

    def beside(a, b, z):
        return [
            n
            for n, (x, y, slot) in enumerate(cells)
            if abs(x - 1 - a) <= 1 and abs(y - 1 - b) <= 1 and abs(slot - z) <= 1
            and not (skip_own and (x, y, slot) == (a + 1, b + 1, z))
        ]

    sum_ref[...] = jnp.zeros((width * 64, S), F32)
    place = [local_ref[pl.ds(k, count, stride=8), :] for k in range(3)]
    radius = local_ref[pl.ds(6, count, stride=8), :]
    rows = row_ids((count, S))
    masks = []
    for c, (a, b, z) in enumerate(CELLS):
        mine = mine_ref[c * 8 : c * 8 + 8, :]
        live = mine[6:7] > 0.0
        low = jnp.min(jnp.where(live, mine, 1e9), axis=1, keepdims=True)
        high = jnp.max(jnp.where(live, mine, -1e9), axis=1, keepdims=True)
        part = slice(first_row(a), first_row(a) + span)
        reach = radius[part] + high[6:7]
        near = reach > 0.0
        inside = set(beside(a, b, z))
        for n in range(part.start, part.stop):
            if n not in inside:
                near = jnp.logical_and(near, rows[part] != n)
        for k in range(3):
            near = jnp.logical_and(near, place[k][part] + reach > low[k : k + 1])
            near = jnp.logical_and(near, place[k][part] - reach < high[k : k + 1])
        masks.append(jnp.where(near, 1.0, 0.0).astype(F32))
    mask = jnp.concatenate(masks, axis=0).astype(BF16)
    upper = one_hot(row_ids((S, 2 * S)) <= lane_ids((S, 2 * S)))
    sums = matmul(mask, upper)
    prefix, amount = sums[:, :S], sums[:, S:]
    before = one_hot(lane_ids((span, span)) < row_ids((span, span)))
    total = None
    for c in range(8):
        part = amount[c * span : (c + 1) * span]
        base = matmul(before, part.astype(BF16))
        base_ref[c * span : (c + 1) * span, :] = base.astype(jnp.int32)
        listed = base[span - 1 : span] + part[span - 1 : span]
        total = listed if total is None else jnp.maximum(total, listed)
    most = total.astype(jnp.int32)[0, 0]
    amount_ref[0 : 8 * span, :] = amount.astype(jnp.int32)
    wanted = lane_ids((8 * span, S)).astype(F32)
    index = jnp.zeros((8 * span, S), jnp.int32)
    for step, probes in ((32, 3), (8, 3), (2, 3), (1, 1)) if cells == OUTSIDE else (
        (64, 1), (32, 1), (16, 1), (8, 1), (4, 1), (2, 1), (1, 1)
    ):
        passed = [
            lane_gather(prefix, index + (step * k + step - 1)) <= wanted for k in range(probes)
        ]
        for below in passed:
            index = jnp.where(below, index + step, index)
    index_ref[0 : 8 * span, :] = index
    empty = jnp.where(row_ids((8, S)) == 6, DEAD, 0.0).astype(F32)

    def gather_tiles(t, carry):
        want = t * S + lane_ids((8 * span, S)) - base_ref[0 : 8 * span, :]
        valid = jnp.logical_and(want >= 0, want < amount_ref[0 : 8 * span, :])
        source = lane_gather(index_ref[0 : 8 * span, :], jnp.clip(want, 0, S - 1))
        chosen_ref[0 : 8 * span, :] = jnp.where(valid, source, -1)
        for c, (a, b, z) in enumerate(CELLS):
            tile = empty
            for n in beside(a, b, z):
                row = c * span + n - first_row(a)
                pick = jnp.broadcast_to(chosen_ref[row : row + 1, :], (8, S))
                values = lane_gather(local_ref[n * 8 : n * 8 + 8, :], jnp.maximum(pick, 0))
                tile = jnp.where(pick >= 0, values, tile)
            store_listed(list_ref, t, c, chunk, tile)
        return carry

    gather_tiles(0, 0)
    lax.fori_loop(1, (most + (S - 1)) // S, gather_tiles, 0)

    lax.fori_loop(
        0, (most + (chunk - 1)) // chunk, pair_step(width, chunk, mine_ref, list_ref, sum_ref), 0
    )
    return collected(width, sum_ref)


def own_sums(width, scratch):
    mine_ref, list_ref, sum_ref = scratch
    sum_ref[...] = jnp.zeros((width * 64, S), F32)
    for c in range(8):
        store_listed(list_ref, 0, c, 64, mine_ref[c * 8 : c * 8 + 8, :])
    step = pair_step(width, 64, mine_ref, list_ref, sum_ref)
    for part in range(2):
        step(part, 0)
    return collected(width, sum_ref)


def mass_of(radius):
    scaled = radius / RADIUS_REF
    return scaled * scaled * scaled


def fill_start(cells, read, own, depth, scratch):
    for n, (x, y, slot) in enumerate(cells):
        scratch[0][n * 8 : n * 8 + 8, :] = local_state(read(x, y, slot), centre_of(x, y, slot, depth))
    for c, (a, b, z) in enumerate(CELLS):
        scratch[1][c * 8 : c * 8 + 8, :] = local_state(
            own[c * 8 : c * 8 + 8, :], centre_of(a + 1, b + 1, z, depth)
        )


def place_state(ref, start, state):
    ref[start : start + 3, :] = state[0]
    ref[start + 3 : start + 6, :] = state[1]
    ref[start + 6 : start + 8, :] = state[2]


def fill_stepped(cells, read, speed, own, own_speed, depth, scratch):
    for n, (x, y, slot) in enumerate(cells):
        state = stepped_state(read(x, y, slot), speed(x, y, slot), centre_of(x, y, slot, depth))
        place_state(scratch[0], n * 8, state)
    for c, (a, b, z) in enumerate(CELLS):
        state = stepped_state(
            own[c * 8 : c * 8 + 8, :],
            own_speed[c * 4 : c * 4 + 4, :],
            centre_of(a + 1, b + 1, z, depth),
        )
        place_state(scratch[1], c * 8, state)


def step_own(own, sums_out, *scratch):
    depth = lax.axis_index("depth")
    for c, (a, b, z) in enumerate(CELLS):
        scratch[0][c * 8 : c * 8 + 8, :] = local_state(
            own[c * 8 : c * 8 + 8, :], centre_of(a + 1, b + 1, z, depth)
        )
    sums_out[...] = own_sums(3, scratch)


def step_inside(sums_in, *refs):
    pieces, sums_out, scratch = refs[:-9], refs[-9], refs[-8:]
    fill_start(INSIDE, plane_reader(pieces, 8), pieces[0], lax.axis_index("depth"), scratch)
    sums_out[...] = sums_in[...] + contact_sums(INSIDE, 3, 64, scratch, True)


def step_outside(own, sums_in, far, near, own_out, inner_out, *scratch):
    fill_start(OUTSIDE, down_reader((far, near), 8), own, lax.axis_index("depth"), scratch)
    sums = sums_in[...] + contact_sums(OUTSIDE, 3, 64, scratch)
    radius = own[pl.ds(6, 8, stride=8), :]
    safe_mass = jnp.where(radius > 0.0, mass_of(radius), 1.0)
    for k in range(3):
        velocity = own[pl.ds(3 + k, 8, stride=8), :] + TIME_STEP * sums[k * 8 : k * 8 + 8] / safe_mass
        for c in range(8):
            own_out[c * 4 + k : c * 4 + k + 1, :] = velocity[c : c + 1]
    for c in range(8):
        own_out[c * 4 + 3 : c * 4 + 4, :] = jnp.zeros((1, S), F32)
    for column in range(4):
        inner_out[column * 4 : column * 4 + 4, :] = own_out[column * 8 + 4 : column * 8 + 8, :]


def field_own(
    grid, own, own_speed, sums_out, high_out, low_out, chosen_out, *scratch
):
    depth = lax.axis_index("depth")
    down = lax.axis_index("down")
    cross = lax.axis_index("cross")
    rows = row_ids((64, S))
    near_x, near_y, near_z = rows // 16 - 1, (rows // 4) % 4 - 1, rows % 4 - 1
    centres = [index.astype(F32) - 0.5 for index in (near_x, near_y, near_z)]
    kernels = []
    for c, (a, b, z) in enumerate(CELLS):
        state = stepped_state(
            own[c * 8 : c * 8 + 8, :],
            own_speed[c * 4 : c * 4 + 4, :],
            centre_of(a + 1, b + 1, z, depth),
        )
        place = state[0]
        place_state(scratch[0], c * 8, state)
        squared = jnp.zeros((64, S), F32)
        for k in range(3):
            gap = place[k : k + 1] - centres[k]
            squared = squared + gap * gap
        kernel = jnp.exp(squared * (-0.5 / (KERNEL_WIDTH * KERNEL_WIDTH))) / KERNEL_NORM
        beside = jnp.logical_and(
            jnp.logical_and(jnp.abs(near_x - a) <= 1, jnp.abs(near_y - b) <= 1),
            jnp.abs(near_z - jnp.where(depth == z, 0, 1)) <= 1,
        )
        kernels.append(jnp.where(beside, kernel, 0.0))
    kernel_high, kernel_low = split(jnp.concatenate(kernels, axis=1))
    high_out[...] = kernel_high
    low_out[...] = kernel_low.astype(BF16)
    size_x, size_y, size_z = grid
    nodes = size_x * size_y * size_z
    lanes = lane_ids((64, nodes))
    row = row_ids((64, nodes))
    target_x = (down * 2 + row // 16 - 1 + size_x) % size_x
    target_y = (cross * 2 + (row // 4) % 4 - 1 + size_y) % size_y
    target_z = depth * 2 + row % 4 - 1
    inside = jnp.logical_and(target_z >= 0, target_z < size_z)
    target = (target_x * size_y + target_y) * size_z + target_z
    sums_out[...] = own_sums(9, scratch)
    chosen_out[...] = one_hot(jnp.logical_and(inside, lanes == target))


def field_inside(sums_in, coefficients, *refs):
    split_at = (len(refs) - 10) // 2
    pieces, speeds, scratch = refs[:split_at], refs[split_at:-10], refs[-8:]
    sums_out, model_out = refs[-10:-8]
    model_out[...] = coefficients[...]
    read, speed = plane_reader(pieces, 8), plane_reader(speeds, 4)
    fill_stepped(INSIDE, read, speed, pieces[0], speeds[0], lax.axis_index("depth"), scratch)
    sums_out[...] = sums_in[...] + contact_sums(INSIDE, 9, 64, scratch, True)


def field_outside(
    own, own_speed, sums_in, far_old, near_old, far_speed, near_speed, kernel_high, kernel_low, chosen,
    force_out, node_out, moment_ref, *scratch
):
    depth = lax.axis_index("depth")
    read, speed = down_reader((far_old, near_old), 8), down_reader((far_speed, near_speed), 4)
    fill_stepped(OUTSIDE, read, speed, own, own_speed, depth, scratch)
    sums = sums_in[...] + contact_sums(OUTSIDE, 9, 64, scratch)
    force_out[...] = sums[0:24]
    radius = own[pl.ds(6, 8, stride=8), :]
    mass = jnp.where(radius > 0.0, mass_of(radius), 0.0)
    moments = [mass] + [mass * own_speed[pl.ds(k, 8, stride=4), :] for k in range(3)]
    moments += [0.5 * sums[k * 8 : k * 8 + 8] for k in range(3, 9)]
    moment_ref[...] = jnp.zeros((16, 8 * S), F32)
    for m, moment in enumerate(moments):
        for c in range(8):
            moment_ref[m : m + 1, c * S : (c + 1) * S] = moment[c : c + 1]
    moment_high, moment_low = split(moment_ref[...])
    wide_part = matmul_turned(
        jnp.concatenate([moment_high, moment_low.astype(BF16)], axis=0), kernel_high[...]
    )
    near = wide_part[0:16] + wide_part[16:32] + matmul_turned(moment_high, kernel_low[...])
    near_high, rest = split(near)
    near_middle, near_low = split(rest)
    placed = matmul(
        jnp.concatenate([near_high, near_middle, near_low.astype(BF16)], axis=0), chosen[...]
    )
    node_out[...] = placed[0:16] + placed[16:32] + placed[32:48]


def library_kernel(grid, coefficients, *refs):
    fields = tree_sum([ref[...] for ref in refs[:-8]])
    speed, force, velocity_out, force_out, residual_out, gram_out, moment_out, terms = refs[-8:]
    flat = lax.axis_index("depth") == 0
    for k in range(3):
        for a in range(2):
            for b in range(2):
                c = a * 4 + b * 2
                layers = [speed[(c + z) * 4 + k : (c + z) * 4 + k + 1, :] for z in range(2)]
                pulls = [force[k * 8 + c + z : k * 8 + c + z + 1, :] for z in range(2)]
                for z in range(2):
                    velocity_out[k, a, b, z : z + 1, :] = jnp.where(flat, layers[z], layers[1 - z])
                    force_out[k, a, b, z : z + 1, :] = jnp.where(flat, pulls[z], pulls[1 - z])
    size_x, size_y, size_z = grid
    nodes = size_x * size_y * size_z
    lanes = lax.broadcasted_iota(jnp.int32, (1, nodes), 1)
    node_x = lanes // (size_y * size_z)
    node_y = (lanes // size_z) % size_y
    node_z = lanes % size_z
    rows = row_ids((8, nodes))
    density = fields[0:1]
    values = jnp.where(rows == 0, fields[0:8], fields[0:8] / (density + MASS_SHIFT))

    def moved(value, step):
        return pltpu.roll(value, step % nodes, 1)

    plane = size_y * size_z
    slope_x = (moved(values, -plane) - moved(values, plane)) * 0.5
    after_y = jnp.where(
        node_y == size_y - 1, moved(values, (size_y - 1) * size_z), moved(values, -size_z)
    )
    before_y = jnp.where(
        node_y == 0, moved(values, -(size_y - 1) * size_z), moved(values, size_z)
    )
    slope_y = (after_y - before_y) * 0.5
    after_z = jnp.where(node_z == size_z - 1, 0.0, moved(values, -1))
    before_z = jnp.where(node_z == 0, 0.0, moved(values, 1))
    slope_z = (after_z - before_z) * 0.5
    slopes = [[table[k : k + 1] for k in range(4)] for table in (slope_x, slope_y, slope_z)]
    strain = [
        [0.5 * (slopes[left][1 + right] + slopes[right][1 + left]) for right in range(3)]
        for left in range(3)
    ]
    divergence = strain[0][0] + strain[1][1] + strain[2][2]
    rate_sum = jnp.zeros_like(density)
    for left in range(3):
        for right in range(3):
            entry = strain[left][right]
            if left == right:
                entry = entry - divergence / 3.0
            rate_sum = rate_sum + entry * entry
    shear_rate = jnp.sqrt(2.0 * rate_sum + 0.01)
    stress = [fields[4 + k : 5 + k] for k in range(6)]
    pressure = (stress[0] + stress[3] + stress[5]) / 3.0
    deviator = (
        (stress[0] - pressure) ** 2
        + (stress[3] - pressure) ** 2
        + (stress[5] - pressure) ** 2
        + 2.0 * (stress[1] ** 2 + stress[2] ** 2 + stress[4] ** 2)
    )
    shear_stress = jnp.sqrt(0.5 * deviator + 0.01)
    pressure_scale = jnp.sqrt(pressure * pressure + 1.0)
    friction = shear_stress / pressure_scale
    features = [
        density,
        pressure / pressure_scale,
        shear_rate,
        shear_rate / jnp.sqrt(pressure_scale),
        divergence,
        slopes[0][0],
        slopes[1][0],
        slopes[2][0],
    ]
    entries = list(features)
    for left in range(8):
        for right in range(left, 8):
            entries.append(features[left] * features[right])
    for left in range(1, 5):
        entries.append(features[left] * features[left] * features[left])
    for k, entry in enumerate(entries):
        terms[k : k + 1, :] = entry
    table = terms[...]
    model = lax.dot_general(
        jnp.broadcast_to(coefficients[...], (8, TERMS)),
        table,
        (((1,), (0,)), ((), ())),
        precision=lax.Precision.HIGHEST,
        preferred_element_type=F32,
    )
    residual = friction - model[0:1]
    gram_out[...] = (
        lax.dot_general(
            table,
            table,
            (((1,), (1,)), ((), ())),
            precision=lax.Precision.HIGHEST,
            preferred_element_type=F32,
        )
        / nodes
    )
    moment = lax.dot_general(
        jnp.broadcast_to(friction, (8, nodes)),
        table,
        (((1,), (1,)), ((), ())),
        precision=lax.Precision.HIGHEST,
        preferred_element_type=F32,
    )
    moment_out[...] = moment[0:1] / nodes
    down = lax.axis_index("down")
    cross = lax.axis_index("cross")
    depth = lax.axis_index("depth")
    b_rows = lax.broadcasted_iota(jnp.int32, (2, 1), 0)
    z_lanes = lax.broadcasted_iota(jnp.int32, (2, 2), 1)
    for a in range(2):
        mine = jnp.logical_and(node_x == down * 2 + a, node_y == cross * 2 + b_rows)
        column = [
            jnp.sum(
                jnp.where(jnp.logical_and(mine, node_z == depth * 2 + z), residual, 0.0),
                axis=1,
                keepdims=True,
            )
            for z in range(2)
        ]
        residual_out[a] = jnp.where(z_lanes == 0, column[0], column[1])


def ring(axis, step):
    peers = lax.axis_size(axis)
    return [(i, (i + step) % peers) for i in range(peers)]


def exchange(own, inner, height, joined, beside=None):
    cross = lax.axis_size("cross")

    def cells(block, first, count):
        return block[first * height : (first + count) * height]

    if cross == 2 and not joined:
        side = lax.ppermute(own, "cross", [(0, 1), (1, 0)])
    depth_halo = lax.ppermute(inner, "depth", [(0, 1), (1, 0)])
    if cross == 2:
        if joined:
            side = lax.ppermute(
                jnp.concatenate([own, depth_halo], axis=0), "cross", [(0, 1), (1, 0)]
            )
            diag = cells(side, 8, 4)
            sides = [side]
        else:
            diag = lax.ppermute(inner, ("cross", "depth"), [(i, 3 - i) for i in range(4)])
            sides = [side, diag]

        def lateral(x):
            return [
                cells(side, x * 4 + 2, 2),
                cells(side, x * 4, 2),
                cells(diag, x * 2 + 1, 1),
                cells(diag, x * 2, 1),
            ]

    else:
        pairs = [(i * 2 + j, ((i + 1) % cross) * 2 + 1 - j) for i in range(cross) for j in range(2)]
        back = [(i * 2 + j, ((i - 1) % cross) * 2 + 1 - j) for i in range(cross) for j in range(2)]
        last = jnp.concatenate([cells(own, 2, 2), cells(own, 6, 2)], axis=0)
        first = jnp.concatenate([cells(own, 0, 2), cells(own, 4, 2)], axis=0)
        last_inner = jnp.concatenate([cells(inner, 1, 1), cells(inner, 3, 1)], axis=0)
        first_inner = jnp.concatenate([cells(inner, 0, 1), cells(inner, 2, 1)], axis=0)
        before = lax.ppermute(last, "cross", ring("cross", 1))
        after = lax.ppermute(first, "cross", ring("cross", -1))
        diag_before = lax.ppermute(last_inner, ("cross", "depth"), pairs)
        diag_after = lax.ppermute(first_inner, ("cross", "depth"), back)
        sides = [before, after, diag_before, diag_after]

        def lateral(x):
            return [
                cells(before, x * 2, 2),
                cells(after, x * 2, 2),
                cells(diag_before, x, 1),
                cells(diag_after, x, 1),
            ]

    def face(x):
        return jnp.concatenate([cells(own, x * 4, 4), cells(depth_halo, x * 2, 2)] + lateral(x), axis=0)

    downs = lax.axis_size("down")
    last, first = face(1), face(0)
    if beside is not None:
        mine, depth_halo = lax.optimization_barrier((own, depth_halo))
        last, first, result = lax.optimization_barrier((last, first, beside(mine)))
    if downs % 2 == 0:
        even = lax.rem(lax.axis_index("down"), 2) == 0
        near = [(i, i ^ 1) for i in range(downs)]
        far = [(i, (i - 1 + 2 * (i % 2)) % downs) for i in range(downs)]
        outside = [
            lax.ppermute(jnp.where(even, first, last), "down", far),
            lax.ppermute(jnp.where(even, last, first), "down", near),
        ]
    else:
        outside = [
            lax.ppermute(last, "down", ring("down", 1)),
            lax.ppermute(first, "down", ring("down", -1)),
        ]
    if beside is not None:
        return [own, depth_halo] + sides, outside, result
    return [own, depth_halo] + sides, outside


def summed_parts(value, fast, slow):
    total = fast * slow
    near = [1 << k for k in range(fast.bit_length() - 1)][::-1]
    far = [fast << k for k in range(slow.bit_length() - 1)]
    if 1 << (len(near) + len(far)) != total:
        return [lax.psum(value, ("down", "cross", "depth"))]
    parts = [value]
    for k in range(max(len(near), len(far))):
        value = tree_sum(parts)
        masks = near[k : k + 1] + far[k : k + 1]
        if len(masks) == 2:
            masks.append(masks[0] ^ masks[1])
        parts = [value] + [
            lax.ppermute(value, ("down", "cross", "depth"), [(i, i ^ mask) for i in range(total)])
            for mask in masks
        ]
    return parts


def tree_sum(parts):
    while len(parts) > 1:
        parts = [parts[k] + parts[k + 1] for k in range(0, len(parts), 2)]
    return parts[0]


def body(positions, velocities, sphere_radii, counts, coefficients):
    down, cross, depth = (lax.axis_size(name) for name in ("down", "cross", "depth"))
    grid = (2 * down, 2 * cross, 2 * depth)
    nodes = grid[0] * grid[1] * grid[2]
    params = pltpu.CompilerParams(vmem_limit_bytes=VMEM_LIMIT)
    vector_shape = jax.ShapeDtypeStruct((3, 2, 2, 2, S), F32)

    def rows(count):
        return jax.ShapeDtypeStruct((count, S), F32)

    def call(kernel, inputs, outputs, scratch, name, vectors=0):
        return pl.pallas_call(
            kernel,
            out_shape=outputs,
            in_specs=[VMEM_SPEC] * len(inputs),
            out_specs=jax.tree.map(lambda _: VMEM_SPEC, outputs),
            scratch_shapes=scratch,
            compiler_params=params,
            cost_estimate=pl.CostEstimate(flops=vectors, bytes_accessed=1 << 20, transcendentals=0),
            name=name,
        )(*inputs)

    own, inner = pl.pallas_call(
        pack_kernel,
        out_shape=(rows(64), rows(32)),
        in_specs=[pl.BlockSpec(memory_space=pl.ANY)] * 4,
        out_specs=(VMEM_SPEC, VMEM_SPEC),
        scratch_shapes=[
            pltpu.SMEM((2, 2, 2), jnp.int32),
            pltpu.VMEM((3, 2, 2, 2, S), F32),
            pltpu.VMEM((3, 2, 2, 2, S), F32),
            pltpu.VMEM((2, 2, 2, S), F32),
            pltpu.SemaphoreType.DMA((4,)),
        ],
        compiler_params=pltpu.CompilerParams(vmem_limit_bytes=60 * 1024 * 1024),
        name="pack",
    )(counts, positions, velocities, sphere_radii)
    def own_scratch(width):
        return [
            pltpu.VMEM((8 * 8, S), F32),
            pltpu.VMEM((8 * S, 32), F32),
            pltpu.VMEM((width * 8 * 8, S), F32),
        ]

    inside, outside, sums = exchange(
        own,
        inner,
        8,
        True,
        lambda mine: call(step_own, [mine], rows(24), own_scratch(3), "step_own", 1 << 30),
    )
    sums = call(
        step_inside, [sums] + inside, rows(24), contact_scratch(INSIDE, 3), "step_inside", 1 << 31
    )
    own_speed, inner_speed = call(
        step_outside, [own, sums] + outside, (rows(32), rows(16)), contact_scratch(OUTSIDE, 3), "step_outside", 1 << 30
    )
    table = jax.ShapeDtypeStruct((64, 8 * S), BF16)
    inside_speed, outside_speed, weights = exchange(
        own_speed,
        inner_speed,
        4,
        False,
        lambda speed: call(
            functools.partial(field_own, grid),
            [own, speed],
            (
                rows(72),
                table,
                table,
                jax.ShapeDtypeStruct((64, nodes), BF16),
            ),
            own_scratch(9),
            "field_own",
            1 << 30,
        ),
    )
    sums, model = call(
        field_inside,
        [weights[0], coefficients.reshape(1, TERMS)] + inside + inside_speed,
        (rows(72), jax.ShapeDtypeStruct((1, TERMS), F32)),
        contact_scratch(INSIDE, 9),
        "field_inside",
        1 << 31,
    )
    force, partial = call(
        field_outside,
        [own, own_speed, sums] + outside + outside_speed + list(weights[1:4]),
        (rows(24), jax.ShapeDtypeStruct((16, nodes), F32)),
        [pltpu.VMEM((16, 8 * S), F32)] + contact_scratch(OUTSIDE, 9),
        "field_outside",
        1 << 30,
    )
    parts = summed_parts(partial, depth * cross, down)
    velocity_new, force_next, residual_field, gram_matrix, moment = pl.pallas_call(
        functools.partial(library_kernel, grid),
        out_shape=(
            vector_shape,
            vector_shape,
            jax.ShapeDtypeStruct((2, 2, 2), F32),
            jax.ShapeDtypeStruct((TERMS, TERMS), F32),
            jax.ShapeDtypeStruct((1, TERMS), F32),
        ),
        in_specs=[VMEM_SPEC] * (3 + len(parts)),
        out_specs=(VMEM_SPEC,) * 5,
        scratch_shapes=[pltpu.VMEM((TERMS, nodes), F32)],
        compiler_params=params,
        name="library",
    )(model, *parts, own_speed, force)
    return (velocity_new, force_next, residual_field, gram_matrix, moment.reshape(TERMS))


def solution(mesh):
    return jax.shard_map(
        body,
        mesh=mesh,
        in_specs=(
            P(None, ("groups", "down"), "cross", "depth", None),
            P(None, ("groups", "down"), "cross", "depth", None),
            P(("groups", "down"), "cross", "depth", None),
            P(("groups", "down"), "cross", "depth"),
            P(),
        ),
        out_specs=(
            P(None, ("groups", "down"), "cross", "depth", None),
            P(None, ("groups", "down"), "cross", "depth", None),
            P(("groups", "down"), "cross", "depth"),
            P("groups", None),
            P("groups"),
        ),
        check_vma=False,
    )
```
